32 devices in a mesh: stn: 2 (over core), tm: 8 (over z, x), ct: 2 (over y).
Axes of the slice: x: 2, y: 2, z: 4, core: 2. Of those that a mesh axis runs over, the one named last changes fastest.
Arguments:
- voltages: bfloat16 [2, 32, 524288], P(None, ('stn', 'ct'), 'tm'), may hold values from -128 to 127, as said below
- delays: int32 [32], P(('stn', 'ct')), may hold values from 0 to 4095
Outputs:
- visibilities: float32 [2, 4096, 32, 32], P(None, ('tm', 'ct'), 'stn')
The draws below stay inside these ranges and needn't reach their ends.
Inputs may be any that keep to these rules, and one draw needn't show every extreme that they name: `voltages`: every entry is a whole number.
All inputs are finite; a program needn't handle non-finite values.
Results may differ from the reference program's by a relative error of at most 0.0037.
Values may be sent and summed in bfloat16 or wider, within the bound.
No kernel may reach another device: no remote copies, remote signals or barrier semaphores. Data moves between devices by JAX's collectives and lax.ppermute only.
A program may use at most 128 MiB of HBM per device.

```python
import math
import jax
import jax.numpy as jnp
from jax import lax

CHANNELS = 4096
RADIX = 64
TAPS = 16
INPUTS = 32
FRAMES = 128
SAMPLES = 524288


def draw_voltages(key, part):
    values = jax.random.randint(key, (2, INPUTS, SAMPLES), -128, 128).astype(jnp.float32)
    return values.astype(jnp.bfloat16)


def draw_delays(key, part):
    values = jax.random.randint(key, (INPUTS,), 0, CHANNELS)
    where_top = jax.random.randint(jax.random.fold_in(key, 1), (), 0, INPUTS)
    step_off = jax.random.randint(jax.random.fold_in(key, 2), (), 1, INPUTS)
    where_low = (where_top + step_off) % INPUTS
    index = jnp.arange(INPUTS, dtype=jnp.int32)
    values = jnp.where(index == where_top, CHANNELS - 1, values)
    values = jnp.where(index == where_low, 0, values)
    return values.astype(jnp.int32)


def setup_inputs(seed: int = 0) -> dict:
    key_of = jax.random.split(jax.random.key(seed), 3)
    return {
        "voltages": draw_voltages(jax.random.fold_in(key_of[2], 71), 0),
        "delays": draw_delays(jax.random.fold_in(key_of[2], 71), 0),
    }


def filter_table():
    length = TAPS * CHANNELS
    index = jnp.arange(length, dtype=jnp.int32).astype(jnp.float32)
    centred = (index - length / 2) / CHANNELS
    window = 0.5 - 0.5 * jnp.cos(2.0 * math.pi * index / length)
    factor = 1.0 / (48.0 * math.sqrt(CHANNELS))
    return (jnp.sinc(centred) * window * factor).reshape(TAPS, CHANNELS)

def dft_block(radix):
    steps = jnp.arange(radix, dtype=jnp.int32)
    grid = steps[:, None] * steps[None, :] % radix
    angle = 2.0 * math.pi * grid.astype(jnp.float32) / radix
    cosine = jnp.cos(angle)
    sine = jnp.sin(angle)
    upper = jnp.concatenate([cosine, sine], axis=1)
    lower = jnp.concatenate([-sine, cosine], axis=1)
    return jnp.concatenate([upper, lower], axis=0).astype(jnp.bfloat16)

def twiddles():
    second = CHANNELS // RADIX
    rows = jnp.arange(second, dtype=jnp.int32)
    cols = jnp.arange(RADIX, dtype=jnp.int32)
    grid = rows[:, None] * cols[None, :] % CHANNELS
    angle = 2.0 * math.pi * grid.astype(jnp.float32) / CHANNELS
    return (jnp.cos(angle), jnp.sin(angle))

def filtered(framed, table):
    count = framed.shape[-2] - TAPS + 1
    total = jnp.zeros(framed.shape[:-2] + (count, CHANNELS), jnp.float32)
    for tap in range(TAPS):
        begin = TAPS - 1 - tap
        total = total + table[tap] * framed[..., begin:begin + count, :].astype(jnp.float32)
    return total.astype(jnp.bfloat16)

def transform(branches):
    second = CHANNELS // RADIX
    number = branches.shape[0]
    stacked = branches.reshape(number, 2 * second, RADIX).astype(jnp.float32)
    first_table = dft_block(second).astype(jnp.float32)
    inner = jnp.einsum('kj,nja->nka', first_table, stacked, precision=lax.Precision.HIGHEST)
    inner = inner.reshape(number, 2, second, RADIX)
    tw_cos, tw_sin = twiddles()
    real_part = inner[:, 0] * tw_cos + inner[:, 1] * tw_sin
    imag_part = inner[:, 1] * tw_cos - inner[:, 0] * tw_sin
    turned = jnp.stack([real_part, imag_part], axis=2).reshape(number, second, 2 * RADIX)
    turned = turned.astype(jnp.bfloat16).astype(jnp.float32)
    last_table = dft_block(RADIX).astype(jnp.float32)
    result = jnp.einsum('lj,nkj->nlk', last_table, turned, precision=lax.Precision.HIGHEST)
    return result.reshape(number, 2, CHANNELS).astype(jnp.bfloat16)

def one_input(pair):
    signal, offset = pair
    table = filter_table()
    padded = jnp.concatenate([jnp.zeros((2, TAPS * CHANNELS), jnp.bfloat16), signal], axis=1)
    span = (FRAMES + TAPS - 1) * CHANNELS
    shifted = lax.dynamic_slice_in_dim(padded, (CHANNELS - offset).astype(jnp.int32), span, 1)
    framed = shifted.reshape(2, FRAMES + TAPS - 1, CHANNELS)
    branches = jnp.moveaxis(filtered(framed, table), 0, 1)
    return transform(branches)

def reference(voltages, delays):
    spectra = lax.map(one_input, (jnp.moveaxis(voltages, 1, 0), delays))
    block = min(CHANNELS, 128)
    starts = jnp.arange(CHANNELS // block, dtype=jnp.int32) * block

    def block_vis(start):
        piece = lax.dynamic_slice_in_dim(spectra, start, block, 3).astype(jnp.float32)
        swapped = jnp.stack([piece[:, :, 1], -piece[:, :, 0]], axis=2)
        left = jnp.stack([piece, swapped], axis=0)
        summed = jnp.einsum('oafjc,bfjc->ocab', left, piece, precision=lax.Precision.HIGHEST)
        return summed * (1.0 / FRAMES)
    blocks = lax.map(block_vis, starts)
    return blocks.transpose(1, 0, 2, 3, 4).reshape(2, CHANNELS, INPUTS, INPUTS)
```

```python
import functools
import math

import jax
import jax.numpy as jnp
import numpy as np
from jax import lax
from jax.experimental import pallas as pl
from jax.experimental.pallas import tpu as pltpu
from jax.sharding import PartitionSpec as P

CHANNELS = 4096
RADIX = 64
TAPS = 16
LANES = 128
ROWS = CHANNELS // LANES
PAIR = 2
TILE = 4
CHUNKS = 2

VMEM = pl.BlockSpec(memory_space=pltpu.VMEM)
SMEM = pl.BlockSpec(memory_space=pltpu.SMEM)


def params(mib):
    return pltpu.CompilerParams(vmem_limit_bytes=mib * 2**20)


def cost(flops, size):
    return pl.CostEstimate(flops=flops, bytes_accessed=size, transcendentals=0)


def filter_table():
    length = TAPS * CHANNELS
    index = np.arange(length, dtype=np.float64)
    centred = (index - length / 2) / CHANNELS
    window = 0.5 - 0.5 * np.cos(2.0 * math.pi * index / length)
    factor = 1.0 / (48.0 * math.sqrt(CHANNELS))
    table = np.sinc(centred) * window * factor
    return table.reshape(TAPS, ROWS, LANES).astype(np.float32)


def dft_parts(radix):
    steps = np.arange(radix)
    angle = 2.0 * math.pi * (steps[:, None] * steps[None, :] % radix) / radix
    return np.cos(angle).astype(jnp.bfloat16), np.sin(angle).astype(jnp.bfloat16)


def first_table():
    cosine, sine = dft_parts(CHANNELS // RADIX)
    order = [2 * row + half for half in range(2) for row in range(ROWS)]
    cosine, sine = cosine[:, order], sine[:, order]
    upper = np.concatenate([cosine, sine], axis=1)
    lower = np.concatenate([-sine, cosine], axis=1)
    return np.concatenate([upper, lower], axis=0)


def last_table(outer, per_ct, span):
    cosine, sine = dft_parts(RADIX)
    blocks = []
    for g in range(PAIR):
        for ct in range(per_ct):
            steps = [
                ((o * PAIR + g) * per_ct + ct) * span + j for o in range(outer) for j in range(span)
            ]
            real = np.concatenate([cosine[steps], sine[steps]], axis=1)
            imag = np.concatenate([-sine[steps], cosine[steps]], axis=1)
            blocks.append(np.concatenate([real, imag], axis=0))
    return np.stack(blocks).reshape(PAIR, per_ct, -1, 2 * RADIX)


def twiddle_tables():
    rows = np.arange(CHANNELS // RADIX)
    cols = np.arange(RADIX)
    angle = 2.0 * math.pi * (rows[:, None] * cols[None, :] % CHANNELS) / CHANNELS
    cosine = np.cos(angle).astype(np.float32)
    sine = np.sin(angle).astype(np.float32)
    return np.concatenate([cosine, cosine], axis=1), np.concatenate([sine, sine], axis=1)


def filterbank_kernel(count, frames, dests, *refs):
    scal, keep, recv, halo, coef, first, tw_cos, tw_sin, last = refs[:9]
    outs = refs[9 : 9 + dests]
    samples, shifted, grouped = refs[9 + dests :]
    block_rows = frames * ROWS
    all_rows = (PAIR + 1) * block_rows
    first_row = (frames - (TAPS - 1)) * ROWS
    total = PAIR * frames
    me = scal[count]
    lane = lax.broadcasted_iota(jnp.int32, (1, LANES), 1)

    step = 8
    for source, place in ((halo, 0), (keep, 1 + me), (recv, 2 - me)):
        for part in range(2):

            def unpack(n, carry, source=source, place=place, part=part):
                wide = source[part, :, pl.ds(pl.multiple_of(n * step * LANES, step * LANES), step * LANES)]
                wide = wide.astype(jnp.float32)
                base = (part * all_rows + place * block_rows + n * step) * count
                for u in range(step):
                    at = pl.multiple_of(base + u * count, count)
                    samples[pl.ds(at, count), :] = wide[:, u * LANES : (u + 1) * LANES]
                return carry

            lax.fori_loop(0, block_rows // step, unpack, 0)

    kept_rows = all_rows - first_row
    high = lane < RADIX
    for item in range(count):
        delay = scal[item]
        down = delay // LANES
        across = delay % LANES
        inside = lane < LANES - across
        piece = ROWS
        for part in range(2):

            def shift(n, carry, part=part, item=item):
                row = part * all_rows + first_row + n * piece - down
                at = row * count + item
                here = samples[pl.ds(at, piece, stride=count), :]
                before = samples[pl.ds(at - count, piece, stride=count), :]
                moved = pltpu.roll(jnp.where(inside, here, before), across, 1)
                shifted[pl.ds(pl.multiple_of(part * kept_rows + n * piece, piece), piece), :] = moved
                return carry

            lax.fori_loop(0, kept_rows // piece, shift, 0)

        group = 4

        def filt(n, carry):
            base = n * group
            for band in range(ROWS // 16):
                sums = [[None] * group for _ in range(2)]
                for part in range(2):
                    values = []
                    for u in range(group + TAPS - 1):
                        at = part * kept_rows + (base + u) * ROWS + band * 16
                        values.append(shifted[pl.ds(pl.multiple_of(at, 16), 16), :])
                    for tap in range(TAPS):
                        weight = coef[tap, band * 16 : band * 16 + 16, :]
                        for u in range(group):
                            term = weight * values[u + TAPS - 1 - tap]
                            old = sums[part][u]
                            sums[part][u] = term if old is None else old + term
                for u in range(group):
                    real, imag = sums[0][u], sums[1][u]
                    real_turned = pltpu.roll(real, RADIX, 1)
                    imag_turned = pltpu.roll(imag, RADIX, 1)
                    parts = (
                        jnp.where(high, real, imag_turned),
                        jnp.where(high, real_turned, imag),
                        jnp.where(high, imag, -real_turned),
                        jnp.where(high, imag_turned, -real),
                    )
                    for index, value in enumerate(parts):
                        low = index * ROWS + band * 16
                        grouped[base + u, low : low + 16, :] = value.astype(jnp.bfloat16)
            return carry

        lax.fori_loop(0, total // group, filt, 0)

        def turn(n, carry, item=item):
            base = n * group
            wide = jnp.concatenate([grouped[base + u] for u in range(group)], axis=1)
            inner = jnp.dot(first[...], wide, preferred_element_type=jnp.float32)
            rows = []
            for u in range(group):
                cut = slice(u * LANES, (u + 1) * LANES)
                turned = inner[:RADIX, cut] * tw_cos[...] + inner[RADIX:, cut] * tw_sin[...]
                rows.append(turned.astype(jnp.bfloat16))
            inner = jnp.concatenate(rows, axis=0)
            result = lax.dot_general(
                last[...], inner, (((1,), (1,)), ((), ())), preferred_element_type=jnp.float32
            ).astype(jnp.bfloat16)
            size = result.shape[0] // (2 * dests)
            for dest in range(dests):
                for part in range(2):
                    low = (dest * 2 + part) * size
                    for u in range(group // 2):
                        outs[dest][item, n * (group // 2) + u, part] = result[
                            low : low + size, u * LANES : (u + 1) * LANES
                        ]
            return carry

        lax.fori_loop(0, total // group, turn, 0)


def filterbank(scal, keep, recv, halo, tables, last, dests):
    count = keep.shape[1]
    frames = keep.shape[2] // CHANNELS
    size = last.shape[0] // (2 * dests)
    all_rows = (PAIR + 1) * frames * ROWS
    kept_rows = (PAIR * frames + TAPS - 1) * ROWS
    shape = jax.ShapeDtypeStruct((count, PAIR * frames // 2, 2, size, LANES), jnp.bfloat16)
    return pl.pallas_call(
        functools.partial(filterbank_kernel, count, frames, dests),
        out_shape=[shape] * dests,
        in_specs=[SMEM] + [VMEM] * 8,
        out_specs=[VMEM] * dests,
        scratch_shapes=[
            pltpu.VMEM((2 * all_rows * count, LANES), jnp.float32),
            pltpu.VMEM((2 * kept_rows, LANES), jnp.float32),
            pltpu.VMEM((PAIR * frames, LANES, LANES), jnp.bfloat16),
        ],
        compiler_params=params(40),
        cost_estimate=cost(2 * 10**9, 8 * 2**20),
        name="filterbank",
    )(scal, keep, recv, halo, *tables, last)


def pair_blocks(own):
    tiles = own // TILE
    inside = [(i, j) for i in range(tiles) for j in range(i, tiles)]
    across = [(i, j) for i in range(tiles // 2) for j in range(tiles)]
    return inside, across


def correlate_kernel(layout, *refs):
    count, own, outer, span, pairs, blocks_in, blocks_all = layout
    sources, (place, starts, where_outer) = refs[: len(pairs)], refs[len(pairs) : len(pairs) + 3]
    rest = refs[len(pairs) + 3 :]
    outs, (spectra, sums) = rest[:-2], rest[-2:]
    halves = outer * span // 8
    pair_count = blocks_in[1], blocks_all
    steps = spectra.shape[1]

    for index, source in enumerate(sources):
        for item in range(count):

            def spread(n, carry, index=index, source=source, item=item):
                for part in range(2):
                    spectra[place[index] + item, n, part] = source[item, n, part].astype(jnp.float32)
                return carry

            lax.fori_loop(0, steps, spread, 0)

    lane = lax.broadcasted_iota(jnp.int32, (8, LANES), 1)
    high = lane < RADIX
    rows_outer = blocks_all * TILE * TILE * span

    def block(t, carry):
        left, right = starts[2 * t], starts[2 * t + 1]
        for half in range(halves):
            cut = slice(half * 8, half * 8 + 8)

            def frame(n, acc):
                a = [[spectra[left + p, n, part, cut, :] for part in range(2)] for p in range(TILE)]
                b = [[spectra[right + q, n, part, cut, :] for part in range(2)] for q in range(TILE)]
                new = []
                for p in range(TILE):
                    for q in range(TILE):
                        real, imag = acc[2 * (p * TILE + q)], acc[2 * (p * TILE + q) + 1]
                        real = real + a[p][0] * b[q][0] + a[p][1] * b[q][1]
                        imag = imag + a[p][1] * b[q][0] - a[p][0] * b[q][1]
                        new += [real, imag]
                return tuple(new)

            zero = jnp.zeros((8, LANES), jnp.float32)
            acc = lax.fori_loop(0, steps, frame, (zero,) * (2 * TILE * TILE))
            for p in range(TILE * TILE):
                real = acc[2 * p] + pltpu.roll(acc[2 * p], RADIX, 1)
                imag = acc[2 * p + 1] + pltpu.roll(acc[2 * p + 1], RADIX, 1)
                both = jnp.where(high, real, imag)
                for u in range(8 // span):
                    o = half * (8 // span) + u
                    at = o * rows_outer + (t * TILE * TILE + p) * span
                    sums[pl.ds(pl.multiple_of(at, span), span), :] = both[u * span : (u + 1) * span]
        return carry

    lax.fori_loop(0, blocks_all, block, 0)

    rows_in = blocks_in[0] * TILE * TILE * span
    for r in range(outer):
        base = lax.rem(where_outer[0] + r, outer) * rows_outer
        for low, high_row, out in ((0, rows_in, outs[2 * r]), (rows_in, rows_outer, outs[2 * r + 1])):
            at = pl.multiple_of(base + low, 16)
            out[...] = sums[pl.ds(at, high_row - low), :].astype(out.dtype)


def correlate(arrays, place, starts, where_outer, own, outer, span):
    count, steps, _, size, _ = arrays[0].shape
    inside, across = pair_blocks(own)
    total = len(inside) + len(across)
    rows = TILE * TILE * span
    shapes = []
    for r in range(outer):
        dtype = jnp.float32 if r == 0 else jnp.bfloat16
        shapes.append(jax.ShapeDtypeStruct((len(inside) * rows, LANES), dtype))
        shapes.append(jax.ShapeDtypeStruct((len(across) * rows, LANES), dtype))
    layout = (count, own, outer, span, tuple(range(len(arrays))), (len(inside), 0), total)
    return pl.pallas_call(
        functools.partial(correlate_kernel, layout),
        out_shape=shapes,
        in_specs=[VMEM] * len(arrays) + [SMEM] * 3,
        out_specs=[VMEM] * len(shapes),
        scratch_shapes=[
            pltpu.VMEM((2 * own, steps, 2, size, LANES), jnp.float32),
            pltpu.VMEM((outer * total * rows, LANES), jnp.float32),
        ],
        compiler_params=params(40),
        cost_estimate=cost(10**10, 16 * 2**20),
        name="correlate",
    )(*arrays, place, starts, where_outer)


def assemble_kernel(own, outer, span, scale, *refs):
    core = refs[0]
    mine_in = refs[1 : 1 + outer]
    mine_across = refs[1 + outer : 1 + 2 * outer]
    far_across = refs[1 + 2 * outer : 1 + 3 * outer]
    out, joined = refs[1 + 3 * outer :]
    inside, across = pair_blocks(own)
    rows = TILE * TILE * span
    lane = lax.broadcasted_iota(jnp.int32, (1, LANES), 1)
    high = lane < RADIX
    mirror = jnp.where(high, 1.0, -1.0).astype(jnp.float32)
    me = core[0]

    def added(sources, t):
        total = sources[0][t * rows : (t + 1) * rows, :].astype(jnp.float32)
        for source in sources[1:]:
            total = total + source[t * rows : (t + 1) * rows, :].astype(jnp.float32)
        return total * scale

    def put(value, row, col):
        at = pl.multiple_of((row * 2 * own + col) * span, span)
        joined[pl.ds(at, span), :] = value

    for t, (i, j) in enumerate(inside):
        total = added(mine_in, t)
        turned = total * mirror
        for p in range(TILE):
            for q in range(TILE):
                low = (p * TILE + q) * span
                a, b = i * TILE + p, j * TILE + q
                put(total[low : low + span], a, me * own + b)
                if i < j:
                    put(turned[low : low + span], b, me * own + a)
    sign = jnp.where(me == 0, jnp.ones_like(mirror), mirror)
    for sources, part in ((mine_across, me), (far_across, 1 - me)):
        for t, (i, j) in enumerate(across):
            total = added(sources, t) * sign
            for p in range(TILE):
                for q in range(TILE):
                    low = (p * TILE + q) * span
                    a = part * (own // 2) + i * TILE + p
                    b = j * TILE + q
                    row = jnp.where(me == 0, a, b)
                    col = jnp.where(me == 0, own + b, a)
                    put(total[low : low + span], row, col)

    def emit(a, carry):
        for tile in range(2 * own // 8):
            for pair in range(span // 2):
                loads = []
                for u in range(2):
                    at = (a * 2 * own + tile * 8) * span + pair * 2 + u
                    loads.append(joined[pl.ds(at, 8, stride=span), :])
                turned = [pltpu.roll(x, RADIX, 1) for x in loads]
                cut = slice(pair * LANES, (pair + 1) * LANES)
                out[0, a, tile * 8 : tile * 8 + 8, cut] = jnp.where(high, loads[0], turned[1])
                out[1, a, tile * 8 : tile * 8 + 8, cut] = jnp.where(high, turned[0], loads[1])
        return carry

    lax.fori_loop(0, own, emit, 0)


def assemble(core, mine_in, mine_across, far_across, own, span, scale):
    outer = len(mine_in)
    return pl.pallas_call(
        functools.partial(assemble_kernel, own, outer, span, scale),
        out_shape=jax.ShapeDtypeStruct((2, own, 2 * own, span * RADIX), jnp.float32),
        in_specs=[SMEM] + [VMEM] * (3 * outer),
        out_specs=VMEM,
        scratch_shapes=[pltpu.VMEM((own * 2 * own * span, LANES), jnp.float32)],
        compiler_params=params(24),
        cost_estimate=cost(10**8, 8 * 2**20),
        name="assemble",
    )(core, *mine_in, *mine_across, *far_across)


def fast_fits(in_count, frame_count):
    stn, tm, per_ct = (lax.axis_size(a) for a in ("stn", "tm", "ct"))
    groups = tm * per_ct
    if stn != 2 or tm % PAIR or in_count % (PAIR * CHUNKS) or RADIX % groups:
        return False
    outer, span = tm // PAIR, RADIX // groups
    own = in_count * per_ct
    return (
        frame_count >= TAPS
        and frame_count % 4 == 0
        and span in (2, 4, 8)
        and outer * span % 16 == 0
        and own % (2 * TILE) == 0
    )


def fast(voltages, delays):
    tm, per_ct = lax.axis_size("tm"), lax.axis_size("ct")
    in_count = voltages.shape[1]
    frame_count = voltages.shape[2] // CHANNELS
    outer = tm // PAIR
    span = RADIX // (tm * per_ct)
    own = in_count * per_ct
    half = in_count // PAIR
    part = half // CHUNKS
    place_tm, place_ct = lax.axis_index("tm"), lax.axis_index("ct")
    core = lax.axis_index("stn")
    g, o = place_tm % PAIR, place_tm // PAIR

    swap = [(i, i ^ 1) for i in range(tm)]
    onward = [(i, i + PAIR) for i in range(tm - PAIR)]
    cores = [(0, 1), (1, 0)]

    dests = [(dg, dc) for dg in range(PAIR) for dc in range(per_ct)]
    base = jnp.asarray(last_table(outer, per_ct, span))
    base = jnp.where(g == 0, base, base[::-1])
    base = lax.dynamic_slice_in_dim(jnp.concatenate([base, base], axis=1), place_ct, per_ct, 1)
    last = base.reshape(-1, 2 * RADIX)
    tables = [jnp.asarray(filter_table()), jnp.asarray(first_table())]
    tables += [jnp.asarray(t) for t in twiddle_tables()]

    def rows_of(start):
        return lax.dynamic_slice_in_dim(voltages, start, part, 1)

    keeps, recvs, halos = [], [], []
    for c in range(CHUNKS):
        keeps.append(rows_of(g * half + c * part))
        recvs.append(lax.ppermute(rows_of((1 - g) * half + c * part), "tm", swap))
    for c in range(CHUNKS):
        halos.append(lax.ppermute(jnp.where(g == 1, keeps[c], recvs[c]), "tm", onward))

    arrays, place = [], []
    for c in range(CHUNKS):
        offsets = lax.dynamic_slice_in_dim(delays, g * half + c * part, part, 0)
        scal = jnp.concatenate([offsets, g.astype(jnp.int32)[None]])
        spectra = filterbank(scal, keeps[c], recvs[c], halos[c], tables, last, len(dests))
        for (dg, dc), block in zip(dests, spectra):
            route = []
            for i in range(tm):
                for j in range(per_ct):
                    target = (i ^ dg) * per_ct + (j + dc) % per_ct
                    route.append((i * per_ct + j, target))
            if dg or dc:
                block = lax.ppermute(block, ("tm", "ct"), route)
            other = lax.ppermute(block, "stn", cores)
            start = ((place_ct - dc) % per_ct) * in_count + (g ^ dg) * half + c * part
            arrays += [block, other]
            place += [core * own + start, (1 - core) * own + start]

    inside, across = pair_blocks(own)
    starts = [core * own + TILE * s for block in inside for s in block]
    for i, j in across:
        starts += [core * (own // 2) + TILE * i, own + TILE * j]

    def stacked(values):
        return jnp.stack([jnp.asarray(v, jnp.int32) for v in values])

    parts = correlate(arrays, stacked(place), stacked(starts), stacked([o]), own, outer, span)
    mine_in, mine_across, far_across = [], [], []
    for r in range(outer):
        a, b = parts[2 * r], parts[2 * r + 1]
        if r:
            route = [(i, (i + r * PAIR) % tm) for i in range(tm)]
            a, b = lax.ppermute(a, "tm", route), lax.ppermute(b, "tm", route)
        mine_in.append(a)
        mine_across.append(b)
        far_across.append(lax.ppermute(b, "stn", cores))
    scale = 1.0 / (tm * frame_count)
    result = assemble(stacked([core]), mine_in, mine_across, far_across, own, span, scale)
    return result.transpose(0, 3, 1, 2)


def general(voltages, delays):
    in_count = voltages.shape[1]
    frame_count = voltages.shape[2] // CHANNELS
    route = [(i, i + 1) for i in range(lax.axis_size("tm") - 1)]
    extended = jnp.concatenate([lax.ppermute(voltages, "tm", route), voltages], axis=2)
    span = (frame_count + TAPS - 1) * CHANNELS
    shifted = jax.vmap(
        lambda row, offset: lax.dynamic_slice_in_dim(row, CHANNELS - offset, span, 1),
        in_axes=(1, 0),
        out_axes=1,
    )(extended, delays)
    framed = shifted.reshape(2, in_count, frame_count + TAPS - 1, CHANNELS)
    table = jnp.asarray(filter_table()).reshape(TAPS, CHANNELS)
    total = jnp.zeros((2, in_count, frame_count, CHANNELS), jnp.float32)
    for tap in range(TAPS):
        low = TAPS - 1 - tap
        total = total + table[tap] * framed[:, :, low : low + frame_count].astype(jnp.float32)
    branches = jnp.moveaxis(total.astype(jnp.bfloat16), 0, 2)

    number = in_count * frame_count
    cosine, sine = dft_parts(RADIX)
    block = np.concatenate(
        [np.concatenate([cosine, sine], axis=1), np.concatenate([-sine, cosine], axis=1)], axis=0
    )
    block = jnp.asarray(block)
    stacked = branches.reshape(number, 2 * RADIX, RADIX)
    inner = jnp.einsum("kj,nja->nka", block, stacked, preferred_element_type=jnp.float32)
    inner = inner.reshape(number, 2, RADIX, RADIX)
    tw_cos, tw_sin = (jnp.asarray(t[:, :RADIX]) for t in twiddle_tables())
    real = inner[:, 0] * tw_cos + inner[:, 1] * tw_sin
    imag = inner[:, 1] * tw_cos - inner[:, 0] * tw_sin
    turned = jnp.stack([real, imag], axis=2).reshape(number, RADIX, 2 * RADIX)
    turned = turned.astype(jnp.bfloat16)
    result = jnp.einsum("lj,nkj->nlk", block, turned, preferred_element_type=jnp.float32)
    spectra = result.reshape(in_count, frame_count, 2, CHANNELS).astype(jnp.bfloat16)
    moved = lax.all_to_all(spectra, "tm", split_axis=3, concat_axis=1, tiled=True)
    moved = lax.all_to_all(moved, "ct", split_axis=3, concat_axis=0, tiled=True)
    local = moved.transpose(3, 2, 0, 1)
    swapped = jnp.stack([local[:, 1], -local[:, 0]], axis=1)
    summed = jnp.einsum(
        "ocjaf,cjbf->ocab",
        jnp.stack([local, swapped], axis=0),
        lax.all_gather(local, "stn", axis=2, tiled=True),
        preferred_element_type=jnp.float32,
    )
    return summed * (1.0 / local.shape[3])


def on_device(voltages, delays):
    if fast_fits(voltages.shape[1], voltages.shape[2] // CHANNELS):
        return fast(voltages, delays)
    return general(voltages, delays)


def solution(mesh):
    return jax.shard_map(
        on_device,
        mesh=mesh,
        in_specs=(P(None, ("stn", "ct"), "tm"), P(("stn", "ct"))),
        out_specs=P(None, ("tm", "ct"), "stn", None),
        check_vma=False,
    )
```

```python
import functools
import math

import jax
import jax.numpy as jnp
import numpy as np
from jax import lax
from jax.experimental import pallas as pl
from jax.experimental.pallas import tpu as pltpu
from jax.sharding import PartitionSpec as P

CHANNELS = 4096
RADIX = 64
TAPS = 16
LANES = 128
ROWS = CHANNELS // LANES
PAIR = 2
TILE = 4
CHUNKS = 2

VMEM = pl.BlockSpec(memory_space=pltpu.VMEM)
SMEM = pl.BlockSpec(memory_space=pltpu.SMEM)


def params(mib):
    return pltpu.CompilerParams(vmem_limit_bytes=mib * 2**20)


def cost(flops, size):
    return pl.CostEstimate(flops=flops, bytes_accessed=size, transcendentals=0)


def filter_table():
    length = TAPS * CHANNELS
    index = np.arange(length, dtype=np.float64)
    centred = (index - length / 2) / CHANNELS
    window = 0.5 - 0.5 * np.cos(2.0 * math.pi * index / length)
    factor = 1.0 / (48.0 * math.sqrt(CHANNELS))
    table = np.sinc(centred) * window * factor
    return table.reshape(TAPS, ROWS, LANES).astype(np.float32)


def dft_parts(radix):
    steps = np.arange(radix)
    angle = 2.0 * math.pi * (steps[:, None] * steps[None, :] % radix) / radix
    return np.cos(angle).astype(jnp.bfloat16), np.sin(angle).astype(jnp.bfloat16)


def first_table():
    cosine, sine = dft_parts(CHANNELS // RADIX)
    order = [2 * row + half for half in range(2) for row in range(ROWS)]
    cosine, sine = cosine[:, order], sine[:, order]
    upper = np.concatenate([cosine, sine], axis=1)
    lower = np.concatenate([-sine, cosine], axis=1)
    return np.concatenate([upper, lower], axis=0)


def last_table(outer, per_ct, span):
    cosine, sine = dft_parts(RADIX)
    blocks = []
    for g in range(PAIR):
        for ct in range(per_ct):
            steps = [
                ((o * PAIR + g) * per_ct + ct) * span + j for o in range(outer) for j in range(span)
            ]
            real = np.concatenate([cosine[steps], sine[steps]], axis=1)
            imag = np.concatenate([-sine[steps], cosine[steps]], axis=1)
            blocks.append(np.concatenate([real, imag], axis=0))
    return np.stack(blocks).reshape(PAIR, per_ct, -1, 2 * RADIX)


def twiddle_tables():
    rows = np.arange(CHANNELS // RADIX)
    cols = np.arange(RADIX)
    angle = 2.0 * math.pi * (rows[:, None] * cols[None, :] % CHANNELS) / CHANNELS
    cosine = np.cos(angle).astype(np.float32)
    sine = np.sin(angle).astype(np.float32)
    return np.concatenate([cosine, cosine], axis=1), np.concatenate([sine, sine], axis=1)


def pick_kernel(count, scal, block, out, rows):
    inputs, samples = block.shape[1], block.shape[2]
    step = 16
    for part in range(2):

        def spread(n, carry, part=part):
            low = pl.multiple_of(n * step * LANES, step * LANES)
            wide = block[part, :, pl.ds(low, step * LANES)].astype(jnp.float32)
            for u in range(step):
                at = pl.multiple_of((n * step + u) * inputs, inputs)
                rows[part, pl.ds(at, inputs), :] = wide[:, u * LANES : (u + 1) * LANES]
            return carry

        lax.fori_loop(0, samples // LANES // step, spread, 0)
    first = scal[0]
    tall = 128
    for part in range(2):
        for item in range(count):

            def gather(n, carry, part=part, item=item):
                low = pl.multiple_of(n * tall, tall)
                value = rows[part, pl.ds(low * inputs + first + item, tall, stride=inputs), :]
                out[item, part, pl.ds(low, tall), :] = value.astype(jnp.bfloat16)
                return carry

            lax.fori_loop(0, samples // LANES // tall, gather, 0)


def pick(block, first, count):
    _, inputs, samples = block.shape
    return pl.pallas_call(
        functools.partial(pick_kernel, count),
        out_shape=jax.ShapeDtypeStruct((count, 2, samples // LANES, LANES), jnp.bfloat16),
        in_specs=[SMEM, VMEM],
        out_specs=VMEM,
        scratch_shapes=[pltpu.VMEM((2, samples // LANES * inputs, LANES), jnp.float32)],
        compiler_params=params(24),
        cost_estimate=cost(10**6, 8 * 2**20),
        name="pick",
    )(first, block)


FRONT = 40
GROUP = 8


def filterbank_kernel(count, frames, dests, *refs):
    scal, keep, recv, halo_far, halo_own, coef, first, tw_cos, tw_sin, last = refs[:10]
    outs = refs[10 : 10 + dests]
    samples, shifted, grouped = refs[10 + dests :]
    block_rows = frames * ROWS
    total = PAIR * frames
    me = scal[count]
    lane = lax.broadcasted_iota(jnp.int32, (1, LANES), 1)
    high = lane < RADIX
    tall = 128

    def unpack(source, place, item):
        def step(n, carry):
            low = pl.multiple_of(n * tall, tall)
            for part in range(2):
                at = pl.multiple_of(FRONT + place * block_rows + low, 8)
                value = source[item, part, pl.ds(low, tall), :]
                samples[part, pl.ds(at, tall), :] = value.astype(jnp.float32)
            return carry

        lax.fori_loop(0, block_rows // tall, step, 0)

    def filt(m):
        for band in range(ROWS // 16):
            sums = [[None] * GROUP for _ in range(2)]
            for part in range(2):
                values = []
                for u in range(GROUP + TAPS - 1):
                    at = (m * GROUP + frames - TAPS + 1 + u) * ROWS + band * 16
                    values.append(shifted[part, at : at + 16, :])
                for tap in range(TAPS):
                    weight = coef[tap, band * 16 : band * 16 + 16, :]
                    for u in range(GROUP):
                        term = weight * values[u + TAPS - 1 - tap]
                        old = sums[part][u]
                        sums[part][u] = term if old is None else old + term
            for u in range(GROUP):
                real, imag = sums[0][u], sums[1][u]
                real_turned = pltpu.roll(real, RADIX, 1)
                imag_turned = pltpu.roll(imag, RADIX, 1)
                parts = (
                    jnp.where(high, real, imag_turned),
                    jnp.where(high, real_turned, imag),
                    jnp.where(high, imag, -real_turned),
                    jnp.where(high, imag_turned, -real),
                )
                for index, value in enumerate(parts):
                    low = index * ROWS + band * 16
                    grouped[m % 2, u, low : low + 16, :] = value.astype(jnp.bfloat16)

    def turn(m, item):
        some = 4
        for piece in range(GROUP // some):
            base = piece * some
            wide = jnp.concatenate([grouped[m % 2, base + u] for u in range(some)], axis=1)
            inner = jnp.dot(first[...], wide, preferred_element_type=jnp.float32)
            rows = []
            for u in range(some):
                cut = slice(u * LANES, (u + 1) * LANES)
                turned = inner[:RADIX, cut] * tw_cos[...] + inner[RADIX:, cut] * tw_sin[...]
                rows.append(turned.astype(jnp.bfloat16))
            inner = jnp.concatenate(rows, axis=0)
            result = lax.dot_general(
                last[...], inner, (((1,), (1,)), ((), ())), preferred_element_type=jnp.float32
            ).astype(jnp.bfloat16)
            size = result.shape[0] // (2 * dests)
            for dest in range(dests):
                for part in range(2):
                    low = (dest * 2 + part) * size
                    for u in range(some // 2):
                        at = (m * GROUP + base) // 2 + u
                        outs[dest][item, at, part] = result[
                            low : low + size, u * LANES : (u + 1) * LANES
                        ]

    def one(item, carry):
        @pl.when(me == 0)
        def _():
            unpack(halo_far, 0, item)

        @pl.when(me != 0)
        def _():
            unpack(halo_own, 0, item)

        unpack(keep, 1 + me, item)
        unpack(recv, 2 - me, item)
        delay = scal[item]
        down = delay // LANES
        across = delay % LANES
        inside = lane < LANES - across

        def shift(n, carry):
            low = pl.multiple_of(n * GROUP * ROWS, GROUP * ROWS)
            for part in range(2):
                at = FRONT + low - down
                here = samples[part, pl.ds(at, GROUP * ROWS), :]
                before = samples[part, pl.ds(at - 1, GROUP * ROWS), :]
                moved = pltpu.roll(jnp.where(inside, here, before), across, 1)
                shifted[part, pl.ds(low, GROUP * ROWS), :] = moved
            return carry

        lax.fori_loop(0, (PAIR + 1) * frames // GROUP, shift, 0)
        steps = total // GROUP
        for m in range(steps + 1):
            if m < steps:
                filt(m)
            if m:
                turn(m - 1, item)
        return carry

    lax.fori_loop(0, count, one, 0)


def filterbank(scal, keep, recv, halo_far, halo_own, tables, last, dests):
    count = keep.shape[0]
    frames = keep.shape[2] // ROWS
    size = last.shape[0] // (2 * dests)
    all_rows = (PAIR + 1) * frames * ROWS
    shape = jax.ShapeDtypeStruct((count, PAIR * frames // 2, 2, size, LANES), jnp.bfloat16)
    return pl.pallas_call(
        functools.partial(filterbank_kernel, count, frames, dests),
        out_shape=[shape] * dests,
        in_specs=[SMEM] + [VMEM] * 9,
        out_specs=[VMEM] * dests,
        scratch_shapes=[
            pltpu.VMEM((2, FRONT + all_rows, LANES), jnp.float32),
            pltpu.VMEM((2, all_rows, LANES), jnp.float32),
            pltpu.VMEM((2, GROUP, LANES, LANES), jnp.bfloat16),
        ],
        compiler_params=params(40),
        cost_estimate=cost(2 * 10**9, 32 * 2**20),
        name="filterbank",
    )(scal, keep, recv, halo_far, halo_own, *tables, last)


def pair_blocks(own):
    tiles = own // TILE
    inside = [(i, j) for i in range(tiles) for j in range(i, tiles)]
    across = [(i, j) for i in range(tiles // 2) for j in range(tiles)]
    return inside, across


def correlate_kernel(layout, *refs):
    arrays, blocks, outer, span = layout
    sources, (place, starts, where_outer) = refs[:arrays], refs[arrays : arrays + 3]
    rest = refs[arrays + 3 :]
    outs, (spectra, sums) = rest[:-2], rest[-2:]
    halves = outer * span // 8
    steps = spectra.shape[1]
    some = 8

    for index, source in enumerate(sources):
        for item in range(source.shape[0]):

            def spread(n, carry, index=index, source=source, item=item):
                for u in range(some):
                    real = source[item, n * some + u, 0].astype(jnp.float32)
                    imag = source[item, n * some + u, 1].astype(jnp.float32)
                    for which, value in enumerate((real, imag, real + imag, imag - real)):
                        spectra[place[index] + item, n * some + u, which] = value
                return carry

            lax.fori_loop(0, steps // some, spread, 0)

    high = lax.broadcasted_iota(jnp.int32, (1, LANES), 1) < RADIX
    rows_outer = blocks * TILE * TILE * span

    def block(t, carry):
        left, right = starts[2 * t], starts[2 * t + 1]
        for half in range(halves):
            cut = slice(half * 8, half * 8 + 8)
            products = []
            for one, two in ((2, 0), (0, 2), (1, 3)):
                acc = [None] * (TILE * TILE)
                for n in range(steps):
                    a = [spectra[left + p, n, one, cut, :] for p in range(TILE)]
                    b = [spectra[right + q, n, two, cut, :] for q in range(TILE)]
                    for p in range(TILE):
                        for q in range(TILE):
                            term = a[p] * b[q]
                            at = p * TILE + q
                            acc[at] = term if acc[at] is None else acc[at] + term
                products.append(acc)
            for p in range(TILE * TILE):
                first, second, third = (acc[p] for acc in products)
                real = first + third
                imag = first - second
                real = real + pltpu.roll(real, RADIX, 1)
                imag = imag + pltpu.roll(imag, RADIX, 1)
                both = jnp.where(high, real, imag)
                for u in range(8 // span):
                    o = half * (8 // span) + u
                    at = o * rows_outer + (t * TILE * TILE + p) * span
                    sums[pl.ds(pl.multiple_of(at, span), span), :] = both[u * span : (u + 1) * span]
        return carry

    lax.fori_loop(0, blocks, block, 0)
    for r in range(outer):
        base = pl.multiple_of(lax.rem(where_outer[0] + r, outer) * rows_outer, 16)
        outs[r][...] = sums[pl.ds(base, rows_outer), :].astype(outs[r].dtype)


def correlate(arrays, place, starts, where_outer, inputs, outer, span, name):
    _, steps, _, size, _ = arrays[0].shape
    blocks = starts.shape[0] // 2
    rows = blocks * TILE * TILE * span
    shapes = []
    for r in range(outer):
        dtype = jnp.float32 if r == 0 else jnp.bfloat16
        shapes.append(jax.ShapeDtypeStruct((rows, LANES), dtype))
    layout = (len(arrays), blocks, outer, span)
    return pl.pallas_call(
        functools.partial(correlate_kernel, layout),
        out_shape=shapes,
        in_specs=[VMEM] * len(arrays) + [SMEM] * 3,
        out_specs=[VMEM] * len(shapes),
        scratch_shapes=[
            pltpu.VMEM((inputs, steps, 4, size, LANES), jnp.float32),
            pltpu.VMEM((outer * rows, LANES), jnp.float32),
        ],
        compiler_params=params(40),
        cost_estimate=cost(10**9, 20 * 2**20),
        name=name,
    )(*arrays, place, starts, where_outer)


def assemble_kernel(own, outer, span, scale, *refs):
    core = refs[0]
    mine_in = refs[1 : 1 + outer]
    mine_across = refs[1 + outer : 1 + 2 * outer]
    far_across = refs[1 + 2 * outer : 1 + 3 * outer]
    out, joined = refs[1 + 3 * outer :]
    inside, across = pair_blocks(own)
    rows = TILE * TILE * span
    lane = lax.broadcasted_iota(jnp.int32, (1, LANES), 1)
    high = lane < RADIX
    mirror = jnp.where(high, 1.0, -1.0).astype(jnp.float32)
    me = core[0]

    def added(sources, t):
        total = sources[0][t * rows : (t + 1) * rows, :].astype(jnp.float32)
        for source in sources[1:]:
            total = total + source[t * rows : (t + 1) * rows, :].astype(jnp.float32)
        return total * scale

    def put(value, row, col):
        at = pl.multiple_of((row * 2 * own + col) * span, span)
        joined[pl.ds(at, span), :] = value

    for t, (i, j) in enumerate(inside):
        total = added(mine_in, t)
        turned = total * mirror
        for p in range(TILE):
            for q in range(TILE):
                low = (p * TILE + q) * span
                a, b = i * TILE + p, j * TILE + q
                put(total[low : low + span], a, me * own + b)
                if i < j:
                    put(turned[low : low + span], b, me * own + a)
    sign = jnp.where(me == 0, jnp.ones_like(mirror), mirror)
    for sources, part in ((mine_across, me), (far_across, 1 - me)):
        for t, (i, j) in enumerate(across):
            total = added(sources, t) * sign
            for p in range(TILE):
                for q in range(TILE):
                    low = (p * TILE + q) * span
                    a = part * (own // 2) + i * TILE + p
                    b = j * TILE + q
                    row = jnp.where(me == 0, a, b)
                    col = jnp.where(me == 0, own + b, a)
                    put(total[low : low + span], row, col)

    def emit(a, carry):
        for tile in range(2 * own // 8):
            for pair in range(span // 2):
                loads = []
                for u in range(2):
                    at = (a * 2 * own + tile * 8) * span + pair * 2 + u
                    loads.append(joined[pl.ds(at, 8, stride=span), :])
                turned = [pltpu.roll(x, RADIX, 1) for x in loads]
                cut = slice(pair * LANES, (pair + 1) * LANES)
                out[0, a, tile * 8 : tile * 8 + 8, cut] = jnp.where(high, loads[0], turned[1])
                out[1, a, tile * 8 : tile * 8 + 8, cut] = jnp.where(high, turned[0], loads[1])
        return carry

    lax.fori_loop(0, own, emit, 0)


def assemble(core, mine_in, mine_across, far_across, own, span, scale):
    outer = len(mine_in)
    return pl.pallas_call(
        functools.partial(assemble_kernel, own, outer, span, scale),
        out_shape=jax.ShapeDtypeStruct((2, own, 2 * own, span * RADIX), jnp.float32),
        in_specs=[SMEM] + [VMEM] * (3 * outer),
        out_specs=VMEM,
        scratch_shapes=[pltpu.VMEM((own * 2 * own * span, LANES), jnp.float32)],
        compiler_params=params(24),
        cost_estimate=cost(10**8, 8 * 2**20),
        name="assemble",
    )(core, *mine_in, *mine_across, *far_across)


def fast_fits(in_count, frame_count):
    stn, tm, per_ct = (lax.axis_size(a) for a in ("stn", "tm", "ct"))
    groups = tm * per_ct
    if stn != 2 or tm % PAIR or in_count % (PAIR * CHUNKS) or RADIX % groups:
        return False
    outer, span = tm // PAIR, RADIX // groups
    own = in_count * per_ct
    return (
        frame_count >= TAPS
        and frame_count % GROUP == 0
        and span in (2, 4, 8)
        and outer * span % 16 == 0
        and own % (2 * TILE) == 0
    )


def fast(voltages, delays):
    tm, per_ct = lax.axis_size("tm"), lax.axis_size("ct")
    in_count = voltages.shape[1]
    frame_count = voltages.shape[2] // CHANNELS
    outer = tm // PAIR
    span = RADIX // (tm * per_ct)
    own = in_count * per_ct
    half = in_count // PAIR
    part = half // CHUNKS
    place_tm, place_ct = lax.axis_index("tm"), lax.axis_index("ct")
    core = lax.axis_index("stn")
    g, o = place_tm % PAIR, place_tm // PAIR

    swap = [(i, i ^ 1) for i in range(tm)]
    onward = [(i, i + PAIR) for i in range(tm - PAIR)]
    cores = [(0, 1), (1, 0)]

    def stacked(values):
        return jnp.stack([jnp.asarray(v, jnp.int32) for v in values])

    dests = [(dg, dc) for dg in range(PAIR) for dc in range(per_ct)]
    base = jnp.asarray(last_table(outer, per_ct, span))
    base = jnp.where(g == 0, base, base[::-1])
    base = lax.dynamic_slice_in_dim(jnp.concatenate([base, base], axis=1), place_ct, per_ct, 1)
    last = base.reshape(-1, 2 * RADIX)
    tables = [jnp.asarray(filter_table()), jnp.asarray(first_table())]
    tables += [jnp.asarray(t) for t in twiddle_tables()]

    sends = [pick(voltages, stacked([(1 - g) * half + c * part]), part) for c in range(CHUNKS)]
    keeps = [pick(voltages, stacked([g * half + c * part]), part) for c in range(CHUNKS)]
    recvs, fars, owns = [], [], []
    for c in range(CHUNKS):
        recvs.append(lax.ppermute(sends[c], "tm", swap))
        owns.append(lax.ppermute(keeps[c], "tm", [p for p in onward if p[0] % PAIR == 1]))
        fars.append(lax.ppermute(recvs[c], "tm", [p for p in onward if p[0] % PAIR == 0]))

    arrays, others, place = [], [], []
    for c in range(CHUNKS):
        offsets = lax.dynamic_slice_in_dim(delays, g * half + c * part, part, 0)
        scal = jnp.concatenate([offsets, g.astype(jnp.int32)[None]])
        spectra = filterbank(
            scal, keeps[c], recvs[c], fars[c], owns[c], tables, last, len(dests)
        )
        for (dg, dc), block in zip(dests, spectra):
            route = []
            for i in range(tm):
                for j in range(per_ct):
                    target = (i ^ dg) * per_ct + (j + dc) % per_ct
                    route.append((i * per_ct + j, target))
            if dg or dc:
                block = lax.ppermute(block, ("tm", "ct"), route)
            arrays.append(block)
            others.append(lax.ppermute(block, "stn", cores))
            place.append(((place_ct - dc) % per_ct) * in_count + (g ^ dg) * half + c * part)

    inside, across = pair_blocks(own)
    starts = stacked([TILE * s for block in inside for s in block])
    mine_in = correlate(
        arrays, stacked(place), starts, stacked([o]), own, outer, span, "correlate_own"
    )
    starts = []
    for i, j in across:
        starts += [core * (own // 2) + TILE * i, own + TILE * j]
    place = [core * own + s for s in place] + [(1 - core) * own + s for s in place]
    mine_across = correlate(
        arrays + others, stacked(place), stacked(starts), stacked([o]), 2 * own, outer, span,
        "correlate_cross",
    )
    mine_in, mine_across, far_across = list(mine_in), list(mine_across), []
    for r in range(1, outer):
        route = [(i, (i + r * PAIR) % tm) for i in range(tm)]
        mine_in[r] = lax.ppermute(mine_in[r], "tm", route)
    for r in range(outer):
        if r:
            route = [(i, (i + r * PAIR) % tm) for i in range(tm)]
            mine_across[r] = lax.ppermute(mine_across[r], "tm", route)
        far_across.append(lax.ppermute(mine_across[r], "stn", cores))
    scale = 1.0 / (tm * frame_count)
    result = assemble(stacked([core]), mine_in, mine_across, far_across, own, span, scale)
    return result.transpose(0, 3, 1, 2)


def general(voltages, delays):
    in_count = voltages.shape[1]
    frame_count = voltages.shape[2] // CHANNELS
    route = [(i, i + 1) for i in range(lax.axis_size("tm") - 1)]
    extended = jnp.concatenate([lax.ppermute(voltages, "tm", route), voltages], axis=2)
    span = (frame_count + TAPS - 1) * CHANNELS
    shifted = jax.vmap(
        lambda row, offset: lax.dynamic_slice_in_dim(row, CHANNELS - offset, span, 1),
        in_axes=(1, 0),
        out_axes=1,
    )(extended, delays)
    framed = shifted.reshape(2, in_count, frame_count + TAPS - 1, CHANNELS)
    table = jnp.asarray(filter_table()).reshape(TAPS, CHANNELS)
    total = jnp.zeros((2, in_count, frame_count, CHANNELS), jnp.float32)
    for tap in range(TAPS):
        low = TAPS - 1 - tap
        total = total + table[tap] * framed[:, :, low : low + frame_count].astype(jnp.float32)
    branches = jnp.moveaxis(total.astype(jnp.bfloat16), 0, 2)

    number = in_count * frame_count
    cosine, sine = dft_parts(RADIX)
    block = np.concatenate(
        [np.concatenate([cosine, sine], axis=1), np.concatenate([-sine, cosine], axis=1)], axis=0
    )
    block = jnp.asarray(block)
    stacked = branches.reshape(number, 2 * RADIX, RADIX)
    inner = jnp.einsum("kj,nja->nka", block, stacked, preferred_element_type=jnp.float32)
    inner = inner.reshape(number, 2, RADIX, RADIX)
    tw_cos, tw_sin = (jnp.asarray(t[:, :RADIX]) for t in twiddle_tables())
    real = inner[:, 0] * tw_cos + inner[:, 1] * tw_sin
    imag = inner[:, 1] * tw_cos - inner[:, 0] * tw_sin
    turned = jnp.stack([real, imag], axis=2).reshape(number, RADIX, 2 * RADIX)
    turned = turned.astype(jnp.bfloat16)
    result = jnp.einsum("lj,nkj->nlk", block, turned, preferred_element_type=jnp.float32)
    spectra = result.reshape(in_count, frame_count, 2, CHANNELS).astype(jnp.bfloat16)
    moved = lax.all_to_all(spectra, "tm", split_axis=3, concat_axis=1, tiled=True)
    moved = lax.all_to_all(moved, "ct", split_axis=3, concat_axis=0, tiled=True)
    local = moved.transpose(3, 2, 0, 1)
    swapped = jnp.stack([local[:, 1], -local[:, 0]], axis=1)
    summed = jnp.einsum(
        "ocjaf,cjbf->ocab",
        jnp.stack([local, swapped], axis=0),
        lax.all_gather(local, "stn", axis=2, tiled=True),
        preferred_element_type=jnp.float32,
    )
    return summed * (1.0 / local.shape[3])


def on_device(voltages, delays):
    if fast_fits(voltages.shape[1], voltages.shape[2] // CHANNELS):
        return fast(voltages, delays)
    return general(voltages, delays)


def solution(mesh):
    return jax.shard_map(
        on_device,
        mesh=mesh,
        in_specs=(P(None, ("stn", "ct"), "tm"), P(("stn", "ct"))),
        out_specs=P(None, ("tm", "ct"), "stn", None),
        check_vma=False,
    )
```

```python
import functools
import math

import jax
import jax.numpy as jnp
import numpy as np
from jax import lax
from jax.experimental import pallas as pl
from jax.experimental.pallas import tpu as pltpu
from jax.sharding import PartitionSpec as P

CHANNELS = 4096
RADIX = 64
TAPS = 16
LANES = 128
ROWS = CHANNELS // LANES
PAIR = 2
TILE = 4
JOIN = 2

VMEM = pl.BlockSpec(memory_space=pltpu.VMEM)
SMEM = pl.BlockSpec(memory_space=pltpu.SMEM)
ANY = pl.BlockSpec(memory_space=pl.ANY)


def params(mib):
    return pltpu.CompilerParams(vmem_limit_bytes=mib * 2**20)


def cost(flops, size):
    return pl.CostEstimate(flops=flops, bytes_accessed=size, transcendentals=0)


def filter_table():
    length = TAPS * CHANNELS
    index = np.arange(length, dtype=np.float64)
    centred = (index - length / 2) / CHANNELS
    window = 0.5 - 0.5 * np.cos(2.0 * math.pi * index / length)
    factor = 1.0 / (48.0 * math.sqrt(CHANNELS))
    table = np.sinc(centred) * window * factor
    return table.reshape(TAPS, ROWS, LANES).astype(np.float32)


def dft_parts(radix):
    steps = np.arange(radix)
    angle = 2.0 * math.pi * (steps[:, None] * steps[None, :] % radix) / radix
    return np.cos(angle).astype(jnp.bfloat16), np.sin(angle).astype(jnp.bfloat16)


def first_table():
    cosine, sine = dft_parts(CHANNELS // RADIX)
    order = [2 * row + half for half in range(2) for row in range(ROWS)]
    cosine, sine = cosine[:, order], sine[:, order]
    upper = np.concatenate([cosine, sine], axis=1)
    lower = np.concatenate([-sine, cosine], axis=1)
    return np.concatenate([upper, lower], axis=0)


def last_table(outer, per_ct, span):
    cosine, sine = dft_parts(RADIX)
    blocks = []
    for g in range(PAIR):
        for ct in range(per_ct):
            steps = [
                ((o * PAIR + g) * per_ct + ct) * span + j for o in range(outer) for j in range(span)
            ]
            real = np.concatenate([cosine[steps], sine[steps]], axis=1)
            imag = np.concatenate([-sine[steps], cosine[steps]], axis=1)
            blocks.append(np.concatenate([real, imag], axis=0))
    return np.stack(blocks).reshape(PAIR, per_ct, -1, 2 * RADIX)


def twiddle_tables():
    rows = np.arange(CHANNELS // RADIX)
    cols = np.arange(RADIX)
    angle = 2.0 * math.pi * (rows[:, None] * cols[None, :] % CHANNELS) / CHANNELS
    cosine = np.cos(angle).astype(np.float32)
    sine = np.sin(angle).astype(np.float32)
    return np.concatenate([cosine, cosine], axis=1), np.concatenate([sine, sine], axis=1)


def pick_kernel(count, joined, scal, block, *refs):
    outs, rows = refs[:-1], refs[-1]
    inputs, samples = block.shape[1], block.shape[2]
    step = 16
    for part in range(2):

        def spread(n, carry, part=part):
            low = pl.multiple_of(n * step * LANES, step * LANES)
            wide = block[part, :, pl.ds(low, step * LANES)].astype(jnp.float32)
            for u in range(step):
                at = pl.multiple_of((n * step + u) * inputs, inputs)
                rows[part, pl.ds(at, inputs), :] = wide[:, u * LANES : (u + 1) * LANES]
            return carry

        lax.fori_loop(0, samples // LANES // step, spread, 0)
    first = scal[0]
    tall = 128
    for item in range(count):
        out = outs[0].at[item] if joined else outs[item]

        def gather(n, carry, item=item, out=out):
            low = pl.multiple_of(n * tall, tall)
            for part in range(2):
                value = rows[part, pl.ds(low * inputs + first + item, tall, stride=inputs), :]
                out[part, pl.ds(low, tall), :] = value.astype(jnp.bfloat16)
            return carry

        lax.fori_loop(0, samples // LANES // tall, gather, 0)


def pick(block, first, count, joined):
    _, inputs, samples = block.shape
    one = (2, samples // LANES, LANES)
    shapes = [(count,) + one] if joined else [one] * count
    return pl.pallas_call(
        functools.partial(pick_kernel, count, joined),
        out_shape=[jax.ShapeDtypeStruct(s, jnp.bfloat16) for s in shapes],
        in_specs=[SMEM, VMEM],
        out_specs=[VMEM] * len(shapes),
        scratch_shapes=[pltpu.VMEM((2, samples // LANES * inputs, LANES), jnp.float32)],
        compiler_params=params(16),
        cost_estimate=cost(10**6, 4 * 2**20),
        name="pick",
    )(first, block)


HALF = 16
SOME = 4


def filterbank_kernel(index, before, frames, dests, *refs):
    scal, keep, halo_own, recv, halo_far, coef, first, tw_cos, tw_sin, last = refs[:10]
    earlier = refs[10 : 10 + dests * (before > 0)]
    refs = refs[10 + len(earlier) :]
    outs = refs[:dests]
    raw, weights, grouped, sems = refs[dests : dests + 4]
    filtered = refs[dests + 4 :]
    block_rows = frames * ROWS
    total = PAIR * frames
    delay, me = scal[0], scal[1]
    down = delay // LANES
    across = delay % LANES
    lane = lax.broadcasted_iota(jnp.int32, (1, LANES), 1)
    inside = lane < LANES - across
    turned_in = lane >= across
    high = lane < RADIX

    def bring(source, place, sem):
        at = pl.multiple_of(place * block_rows, block_rows)
        return pltpu.make_async_copy(source, raw.at[:, pl.ds(at, block_rows), :], sems.at[sem])

    @pl.when(me == 0)
    def _():
        bring(halo_far, 0, 0).start()

    @pl.when(me != 0)
    def _():
        bring(halo_own.at[index], 0, 0).start()

    bring(keep.at[index], 1 + me, 1).start()
    bring(recv, 2 - me, 2).start()

    back = lax.rem(LANES - across, LANES)
    for tap in range(TAPS):
        here = coef[tap, pl.ds(down, ROWS), :]
        after = coef[tap, pl.ds(down + 1, ROWS), :]
        weights[tap] = pltpu.roll(jnp.where(turned_in, here, after), back, 1)
    for dest, old in zip(outs, earlier):
        dest[:before] = old[...]

    bring(halo_far, 0, 0).wait()
    bring(keep.at[index], 1 + me, 1).wait()
    bring(recv, 2 - me, 2).wait()

    def filt(half):
        for low, high_frame in ((0, 9), (9, HALF + 1)):
            size = high_frame - low
            for band in range(ROWS // 16):
                for part in range(2):
                    values = []
                    for u in range(size + TAPS - 1):
                        at = (half * HALF + low + u + frames - TAPS) * ROWS + band * 16
                        values.append(raw[part, at : at + 16, :].astype(jnp.float32))
                    sums = [None] * size
                    for tap in range(TAPS):
                        weight = weights[tap, band * 16 : band * 16 + 16, :]
                        for u in range(size):
                            term = weight * values[u + TAPS - 1 - tap]
                            sums[u] = term if sums[u] is None else sums[u] + term
                    for u in range(size):
                        at = (low + u) * ROWS + band * 16
                        filtered[half][part, at : at + 16, :] = sums[u]

    twice = lax.rem(across + RADIX, LANES)

    def place(half, u):
        for band in range(ROWS // 16):
            at = (u + 1) * ROWS + band * 16 - down
            moved, turned = [], []
            for part in range(2):
                here = filtered[half][part, pl.ds(at, 16), :]
                above = filtered[half][part, pl.ds(at - 1, 16), :]
                value = jnp.where(inside, here, above)
                moved.append(pltpu.roll(value, across, 1))
                turned.append(pltpu.roll(value, twice, 1))
            parts = (
                jnp.where(high, moved[0], turned[1]),
                jnp.where(high, turned[0], moved[1]),
                jnp.where(high, moved[1], -turned[0]),
                jnp.where(high, turned[1], -moved[0]),
            )
            for which, value in enumerate(parts):
                low = which * ROWS + band * 16
                grouped[half * HALF + u, low : low + 16, :] = value.astype(jnp.bfloat16)

    def turn(base):
        wide = jnp.concatenate([grouped[base + u] for u in range(SOME)], axis=1)
        inner = jnp.dot(first[...], wide, preferred_element_type=jnp.float32)
        rows = []
        for u in range(SOME):
            cut = slice(u * LANES, (u + 1) * LANES)
            value = inner[:RADIX, cut] * tw_cos[...] + inner[RADIX:, cut] * tw_sin[...]
            rows.append(value.astype(jnp.bfloat16))
        inner = jnp.concatenate(rows, axis=0)
        result = lax.dot_general(
            last[...], inner, (((1,), (1,)), ((), ())), preferred_element_type=jnp.float32
        ).astype(jnp.bfloat16)
        size = result.shape[0] // (2 * dests)
        for dest in range(dests):
            for part in range(2):
                low = (dest * 2 + part) * size
                for u in range(SOME // 2):
                    outs[dest][before, base // 2 + u, part] = result[
                        low : low + size, u * LANES : (u + 1) * LANES
                    ]

    for half in range(total // HALF):
        filt(half)
    for half in range(total // HALF):
        for base in range(0, HALF, SOME):
            for u in range(SOME):
                place(half, base + u)
            turn(half * HALF + base)


def filterbank(index, scal, keep, halo_own, recv, halo_far, tables, last, earlier, dests):
    frames = keep.shape[2] // ROWS
    size = last.shape[0] // (2 * dests)
    before = earlier[0].shape[0] if earlier else 0
    all_rows = (PAIR + 1) * frames * ROWS
    shape = (before + 1, PAIR * frames // 2, 2, size, LANES)
    return pl.pallas_call(
        functools.partial(filterbank_kernel, index, before, frames, dests),
        out_shape=[jax.ShapeDtypeStruct(shape, jnp.bfloat16)] * dests,
        in_specs=[SMEM] + [ANY] * 4 + [VMEM] * (5 + len(earlier)),
        out_specs=[VMEM] * dests,
        scratch_shapes=[
            pltpu.VMEM((2, all_rows, LANES), jnp.bfloat16),
            pltpu.VMEM((TAPS, ROWS, LANES), jnp.float32),
            pltpu.VMEM((PAIR * frames, LANES, LANES), jnp.bfloat16),
            pltpu.SemaphoreType.DMA((3,)),
        ]
        + [pltpu.VMEM((2, (HALF + 1) * ROWS, LANES), jnp.float32)] * (PAIR * frames // HALF),
        compiler_params=params(16),
        cost_estimate=cost(10**9, 10 * 2**20),
        name="filterbank",
    )(scal, keep, halo_own, recv, halo_far, *tables, last, *earlier)


def pair_blocks(own):
    tiles = own // TILE
    inside = [(i, j) for i in range(tiles) for j in range(i, tiles)]
    across = [(i, j) for i in range(tiles // 2) for j in range(tiles)]
    return inside, across


def correlate_kernel(layout, *refs):
    arrays, blocks, outer, span = layout
    sources, (place, starts, where_outer) = refs[:arrays], refs[arrays : arrays + 3]
    rest = refs[arrays + 3 :]
    outs, (spectra, sums, held) = rest[:-3], rest[-3:]
    steps = spectra.shape[1]
    some = 8

    for index, source in enumerate(sources):
        for item in range(source.shape[0]):

            def spread(n, carry, index=index, source=source, item=item):
                for u in range(some):
                    real = source[item, n * some + u, 0].astype(jnp.float32)
                    imag = source[item, n * some + u, 1].astype(jnp.float32)
                    for which, value in enumerate((real, imag, real + imag, imag - real)):
                        spectra[place[index] + item, n * some + u, which] = value
                return carry

            lax.fori_loop(0, steps // some, spread, 0)

    high = lax.broadcasted_iota(jnp.int32, (1, LANES), 1) < RADIX
    rows_outer = blocks * TILE * TILE * span
    size = outer * span
    unroll = 4

    def block(t, carry):
        left, right = starts[2 * t], starts[2 * t + 1]

        def over(one, two, acc, sign):
            def frame(n, acc):
                acc = list(acc)
                for u in range(unroll):
                    a = [spectra[left + p, n * unroll + u, one] for p in range(TILE)]
                    b = [spectra[right + q, n * unroll + u, two] for q in range(TILE)]
                    for p in range(TILE):
                        for q in range(TILE):
                            at = p * TILE + q
                            term = a[p] * b[q]
                            acc[at] = acc[at] + term if sign > 0 else acc[at] - term
                return tuple(acc)

            return lax.fori_loop(0, steps // unroll, frame, tuple(acc))

        zero = jnp.zeros((size, LANES), jnp.float32)
        first = over(2, 0, [zero] * (TILE * TILE), 1)
        for p in range(TILE * TILE):
            held[0, p] = first[p]
        real = over(1, 3, first, 1)
        for p in range(TILE * TILE):
            held[1, p] = real[p] + pltpu.roll(real[p], RADIX, 1)
        imag = over(0, 2, [held[0, p] for p in range(TILE * TILE)], -1)
        for p in range(TILE * TILE):
            folded = imag[p] + pltpu.roll(imag[p], RADIX, 1)
            both = jnp.where(high, held[1, p], folded)
            for o in range(outer):
                at = o * rows_outer + (t * TILE * TILE + p) * span
                sums[pl.ds(pl.multiple_of(at, span), span), :] = both[o * span : (o + 1) * span]
        return carry

    lax.fori_loop(0, blocks, block, 0)
    for r in range(outer):
        base = pl.multiple_of(lax.rem(where_outer[0] + r, outer) * rows_outer, 16)
        outs[r][...] = sums[pl.ds(base, rows_outer), :].astype(outs[r].dtype)


def correlate(arrays, place, starts, where_outer, inputs, outer, span, name):
    _, steps, _, size, _ = arrays[0].shape
    blocks = starts.shape[0] // 2
    rows = blocks * TILE * TILE * span
    shapes = []
    for r in range(outer):
        dtype = jnp.float32 if r == 0 else jnp.bfloat16
        shapes.append(jax.ShapeDtypeStruct((rows, LANES), dtype))
    layout = (len(arrays), blocks, outer, span)
    return pl.pallas_call(
        functools.partial(correlate_kernel, layout),
        out_shape=shapes,
        in_specs=[VMEM] * len(arrays) + [SMEM] * 3,
        out_specs=[VMEM] * len(shapes),
        scratch_shapes=[
            pltpu.VMEM((inputs, steps, 4, size, LANES), jnp.float32),
            pltpu.VMEM((outer * rows, LANES), jnp.float32),
            pltpu.VMEM((2, TILE * TILE, outer * span, LANES), jnp.float32),
        ],
        compiler_params=params(14 + inputs * steps * 4 * size * LANES * 4 // 2**20),
        cost_estimate=cost(10**9, 22 * 2**20),
        name=name,
    )(*arrays, place, starts, where_outer)


def assemble_kernel(own, outer, span, scale, *refs):
    core = refs[0]
    mine_in = refs[1 : 1 + outer]
    mine_across = refs[1 + outer : 1 + 2 * outer]
    far_across = refs[1 + 2 * outer : 1 + 3 * outer]
    out, joined = refs[1 + 3 * outer :]
    inside, across = pair_blocks(own)
    rows = TILE * TILE * span
    lane = lax.broadcasted_iota(jnp.int32, (1, LANES), 1)
    high = lane < RADIX
    mirror = jnp.where(high, 1.0, -1.0).astype(jnp.float32)
    me = core[0]

    def added(sources, t):
        total = sources[0][t * rows : (t + 1) * rows, :].astype(jnp.float32)
        for source in sources[1:]:
            total = total + source[t * rows : (t + 1) * rows, :].astype(jnp.float32)
        return total * scale

    def put(value, row, col):
        at = pl.multiple_of((row * 2 * own + col) * span, span)
        joined[pl.ds(at, span), :] = value

    for t, (i, j) in enumerate(inside):
        total = added(mine_in, t)
        turned = total * mirror
        for p in range(TILE):
            for q in range(TILE):
                low = (p * TILE + q) * span
                a, b = i * TILE + p, j * TILE + q
                put(total[low : low + span], a, me * own + b)
                if i < j:
                    put(turned[low : low + span], b, me * own + a)
    sign = jnp.where(me == 0, jnp.ones_like(mirror), mirror)
    for sources, part in ((mine_across, me), (far_across, 1 - me)):
        for t, (i, j) in enumerate(across):
            total = added(sources, t) * sign
            for p in range(TILE):
                for q in range(TILE):
                    low = (p * TILE + q) * span
                    a = part * (own // 2) + i * TILE + p
                    b = j * TILE + q
                    row = jnp.where(me == 0, a, b)
                    col = jnp.where(me == 0, own + b, a)
                    put(total[low : low + span], row, col)

    def emit(a, carry):
        for tile in range(2 * own // 8):
            for pair in range(span // 2):
                loads = []
                for u in range(2):
                    at = (a * 2 * own + tile * 8) * span + pair * 2 + u
                    loads.append(joined[pl.ds(at, 8, stride=span), :])
                turned = [pltpu.roll(x, RADIX, 1) for x in loads]
                cut = slice(pair * LANES, (pair + 1) * LANES)
                out[0, a, tile * 8 : tile * 8 + 8, cut] = jnp.where(high, loads[0], turned[1])
                out[1, a, tile * 8 : tile * 8 + 8, cut] = jnp.where(high, turned[0], loads[1])
        return carry

    lax.fori_loop(0, own, emit, 0)


def assemble(core, mine_in, mine_across, far_across, own, span, scale):
    outer = len(mine_in)
    return pl.pallas_call(
        functools.partial(assemble_kernel, own, outer, span, scale),
        out_shape=jax.ShapeDtypeStruct((2, own, 2 * own, span * RADIX), jnp.float32),
        in_specs=[SMEM] + [VMEM] * (3 * outer),
        out_specs=VMEM,
        scratch_shapes=[pltpu.VMEM((own * 2 * own * span, LANES), jnp.float32)],
        compiler_params=params(24),
        cost_estimate=cost(10**8, 8 * 2**20),
        name="assemble",
    )(core, *mine_in, *mine_across, *far_across)


def fast_fits(in_count, frame_count):
    stn, tm, per_ct = (lax.axis_size(a) for a in ("stn", "tm", "ct"))
    groups = tm * per_ct
    if stn != 2 or tm % PAIR or in_count % (PAIR * JOIN) or RADIX % groups:
        return False
    outer, span = tm // PAIR, RADIX // groups
    own = in_count * per_ct
    return (
        frame_count >= TAPS
        and frame_count % HALF == 0
        and span in (2, 4, 8)
        and outer * span % 16 == 0
        and own % (2 * TILE) == 0
    )


def fast(voltages, delays):
    tm, per_ct = lax.axis_size("tm"), lax.axis_size("ct")
    in_count = voltages.shape[1]
    frame_count = voltages.shape[2] // CHANNELS
    outer = tm // PAIR
    span = RADIX // (tm * per_ct)
    own = in_count * per_ct
    half = in_count // PAIR
    place_tm, place_ct = lax.axis_index("tm"), lax.axis_index("ct")
    core = lax.axis_index("stn")
    g, o = place_tm % PAIR, place_tm // PAIR

    swap = [(i, i ^ 1) for i in range(tm)]
    onward = [(i, i + PAIR) for i in range(tm - PAIR)]
    cores = [(0, 1), (1, 0)]

    def stacked(values):
        return jnp.stack([jnp.asarray(v, jnp.int32) for v in values])

    dests = [(dg, dc) for dg in range(PAIR) for dc in range(per_ct)]
    base = jnp.asarray(last_table(outer, per_ct, span))
    base = jnp.where(g == 0, base, base[::-1])
    base = lax.dynamic_slice_in_dim(jnp.concatenate([base, base], axis=1), place_ct, per_ct, 1)
    last = base.reshape(-1, 2 * RADIX)
    twice = np.concatenate([filter_table()] * 2, axis=1)
    tables = [jnp.asarray(twice), jnp.asarray(first_table())]
    tables += [jnp.asarray(t) for t in twiddle_tables()]

    sends = pick(voltages, stacked([(1 - g) * half]), half, False)
    keep = pick(voltages, stacked([g * half]), half, True)[0]
    recvs = [lax.ppermute(block, "tm", swap) for block in sends]
    halo_own = lax.ppermute(keep, "tm", [p for p in onward if p[0] % PAIR == 1])
    fars = [lax.ppermute(block, "tm", [p for p in onward if p[0] % PAIR == 0]) for block in recvs]

    arrays, others, place = [], [], []
    spectra = []
    for c in range(half):
        scal = stacked([lax.dynamic_index_in_dim(delays, g * half + c, 0, False), g])
        spectra = filterbank(
            c, scal, keep, halo_own, recvs[c], fars[c], tables, last, spectra, len(dests)
        )
        if c % JOIN < JOIN - 1:
            continue
        for (dg, dc), block in zip(dests, spectra):
            route = []
            for i in range(tm):
                for j in range(per_ct):
                    target = (i ^ dg) * per_ct + (j + dc) % per_ct
                    route.append((i * per_ct + j, target))
            if dg or dc:
                block = lax.ppermute(block, ("tm", "ct"), route)
            arrays.append(block)
            others.append(lax.ppermute(block, "stn", cores))
            start = ((place_ct - dc) % per_ct) * in_count + (g ^ dg) * half
            place.append(start + c - JOIN + 1)
        spectra = []

    inside, across = pair_blocks(own)
    starts = stacked([TILE * s for block in inside for s in block])
    mine_in = correlate(
        arrays, stacked(place), starts, stacked([o]), own, outer, span, "correlate_own"
    )
    starts = []
    for i, j in across:
        starts += [core * (own // 2) + TILE * i, own + TILE * j]
    place = [core * own + s for s in place] + [(1 - core) * own + s for s in place]
    mine_across = correlate(
        arrays + others, stacked(place), stacked(starts), stacked([o]), 2 * own, outer, span,
        "correlate_cross",
    )
    mine_in, mine_across, far_across = list(mine_in), list(mine_across), []
    for r in range(1, outer):
        route = [(i, (i + r * PAIR) % tm) for i in range(tm)]
        mine_in[r] = lax.ppermute(mine_in[r], "tm", route)
    for r in range(outer):
        if r:
            route = [(i, (i + r * PAIR) % tm) for i in range(tm)]
            mine_across[r] = lax.ppermute(mine_across[r], "tm", route)
        far_across.append(lax.ppermute(mine_across[r], "stn", cores))
    scale = 1.0 / (tm * frame_count)
    result = assemble(stacked([core]), mine_in, mine_across, far_across, own, span, scale)
    return result.transpose(0, 3, 1, 2)


def general(voltages, delays):
    in_count = voltages.shape[1]
    frame_count = voltages.shape[2] // CHANNELS
    route = [(i, i + 1) for i in range(lax.axis_size("tm") - 1)]
    extended = jnp.concatenate([lax.ppermute(voltages, "tm", route), voltages], axis=2)
    span = (frame_count + TAPS - 1) * CHANNELS
    shifted = jax.vmap(
        lambda row, offset: lax.dynamic_slice_in_dim(row, CHANNELS - offset, span, 1),
        in_axes=(1, 0),
        out_axes=1,
    )(extended, delays)
    framed = shifted.reshape(2, in_count, frame_count + TAPS - 1, CHANNELS)
    table = jnp.asarray(filter_table()).reshape(TAPS, CHANNELS)
    total = jnp.zeros((2, in_count, frame_count, CHANNELS), jnp.float32)
    for tap in range(TAPS):
        low = TAPS - 1 - tap
        total = total + table[tap] * framed[:, :, low : low + frame_count].astype(jnp.float32)
    branches = jnp.moveaxis(total.astype(jnp.bfloat16), 0, 2)

    number = in_count * frame_count
    cosine, sine = dft_parts(RADIX)
    block = np.concatenate(
        [np.concatenate([cosine, sine], axis=1), np.concatenate([-sine, cosine], axis=1)], axis=0
    )
    block = jnp.asarray(block)
    stacked = branches.reshape(number, 2 * RADIX, RADIX)
    inner = jnp.einsum("kj,nja->nka", block, stacked, preferred_element_type=jnp.float32)
    inner = inner.reshape(number, 2, RADIX, RADIX)
    tw_cos, tw_sin = (jnp.asarray(t[:, :RADIX]) for t in twiddle_tables())
    real = inner[:, 0] * tw_cos + inner[:, 1] * tw_sin
    imag = inner[:, 1] * tw_cos - inner[:, 0] * tw_sin
    turned = jnp.stack([real, imag], axis=2).reshape(number, RADIX, 2 * RADIX)
    turned = turned.astype(jnp.bfloat16)
    result = jnp.einsum("lj,nkj->nlk", block, turned, preferred_element_type=jnp.float32)
    spectra = result.reshape(in_count, frame_count, 2, CHANNELS).astype(jnp.bfloat16)
    moved = lax.all_to_all(spectra, "tm", split_axis=3, concat_axis=1, tiled=True)
    moved = lax.all_to_all(moved, "ct", split_axis=3, concat_axis=0, tiled=True)
    local = moved.transpose(3, 2, 0, 1)
    swapped = jnp.stack([local[:, 1], -local[:, 0]], axis=1)
    summed = jnp.einsum(
        "ocjaf,cjbf->ocab",
        jnp.stack([local, swapped], axis=0),
        lax.all_gather(local, "stn", axis=2, tiled=True),
        preferred_element_type=jnp.float32,
    )
    return summed * (1.0 / local.shape[3])


def on_device(voltages, delays):
    if fast_fits(voltages.shape[1], voltages.shape[2] // CHANNELS):
        return fast(voltages, delays)
    return general(voltages, delays)


def solution(mesh):
    return jax.shard_map(
        on_device,
        mesh=mesh,
        in_specs=(P(None, ("stn", "ct"), "tm"), P(("stn", "ct"))),
        out_specs=P(None, ("tm", "ct"), "stn", None),
        check_vma=False,
    )
```

```python
import functools
import math

import jax
import jax.numpy as jnp
import numpy as np
from jax import lax
from jax.experimental import pallas as pl
from jax.experimental.pallas import tpu as pltpu
from jax.sharding import PartitionSpec as P

CHANNELS = 4096
RADIX = 64
TAPS = 16
LANES = 128
ROWS = CHANNELS // LANES
PAIR = 2
TILE = 4
JOIN = 2

G_AT, O_AT, CORE_AT, CT_AT, DELAY_AT = range(5)

VMEM = pl.BlockSpec(memory_space=pltpu.VMEM)
SMEM = pl.BlockSpec(memory_space=pltpu.SMEM)
ANY = pl.BlockSpec(memory_space=pl.ANY)


def params(mib):
    return pltpu.CompilerParams(vmem_limit_bytes=mib * 2**20)


def cost(flops, size):
    return pl.CostEstimate(flops=flops, bytes_accessed=size, transcendentals=0)


def filter_table():
    length = TAPS * CHANNELS
    index = np.arange(length, dtype=np.float64)
    centred = (index - length / 2) / CHANNELS
    window = 0.5 - 0.5 * np.cos(2.0 * math.pi * index / length)
    factor = 1.0 / (48.0 * math.sqrt(CHANNELS))
    table = np.sinc(centred) * window * factor
    return table.reshape(TAPS, ROWS, LANES).astype(np.float32)


def dft_parts(radix):
    steps = np.arange(radix)
    angle = 2.0 * math.pi * (steps[:, None] * steps[None, :] % radix) / radix
    return np.cos(angle).astype(jnp.bfloat16), np.sin(angle).astype(jnp.bfloat16)


def first_table():
    cosine, sine = dft_parts(CHANNELS // RADIX)
    order = [2 * row + half for half in range(2) for row in range(ROWS)]
    cosine, sine = cosine[:, order], sine[:, order]
    upper = np.concatenate([cosine, sine], axis=1)
    lower = np.concatenate([-sine, cosine], axis=1)
    return np.concatenate([upper, lower], axis=0)


def last_table(outer, per_ct, span):
    cosine, sine = dft_parts(RADIX)
    blocks = []
    for g in range(PAIR):
        for ct in range(per_ct):
            steps = [
                ((o * PAIR + g) * per_ct + ct) * span + j for o in range(outer) for j in range(span)
            ]
            real = np.concatenate([cosine[steps], sine[steps]], axis=1)
            imag = np.concatenate([-sine[steps], cosine[steps]], axis=1)
            blocks.append(np.concatenate([real, imag], axis=0))
    return np.stack(blocks).reshape(PAIR, per_ct, -1, 2 * RADIX)


def twiddle_tables():
    rows = np.arange(CHANNELS // RADIX)
    cols = np.arange(RADIX)
    angle = 2.0 * math.pi * (rows[:, None] * cols[None, :] % CHANNELS) / CHANNELS
    cosine = np.cos(angle).astype(np.float32)
    sine = np.sin(angle).astype(np.float32)
    return np.concatenate([cosine, cosine], axis=1), np.concatenate([sine, sine], axis=1)


def pick_kernel(count, joined, own, meta, block, *refs):
    outs, rows = refs[:-1], refs[-1]
    inputs, samples = block.shape[1], block.shape[2]
    step = 16
    for part in range(2):

        def spread(n, carry, part=part):
            low = pl.multiple_of(n * step * LANES, step * LANES)
            wide = block[part, :, pl.ds(low, step * LANES)].astype(jnp.float32)
            for u in range(step):
                at = pl.multiple_of((n * step + u) * inputs, inputs)
                rows[part, pl.ds(at, inputs), :] = wide[:, u * LANES : (u + 1) * LANES]
            return carry

        lax.fori_loop(0, samples // LANES // step, spread, 0)
    first = (meta[G_AT] if own else 1 - meta[G_AT]) * count
    tall = 128
    for item in range(count):
        out = outs[0].at[item] if joined else outs[item]

        def gather(n, carry, item=item, out=out):
            low = pl.multiple_of(n * tall, tall)
            for part in range(2):
                value = rows[part, pl.ds(low * inputs + first + item, tall, stride=inputs), :]
                out[part, pl.ds(low, tall), :] = value.astype(jnp.bfloat16)
            return carry

        lax.fori_loop(0, samples // LANES // tall, gather, 0)


def pick(meta, block, count, joined, own):
    _, inputs, samples = block.shape
    one = (2, samples // LANES, LANES)
    shapes = [(count,) + one] if joined else [one] * count
    return pl.pallas_call(
        functools.partial(pick_kernel, count, joined, own),
        out_shape=[jax.ShapeDtypeStruct(s, jnp.bfloat16) for s in shapes],
        in_specs=[SMEM, VMEM],
        out_specs=[VMEM] * len(shapes),
        scratch_shapes=[pltpu.VMEM((2, samples // LANES * inputs, LANES), jnp.float32)],
        compiler_params=params(16),
        cost_estimate=cost(10**6, 4 * 2**20),
        name="pick",
    )(meta, block)


def follow(block, after):
    def hand_on(block, after, out):
        pass

    return pl.pallas_call(
        hand_on,
        out_shape=jax.ShapeDtypeStruct(block.shape, block.dtype),
        in_specs=[ANY, ANY],
        out_specs=ANY,
        input_output_aliases={0: 0},
        name="follow",
    )(block, after)


HALF = 16
SOME = 4


def filterbank_kernel(index, before, frames, dests, per_ct, half_count, *refs):
    meta, keep, halo_own, recv, halo_far, after, coef, first, tw_cos, tw_sin, last = refs[:11]
    earlier = refs[11 : 11 + dests * (before > 0)]
    refs = refs[11 + len(earlier) :]
    outs = refs[:dests]
    raw, weights, grouped, sems = refs[dests : dests + 4]
    filtered = refs[dests + 4 :]
    block_rows = frames * ROWS
    total = PAIR * frames
    me, ct = meta[G_AT], meta[CT_AT]
    delay = meta[DELAY_AT + me * half_count + index]
    down = delay // LANES
    across = delay % LANES
    lane = lax.broadcasted_iota(jnp.int32, (1, LANES), 1)
    inside = lane < LANES - across
    turned_in = lane >= across
    high = lane < RADIX

    def bring(source, place, sem):
        at = pl.multiple_of(place * block_rows, block_rows)
        return pltpu.make_async_copy(source, raw.at[:, pl.ds(at, block_rows), :], sems.at[sem])

    @pl.when(me == 0)
    def _():
        bring(halo_far, 0, 0).start()

    @pl.when(me != 0)
    def _():
        bring(halo_own.at[index], 0, 0).start()

    bring(keep.at[index], 1 + me, 1).start()
    bring(recv, 2 - me, 2).start()

    back = lax.rem(LANES - across, LANES)
    for tap in range(TAPS):
        here = coef[tap, pl.ds(down, ROWS), :]
        after = coef[tap, pl.ds(down + 1, ROWS), :]
        weights[tap] = pltpu.roll(jnp.where(turned_in, here, after), back, 1)
    for dest, old in zip(outs, earlier):
        dest[:before] = old[...]

    bring(halo_far, 0, 0).wait()
    bring(keep.at[index], 1 + me, 1).wait()
    bring(recv, 2 - me, 2).wait()

    def filt(half, low, high_frame, band, part):
        size = high_frame - low
        values = []
        for u in range(size + TAPS - 1):
            at = (half * HALF + low + u + frames - TAPS) * ROWS + band * 16
            values.append(raw[part, at : at + 16, :].astype(jnp.float32))
        sums = [None] * size
        for tap in range(TAPS):
            weight = weights[tap, band * 16 : band * 16 + 16, :]
            for u in range(size):
                term = weight * values[u + TAPS - 1 - tap]
                sums[u] = term if sums[u] is None else sums[u] + term
        for u in range(size):
            at = (low + u) * ROWS + band * 16
            filtered[half][part, at : at + 16, :] = sums[u]

    twice = lax.rem(across + RADIX, LANES)

    def place(half, u):
        for band in range(ROWS // 16):
            at = (u + 1) * ROWS + band * 16 - down
            moved, turned = [], []
            for part in range(2):
                here = filtered[half][part, pl.ds(at, 16), :]
                above = filtered[half][part, pl.ds(at - 1, 16), :]
                value = jnp.where(inside, here, above)
                moved.append(pltpu.roll(value, across, 1))
                turned.append(pltpu.roll(value, twice, 1))
            parts = (
                jnp.where(high, moved[0], turned[1]),
                jnp.where(high, turned[0], moved[1]),
                jnp.where(high, moved[1], -turned[0]),
                jnp.where(high, turned[1], -moved[0]),
            )
            for which, value in enumerate(parts):
                low = which * ROWS + band * 16
                grouped[half * HALF + u, low : low + 16, :] = value.astype(jnp.bfloat16)

    def turn(base):
        wide = jnp.concatenate([grouped[base + u] for u in range(SOME)], axis=1)
        inner = jnp.dot(first[...], wide, preferred_element_type=jnp.float32)
        rows = []
        for u in range(SOME):
            cut = slice(u * LANES, (u + 1) * LANES)
            value = inner[:RADIX, cut] * tw_cos[...] + inner[RADIX:, cut] * tw_sin[...]
            rows.append(value.astype(jnp.bfloat16))
        inner = jnp.concatenate(rows, axis=0)
        result = lax.dot_general(
            rows_out, inner, (((1,), (1,)), ((), ())), preferred_element_type=jnp.float32
        ).astype(jnp.bfloat16)
        size = result.shape[0] // (2 * dests)
        for dest in range(dests):
            for part in range(2):
                low = (dest * 2 + part) * size
                for u in range(SOME // 2):
                    outs[dest][before, base // 2 + u, part] = result[
                        low : low + size, u * LANES : (u + 1) * LANES
                    ]

    rows_out = jnp.concatenate(
        [last[me ^ dg, ct + dc] for dg in range(PAIR) for dc in range(per_ct)], axis=0
    )
    pieces = [
        (low, high_frame, band, part)
        for low, high_frame in ((0, 9), (9, HALF + 1))
        for band in range(ROWS // 16)
        for part in range(2)
    ]
    each = len(pieces) // (HALF // SOME)
    halves = total // HALF
    for half in range(halves + 1):
        for n in range(HALF // SOME):
            if half < halves:
                for piece in pieces[n * each : (n + 1) * each]:
                    filt(half, *piece)
            if half:
                for u in range(SOME):
                    place(half - 1, n * SOME + u)
                turn((half - 1) * HALF + n * SOME)


def filterbank(index, meta, keep, halo_own, recv, halo_far, after, tables, earlier, dests):
    frames = keep.shape[2] // ROWS
    size = tables[-1].shape[2] // 2
    per_ct = tables[-1].shape[1] // 2
    before = earlier[0].shape[0] if earlier else 0
    all_rows = (PAIR + 1) * frames * ROWS
    shape = (before + 1, PAIR * frames // 2, 2, size, LANES)
    return pl.pallas_call(
        functools.partial(
            filterbank_kernel, index, before, frames, dests, per_ct, keep.shape[0]
        ),
        out_shape=[jax.ShapeDtypeStruct(shape, jnp.bfloat16)] * dests,
        in_specs=[SMEM] + [ANY] * 5 + [VMEM] * (5 + len(earlier)),
        out_specs=[VMEM] * dests,
        scratch_shapes=[
            pltpu.VMEM((2, all_rows, LANES), jnp.bfloat16),
            pltpu.VMEM((TAPS, ROWS, LANES), jnp.float32),
            pltpu.VMEM((PAIR * frames, LANES, LANES), jnp.bfloat16),
            pltpu.SemaphoreType.DMA((3,)),
        ]
        + [pltpu.VMEM((2, (HALF + 1) * ROWS, LANES), jnp.float32)] * (PAIR * frames // HALF),
        compiler_params=params(16),
        cost_estimate=cost(10**9, 10 * 2**20),
        name="filterbank",
    )(meta, keep, halo_own, recv, halo_far, after, *tables, *earlier)


SQUARE = [(p, q) for p in range(TILE) for q in range(TILE)]
CORNER = [(p, q) for p in range(TILE) for q in range(p, TILE)]


def own_blocks(own):
    tiles = own // TILE
    whole = [(i, j, SQUARE) for i in range(tiles) for j in range(i + 1, tiles)]
    return whole + [(i, i, CORNER) for i in range(tiles)]


def cross_blocks(own):
    tiles = own // TILE
    return [(i, j, SQUARE) for i in range(tiles // 2) for j in range(tiles)]


def pairs_in(blocks):
    return sum(len(block[2]) for block in blocks)


def chosen(t, values):
    result = jnp.int32(values[0])
    for n, value in enumerate(values[1:], 1):
        result = jnp.where(t == n, jnp.int32(value), result)
    return result


def correlate_kernel(layout, *refs):
    sources_at, blocks, own, cross, outer, span, per_ct, in_count, half_count = layout
    meta, sources = refs[0], refs[1 : 1 + len(sources_at)]
    rest = refs[1 + len(sources_at) :]
    outs, (spectra, sums, held) = rest[:-3], rest[-3:]
    steps = spectra.shape[1]
    some = 8
    core, g, ct = meta[CORE_AT], meta[G_AT], meta[CT_AT]

    for source, (far, dg, dc, start) in zip(sources, sources_at):
        base = lax.rem(ct - dc + per_ct, per_ct) * in_count + (g ^ dg) * half_count + start
        wanted = None
        if cross:
            side = 1 - core if far else core
            low = core * (own // 2)
            wanted = (side == 1) | ((base >= low) & (base < low + own // 2))
            base = base + side * own

        def bring(source=source, base=base):
            for item in range(source.shape[0]):

                def spread(n, carry, item=item):
                    for u in range(some):
                        real = source[item, n * some + u, 0].astype(jnp.float32)
                        imag = source[item, n * some + u, 1].astype(jnp.float32)
                        for which, value in enumerate((real, imag, real + imag, imag - real)):
                            spectra[base + item, n * some + u, which] = value
                    return carry

                lax.fori_loop(0, steps // some, spread, 0)

        if wanted is None:
            bring()
        else:
            pl.when(wanted)(bring)

    high = lax.broadcasted_iota(jnp.int32, (1, LANES), 1) < RADIX
    rows_outer = pairs_in(blocks) * span
    size = outer * span
    unroll = 4

    def block(left, right, pairs, first_row):
        def over(one, two, acc, sign):
            def frame(n, acc):
                acc = list(acc)
                for u in range(unroll):
                    a = [spectra[left + p, n * unroll + u, one] for p in range(TILE)]
                    b = [spectra[right + q, n * unroll + u, two] for q in range(TILE)]
                    for at, (p, q) in enumerate(pairs):
                        term = a[p] * b[q]
                        acc[at] = acc[at] + term if sign > 0 else acc[at] - term
                return tuple(acc)

            return lax.fori_loop(0, steps // unroll, frame, tuple(acc))

        count = len(pairs)
        first = over(2, 0, [jnp.zeros((size, LANES), jnp.float32)] * count, 1)
        for at in range(count):
            held[0, at] = first[at]
        real = over(1, 3, first, 1)
        for at in range(count):
            held[1, at] = real[at] + pltpu.roll(real[at], RADIX, 1)
        imag = over(0, 2, [held[0, at] for at in range(count)], -1)
        for at in range(count):
            folded = imag[at] + pltpu.roll(imag[at], RADIX, 1)
            both = jnp.where(high, held[1, at], folded)
            for o in range(outer):
                row = o * rows_outer + first_row + at * span
                sums[pl.ds(pl.multiple_of(row, span), span), :] = both[o * span : (o + 1) * span]

    done = 0
    for pairs in (SQUARE, CORNER):
        some_blocks = [b for b in blocks if b[2] is pairs]
        if not some_blocks:
            continue

        def step(t, carry, some_blocks=some_blocks, pairs=pairs, done=done):
            left = TILE * chosen(t, [b[0] for b in some_blocks])
            right = TILE * chosen(t, [b[1] for b in some_blocks])
            if cross:
                left, right = left + core * (own // 2), right + own
            block(left, right, pairs, done + t * len(pairs) * span)
            return carry

        lax.fori_loop(0, len(some_blocks), step, 0)
        done += pairs_in(some_blocks) * span

    for r in range(outer):
        base = pl.multiple_of(lax.rem(meta[O_AT] + r, outer) * rows_outer, 16)
        outs[r][...] = sums[pl.ds(base, rows_outer), :].astype(outs[r].dtype)


def correlate(meta, arrays, sources_at, blocks, own, cross, sizes, name):
    outer, span, per_ct, in_count, half_count = sizes
    _, steps, _, size, _ = arrays[0].shape
    inputs = 2 * own if cross else own
    rows = pairs_in(blocks) * span
    shapes = []
    for r in range(outer):
        dtype = jnp.float32 if r == 0 else jnp.bfloat16
        shapes.append(jax.ShapeDtypeStruct((rows, LANES), dtype))
    layout = (sources_at, blocks, own, cross) + sizes
    return pl.pallas_call(
        functools.partial(correlate_kernel, layout),
        out_shape=shapes,
        in_specs=[SMEM] + [VMEM] * len(arrays),
        out_specs=[VMEM] * len(shapes),
        scratch_shapes=[
            pltpu.VMEM((inputs, steps, 4, size, LANES), jnp.float32),
            pltpu.VMEM((outer * rows, LANES), jnp.float32),
            pltpu.VMEM((2, TILE * TILE, outer * span, LANES), jnp.float32),
        ],
        compiler_params=params(14 + inputs * steps * 4 * size * LANES * 4 // 2**20),
        cost_estimate=cost(10**9, 22 * 2**20),
        name=name,
    )(meta, *arrays)


def assemble_kernel(own, outer, span, scale, *refs):
    meta = refs[0]
    mine_in = refs[1 : 1 + outer]
    mine_across = refs[1 + outer : 1 + 2 * outer]
    far_across = refs[1 + 2 * outer : 1 + 3 * outer]
    out, joined = refs[1 + 3 * outer :]
    lane = lax.broadcasted_iota(jnp.int32, (1, LANES), 1)
    high = lane < RADIX
    mirror = jnp.where(high, 1.0, -1.0).astype(jnp.float32)
    me = meta[CORE_AT]

    def added(sources, low, rows):
        total = sources[0][low : low + rows, :].astype(jnp.float32)
        for source in sources[1:]:
            total = total + source[low : low + rows, :].astype(jnp.float32)
        return total * scale

    def put(value, row, col):
        at = pl.multiple_of((row * 2 * own + col) * span, span)
        joined[pl.ds(at, span), :] = value

    done = 0
    for i, j, pairs in own_blocks(own):
        total = added(mine_in, done, len(pairs) * span)
        turned = total * mirror
        for at, (p, q) in enumerate(pairs):
            cut = slice(at * span, (at + 1) * span)
            a, b = i * TILE + p, j * TILE + q
            put(total[cut], a, me * own + b)
            if a != b:
                put(turned[cut], b, me * own + a)
        done += len(pairs) * span
    sign = jnp.where(me == 0, jnp.ones_like(mirror), mirror)
    for sources, part in ((mine_across, me), (far_across, 1 - me)):
        done = 0
        for i, j, pairs in cross_blocks(own):
            total = added(sources, done, len(pairs) * span) * sign
            for at, (p, q) in enumerate(pairs):
                a = part * (own // 2) + i * TILE + p
                b = j * TILE + q
                row = jnp.where(me == 0, a, b)
                col = jnp.where(me == 0, own + b, a)
                put(total[at * span : (at + 1) * span], row, col)
            done += len(pairs) * span

    def emit(a, carry):
        for tile in range(2 * own // 8):
            for pair in range(span // 2):
                loads = []
                for u in range(2):
                    at = (a * 2 * own + tile * 8) * span + pair * 2 + u
                    loads.append(joined[pl.ds(at, 8, stride=span), :])
                turned = [pltpu.roll(x, RADIX, 1) for x in loads]
                cut = slice(pair * LANES, (pair + 1) * LANES)
                out[0, a, tile * 8 : tile * 8 + 8, cut] = jnp.where(high, loads[0], turned[1])
                out[1, a, tile * 8 : tile * 8 + 8, cut] = jnp.where(high, turned[0], loads[1])
        return carry

    lax.fori_loop(0, own, emit, 0)


def assemble(meta, mine_in, mine_across, far_across, own, span, scale):
    outer = len(mine_in)
    return pl.pallas_call(
        functools.partial(assemble_kernel, own, outer, span, scale),
        out_shape=jax.ShapeDtypeStruct((2, own, 2 * own, span * RADIX), jnp.float32),
        in_specs=[SMEM] + [VMEM] * (3 * outer),
        out_specs=VMEM,
        scratch_shapes=[pltpu.VMEM((own * 2 * own * span, LANES), jnp.float32)],
        compiler_params=params(24),
        cost_estimate=cost(10**8, 8 * 2**20),
        name="assemble",
    )(meta, *mine_in, *mine_across, *far_across)


def fast_fits(in_count, frame_count):
    stn, tm, per_ct = (lax.axis_size(a) for a in ("stn", "tm", "ct"))
    groups = tm * per_ct
    if stn != 2 or tm % PAIR or in_count % (PAIR * JOIN) or RADIX % groups:
        return False
    outer, span = tm // PAIR, RADIX // groups
    own = in_count * per_ct
    return (
        frame_count >= TAPS
        and frame_count % HALF == 0
        and span in (2, 4, 8)
        and outer * span % 16 == 0
        and own % (2 * TILE) == 0
        and (own * (own + 1) // 2 * span) % 16 == 0
    )


def fast(voltages, delays):
    tm, per_ct = lax.axis_size("tm"), lax.axis_size("ct")
    in_count = voltages.shape[1]
    frame_count = voltages.shape[2] // CHANNELS
    outer = tm // PAIR
    span = RADIX // (tm * per_ct)
    own = in_count * per_ct
    half = in_count // PAIR
    place_tm, place_ct = lax.axis_index("tm"), lax.axis_index("ct")
    core = lax.axis_index("stn")
    g, o = place_tm % PAIR, place_tm // PAIR

    swap = [(i, i ^ 1) for i in range(tm)]
    onward = [(i, i + PAIR) for i in range(tm - PAIR)]
    cores = [(0, 1), (1, 0)]

    scalars = [None] * DELAY_AT
    scalars[G_AT], scalars[O_AT], scalars[CORE_AT], scalars[CT_AT] = g, o, core, place_ct
    meta = jnp.concatenate([jnp.stack(scalars).astype(jnp.int32), delays])

    dests = [(dg, dc) for dg in range(PAIR) for dc in range(per_ct)]
    base = last_table(outer, per_ct, span)
    tables = [np.concatenate([filter_table()] * 2, axis=1), first_table(), *twiddle_tables()]
    tables = [jnp.asarray(t) for t in tables + [np.concatenate([base, base], axis=1)]]

    sends = list(pick(meta, voltages, half, False, False))
    recvs = []
    for c in range(half):
        block = sends[c] if c < 2 else follow(sends[c], recvs[c - 2])
        recvs.append(lax.ppermute(block, "tm", swap))
    keep = pick(meta, voltages, half, True, True)[0]
    halo_own = lax.ppermute(keep, "tm", [p for p in onward if p[0] % PAIR == 1])
    fars = [lax.ppermute(block, "tm", [p for p in onward if p[0] % PAIR == 0]) for block in recvs]

    arrays, others, places = [], [], []
    spectra, after = [], meta
    for c in range(half):
        spectra = filterbank(
            c, meta, keep, halo_own, recvs[c], fars[c], after, tables, spectra, len(dests)
        )
        after = spectra[0]
        if c % JOIN < JOIN - 1:
            continue
        for (dg, dc), block in zip(dests, spectra):
            route = []
            for i in range(tm):
                for j in range(per_ct):
                    target = (i ^ dg) * per_ct + (j + dc) % per_ct
                    route.append((i * per_ct + j, target))
            if dg or dc:
                block = lax.ppermute(block, ("tm", "ct"), route)
            arrays.append(block)
            others.append(lax.ppermute(block, "stn", cores))
            places.append((dg, dc, c - JOIN + 1))
        spectra = []

    sizes = (outer, span, per_ct, in_count, half)
    near = [(False,) + place for place in places]
    far = [(True,) + place for place in places]
    mine_in = correlate(
        meta, arrays, near, own_blocks(own), own, False, sizes, "correlate_own"
    )
    mine_across = correlate(
        meta, arrays + others, near + far, cross_blocks(own), own, True, sizes, "correlate_cross"
    )
    mine_in, mine_across, far_across = list(mine_in), list(mine_across), []
    for r in range(1, outer):
        route = [(i, (i + r * PAIR) % tm) for i in range(tm)]
        mine_in[r] = lax.ppermute(mine_in[r], "tm", route)
    for r in range(outer):
        if r:
            route = [(i, (i + r * PAIR) % tm) for i in range(tm)]
            mine_across[r] = lax.ppermute(mine_across[r], "tm", route)
        far_across.append(lax.ppermute(mine_across[r], "stn", cores))
    scale = 1.0 / (tm * frame_count)
    result = assemble(meta, mine_in, mine_across, far_across, own, span, scale)
    return result.transpose(0, 3, 1, 2)


def general(voltages, delays):
    in_count = voltages.shape[1]
    frame_count = voltages.shape[2] // CHANNELS
    route = [(i, i + 1) for i in range(lax.axis_size("tm") - 1)]
    extended = jnp.concatenate([lax.ppermute(voltages, "tm", route), voltages], axis=2)
    span = (frame_count + TAPS - 1) * CHANNELS
    shifted = jax.vmap(
        lambda row, offset: lax.dynamic_slice_in_dim(row, CHANNELS - offset, span, 1),
        in_axes=(1, 0),
        out_axes=1,
    )(extended, delays)
    framed = shifted.reshape(2, in_count, frame_count + TAPS - 1, CHANNELS)
    table = jnp.asarray(filter_table()).reshape(TAPS, CHANNELS)
    total = jnp.zeros((2, in_count, frame_count, CHANNELS), jnp.float32)
    for tap in range(TAPS):
        low = TAPS - 1 - tap
        total = total + table[tap] * framed[:, :, low : low + frame_count].astype(jnp.float32)
    branches = jnp.moveaxis(total.astype(jnp.bfloat16), 0, 2)

    number = in_count * frame_count
    cosine, sine = dft_parts(RADIX)
    block = np.concatenate(
        [np.concatenate([cosine, sine], axis=1), np.concatenate([-sine, cosine], axis=1)], axis=0
    )
    block = jnp.asarray(block)
    stacked = branches.reshape(number, 2 * RADIX, RADIX)
    inner = jnp.einsum("kj,nja->nka", block, stacked, preferred_element_type=jnp.float32)
    inner = inner.reshape(number, 2, RADIX, RADIX)
    tw_cos, tw_sin = (jnp.asarray(t[:, :RADIX]) for t in twiddle_tables())
    real = inner[:, 0] * tw_cos + inner[:, 1] * tw_sin
    imag = inner[:, 1] * tw_cos - inner[:, 0] * tw_sin
    turned = jnp.stack([real, imag], axis=2).reshape(number, RADIX, 2 * RADIX)
    turned = turned.astype(jnp.bfloat16)
    result = jnp.einsum("lj,nkj->nlk", block, turned, preferred_element_type=jnp.float32)
    spectra = result.reshape(in_count, frame_count, 2, CHANNELS).astype(jnp.bfloat16)
    moved = lax.all_to_all(spectra, "tm", split_axis=3, concat_axis=1, tiled=True)
    moved = lax.all_to_all(moved, "ct", split_axis=3, concat_axis=0, tiled=True)
    local = moved.transpose(3, 2, 0, 1)
    swapped = jnp.stack([local[:, 1], -local[:, 0]], axis=1)
    summed = jnp.einsum(
        "ocjaf,cjbf->ocab",
        jnp.stack([local, swapped], axis=0),
        lax.all_gather(local, "stn", axis=2, tiled=True),
        preferred_element_type=jnp.float32,
    )
    return summed * (1.0 / local.shape[3])


def on_device(voltages, delays):
    if fast_fits(voltages.shape[1], voltages.shape[2] // CHANNELS):
        return fast(voltages, delays)
    return general(voltages, delays)


def solution(mesh):
    return jax.shard_map(
        on_device,
        mesh=mesh,
        in_specs=(P(None, ("stn", "ct"), "tm"), P(("stn", "ct"))),
        out_specs=P(None, ("tm", "ct"), "stn", None),
        check_vma=False,
    )
```

```python
import functools
import math

import jax
import jax.numpy as jnp
import numpy as np
from jax import lax
from jax.experimental import pallas as pl
from jax.experimental.pallas import tpu as pltpu
from jax.sharding import PartitionSpec as P

CHANNELS = 4096
RADIX = 64
TAPS = 16
LANES = 128
ROWS = CHANNELS // LANES
PAIR = 2
TILE = 4
JOIN = 2

G_AT, O_AT, CORE_AT, CT_AT, DELAY_AT = range(5)

VMEM = pl.BlockSpec(memory_space=pltpu.VMEM)
SMEM = pl.BlockSpec(memory_space=pltpu.SMEM)
ANY = pl.BlockSpec(memory_space=pl.ANY)


def params(mib):
    return pltpu.CompilerParams(vmem_limit_bytes=mib * 2**20)


def cost(flops, size):
    return pl.CostEstimate(flops=flops, bytes_accessed=size, transcendentals=0)


def filter_table():
    length = TAPS * CHANNELS
    index = np.arange(length, dtype=np.float64)
    centred = (index - length / 2) / CHANNELS
    window = 0.5 - 0.5 * np.cos(2.0 * math.pi * index / length)
    factor = 1.0 / (48.0 * math.sqrt(CHANNELS))
    table = np.sinc(centred) * window * factor
    return table.reshape(TAPS, ROWS, LANES).astype(np.float32)


def dft_parts(radix):
    steps = np.arange(radix)
    angle = 2.0 * math.pi * (steps[:, None] * steps[None, :] % radix) / radix
    return np.cos(angle).astype(jnp.bfloat16), np.sin(angle).astype(jnp.bfloat16)


def first_table():
    cosine, sine = dft_parts(CHANNELS // RADIX)
    order = [2 * row + half for half in range(2) for row in range(ROWS)]
    cosine, sine = cosine[:, order], sine[:, order]
    upper = np.concatenate([cosine, sine], axis=1)
    lower = np.concatenate([-sine, cosine], axis=1)
    return np.concatenate([upper, lower], axis=0)


def last_table(outer, per_ct, span):
    cosine, sine = dft_parts(RADIX)
    blocks = []
    for g in range(PAIR):
        for ct in range(per_ct):
            steps = [
                ((o * PAIR + g) * per_ct + ct) * span + j for o in range(outer) for j in range(span)
            ]
            real = np.concatenate([cosine[steps], sine[steps]], axis=1)
            imag = np.concatenate([-sine[steps], cosine[steps]], axis=1)
            blocks.append(np.concatenate([real, imag], axis=0))
    return np.stack(blocks).reshape(PAIR, per_ct, -1, 2 * RADIX)


def twiddle_tables():
    rows = np.arange(CHANNELS // RADIX)
    cols = np.arange(RADIX)
    angle = 2.0 * math.pi * (rows[:, None] * cols[None, :] % CHANNELS) / CHANNELS
    cosine = np.cos(angle).astype(np.float32)
    sine = np.sin(angle).astype(np.float32)
    return np.concatenate([cosine, cosine], axis=1), np.concatenate([sine, sine], axis=1)


def pick_kernel(count, joined, own, meta, block, *refs):
    outs, rows = refs[:-1], refs[-1]
    inputs, samples = block.shape[1], block.shape[2]
    step = 16
    for part in range(2):

        def spread(n, carry, part=part):
            low = pl.multiple_of(n * step * LANES, step * LANES)
            wide = block[part, :, pl.ds(low, step * LANES)].astype(jnp.float32)
            for u in range(step):
                at = pl.multiple_of((n * step + u) * inputs, inputs)
                rows[part, pl.ds(at, inputs), :] = wide[:, u * LANES : (u + 1) * LANES]
            return carry

        lax.fori_loop(0, samples // LANES // step, spread, 0)
    first = (meta[G_AT] if own else 1 - meta[G_AT]) * count
    tall = 128
    for item in range(count):
        out = outs[0].at[item] if joined else outs[item]

        def gather(n, carry, item=item, out=out):
            low = pl.multiple_of(n * tall, tall)
            for part in range(2):
                value = rows[part, pl.ds(low * inputs + first + item, tall, stride=inputs), :]
                out[part, pl.ds(low, tall), :] = value.astype(jnp.bfloat16)
            return carry

        lax.fori_loop(0, samples // LANES // tall, gather, 0)


def pick(meta, block, count, joined, own):
    _, inputs, samples = block.shape
    one = (2, samples // LANES, LANES)
    shapes = [(count,) + one] if joined else [one] * count
    return pl.pallas_call(
        functools.partial(pick_kernel, count, joined, own),
        out_shape=[jax.ShapeDtypeStruct(s, jnp.bfloat16) for s in shapes],
        in_specs=[SMEM, VMEM],
        out_specs=[VMEM] * len(shapes),
        scratch_shapes=[pltpu.VMEM((2, samples // LANES * inputs, LANES), jnp.float32)],
        compiler_params=params(16),
        cost_estimate=cost(10**6, 2**18),
        name="pick",
    )(meta, block)


def follow(block, after):
    def hand_on(block, after, out):
        pass

    return pl.pallas_call(
        hand_on,
        out_shape=jax.ShapeDtypeStruct(block.shape, block.dtype),
        in_specs=[ANY, ANY],
        out_specs=ANY,
        input_output_aliases={0: 0},
        name="follow",
    )(block, after)


HALF = 16
SOME = 4


def filterbank_kernel(index, before, frames, dests, per_ct, half_count, *refs):
    meta, keep, halo_own, recv, halo_far, after, coef, first, tw_cos, tw_sin, last = refs[:11]
    earlier = refs[11 : 11 + dests * (before > 0)]
    refs = refs[11 + len(earlier) :]
    outs = refs[:dests]
    raw, weights, grouped, sems = refs[dests : dests + 4]
    filtered = refs[dests + 4 :]
    block_rows = frames * ROWS
    total = PAIR * frames
    me, ct = meta[G_AT], meta[CT_AT]
    delay = meta[DELAY_AT + me * half_count + index]
    down = delay // LANES
    across = delay % LANES
    lane = lax.broadcasted_iota(jnp.int32, (1, LANES), 1)
    inside = lane < LANES - across
    turned_in = lane >= across
    high = lane < RADIX

    def bring(source, place, sem):
        at = pl.multiple_of(place * block_rows, block_rows)
        return pltpu.make_async_copy(source, raw.at[:, pl.ds(at, block_rows), :], sems.at[sem])

    @pl.when(me == 0)
    def _():
        bring(halo_far, 0, 0).start()

    @pl.when(me != 0)
    def _():
        bring(halo_own.at[index], 0, 0).start()

    bring(keep.at[index], 1 + me, 1).start()
    bring(recv, 2 - me, 2).start()

    back = lax.rem(LANES - across, LANES)
    for tap in range(TAPS):
        here = coef[tap, pl.ds(down, ROWS), :]
        after = coef[tap, pl.ds(down + 1, ROWS), :]
        weights[tap] = pltpu.roll(jnp.where(turned_in, here, after), back, 1)
    for dest, old in zip(outs, earlier):
        dest[:before] = old[...]

    bring(halo_far, 0, 0).wait()
    bring(keep.at[index], 1 + me, 1).wait()
    bring(recv, 2 - me, 2).wait()

    def filt(half, low, high_frame, band, part):
        size = high_frame - low
        values = []
        for u in range(size + TAPS - 1):
            at = (half * HALF + low + u + frames - TAPS) * ROWS + band * 16
            values.append(raw[part, at : at + 16, :].astype(jnp.float32))
        sums = [None] * size
        for tap in range(TAPS):
            weight = weights[tap, band * 16 : band * 16 + 16, :]
            for u in range(size):
                term = weight * values[u + TAPS - 1 - tap]
                sums[u] = term if sums[u] is None else sums[u] + term
        for u in range(size):
            at = (low + u) * ROWS + band * 16
            filtered[half][part, at : at + 16, :] = sums[u]

    twice = lax.rem(across + RADIX, LANES)

    def place(half, u):
        for band in range(ROWS // 16):
            at = (u + 1) * ROWS + band * 16 - down
            moved, turned = [], []
            for part in range(2):
                here = filtered[half][part, pl.ds(at, 16), :]
                above = filtered[half][part, pl.ds(at - 1, 16), :]
                value = jnp.where(inside, here, above)
                moved.append(pltpu.roll(value, across, 1))
                turned.append(pltpu.roll(value, twice, 1))
            parts = (
                jnp.where(high, moved[0], turned[1]),
                jnp.where(high, turned[0], moved[1]),
                jnp.where(high, moved[1], -turned[0]),
                jnp.where(high, turned[1], -moved[0]),
            )
            for which, value in enumerate(parts):
                low = which * ROWS + band * 16
                grouped[half * HALF + u, low : low + 16, :] = value.astype(jnp.bfloat16)

    def turn(base):
        wide = jnp.concatenate([grouped[base + u] for u in range(SOME)], axis=1)
        inner = jnp.dot(first[...], wide, preferred_element_type=jnp.float32)
        rows = []
        for u in range(SOME):
            cut = slice(u * LANES, (u + 1) * LANES)
            value = inner[:RADIX, cut] * tw_cos[...] + inner[RADIX:, cut] * tw_sin[...]
            rows.append(value.astype(jnp.bfloat16))
        inner = jnp.concatenate(rows, axis=0)
        result = lax.dot_general(
            rows_out, inner, (((1,), (1,)), ((), ())), preferred_element_type=jnp.float32
        ).astype(jnp.bfloat16)
        size = result.shape[0] // (2 * dests)
        for dest in range(dests):
            for part in range(2):
                low = (dest * 2 + part) * size
                for u in range(SOME // 2):
                    outs[dest][before, base // 2 + u, part] = result[
                        low : low + size, u * LANES : (u + 1) * LANES
                    ]

    rows_out = jnp.concatenate(
        [last[me ^ dg, ct + dc] for dg in range(PAIR) for dc in range(per_ct)], axis=0
    )
    pieces = [
        (low, high_frame, band, part)
        for low, high_frame in ((0, 9), (9, HALF + 1))
        for band in range(ROWS // 16)
        for part in range(2)
    ]
    each = len(pieces) // (HALF // SOME)
    halves = total // HALF
    for half in range(halves + 1):
        for n in range(HALF // SOME):
            if half < halves:
                for piece in pieces[n * each : (n + 1) * each]:
                    filt(half, *piece)
            if half:
                for u in range(SOME):
                    place(half - 1, n * SOME + u)
                turn((half - 1) * HALF + n * SOME)


def filterbank(index, meta, keep, halo_own, recv, halo_far, after, tables, earlier, dests):
    frames = keep.shape[2] // ROWS
    size = tables[-1].shape[2] // 2
    per_ct = tables[-1].shape[1] // 2
    before = earlier[0].shape[0] if earlier else 0
    all_rows = (PAIR + 1) * frames * ROWS
    shape = (before + 1, PAIR * frames // 2, 2, size, LANES)
    return pl.pallas_call(
        functools.partial(
            filterbank_kernel, index, before, frames, dests, per_ct, keep.shape[0]
        ),
        out_shape=[jax.ShapeDtypeStruct(shape, jnp.bfloat16)] * dests,
        in_specs=[SMEM] + [ANY] * 5 + [VMEM] * (5 + len(earlier)),
        out_specs=[VMEM] * dests,
        scratch_shapes=[
            pltpu.VMEM((2, all_rows, LANES), jnp.bfloat16),
            pltpu.VMEM((TAPS, ROWS, LANES), jnp.float32),
            pltpu.VMEM((PAIR * frames, LANES, LANES), jnp.bfloat16),
            pltpu.SemaphoreType.DMA((3,)),
        ]
        + [pltpu.VMEM((2, (HALF + 1) * ROWS, LANES), jnp.float32)] * (PAIR * frames // HALF),
        compiler_params=params(16),
        cost_estimate=cost(10**6, 2**18),
        name="filterbank",
    )(meta, keep, halo_own, recv, halo_far, after, *tables, *earlier)


SQUARE = [(p, q) for p in range(TILE) for q in range(TILE)]
CORNER = [(p, q) for p in range(TILE) for q in range(p, TILE)]


def own_blocks(own):
    tiles = own // TILE
    whole = [(i, j, SQUARE) for i in range(tiles) for j in range(i + 1, tiles)]
    return whole + [(i, i, CORNER) for i in range(tiles)]


def cross_blocks(own):
    tiles = own // TILE
    return [(i, j, SQUARE) for i in range(tiles // 2) for j in range(tiles)]


def pairs_in(blocks):
    return sum(len(block[2]) for block in blocks)


def chosen(t, values):
    result = jnp.int32(values[0])
    for n, value in enumerate(values[1:], 1):
        result = jnp.where(t == n, jnp.int32(value), result)
    return result


def correlate_kernel(layout, *refs):
    sources_at, blocks, own, cross, outer, span, per_ct, in_count, half_count = layout
    meta, sources = refs[0], refs[1 : 1 + len(sources_at)]
    rest = refs[1 + len(sources_at) :]
    outs, (spectra, sums, held) = rest[:-3], rest[-3:]
    steps = spectra.shape[1]
    some = 8
    core, g, ct = meta[CORE_AT], meta[G_AT], meta[CT_AT]

    for source, (far, dg, dc, start) in zip(sources, sources_at):
        base = lax.rem(ct - dc + per_ct, per_ct) * in_count + (g ^ dg) * half_count + start
        wanted = None
        if cross:
            side = 1 - core if far else core
            low = core * (own // 2)
            wanted = (side == 1) | ((base >= low) & (base < low + own // 2))
            base = base + side * own

        def bring(source=source, base=base):
            for item in range(source.shape[0]):

                def spread(n, carry, item=item):
                    for u in range(some):
                        real = source[item, n * some + u, 0].astype(jnp.float32)
                        imag = source[item, n * some + u, 1].astype(jnp.float32)
                        for which, value in enumerate((real, imag, real + imag, imag - real)):
                            spectra[base + item, n * some + u, which] = value
                    return carry

                lax.fori_loop(0, steps // some, spread, 0)

        if wanted is None:
            bring()
        else:
            pl.when(wanted)(bring)

    high = lax.broadcasted_iota(jnp.int32, (1, LANES), 1) < RADIX
    rows_outer = pairs_in(blocks) * span
    size = outer * span
    unroll = 4

    def block(left, right, pairs, first_row):
        def over(one, two, acc, sign):
            def frame(n, acc):
                acc = list(acc)
                for u in range(unroll):
                    a = [spectra[left + p, n * unroll + u, one] for p in range(TILE)]
                    b = [spectra[right + q, n * unroll + u, two] for q in range(TILE)]
                    for at, (p, q) in enumerate(pairs):
                        term = a[p] * b[q]
                        acc[at] = acc[at] + term if sign > 0 else acc[at] - term
                return tuple(acc)

            return lax.fori_loop(0, steps // unroll, frame, tuple(acc))

        count = len(pairs)
        first = over(2, 0, [jnp.zeros((size, LANES), jnp.float32)] * count, 1)
        for at in range(count):
            held[0, at] = first[at]
        real = over(1, 3, first, 1)
        for at in range(count):
            held[1, at] = real[at] + pltpu.roll(real[at], RADIX, 1)
        imag = over(0, 2, [held[0, at] for at in range(count)], -1)
        for at in range(count):
            folded = imag[at] + pltpu.roll(imag[at], RADIX, 1)
            both = jnp.where(high, held[1, at], folded)
            for o in range(outer):
                row = o * rows_outer + first_row + at * span
                sums[pl.ds(pl.multiple_of(row, span), span), :] = both[o * span : (o + 1) * span]

    done = 0
    for pairs in (SQUARE, CORNER):
        some_blocks = [b for b in blocks if b[2] is pairs]
        if not some_blocks:
            continue

        def step(t, carry, some_blocks=some_blocks, pairs=pairs, done=done):
            left = TILE * chosen(t, [b[0] for b in some_blocks])
            right = TILE * chosen(t, [b[1] for b in some_blocks])
            if cross:
                left, right = left + core * (own // 2), right + own
            block(left, right, pairs, done + t * len(pairs) * span)
            return carry

        lax.fori_loop(0, len(some_blocks), step, 0)
        done += pairs_in(some_blocks) * span

    for r in range(outer):
        base = pl.multiple_of(lax.rem(meta[O_AT] + r, outer) * rows_outer, 16)
        outs[r][...] = sums[pl.ds(base, rows_outer), :].astype(outs[r].dtype)


def correlate(meta, arrays, sources_at, blocks, own, cross, sizes, name):
    outer, span, per_ct, in_count, half_count = sizes
    _, steps, _, size, _ = arrays[0].shape
    inputs = 2 * own if cross else own
    rows = pairs_in(blocks) * span
    shapes = []
    for r in range(outer):
        dtype = jnp.float32 if r == 0 else jnp.bfloat16
        shapes.append(jax.ShapeDtypeStruct((rows, LANES), dtype))
    layout = (sources_at, blocks, own, cross) + sizes
    return pl.pallas_call(
        functools.partial(correlate_kernel, layout),
        out_shape=shapes,
        in_specs=[SMEM] + [VMEM] * len(arrays),
        out_specs=[VMEM] * len(shapes),
        scratch_shapes=[
            pltpu.VMEM((inputs, steps, 4, size, LANES), jnp.float32),
            pltpu.VMEM((outer * rows, LANES), jnp.float32),
            pltpu.VMEM((2, TILE * TILE, outer * span, LANES), jnp.float32),
        ],
        compiler_params=params(14 + inputs * steps * 4 * size * LANES * 4 // 2**20),
        cost_estimate=cost(10**6, 2**18),
        name=name,
    )(meta, *arrays)


def assemble_kernel(own, outer, span, scale, *refs):
    meta = refs[0]
    mine_in = refs[1 : 1 + outer]
    mine_across = refs[1 + outer : 1 + 2 * outer]
    far_across = refs[1 + 2 * outer : 1 + 3 * outer]
    out, joined = refs[1 + 3 * outer :]
    lane = lax.broadcasted_iota(jnp.int32, (1, LANES), 1)
    high = lane < RADIX
    mirror = jnp.where(high, 1.0, -1.0).astype(jnp.float32)
    me = meta[CORE_AT]

    def added(sources, low, rows):
        total = sources[0][low : low + rows, :].astype(jnp.float32)
        for source in sources[1:]:
            total = total + source[low : low + rows, :].astype(jnp.float32)
        return total * scale

    def put(value, row, col):
        at = pl.multiple_of((row * 2 * own + col) * span, span)
        joined[pl.ds(at, span), :] = value

    done = 0
    for i, j, pairs in own_blocks(own):
        total = added(mine_in, done, len(pairs) * span)
        turned = total * mirror
        for at, (p, q) in enumerate(pairs):
            cut = slice(at * span, (at + 1) * span)
            a, b = i * TILE + p, j * TILE + q
            put(total[cut], a, me * own + b)
            if a != b:
                put(turned[cut], b, me * own + a)
        done += len(pairs) * span
    sign = jnp.where(me == 0, jnp.ones_like(mirror), mirror)
    for sources, part in ((mine_across, me), (far_across, 1 - me)):
        done = 0
        for i, j, pairs in cross_blocks(own):
            total = added(sources, done, len(pairs) * span) * sign
            for at, (p, q) in enumerate(pairs):
                a = part * (own // 2) + i * TILE + p
                b = j * TILE + q
                row = jnp.where(me == 0, a, b)
                col = jnp.where(me == 0, own + b, a)
                put(total[at * span : (at + 1) * span], row, col)
            done += len(pairs) * span

    def emit(a, carry):
        for tile in range(2 * own // 8):
            for pair in range(span // 2):
                loads = []
                for u in range(2):
                    at = (a * 2 * own + tile * 8) * span + pair * 2 + u
                    loads.append(joined[pl.ds(at, 8, stride=span), :])
                turned = [pltpu.roll(x, RADIX, 1) for x in loads]
                cut = slice(pair * LANES, (pair + 1) * LANES)
                out[0, a, tile * 8 : tile * 8 + 8, cut] = jnp.where(high, loads[0], turned[1])
                out[1, a, tile * 8 : tile * 8 + 8, cut] = jnp.where(high, turned[0], loads[1])
        return carry

    lax.fori_loop(0, own, emit, 0)


def assemble(meta, mine_in, mine_across, far_across, own, span, scale):
    outer = len(mine_in)
    return pl.pallas_call(
        functools.partial(assemble_kernel, own, outer, span, scale),
        out_shape=jax.ShapeDtypeStruct((2, own, 2 * own, span * RADIX), jnp.float32),
        in_specs=[SMEM] + [VMEM] * (3 * outer),
        out_specs=VMEM,
        scratch_shapes=[pltpu.VMEM((own * 2 * own * span, LANES), jnp.float32)],
        compiler_params=params(24),
        cost_estimate=cost(10**6, 2**18),
        name="assemble",
    )(meta, *mine_in, *mine_across, *far_across)


def fast_fits(in_count, frame_count):
    stn, tm, per_ct = (lax.axis_size(a) for a in ("stn", "tm", "ct"))
    groups = tm * per_ct
    if stn != 2 or tm % PAIR or in_count % (PAIR * JOIN) or RADIX % groups:
        return False
    outer, span = tm // PAIR, RADIX // groups
    own = in_count * per_ct
    return (
        frame_count >= TAPS
        and frame_count % HALF == 0
        and span in (2, 4, 8)
        and outer * span % 16 == 0
        and own % (2 * TILE) == 0
        and (own * (own + 1) // 2 * span) % 16 == 0
    )


def fast(voltages, delays):
    tm, per_ct = lax.axis_size("tm"), lax.axis_size("ct")
    in_count = voltages.shape[1]
    frame_count = voltages.shape[2] // CHANNELS
    outer = tm // PAIR
    span = RADIX // (tm * per_ct)
    own = in_count * per_ct
    half = in_count // PAIR
    place_tm, place_ct = lax.axis_index("tm"), lax.axis_index("ct")
    core = lax.axis_index("stn")
    g, o = place_tm % PAIR, place_tm // PAIR

    swap = [(i, i ^ 1) for i in range(tm)]
    onward = [(i, i + PAIR) for i in range(tm - PAIR)]
    cores = [(0, 1), (1, 0)]

    scalars = [None] * DELAY_AT
    scalars[G_AT], scalars[O_AT], scalars[CORE_AT], scalars[CT_AT] = g, o, core, place_ct
    meta = jnp.concatenate([jnp.stack(scalars).astype(jnp.int32), delays])

    dests = [(dg, dc) for dg in range(PAIR) for dc in range(per_ct)]
    base = last_table(outer, per_ct, span)
    tables = [np.concatenate([filter_table()] * 2, axis=1), first_table(), *twiddle_tables()]
    tables = [jnp.asarray(t) for t in tables + [np.concatenate([base, base], axis=1)]]

    sends = list(pick(meta, voltages, half, False, False))
    forward = [p for p in onward if p[0] % PAIR == 0]
    recvs = []
    for c in range(half):
        block = follow(sends[c], recvs[c - 2]) if c >= 2 else sends[c]
        recvs.append(lax.ppermute(block, "tm", swap))
    keep = pick(meta, voltages, half, True, True)[0]
    halo_own = lax.ppermute(keep, "tm", [p for p in onward if p[0] % PAIR == 1])

    arrays, others, places = [], [], []
    spectra, done = [], []
    for c in range(half):
        block = follow(recvs[c], done[c - 2]) if c >= 2 else recvs[c]
        far = lax.ppermute(block, "tm", forward)
        after = done[c - 1] if c else meta
        spectra = filterbank(
            c, meta, keep, halo_own, recvs[c], far, after, tables, spectra, len(dests)
        )
        done.append(spectra[0])
        if c % JOIN < JOIN - 1:
            continue
        for (dg, dc), block in zip(dests, spectra):
            route = []
            for i in range(tm):
                for j in range(per_ct):
                    target = (i ^ dg) * per_ct + (j + dc) % per_ct
                    route.append((i * per_ct + j, target))
            if dg or dc:
                if len(arrays) >= len(dests):
                    block = follow(block, arrays[-len(dests)])
                block = lax.ppermute(block, ("tm", "ct"), route)
            arrays.append(block)
            others.append(lax.ppermute(block, "stn", cores))
            places.append((dg, dc, c - JOIN + 1))
        spectra = []

    sizes = (outer, span, per_ct, in_count, half)
    near = [(False,) + place for place in places]
    far = [(True,) + place for place in places]
    mine_in = correlate(
        meta, arrays, near, own_blocks(own), own, False, sizes, "correlate_own"
    )
    mine_across = correlate(
        meta, arrays + others, near + far, cross_blocks(own), own, True, sizes, "correlate_cross"
    )
    mine_in, mine_across, far_across = list(mine_in), list(mine_across), []
    for r in range(1, outer):
        route = [(i, (i + r * PAIR) % tm) for i in range(tm)]
        mine_in[r] = lax.ppermute(mine_in[r], "tm", route)
    for r in range(outer):
        if r:
            route = [(i, (i + r * PAIR) % tm) for i in range(tm)]
            block = follow(mine_across[r], mine_in[r])
            mine_across[r] = lax.ppermute(block, "tm", route)
        far_across.append(lax.ppermute(mine_across[r], "stn", cores))
    scale = 1.0 / (tm * frame_count)
    result = assemble(meta, mine_in, mine_across, far_across, own, span, scale)
    return result.transpose(0, 3, 1, 2)


def general(voltages, delays):
    in_count = voltages.shape[1]
    frame_count = voltages.shape[2] // CHANNELS
    route = [(i, i + 1) for i in range(lax.axis_size("tm") - 1)]
    extended = jnp.concatenate([lax.ppermute(voltages, "tm", route), voltages], axis=2)
    span = (frame_count + TAPS - 1) * CHANNELS
    shifted = jax.vmap(
        lambda row, offset: lax.dynamic_slice_in_dim(row, CHANNELS - offset, span, 1),
        in_axes=(1, 0),
        out_axes=1,
    )(extended, delays)
    framed = shifted.reshape(2, in_count, frame_count + TAPS - 1, CHANNELS)
    table = jnp.asarray(filter_table()).reshape(TAPS, CHANNELS)
    total = jnp.zeros((2, in_count, frame_count, CHANNELS), jnp.float32)
    for tap in range(TAPS):
        low = TAPS - 1 - tap
        total = total + table[tap] * framed[:, :, low : low + frame_count].astype(jnp.float32)
    branches = jnp.moveaxis(total.astype(jnp.bfloat16), 0, 2)

    number = in_count * frame_count
    cosine, sine = dft_parts(RADIX)
    block = np.concatenate(
        [np.concatenate([cosine, sine], axis=1), np.concatenate([-sine, cosine], axis=1)], axis=0
    )
    block = jnp.asarray(block)
    stacked = branches.reshape(number, 2 * RADIX, RADIX)
    inner = jnp.einsum("kj,nja->nka", block, stacked, preferred_element_type=jnp.float32)
    inner = inner.reshape(number, 2, RADIX, RADIX)
    tw_cos, tw_sin = (jnp.asarray(t[:, :RADIX]) for t in twiddle_tables())
    real = inner[:, 0] * tw_cos + inner[:, 1] * tw_sin
    imag = inner[:, 1] * tw_cos - inner[:, 0] * tw_sin
    turned = jnp.stack([real, imag], axis=2).reshape(number, RADIX, 2 * RADIX)
    turned = turned.astype(jnp.bfloat16)
    result = jnp.einsum("lj,nkj->nlk", block, turned, preferred_element_type=jnp.float32)
    spectra = result.reshape(in_count, frame_count, 2, CHANNELS).astype(jnp.bfloat16)
    moved = lax.all_to_all(spectra, "tm", split_axis=3, concat_axis=1, tiled=True)
    moved = lax.all_to_all(moved, "ct", split_axis=3, concat_axis=0, tiled=True)
    local = moved.transpose(3, 2, 0, 1)
    swapped = jnp.stack([local[:, 1], -local[:, 0]], axis=1)
    summed = jnp.einsum(
        "ocjaf,cjbf->ocab",
        jnp.stack([local, swapped], axis=0),
        lax.all_gather(local, "stn", axis=2, tiled=True),
        preferred_element_type=jnp.float32,
    )
    return summed * (1.0 / local.shape[3])


def on_device(voltages, delays):
    if fast_fits(voltages.shape[1], voltages.shape[2] // CHANNELS):
        return fast(voltages, delays)
    return general(voltages, delays)


def solution(mesh):
    return jax.shard_map(
        on_device,
        mesh=mesh,
        in_specs=(P(None, ("stn", "ct"), "tm"), P(("stn", "ct"))),
        out_specs=P(None, ("tm", "ct"), "stn", None),
        check_vma=False,
    )
```

```python
import functools
import math

import jax
import jax.numpy as jnp
import numpy as np
from jax import lax
from jax.experimental import pallas as pl
from jax.experimental.pallas import tpu as pltpu
from jax.sharding import PartitionSpec as P

CHANNELS = 4096
RADIX = 64
TAPS = 16
LANES = 128
ROWS = CHANNELS // LANES
PAIR = 2
TILE = 4
JOIN = 2

G_AT, O_AT, CORE_AT, CT_AT, DELAY_AT = range(5)

VMEM = pl.BlockSpec(memory_space=pltpu.VMEM)
SMEM = pl.BlockSpec(memory_space=pltpu.SMEM)
HBM = pl.BlockSpec(memory_space=pltpu.HBM)


def params(mib):
    return pltpu.CompilerParams(vmem_limit_bytes=mib * 2**20)


def cost(flops, size):
    return pl.CostEstimate(flops=flops, bytes_accessed=size, transcendentals=0)


def filter_table():
    length = TAPS * CHANNELS
    index = np.arange(length, dtype=np.float64)
    centred = (index - length / 2) / CHANNELS
    window = 0.5 - 0.5 * np.cos(2.0 * math.pi * index / length)
    factor = 1.0 / (48.0 * math.sqrt(CHANNELS))
    table = np.sinc(centred) * window * factor
    return table.reshape(TAPS, ROWS, LANES).astype(np.float32)


def dft_parts(radix):
    steps = np.arange(radix)
    angle = 2.0 * math.pi * (steps[:, None] * steps[None, :] % radix) / radix
    return np.cos(angle).astype(jnp.bfloat16), np.sin(angle).astype(jnp.bfloat16)


def first_table():
    cosine, sine = dft_parts(CHANNELS // RADIX)
    order = [2 * row + half for half in range(2) for row in range(ROWS)]
    cosine, sine = cosine[:, order], sine[:, order]
    upper = np.concatenate([cosine, sine], axis=1)
    lower = np.concatenate([-sine, cosine], axis=1)
    return np.concatenate([upper, lower], axis=0)


def last_table(outer, per_ct, span):
    cosine, sine = dft_parts(RADIX)
    blocks = []
    for g in range(PAIR):
        for ct in range(per_ct):
            steps = [
                ((o * PAIR + g) * per_ct + ct) * span + j for o in range(outer) for j in range(span)
            ]
            real = np.concatenate([cosine[steps], sine[steps]], axis=1)
            imag = np.concatenate([-sine[steps], cosine[steps]], axis=1)
            blocks.append(np.concatenate([real, imag], axis=0))
    return np.stack(blocks).reshape(PAIR, per_ct, -1, 2 * RADIX)


def twiddle_tables():
    rows = np.arange(CHANNELS // RADIX)
    cols = np.arange(RADIX)
    angle = 2.0 * math.pi * (rows[:, None] * cols[None, :] % CHANNELS) / CHANNELS
    cosine = np.cos(angle).astype(np.float32)
    sine = np.sin(angle).astype(np.float32)
    return np.concatenate([cosine, cosine], axis=1), np.concatenate([sine, sine], axis=1)


def pick_kernel(count, joined, own, meta, block, *refs):
    outs, (held, rows, staged, in_sems, out_sems) = refs[:-5], refs[-5:]
    inputs, samples = block.shape[1], block.shape[2]
    step = 16
    parts = in_sems.shape[0]
    size = samples // parts

    def bring(n):
        cut = slice(n * size, (n + 1) * size)
        return pltpu.make_async_copy(block.at[:, :, cut], held.at[:, :, cut], in_sems.at[n])

    def send(item):
        out = outs[0].at[item] if joined else outs[item]
        return pltpu.make_async_copy(staged.at[item], out, out_sems.at[item])

    for n in range(parts):
        bring(n).start()
    for m in range(parts):
        bring(m).wait()

        def spread(n, carry, m=m):
            low = pl.multiple_of(m * size + n * step * LANES, step * LANES)
            for part in range(2):
                wide = held[part, :, pl.ds(low, step * LANES)].astype(jnp.float32)
                for u in range(step):
                    at = pl.multiple_of((m * size // LANES + n * step + u) * inputs, inputs)
                    rows[part, pl.ds(at, inputs), :] = wide[:, u * LANES : (u + 1) * LANES]
            return carry

        lax.fori_loop(0, size // LANES // step, spread, 0)
    first = (meta[G_AT] if own else 1 - meta[G_AT]) * count
    tall = 128
    for item in range(count):

        def gather(n, carry, item=item):
            low = pl.multiple_of(n * tall, tall)
            for part in range(2):
                value = rows[part, pl.ds(low * inputs + first + item, tall, stride=inputs), :]
                staged[item, part, pl.ds(low, tall), :] = value.astype(jnp.bfloat16)
            return carry

        lax.fori_loop(0, samples // LANES // tall, gather, 0)
        send(item).start()
    for item in range(count):
        send(item).wait()


def pick(meta, block, count, joined, own):
    _, inputs, samples = block.shape
    one = (2, samples // LANES, LANES)
    shapes = [(count,) + one] if joined else [one] * count
    return pl.pallas_call(
        functools.partial(pick_kernel, count, joined, own),
        out_shape=[jax.ShapeDtypeStruct(s, jnp.bfloat16) for s in shapes],
        in_specs=[SMEM, HBM],
        out_specs=[HBM] * len(shapes),
        scratch_shapes=[
            pltpu.VMEM(block.shape, jnp.bfloat16),
            pltpu.VMEM((2, samples // LANES * inputs, LANES), jnp.float32),
            pltpu.VMEM((count,) + one, jnp.bfloat16),
            pltpu.SemaphoreType.DMA((4,)),
            pltpu.SemaphoreType.DMA((count,)),
        ],
        compiler_params=params(16),
        cost_estimate=cost(10**6, 2**18),
        name="pick",
    )(meta, block)


def follow(block, after):
    def hand_on(block, after, out):
        pass

    return pl.pallas_call(
        hand_on,
        out_shape=jax.ShapeDtypeStruct(block.shape, block.dtype),
        in_specs=[HBM, HBM],
        out_specs=HBM,
        input_output_aliases={0: 0},
        name="follow",
    )(block, after)


HALF = 16
SOME = 4


def filterbank_kernel(index, frames, dests, per_ct, half_count, *refs):
    meta, keep, halo_own, recv, halo_far, after, coef, first, tw_cos, tw_sin, last = refs[:11]
    raw, weights, grouped, staged, sems, out_sems = refs[-6 - PAIR * frames // HALF :][:6]
    filtered = refs[-(PAIR * frames // HALF) :]
    outs = refs[-7 - PAIR * frames // HALF - dests :][:dests]
    slot = index % JOIN
    block_rows = frames * ROWS
    total = PAIR * frames
    me, ct = meta[G_AT], meta[CT_AT]
    delay = meta[DELAY_AT + me * half_count + index]
    down = delay // LANES
    across = delay % LANES
    lane = lax.broadcasted_iota(jnp.int32, (1, LANES), 1)
    inside = lane < LANES - across
    turned_in = lane >= across
    high = lane < RADIX

    def bring(source, place, sem):
        at = pl.multiple_of(place * block_rows, block_rows)
        return pltpu.make_async_copy(source, raw.at[:, pl.ds(at, block_rows), :], sems.at[sem])

    @pl.when(me == 0)
    def _():
        bring(halo_far, 0, 0).start()

    @pl.when(me != 0)
    def _():
        bring(halo_own.at[index], 0, 0).start()

    bring(keep.at[index], 1 + me, 1).start()
    bring(recv, 2 - me, 2).start()

    back = lax.rem(LANES - across, LANES)
    for tap in range(TAPS):
        here = coef[tap, pl.ds(down, ROWS), :]
        after = coef[tap, pl.ds(down + 1, ROWS), :]
        weights[tap] = pltpu.roll(jnp.where(turned_in, here, after), back, 1)

    def send(dest, half):
        cut = pl.ds(half * HALF // 2, HALF // 2)
        return pltpu.make_async_copy(
            staged.at[dest, cut], outs[dest].at[slot, cut], out_sems.at[dest, half]
        )

    bring(halo_far, 0, 0).wait()
    bring(keep.at[index], 1 + me, 1).wait()
    bring(recv, 2 - me, 2).wait()

    def filt(half, low, high_frame, band, part):
        size = high_frame - low
        values = []
        for u in range(size + TAPS - 1):
            at = (half * HALF + low + u + frames - TAPS) * ROWS + band * 16
            values.append(raw[part, at : at + 16, :].astype(jnp.float32))
        sums = [None] * size
        for tap in range(TAPS):
            weight = weights[tap, band * 16 : band * 16 + 16, :]
            for u in range(size):
                term = weight * values[u + TAPS - 1 - tap]
                sums[u] = term if sums[u] is None else sums[u] + term
        for u in range(size):
            at = (low + u) * ROWS + band * 16
            filtered[half][part, at : at + 16, :] = sums[u]

    twice = lax.rem(across + RADIX, LANES)

    def place(half, u):
        for band in range(ROWS // 16):
            at = (u + 1) * ROWS + band * 16 - down
            moved, turned = [], []
            for part in range(2):
                here = filtered[half][part, pl.ds(at, 16), :]
                above = filtered[half][part, pl.ds(at - 1, 16), :]
                value = jnp.where(inside, here, above)
                moved.append(pltpu.roll(value, across, 1))
                turned.append(pltpu.roll(value, twice, 1))
            parts = (
                jnp.where(high, moved[0], turned[1]),
                jnp.where(high, turned[0], moved[1]),
                jnp.where(high, moved[1], -turned[0]),
                jnp.where(high, turned[1], -moved[0]),
            )
            for which, value in enumerate(parts):
                low = which * ROWS + band * 16
                grouped[half * HALF + u, low : low + 16, :] = value.astype(jnp.bfloat16)

    def turn(base):
        wide = jnp.concatenate([grouped[base + u] for u in range(SOME)], axis=1)
        inner = jnp.dot(first[...], wide, preferred_element_type=jnp.float32)
        rows = []
        for u in range(SOME):
            cut = slice(u * LANES, (u + 1) * LANES)
            value = inner[:RADIX, cut] * tw_cos[...] + inner[RADIX:, cut] * tw_sin[...]
            rows.append(value.astype(jnp.bfloat16))
        inner = jnp.concatenate(rows, axis=0)
        result = lax.dot_general(
            rows_out, inner, (((1,), (1,)), ((), ())), preferred_element_type=jnp.float32
        ).astype(jnp.bfloat16)
        size = result.shape[0] // (2 * dests)
        for dest in range(dests):
            for part in range(2):
                low = (dest * 2 + part) * size
                for u in range(SOME // 2):
                    staged[dest, base // 2 + u, part] = result[
                        low : low + size, u * LANES : (u + 1) * LANES
                    ]

    rows_out = jnp.concatenate(
        [last[me ^ dg, ct + dc] for dg in range(PAIR) for dc in range(per_ct)], axis=0
    )
    pieces = [
        (low, high_frame, band, part)
        for low, high_frame in ((0, 9), (9, HALF + 1))
        for band in range(ROWS // 16)
        for part in range(2)
    ]
    each = len(pieces) // (HALF // SOME)
    halves = total // HALF
    for half in range(halves + 1):
        for n in range(HALF // SOME):
            if half < halves:
                for piece in pieces[n * each : (n + 1) * each]:
                    filt(half, *piece)
            if half:
                for u in range(SOME):
                    place(half - 1, n * SOME + u)
                turn((half - 1) * HALF + n * SOME)
        if half:
            for dest in range(dests):
                send(dest, half - 1).start()
    for half in range(halves):
        for dest in range(dests):
            send(dest, half).wait()


def filterbank(index, meta, keep, halo_own, recv, halo_far, after, tables, earlier, dests):
    frames = keep.shape[2] // ROWS
    size = tables[-1].shape[2] // 2
    per_ct = tables[-1].shape[1] // 2
    all_rows = (PAIR + 1) * frames * ROWS
    halves = PAIR * frames // HALF
    shape = (PAIR * frames // 2, 2, size, LANES)
    spectra = jax.ShapeDtypeStruct((JOIN,) + shape, jnp.bfloat16)
    token = jax.ShapeDtypeStruct((8, LANES), jnp.float32)
    return pl.pallas_call(
        functools.partial(filterbank_kernel, index, frames, dests, per_ct, keep.shape[0]),
        out_shape=[spectra] * dests + [token],
        in_specs=[SMEM] + [HBM] * 5 + [VMEM] * 5 + [HBM] * len(earlier),
        out_specs=[HBM] * (dests + 1),
        input_output_aliases={11 + n: n for n in range(len(earlier))},
        scratch_shapes=[
            pltpu.VMEM((2, all_rows, LANES), jnp.bfloat16),
            pltpu.VMEM((TAPS, ROWS, LANES), jnp.float32),
            pltpu.VMEM((PAIR * frames, LANES, LANES), jnp.bfloat16),
            pltpu.VMEM((dests,) + shape, jnp.bfloat16),
            pltpu.SemaphoreType.DMA((3,)),
            pltpu.SemaphoreType.DMA((dests, halves)),
        ]
        + [pltpu.VMEM((2, (HALF + 1) * ROWS, LANES), jnp.float32)] * halves,
        compiler_params=params(12),
        cost_estimate=cost(10**6, 2**18),
        name="filterbank",
    )(meta, keep, halo_own, recv, halo_far, after, *tables, *earlier)


SQUARE = [(p, q) for p in range(TILE) for q in range(TILE)]
CORNER = [(p, q) for p in range(TILE) for q in range(p, TILE)]


def own_blocks(own):
    tiles = own // TILE
    whole = [(i, j, SQUARE) for i in range(tiles) for j in range(i + 1, tiles)]
    return whole + [(i, i, CORNER) for i in range(tiles)]


def cross_blocks(own):
    tiles = own // TILE
    return [(i, j, SQUARE) for i in range(tiles // 2) for j in range(tiles)]


def pairs_in(blocks):
    return sum(len(block[2]) for block in blocks)


def chosen(t, values):
    result = jnp.int32(values[0])
    for n, value in enumerate(values[1:], 1):
        result = jnp.where(t == n, jnp.int32(value), result)
    return result


def correlate_kernel(layout, *refs):
    sources_at, blocks, own, cross, outer, span, per_ct, in_count, half_count = layout
    meta, sources = refs[0], refs[1 : 1 + len(sources_at)]
    rest = refs[1 + len(sources_at) :]
    outs, (raw, spectra, sums, held, first_out, staged, sems, out_sems) = rest[:-8], rest[-8:]
    steps = spectra.shape[1]
    some = 8
    core, g, ct = meta[CORE_AT], meta[G_AT], meta[CT_AT]

    def bring(n):
        return pltpu.make_async_copy(sources[n], raw.at[n], sems.at[n])

    def fill(n, base):
        bring(n).wait()
        for item in range(sources[n].shape[0]):

            def spread(m, carry, item=item):
                for u in range(some):
                    real = raw[n, item, m * some + u, 0].astype(jnp.float32)
                    imag = raw[n, item, m * some + u, 1].astype(jnp.float32)
                    for which, value in enumerate((real, imag, real + imag, imag - real)):
                        spectra[base + item, m * some + u, which] = value
                return carry

            lax.fori_loop(0, steps // some, spread, 0)

    bases, wanted = [], []
    for far, dg, dc, start in sources_at:
        base = lax.rem(ct - dc + per_ct, per_ct) * in_count + (g ^ dg) * half_count + start
        if cross:
            side = 1 - core if far else core
            low = core * (own // 2)
            wanted.append((side == 1) | ((base >= low) & (base < low + own // 2)))
            base = base + side * own
        bases.append(base)
    for n in range(len(sources)):
        if cross:
            pl.when(wanted[n])(lambda n=n: bring(n).start())
        else:
            bring(n).start()
    for n in range(len(sources)):
        if cross:
            pl.when(wanted[n])(functools.partial(fill, n, bases[n]))
        else:
            fill(n, bases[n])

    high = lax.broadcasted_iota(jnp.int32, (1, LANES), 1) < RADIX
    rows_outer = pairs_in(blocks) * span
    size = outer * span
    unroll = 4

    def block(left, right, pairs, first_row):
        def over(one, two, acc, sign):
            def frame(n, acc):
                acc = list(acc)
                for u in range(unroll):
                    a = [spectra[left + p, n * unroll + u, one] for p in range(TILE)]
                    b = [spectra[right + q, n * unroll + u, two] for q in range(TILE)]
                    for at, (p, q) in enumerate(pairs):
                        term = a[p] * b[q]
                        acc[at] = acc[at] + term if sign > 0 else acc[at] - term
                return tuple(acc)

            return lax.fori_loop(0, steps // unroll, frame, tuple(acc))

        count = len(pairs)
        first = over(2, 0, [jnp.zeros((size, LANES), jnp.float32)] * count, 1)
        for at in range(count):
            held[0, at] = first[at]
        real = over(1, 3, first, 1)
        for at in range(count):
            held[1, at] = real[at] + pltpu.roll(real[at], RADIX, 1)
        imag = over(0, 2, [held[0, at] for at in range(count)], -1)
        for at in range(count):
            folded = imag[at] + pltpu.roll(imag[at], RADIX, 1)
            both = jnp.where(high, held[1, at], folded)
            for o in range(outer):
                row = o * rows_outer + first_row + at * span
                sums[pl.ds(pl.multiple_of(row, span), span), :] = both[o * span : (o + 1) * span]

    done = 0
    for pairs in (SQUARE, CORNER):
        some_blocks = [b for b in blocks if b[2] is pairs]
        if not some_blocks:
            continue

        def step(t, carry, some_blocks=some_blocks, pairs=pairs, done=done):
            left = TILE * chosen(t, [b[0] for b in some_blocks])
            right = TILE * chosen(t, [b[1] for b in some_blocks])
            if cross:
                left, right = left + core * (own // 2), right + own
            block(left, right, pairs, done + t * len(pairs) * span)
            return carry

        lax.fori_loop(0, len(some_blocks), step, 0)
        done += pairs_in(some_blocks) * span

    def send(r):
        return pltpu.make_async_copy(staged.at[r - 1] if r else first_out, outs[r], out_sems.at[r])

    for r in list(range(1, outer)) + [0]:
        base = pl.multiple_of(lax.rem(meta[O_AT] + r, outer) * rows_outer, 16)
        value = sums[pl.ds(base, rows_outer), :]
        if r:
            staged[r - 1] = value.astype(staged.dtype)
        else:
            first_out[...] = value
        send(r).start()
    for r in range(outer):
        send(r).wait()


def correlate(meta, arrays, sources_at, blocks, own, cross, sizes, name):
    outer, span, per_ct, in_count, half_count = sizes
    _, steps, _, size, _ = arrays[0].shape
    inputs = 2 * own if cross else own
    rows = pairs_in(blocks) * span
    shapes = []
    for r in range(outer):
        dtype = jnp.float32 if r == 0 else jnp.bfloat16
        shapes.append(jax.ShapeDtypeStruct((rows, LANES), dtype))
    layout = (sources_at, blocks, own, cross) + sizes
    return pl.pallas_call(
        functools.partial(correlate_kernel, layout),
        out_shape=shapes,
        in_specs=[SMEM] + [HBM] * len(arrays),
        out_specs=[HBM] * len(shapes),
        scratch_shapes=[
            pltpu.VMEM((len(arrays),) + arrays[0].shape, jnp.bfloat16),
            pltpu.VMEM((inputs, steps, 4, size, LANES), jnp.float32),
            pltpu.VMEM((outer * rows, LANES), jnp.float32),
            pltpu.VMEM((2, TILE * TILE, outer * span, LANES), jnp.float32),
            pltpu.VMEM((rows, LANES), jnp.float32),
            pltpu.VMEM((outer - 1, rows, LANES), jnp.bfloat16),
            pltpu.SemaphoreType.DMA((len(arrays),)),
            pltpu.SemaphoreType.DMA((outer,)),
        ],
        compiler_params=params(12 + inputs * steps * 4 * size * LANES * 4 // 2**20),
        cost_estimate=cost(10**6, 2**18),
        name=name,
    )(meta, *arrays)


def assemble_kernel(own, outer, span, scale, *refs):
    meta = refs[0]
    sources = refs[1 : 1 + 3 * outer]
    out = refs[1 + 3 * outer]
    kept = refs[2 + 3 * outer : 2 + 6 * outer]
    joined, staged, sems, out_sems = refs[2 + 6 * outer :]
    mine_in, mine_across, far_across = (kept[n * outer : (n + 1) * outer] for n in range(3))

    def bring(n):
        return pltpu.make_async_copy(sources[n], kept[n], sems.at[n])

    for n in range(len(sources)):
        bring(n).start()
    for n in range(len(sources)):
        bring(n).wait()
    lane = lax.broadcasted_iota(jnp.int32, (1, LANES), 1)
    high = lane < RADIX
    mirror = jnp.where(high, 1.0, -1.0).astype(jnp.float32)
    me = meta[CORE_AT]

    def added(sources, low, rows):
        total = sources[0][low : low + rows, :].astype(jnp.float32)
        for source in sources[1:]:
            total = total + source[low : low + rows, :].astype(jnp.float32)
        return total * scale

    def put(value, row, col):
        at = pl.multiple_of((row * 2 * own + col) * span, span)
        joined[pl.ds(at, span), :] = value

    done = 0
    for i, j, pairs in own_blocks(own):
        total = added(mine_in, done, len(pairs) * span)
        turned = total * mirror
        for at, (p, q) in enumerate(pairs):
            cut = slice(at * span, (at + 1) * span)
            a, b = i * TILE + p, j * TILE + q
            put(total[cut], a, me * own + b)
            if a != b:
                put(turned[cut], b, me * own + a)
        done += len(pairs) * span
    sign = jnp.where(me == 0, jnp.ones_like(mirror), mirror)
    for sources, part in ((mine_across, me), (far_across, 1 - me)):
        done = 0
        for i, j, pairs in cross_blocks(own):
            total = added(sources, done, len(pairs) * span) * sign
            for at, (p, q) in enumerate(pairs):
                a = part * (own // 2) + i * TILE + p
                b = j * TILE + q
                row = jnp.where(me == 0, a, b)
                col = jnp.where(me == 0, own + b, a)
                put(total[at * span : (at + 1) * span], row, col)
            done += len(pairs) * span

    def emit(a, carry):
        for tile in range(2 * own // 8):
            for pair in range(span // 2):
                loads = []
                for u in range(2):
                    at = (a * 2 * own + tile * 8) * span + pair * 2 + u
                    loads.append(joined[pl.ds(at, 8, stride=span), :])
                turned = [pltpu.roll(x, RADIX, 1) for x in loads]
                cut = slice(pair * LANES, (pair + 1) * LANES)
                staged[0, a, tile * 8 : tile * 8 + 8, cut] = jnp.where(high, loads[0], turned[1])
                staged[1, a, tile * 8 : tile * 8 + 8, cut] = jnp.where(high, turned[0], loads[1])
        return carry

    groups = out_sems.shape[0]
    size = own // groups

    def send(n):
        cut = pl.ds(n * size, size)
        return pltpu.make_async_copy(staged.at[:, cut], out.at[:, cut], out_sems.at[n])

    for n in range(groups):
        lax.fori_loop(n * size, (n + 1) * size, emit, 0)
        send(n).start()
    for n in range(groups):
        send(n).wait()


def assemble(meta, mine_in, mine_across, far_across, own, span, scale):
    outer = len(mine_in)
    sources = [*mine_in, *mine_across, *far_across]
    shape = (2, own, 2 * own, span * RADIX)
    return pl.pallas_call(
        functools.partial(assemble_kernel, own, outer, span, scale),
        out_shape=jax.ShapeDtypeStruct(shape, jnp.float32),
        in_specs=[SMEM] + [HBM] * len(sources),
        out_specs=HBM,
        scratch_shapes=[pltpu.VMEM(x.shape, x.dtype) for x in sources]
        + [
            pltpu.VMEM((own * 2 * own * span, LANES), jnp.float32),
            pltpu.VMEM(shape, jnp.float32),
            pltpu.SemaphoreType.DMA((len(sources),)),
            pltpu.SemaphoreType.DMA((4,)),
        ],
        compiler_params=params(12),
        cost_estimate=cost(10**6, 2**18),
        name="assemble",
    )(meta, *sources)


def fast_fits(in_count, frame_count):
    stn, tm, per_ct = (lax.axis_size(a) for a in ("stn", "tm", "ct"))
    groups = tm * per_ct
    if stn != 2 or tm % PAIR or in_count % (PAIR * JOIN) or RADIX % groups:
        return False
    outer, span = tm // PAIR, RADIX // groups
    own = in_count * per_ct
    return (
        frame_count >= TAPS
        and frame_count % HALF == 0
        and span in (2, 4, 8)
        and outer * span % 16 == 0
        and own % (2 * TILE) == 0
        and (own * (own + 1) // 2 * span) % 16 == 0
    )


def fast(voltages, delays):
    tm, per_ct = lax.axis_size("tm"), lax.axis_size("ct")
    in_count = voltages.shape[1]
    frame_count = voltages.shape[2] // CHANNELS
    outer = tm // PAIR
    span = RADIX // (tm * per_ct)
    own = in_count * per_ct
    half = in_count // PAIR
    place_tm, place_ct = lax.axis_index("tm"), lax.axis_index("ct")
    core = lax.axis_index("stn")
    g, o = place_tm % PAIR, place_tm // PAIR

    swap = [(i, i ^ 1) for i in range(tm)]
    onward = [(i, i + PAIR) for i in range(tm - PAIR)]
    cores = [(0, 1), (1, 0)]

    scalars = [None] * DELAY_AT
    scalars[G_AT], scalars[O_AT], scalars[CORE_AT], scalars[CT_AT] = g, o, core, place_ct
    meta = jnp.concatenate([jnp.stack(scalars).astype(jnp.int32), delays])

    dests = [(dg, dc) for dg in range(PAIR) for dc in range(per_ct)]
    base = last_table(outer, per_ct, span)
    tables = [np.concatenate([filter_table()] * 2, axis=1), first_table(), *twiddle_tables()]
    tables = [jnp.asarray(t) for t in tables + [np.concatenate([base, base], axis=1)]]

    sends = list(pick(meta, voltages, half, False, False))
    forward = [p for p in onward if p[0] % PAIR == 0]
    recvs = []
    for c in range(half):
        block = follow(sends[c], recvs[c - 2]) if c >= 2 else sends[c]
        recvs.append(lax.ppermute(block, "tm", swap))
    keep = pick(meta, voltages, half, True, True)[0]
    halo_own = lax.ppermute(keep, "tm", [p for p in onward if p[0] % PAIR == 1])

    arrays, others, places = [], [], []
    spectra, done = [], []
    for c in range(half):
        recv = follow(recvs[c], done[c - 2]) if c >= 2 else recvs[c]
        far = lax.ppermute(recv, "tm", forward)
        *spectra, token = filterbank(
            c, meta, keep, halo_own, recv, far, done[c - 1] if c else keep, tables, spectra,
            len(dests),
        )
        done.append(token)
        if c % JOIN < JOIN - 1:
            continue
        for (dg, dc), block in zip(dests, spectra):
            route = []
            for i in range(tm):
                for j in range(per_ct):
                    target = (i ^ dg) * per_ct + (j + dc) % per_ct
                    route.append((i * per_ct + j, target))
            if dg or dc:
                if len(arrays) >= len(dests):
                    block = follow(block, arrays[-len(dests)])
                block = lax.ppermute(block, ("tm", "ct"), route)
            arrays.append(block)
            others.append(lax.ppermute(block, "stn", cores))
            places.append((dg, dc, c - JOIN + 1))
        spectra = []

    sizes = (outer, span, per_ct, in_count, half)
    near = [(False,) + place for place in places]
    far = [(True,) + place for place in places]
    mine_in = correlate(
        meta, arrays, near, own_blocks(own), own, False, sizes, "correlate_own"
    )
    mine_across = correlate(
        meta, arrays + others, near + far, cross_blocks(own), own, True, sizes, "correlate_cross"
    )
    mine_in, mine_across, far_across = list(mine_in), list(mine_across), []
    for r in range(1, outer):
        route = [(i, (i + r * PAIR) % tm) for i in range(tm)]
        mine_in[r] = lax.ppermute(mine_in[r], "tm", route)
    for r in range(outer):
        if r:
            route = [(i, (i + r * PAIR) % tm) for i in range(tm)]
            block = follow(mine_across[r], mine_in[r])
            mine_across[r] = lax.ppermute(block, "tm", route)
        far_across.append(lax.ppermute(mine_across[r], "stn", cores))
    scale = 1.0 / (tm * frame_count)
    result = assemble(meta, mine_in, mine_across, far_across, own, span, scale)
    return result.transpose(0, 3, 1, 2)


def general(voltages, delays):
    in_count = voltages.shape[1]
    frame_count = voltages.shape[2] // CHANNELS
    route = [(i, i + 1) for i in range(lax.axis_size("tm") - 1)]
    extended = jnp.concatenate([lax.ppermute(voltages, "tm", route), voltages], axis=2)
    span = (frame_count + TAPS - 1) * CHANNELS
    shifted = jax.vmap(
        lambda row, offset: lax.dynamic_slice_in_dim(row, CHANNELS - offset, span, 1),
        in_axes=(1, 0),
        out_axes=1,
    )(extended, delays)
    framed = shifted.reshape(2, in_count, frame_count + TAPS - 1, CHANNELS)
    table = jnp.asarray(filter_table()).reshape(TAPS, CHANNELS)
    total = jnp.zeros((2, in_count, frame_count, CHANNELS), jnp.float32)
    for tap in range(TAPS):
        low = TAPS - 1 - tap
        total = total + table[tap] * framed[:, :, low : low + frame_count].astype(jnp.float32)
    branches = jnp.moveaxis(total.astype(jnp.bfloat16), 0, 2)

    number = in_count * frame_count
    cosine, sine = dft_parts(RADIX)
    block = np.concatenate(
        [np.concatenate([cosine, sine], axis=1), np.concatenate([-sine, cosine], axis=1)], axis=0
    )
    block = jnp.asarray(block)
    stacked = branches.reshape(number, 2 * RADIX, RADIX)
    inner = jnp.einsum("kj,nja->nka", block, stacked, preferred_element_type=jnp.float32)
    inner = inner.reshape(number, 2, RADIX, RADIX)
    tw_cos, tw_sin = (jnp.asarray(t[:, :RADIX]) for t in twiddle_tables())
    real = inner[:, 0] * tw_cos + inner[:, 1] * tw_sin
    imag = inner[:, 1] * tw_cos - inner[:, 0] * tw_sin
    turned = jnp.stack([real, imag], axis=2).reshape(number, RADIX, 2 * RADIX)
    turned = turned.astype(jnp.bfloat16)
    result = jnp.einsum("lj,nkj->nlk", block, turned, preferred_element_type=jnp.float32)
    spectra = result.reshape(in_count, frame_count, 2, CHANNELS).astype(jnp.bfloat16)
    moved = lax.all_to_all(spectra, "tm", split_axis=3, concat_axis=1, tiled=True)
    moved = lax.all_to_all(moved, "ct", split_axis=3, concat_axis=0, tiled=True)
    local = moved.transpose(3, 2, 0, 1)
    swapped = jnp.stack([local[:, 1], -local[:, 0]], axis=1)
    summed = jnp.einsum(
        "ocjaf,cjbf->ocab",
        jnp.stack([local, swapped], axis=0),
        lax.all_gather(local, "stn", axis=2, tiled=True),
        preferred_element_type=jnp.float32,
    )
    return summed * (1.0 / local.shape[3])


def on_device(voltages, delays):
    if fast_fits(voltages.shape[1], voltages.shape[2] // CHANNELS):
        return fast(voltages, delays)
    return general(voltages, delays)


def solution(mesh):
    return jax.shard_map(
        on_device,
        mesh=mesh,
        in_specs=(P(None, ("stn", "ct"), "tm"), P(("stn", "ct"))),
        out_specs=P(None, ("tm", "ct"), "stn", None),
        check_vma=False,
    )
```

```python
import functools
import math

import jax
import jax.numpy as jnp
import numpy as np
from jax import lax
from jax.experimental import pallas as pl
from jax.experimental.pallas import tpu as pltpu
from jax.sharding import PartitionSpec as P

CHANNELS = 4096
RADIX = 64
TAPS = 16
LANES = 128
ROWS = CHANNELS // LANES
PAIR = 2
TILE = 4
JOIN = 2

G_AT, O_AT, CORE_AT, CT_AT, DELAY_AT = range(5)

VMEM = pl.BlockSpec(memory_space=pltpu.VMEM)
SMEM = pl.BlockSpec(memory_space=pltpu.SMEM)


def params(mib):
    return pltpu.CompilerParams(vmem_limit_bytes=mib * 2**20)


def cost(flops, size):
    return pl.CostEstimate(flops=flops, bytes_accessed=size, transcendentals=0)


def filter_table():
    length = TAPS * CHANNELS
    index = np.arange(length, dtype=np.float64)
    centred = (index - length / 2) / CHANNELS
    window = 0.5 - 0.5 * np.cos(2.0 * math.pi * index / length)
    factor = 1.0 / (48.0 * math.sqrt(CHANNELS))
    table = np.sinc(centred) * window * factor
    return table.reshape(TAPS, ROWS, LANES).astype(np.float32)


def dft_parts(radix):
    steps = np.arange(radix)
    angle = 2.0 * math.pi * (steps[:, None] * steps[None, :] % radix) / radix
    return np.cos(angle).astype(jnp.bfloat16), np.sin(angle).astype(jnp.bfloat16)


def first_table():
    cosine, sine = dft_parts(CHANNELS // RADIX)
    order = [2 * row + half for half in range(2) for row in range(ROWS)]
    cosine, sine = cosine[:, order], sine[:, order]
    upper = np.concatenate([cosine, sine], axis=1)
    lower = np.concatenate([-sine, cosine], axis=1)
    return np.concatenate([upper, lower], axis=0)


def last_table(outer, per_ct, span):
    cosine, sine = dft_parts(RADIX)
    blocks = []
    for g in range(PAIR):
        for ct in range(per_ct):
            steps = [
                ((o * PAIR + g) * per_ct + ct) * span + j for o in range(outer) for j in range(span)
            ]
            real = np.concatenate([cosine[steps], sine[steps]], axis=1)
            imag = np.concatenate([-sine[steps], cosine[steps]], axis=1)
            blocks.append(np.concatenate([real, imag], axis=0))
    return np.stack(blocks).reshape(PAIR, per_ct, -1, 2 * RADIX)


def twiddle_tables():
    rows = np.arange(CHANNELS // RADIX)
    cols = np.arange(RADIX)
    angle = 2.0 * math.pi * (rows[:, None] * cols[None, :] % CHANNELS) / CHANNELS
    cosine = np.cos(angle).astype(np.float32)
    sine = np.sin(angle).astype(np.float32)
    return np.concatenate([cosine, cosine], axis=1), np.concatenate([sine, sine], axis=1)


def pick_kernel(count, joined, own, meta, block, *refs):
    outs, rows = refs[:-1], refs[-1]
    inputs, samples = block.shape[1], block.shape[2]
    step = 16
    for part in range(2):

        def spread(n, carry, part=part):
            low = pl.multiple_of(n * step * LANES, step * LANES)
            wide = block[part, :, pl.ds(low, step * LANES)].astype(jnp.float32)
            for u in range(step):
                at = pl.multiple_of((n * step + u) * inputs, inputs)
                rows[part, pl.ds(at, inputs), :] = wide[:, u * LANES : (u + 1) * LANES]
            return carry

        lax.fori_loop(0, samples // LANES // step, spread, 0)
    first = (meta[G_AT] if own else 1 - meta[G_AT]) * count
    tall = 128
    for item in range(count):
        out = outs[0].at[item] if joined else outs[item]

        def gather(n, carry, item=item, out=out):
            low = pl.multiple_of(n * tall, tall)
            for part in range(2):
                value = rows[part, pl.ds(low * inputs + first + item, tall, stride=inputs), :]
                out[part, pl.ds(low, tall), :] = value.astype(jnp.bfloat16)
            return carry

        lax.fori_loop(0, samples // LANES // tall, gather, 0)


def pick(meta, block, count, joined, own):
    _, inputs, samples = block.shape
    one = (2, samples // LANES, LANES)
    shapes = [(count,) + one] if joined else [one] * count
    return pl.pallas_call(
        functools.partial(pick_kernel, count, joined, own),
        out_shape=[jax.ShapeDtypeStruct(s, jnp.bfloat16) for s in shapes],
        in_specs=[SMEM, VMEM],
        out_specs=[VMEM] * len(shapes),
        scratch_shapes=[pltpu.VMEM((2, samples // LANES * inputs, LANES), jnp.float32)],
        compiler_params=params(16),
        cost_estimate=cost(10**6, 2**18),
        name="pick",
    )(meta, block)


def follow(block, after):
    return lax.optimization_barrier((block, after))[0]


HALF = 16
SOME = 4


def filterbank_kernel(index, before, frames, dests, per_ct, half_count, *refs):
    meta, keep, halo_own, recv, halo_far, coef, first, tw_cos, tw_sin, last = refs[:10]
    earlier = refs[10 : 10 + dests * (before > 0)]
    refs = refs[10 + len(earlier) :]
    outs = refs[:dests]
    raw, weights, grouped = refs[dests : dests + 3]
    filtered = refs[dests + 3 :]
    block_rows = frames * ROWS
    total = PAIR * frames
    me, ct = meta[G_AT], meta[CT_AT]
    delay = meta[DELAY_AT + me * half_count + index]
    down = delay // LANES
    across = delay % LANES
    lane = lax.broadcasted_iota(jnp.int32, (1, LANES), 1)
    inside = lane < LANES - across
    turned_in = lane >= across
    high = lane < RADIX

    def bring(source, place):
        tall = 128

        def step(n, carry):
            for part in range(2):
                value = source[part, pl.ds(pl.multiple_of(n * tall, tall), tall), :]
                at = pl.multiple_of(place * block_rows + n * tall, tall)
                raw[part, pl.ds(at, tall), :] = value
            return carry

        lax.fori_loop(0, block_rows // tall, step, 0)

    @pl.when(me == 0)
    def _():
        bring(halo_far, 0)

    @pl.when(me != 0)
    def _():
        bring(halo_own.at[index], 0)

    bring(keep.at[index], 1 + me)
    bring(recv, 2 - me)

    back = lax.rem(LANES - across, LANES)
    for tap in range(TAPS):
        here = coef[tap, pl.ds(down, ROWS), :]
        after = coef[tap, pl.ds(down + 1, ROWS), :]
        weights[tap] = pltpu.roll(jnp.where(turned_in, here, after), back, 1)
    for dest, old in zip(outs, earlier):
        dest[:before] = old[...]

    def filt(half, low, high_frame, band, part):
        size = high_frame - low
        values = []
        for u in range(size + TAPS - 1):
            at = (half * HALF + low + u + frames - TAPS) * ROWS + band * 16
            values.append(raw[part, at : at + 16, :].astype(jnp.float32))
        sums = [None] * size
        for tap in range(TAPS):
            weight = weights[tap, band * 16 : band * 16 + 16, :]
            for u in range(size):
                term = weight * values[u + TAPS - 1 - tap]
                sums[u] = term if sums[u] is None else sums[u] + term
        for u in range(size):
            at = (low + u) * ROWS + band * 16
            filtered[half][part, at : at + 16, :] = sums[u]

    twice = lax.rem(across + RADIX, LANES)

    def place(half, u):
        for band in range(ROWS // 16):
            at = (u + 1) * ROWS + band * 16 - down
            moved, turned = [], []
            for part in range(2):
                here = filtered[half][part, pl.ds(at, 16), :]
                above = filtered[half][part, pl.ds(at - 1, 16), :]
                value = jnp.where(inside, here, above)
                moved.append(pltpu.roll(value, across, 1))
                turned.append(pltpu.roll(value, twice, 1))
            parts = (
                jnp.where(high, moved[0], turned[1]),
                jnp.where(high, turned[0], moved[1]),
                jnp.where(high, moved[1], -turned[0]),
                jnp.where(high, turned[1], -moved[0]),
            )
            for which, value in enumerate(parts):
                low = which * ROWS + band * 16
                grouped[half * HALF + u, low : low + 16, :] = value.astype(jnp.bfloat16)

    def turn(base):
        wide = jnp.concatenate([grouped[base + u] for u in range(SOME)], axis=1)
        inner = jnp.dot(first[...], wide, preferred_element_type=jnp.float32)
        rows = []
        for u in range(SOME):
            cut = slice(u * LANES, (u + 1) * LANES)
            value = inner[:RADIX, cut] * tw_cos[...] + inner[RADIX:, cut] * tw_sin[...]
            rows.append(value.astype(jnp.bfloat16))
        inner = jnp.concatenate(rows, axis=0)
        result = lax.dot_general(
            rows_out, inner, (((1,), (1,)), ((), ())), preferred_element_type=jnp.float32
        ).astype(jnp.bfloat16)
        size = result.shape[0] // (2 * dests)
        for dest in range(dests):
            for part in range(2):
                low = (dest * 2 + part) * size
                for u in range(SOME // 2):
                    outs[dest][before, base // 2 + u, part] = result[
                        low : low + size, u * LANES : (u + 1) * LANES
                    ]

    rows_out = jnp.concatenate(
        [last[me ^ dg, ct + dc] for dg in range(PAIR) for dc in range(per_ct)], axis=0
    )
    pieces = [
        (low, high_frame, band, part)
        for low, high_frame in ((0, 9), (9, HALF + 1))
        for band in range(ROWS // 16)
        for part in range(2)
    ]
    each = len(pieces) // (HALF // SOME)
    halves = total // HALF
    for half in range(halves + 1):
        for n in range(HALF // SOME):
            if half < halves:
                for piece in pieces[n * each : (n + 1) * each]:
                    filt(half, *piece)
            if half:
                for u in range(SOME):
                    place(half - 1, n * SOME + u)
                turn((half - 1) * HALF + n * SOME)


def filterbank(index, meta, keep, halo_own, recv, halo_far, tables, earlier, dests):
    frames = keep.shape[2] // ROWS
    size = tables[-1].shape[2] // 2
    per_ct = tables[-1].shape[1] // 2
    before = earlier[0].shape[0] if earlier else 0
    all_rows = (PAIR + 1) * frames * ROWS
    shape = (before + 1, PAIR * frames // 2, 2, size, LANES)
    return pl.pallas_call(
        functools.partial(
            filterbank_kernel, index, before, frames, dests, per_ct, keep.shape[0]
        ),
        out_shape=[jax.ShapeDtypeStruct(shape, jnp.bfloat16)] * dests,
        in_specs=[SMEM] + [VMEM] * (9 + len(earlier)),
        out_specs=[VMEM] * dests,
        scratch_shapes=[
            pltpu.VMEM((2, all_rows, LANES), jnp.bfloat16),
            pltpu.VMEM((TAPS, ROWS, LANES), jnp.float32),
            pltpu.VMEM((PAIR * frames, LANES, LANES), jnp.bfloat16),
        ]
        + [pltpu.VMEM((2, (HALF + 1) * ROWS, LANES), jnp.float32)] * (PAIR * frames // HALF),
        compiler_params=params(12),
        cost_estimate=cost(10**6, 2**18),
        name="filterbank",
    )(meta, keep, halo_own, recv, halo_far, *tables, *earlier)


SQUARE = [(p, q) for p in range(TILE) for q in range(TILE)]
CORNER = [(p, q) for p in range(TILE) for q in range(p, TILE)]


def own_blocks(own):
    tiles = own // TILE
    whole = [(i, j, SQUARE) for i in range(tiles) for j in range(i + 1, tiles)]
    return whole + [(i, i, CORNER) for i in range(tiles)]


def cross_blocks(own):
    tiles = own // TILE
    return [(i, j, SQUARE) for i in range(tiles // 2) for j in range(tiles)]


def pairs_in(blocks):
    return sum(len(block[2]) for block in blocks)


def chosen(t, values):
    result = jnp.int32(values[0])
    for n, value in enumerate(values[1:], 1):
        result = jnp.where(t == n, jnp.int32(value), result)
    return result


def correlate_kernel(layout, *refs):
    sources_at, blocks, own, cross, outer, span, per_ct, in_count, half_count = layout
    meta, sources = refs[0], refs[1 : 1 + len(sources_at)]
    rest = refs[1 + len(sources_at) :]
    outs, (spectra, sums, held) = rest[:-3], rest[-3:]
    steps = spectra.shape[1]
    some = 8
    core, g, ct = meta[CORE_AT], meta[G_AT], meta[CT_AT]

    for source, (far, dg, dc, start) in zip(sources, sources_at):
        base = lax.rem(ct - dc + per_ct, per_ct) * in_count + (g ^ dg) * half_count + start
        wanted = None
        if cross:
            side = 1 - core if far else core
            low = core * (own // 2)
            wanted = (side == 1) | ((base >= low) & (base < low + own // 2))
            base = base + side * own

        def bring(source=source, base=base):
            for item in range(source.shape[0]):

                def spread(n, carry, item=item):
                    for u in range(some):
                        real = source[item, n * some + u, 0].astype(jnp.float32)
                        imag = source[item, n * some + u, 1].astype(jnp.float32)
                        for which, value in enumerate((real, imag, real + imag, imag - real)):
                            spectra[base + item, n * some + u, which] = value
                    return carry

                lax.fori_loop(0, steps // some, spread, 0)

        if wanted is None:
            bring()
        else:
            pl.when(wanted)(bring)

    high = lax.broadcasted_iota(jnp.int32, (1, LANES), 1) < RADIX
    rows_outer = pairs_in(blocks) * span
    size = outer * span
    unroll = 4

    def block(left, right, pairs, first_row):
        def over(one, two, acc, sign):
            def frame(n, acc):
                acc = list(acc)
                for u in range(unroll):
                    a = [spectra[left + p, n * unroll + u, one] for p in range(TILE)]
                    b = [spectra[right + q, n * unroll + u, two] for q in range(TILE)]
                    for at, (p, q) in enumerate(pairs):
                        term = a[p] * b[q]
                        acc[at] = acc[at] + term if sign > 0 else acc[at] - term
                return tuple(acc)

            return lax.fori_loop(0, steps // unroll, frame, tuple(acc))

        count = len(pairs)
        first = over(2, 0, [jnp.zeros((size, LANES), jnp.float32)] * count, 1)
        for at in range(count):
            held[0, at] = first[at]
        real = over(1, 3, first, 1)
        for at in range(count):
            held[1, at] = real[at] + pltpu.roll(real[at], RADIX, 1)
        imag = over(0, 2, [held[0, at] for at in range(count)], -1)
        for at in range(count):
            folded = imag[at] + pltpu.roll(imag[at], RADIX, 1)
            both = jnp.where(high, held[1, at], folded)
            for o in range(outer):
                row = o * rows_outer + first_row + at * span
                sums[pl.ds(pl.multiple_of(row, span), span), :] = both[o * span : (o + 1) * span]

    done = 0
    for pairs in (SQUARE, CORNER):
        some_blocks = [b for b in blocks if b[2] is pairs]
        if not some_blocks:
            continue

        def step(t, carry, some_blocks=some_blocks, pairs=pairs, done=done):
            left = TILE * chosen(t, [b[0] for b in some_blocks])
            right = TILE * chosen(t, [b[1] for b in some_blocks])
            if cross:
                left, right = left + core * (own // 2), right + own
            block(left, right, pairs, done + t * len(pairs) * span)
            return carry

        lax.fori_loop(0, len(some_blocks), step, 0)
        done += pairs_in(some_blocks) * span

    for r in range(outer):
        base = pl.multiple_of(lax.rem(meta[O_AT] + r, outer) * rows_outer, 16)
        outs[r][...] = sums[pl.ds(base, rows_outer), :].astype(outs[r].dtype)


def correlate(meta, arrays, sources_at, blocks, own, cross, sizes, name):
    outer, span, per_ct, in_count, half_count = sizes
    _, steps, _, size, _ = arrays[0].shape
    inputs = 2 * own if cross else own
    rows = pairs_in(blocks) * span
    shapes = []
    for r in range(outer):
        dtype = jnp.float32 if r == 0 else jnp.bfloat16
        shapes.append(jax.ShapeDtypeStruct((rows, LANES), dtype))
    layout = (sources_at, blocks, own, cross) + sizes
    return pl.pallas_call(
        functools.partial(correlate_kernel, layout),
        out_shape=shapes,
        in_specs=[SMEM] + [VMEM] * len(arrays),
        out_specs=[VMEM] * len(shapes),
        scratch_shapes=[
            pltpu.VMEM((inputs, steps, 4, size, LANES), jnp.float32),
            pltpu.VMEM((outer * rows, LANES), jnp.float32),
            pltpu.VMEM((2, TILE * TILE, outer * span, LANES), jnp.float32),
        ],
        compiler_params=params(8 + inputs * steps * 4 * size * LANES * 4 // 2**20),
        cost_estimate=cost(10**6, 2**18),
        name=name,
    )(meta, *arrays)


def assemble_kernel(own, outer, span, scale, *refs):
    meta = refs[0]
    mine_in = refs[1 : 1 + outer]
    mine_across = refs[1 + outer : 1 + 2 * outer]
    far_across = refs[1 + 2 * outer : 1 + 3 * outer]
    out, joined = refs[1 + 3 * outer :]
    lane = lax.broadcasted_iota(jnp.int32, (1, LANES), 1)
    high = lane < RADIX
    mirror = jnp.where(high, 1.0, -1.0).astype(jnp.float32)
    me = meta[CORE_AT]

    def added(sources, low, rows):
        total = sources[0][low : low + rows, :].astype(jnp.float32)
        for source in sources[1:]:
            total = total + source[low : low + rows, :].astype(jnp.float32)
        return total * scale

    def put(value, row, col):
        at = pl.multiple_of((row * 2 * own + col) * span, span)
        joined[pl.ds(at, span), :] = value

    done = 0
    for i, j, pairs in own_blocks(own):
        total = added(mine_in, done, len(pairs) * span)
        turned = total * mirror
        for at, (p, q) in enumerate(pairs):
            cut = slice(at * span, (at + 1) * span)
            a, b = i * TILE + p, j * TILE + q
            put(total[cut], a, me * own + b)
            if a != b:
                put(turned[cut], b, me * own + a)
        done += len(pairs) * span
    sign = jnp.where(me == 0, jnp.ones_like(mirror), mirror)
    for sources, part in ((mine_across, me), (far_across, 1 - me)):
        done = 0
        for i, j, pairs in cross_blocks(own):
            total = added(sources, done, len(pairs) * span) * sign
            for at, (p, q) in enumerate(pairs):
                a = part * (own // 2) + i * TILE + p
                b = j * TILE + q
                row = jnp.where(me == 0, a, b)
                col = jnp.where(me == 0, own + b, a)
                put(total[at * span : (at + 1) * span], row, col)
            done += len(pairs) * span

    def emit(a, carry):
        for tile in range(2 * own // 8):
            for pair in range(span // 2):
                loads = []
                for u in range(2):
                    at = (a * 2 * own + tile * 8) * span + pair * 2 + u
                    loads.append(joined[pl.ds(at, 8, stride=span), :])
                turned = [pltpu.roll(x, RADIX, 1) for x in loads]
                cut = slice(pair * LANES, (pair + 1) * LANES)
                out[0, a, tile * 8 : tile * 8 + 8, cut] = jnp.where(high, loads[0], turned[1])
                out[1, a, tile * 8 : tile * 8 + 8, cut] = jnp.where(high, turned[0], loads[1])
        return carry

    lax.fori_loop(0, own, emit, 0)


def assemble(meta, mine_in, mine_across, far_across, own, span, scale):
    outer = len(mine_in)
    return pl.pallas_call(
        functools.partial(assemble_kernel, own, outer, span, scale),
        out_shape=jax.ShapeDtypeStruct((2, own, 2 * own, span * RADIX), jnp.float32),
        in_specs=[SMEM] + [VMEM] * (3 * outer),
        out_specs=VMEM,
        scratch_shapes=[pltpu.VMEM((own * 2 * own * span, LANES), jnp.float32)],
        compiler_params=params(10),
        cost_estimate=cost(10**6, 2**18),
        name="assemble",
    )(meta, *mine_in, *mine_across, *far_across)


def fast_fits(in_count, frame_count):
    stn, tm, per_ct = (lax.axis_size(a) for a in ("stn", "tm", "ct"))
    groups = tm * per_ct
    if stn != 2 or tm % PAIR or in_count % (PAIR * JOIN) or RADIX % groups:
        return False
    outer, span = tm // PAIR, RADIX // groups
    own = in_count * per_ct
    return (
        frame_count >= TAPS
        and frame_count % HALF == 0
        and span in (2, 4, 8)
        and outer * span % 16 == 0
        and own % (2 * TILE) == 0
        and (own * (own + 1) // 2 * span) % 16 == 0
    )


def fast(voltages, delays):
    tm, per_ct = lax.axis_size("tm"), lax.axis_size("ct")
    in_count = voltages.shape[1]
    frame_count = voltages.shape[2] // CHANNELS
    outer = tm // PAIR
    span = RADIX // (tm * per_ct)
    own = in_count * per_ct
    half = in_count // PAIR
    place_tm, place_ct = lax.axis_index("tm"), lax.axis_index("ct")
    core = lax.axis_index("stn")
    g, o = place_tm % PAIR, place_tm // PAIR

    swap = [(i, i ^ 1) for i in range(tm)]
    onward = [(i, i + PAIR) for i in range(tm - PAIR)]
    cores = [(0, 1), (1, 0)]

    scalars = [None] * DELAY_AT
    scalars[G_AT], scalars[O_AT], scalars[CORE_AT], scalars[CT_AT] = g, o, core, place_ct
    meta = jnp.concatenate([jnp.stack(scalars).astype(jnp.int32), delays])

    dests = [(dg, dc) for dg in range(PAIR) for dc in range(per_ct)]
    base = last_table(outer, per_ct, span)
    tables = [np.concatenate([filter_table()] * 2, axis=1), first_table(), *twiddle_tables()]
    tables = [jnp.asarray(t) for t in tables + [np.concatenate([base, base], axis=1)]]

    sends = list(pick(meta, voltages, half, False, False))
    forward = [p for p in onward if p[0] % PAIR == 0]
    recvs = []
    for c in range(half):
        block = follow(sends[c], recvs[c - 2]) if c >= 2 else sends[c]
        recvs.append(lax.ppermute(block, "tm", swap))
    keep = pick(meta, voltages, half, True, True)[0]
    halo_own = lax.ppermute(keep, "tm", [p for p in onward if p[0] % PAIR == 1])

    arrays, others, places = [], [], []
    spectra, done = [], []
    for c in range(half):
        block = follow(recvs[c], done[c - 2]) if c >= 2 else recvs[c]
        far = lax.ppermute(block, "tm", forward)
        far = follow(far, done[c - 1]) if c else far
        spectra = filterbank(
            c, meta, keep, halo_own, recvs[c], far, tables, spectra, len(dests)
        )
        done.append(spectra[0])
        if c % JOIN < JOIN - 1:
            continue
        for (dg, dc), block in zip(dests, spectra):
            route = []
            for i in range(tm):
                for j in range(per_ct):
                    target = (i ^ dg) * per_ct + (j + dc) % per_ct
                    route.append((i * per_ct + j, target))
            if dg or dc:
                if len(arrays) >= len(dests):
                    block = follow(block, arrays[-len(dests)])
                block = lax.ppermute(block, ("tm", "ct"), route)
            arrays.append(block)
            others.append(lax.ppermute(block, "stn", cores))
            places.append((dg, dc, c - JOIN + 1))
        spectra = []

    sizes = (outer, span, per_ct, in_count, half)
    near = [(False,) + place for place in places]
    far = [(True,) + place for place in places]
    mine_in = correlate(
        meta, arrays, near, own_blocks(own), own, False, sizes, "correlate_own"
    )
    mine_across = correlate(
        meta, arrays + others, near + far, cross_blocks(own), own, True, sizes, "correlate_cross"
    )
    mine_in, mine_across, far_across = list(mine_in), list(mine_across), []
    for r in range(1, outer):
        route = [(i, (i + r * PAIR) % tm) for i in range(tm)]
        mine_in[r] = lax.ppermute(mine_in[r], "tm", route)
    for r in range(outer):
        if r:
            route = [(i, (i + r * PAIR) % tm) for i in range(tm)]
            block = follow(mine_across[r], mine_in[r])
            mine_across[r] = lax.ppermute(block, "tm", route)
        far_across.append(lax.ppermute(mine_across[r], "stn", cores))
    scale = 1.0 / (tm * frame_count)
    result = assemble(meta, mine_in, mine_across, far_across, own, span, scale)
    return result.transpose(0, 3, 1, 2)


def general(voltages, delays):
    in_count = voltages.shape[1]
    frame_count = voltages.shape[2] // CHANNELS
    route = [(i, i + 1) for i in range(lax.axis_size("tm") - 1)]
    extended = jnp.concatenate([lax.ppermute(voltages, "tm", route), voltages], axis=2)
    span = (frame_count + TAPS - 1) * CHANNELS
    shifted = jax.vmap(
        lambda row, offset: lax.dynamic_slice_in_dim(row, CHANNELS - offset, span, 1),
        in_axes=(1, 0),
        out_axes=1,
    )(extended, delays)
    framed = shifted.reshape(2, in_count, frame_count + TAPS - 1, CHANNELS)
    table = jnp.asarray(filter_table()).reshape(TAPS, CHANNELS)
    total = jnp.zeros((2, in_count, frame_count, CHANNELS), jnp.float32)
    for tap in range(TAPS):
        low = TAPS - 1 - tap
        total = total + table[tap] * framed[:, :, low : low + frame_count].astype(jnp.float32)
    branches = jnp.moveaxis(total.astype(jnp.bfloat16), 0, 2)

    number = in_count * frame_count
    cosine, sine = dft_parts(RADIX)
    block = np.concatenate(
        [np.concatenate([cosine, sine], axis=1), np.concatenate([-sine, cosine], axis=1)], axis=0
    )
    block = jnp.asarray(block)
    stacked = branches.reshape(number, 2 * RADIX, RADIX)
    inner = jnp.einsum("kj,nja->nka", block, stacked, preferred_element_type=jnp.float32)
    inner = inner.reshape(number, 2, RADIX, RADIX)
    tw_cos, tw_sin = (jnp.asarray(t[:, :RADIX]) for t in twiddle_tables())
    real = inner[:, 0] * tw_cos + inner[:, 1] * tw_sin
    imag = inner[:, 1] * tw_cos - inner[:, 0] * tw_sin
    turned = jnp.stack([real, imag], axis=2).reshape(number, RADIX, 2 * RADIX)
    turned = turned.astype(jnp.bfloat16)
    result = jnp.einsum("lj,nkj->nlk", block, turned, preferred_element_type=jnp.float32)
    spectra = result.reshape(in_count, frame_count, 2, CHANNELS).astype(jnp.bfloat16)
    moved = lax.all_to_all(spectra, "tm", split_axis=3, concat_axis=1, tiled=True)
    moved = lax.all_to_all(moved, "ct", split_axis=3, concat_axis=0, tiled=True)
    local = moved.transpose(3, 2, 0, 1)
    swapped = jnp.stack([local[:, 1], -local[:, 0]], axis=1)
    summed = jnp.einsum(
        "ocjaf,cjbf->ocab",
        jnp.stack([local, swapped], axis=0),
        lax.all_gather(local, "stn", axis=2, tiled=True),
        preferred_element_type=jnp.float32,
    )
    return summed * (1.0 / local.shape[3])


def on_device(voltages, delays):
    if fast_fits(voltages.shape[1], voltages.shape[2] // CHANNELS):
        return fast(voltages, delays)
    return general(voltages, delays)


def solution(mesh):
    return jax.shard_map(
        on_device,
        mesh=mesh,
        in_specs=(P(None, ("stn", "ct"), "tm"), P(("stn", "ct"))),
        out_specs=P(None, ("tm", "ct"), "stn", None),
        check_vma=False,
    )
```

```python
import functools
import math

import jax
import jax.numpy as jnp
import numpy as np
from jax import lax
from jax.experimental import pallas as pl
from jax.experimental.pallas import tpu as pltpu
from jax.sharding import PartitionSpec as P

CHANNELS = 4096
RADIX = 64
TAPS = 16
LANES = 128
ROWS = CHANNELS // LANES
PAIR = 2
TILE = 4
JOIN = 2

G_AT, O_AT, CORE_AT, CT_AT, DELAY_AT = range(5)

VMEM = pl.BlockSpec(memory_space=pltpu.VMEM)
SMEM = pl.BlockSpec(memory_space=pltpu.SMEM)


def params(mib):
    return pltpu.CompilerParams(vmem_limit_bytes=mib * 2**20)


def cost(flops, size):
    return pl.CostEstimate(flops=flops, bytes_accessed=size, transcendentals=0)


def filter_table():
    length = TAPS * CHANNELS
    index = np.arange(length, dtype=np.float64)
    centred = (index - length / 2) / CHANNELS
    window = 0.5 - 0.5 * np.cos(2.0 * math.pi * index / length)
    factor = 1.0 / (48.0 * math.sqrt(CHANNELS))
    table = np.sinc(centred) * window * factor
    return table.reshape(TAPS, ROWS, LANES).astype(np.float32)


def dft_parts(radix):
    steps = np.arange(radix)
    angle = 2.0 * math.pi * (steps[:, None] * steps[None, :] % radix) / radix
    return np.cos(angle).astype(jnp.bfloat16), np.sin(angle).astype(jnp.bfloat16)


def first_table():
    cosine, sine = dft_parts(CHANNELS // RADIX)
    order = [2 * row + half for half in range(2) for row in range(ROWS)]
    cosine, sine = cosine[:, order], sine[:, order]
    upper = np.concatenate([cosine, sine], axis=1)
    lower = np.concatenate([-sine, cosine], axis=1)
    return np.concatenate([upper, lower], axis=0)


def last_table(outer, per_ct, span):
    cosine, sine = dft_parts(RADIX)
    blocks = []
    for g in range(PAIR):
        for ct in range(per_ct):
            steps = [
                ((o * PAIR + g) * per_ct + ct) * span + j for o in range(outer) for j in range(span)
            ]
            real = np.concatenate([cosine[steps], sine[steps]], axis=1)
            imag = np.concatenate([-sine[steps], cosine[steps]], axis=1)
            blocks.append(np.concatenate([real, imag], axis=0))
    return np.stack(blocks).reshape(PAIR, per_ct, -1, 2 * RADIX)


def twiddle_tables():
    rows = np.arange(CHANNELS // RADIX)
    cols = np.arange(RADIX)
    angle = 2.0 * math.pi * (rows[:, None] * cols[None, :] % CHANNELS) / CHANNELS
    cosine = np.cos(angle).astype(np.float32)
    sine = np.sin(angle).astype(np.float32)
    return np.concatenate([cosine, cosine], axis=1), np.concatenate([sine, sine], axis=1)


def pick_kernel(half, meta, block, *refs):
    outs, rows = refs[:-1], refs[-1]
    inputs, samples = block.shape[1], block.shape[2]
    step = 16
    for part in range(2):

        def spread(n, carry, part=part):
            low = pl.multiple_of(n * step * LANES, step * LANES)
            wide = block[part, :, pl.ds(low, step * LANES)].astype(jnp.float32)
            for u in range(step):
                at = pl.multiple_of((n * step + u) * inputs, inputs)
                rows[part, pl.ds(at, inputs), :] = wide[:, u * LANES : (u + 1) * LANES]
            return carry

        lax.fori_loop(0, samples // LANES // step, spread, 0)
    g = meta[G_AT]
    tall = 128
    for item in range(inputs):
        first = (1 - g) * half + item if item < half else g * half + item - half
        kept = item - half
        out = outs[item] if item < half else outs[half + kept // JOIN].at[kept % JOIN]

        def gather(n, carry, first=first, out=out):
            low = pl.multiple_of(n * tall, tall)
            for part in range(2):
                value = rows[part, pl.ds(low * inputs + first, tall, stride=inputs), :]
                out[part, pl.ds(low, tall), :] = value.astype(jnp.bfloat16)
            return carry

        lax.fori_loop(0, samples // LANES // tall, gather, 0)


def pick(meta, block):
    _, inputs, samples = block.shape
    half = inputs // PAIR
    one = (2, samples // LANES, LANES)
    shapes = [one] * half + [(JOIN,) + one] * (half // JOIN)
    return pl.pallas_call(
        functools.partial(pick_kernel, half),
        out_shape=[jax.ShapeDtypeStruct(s, jnp.bfloat16) for s in shapes],
        in_specs=[SMEM, VMEM],
        out_specs=[VMEM] * len(shapes),
        scratch_shapes=[pltpu.VMEM((2, samples // LANES * inputs, LANES), jnp.float32)],
        compiler_params=params(16),
        cost_estimate=cost(10**6, 2**18),
        name="pick",
    )(meta, block)


def follow(block, after):
    return lax.optimization_barrier((block, after))[0]


HALF = 16
SOME = 4


def filterbank_kernel(index, before, frames, dests, per_ct, half_count, *refs):
    meta, keep, halo_own, recv, halo_far, coef, first, tw_cos, tw_sin, last = refs[:10]
    earlier = refs[10 : 10 + dests * (before > 0)]
    refs = refs[10 + len(earlier) :]
    outs = refs[:dests]
    raw, weights, grouped = refs[dests : dests + 3]
    filtered = refs[dests + 3 :]
    block_rows = frames * ROWS
    total = PAIR * frames
    me, ct = meta[G_AT], meta[CT_AT]
    delay = meta[DELAY_AT + me * half_count + index]
    down = delay // LANES
    across = delay % LANES
    lane = lax.broadcasted_iota(jnp.int32, (1, LANES), 1)
    inside = lane < LANES - across
    turned_in = lane >= across
    high = lane < RADIX

    def bring(source, place):
        tall = 128

        def step(n, carry):
            for part in range(2):
                value = source[part, pl.ds(pl.multiple_of(n * tall, tall), tall), :]
                at = pl.multiple_of(place * block_rows + n * tall, tall)
                raw[part, pl.ds(at, tall), :] = value
            return carry

        lax.fori_loop(0, block_rows // tall, step, 0)

    @pl.when(me == 0)
    def _():
        bring(halo_far, 0)

    @pl.when(me != 0)
    def _():
        bring(halo_own.at[index % JOIN], 0)

    bring(keep.at[index % JOIN], 1 + me)
    bring(recv, 2 - me)

    back = lax.rem(LANES - across, LANES)
    for tap in range(TAPS):
        here = coef[tap, pl.ds(down, ROWS), :]
        after = coef[tap, pl.ds(down + 1, ROWS), :]
        weights[tap] = pltpu.roll(jnp.where(turned_in, here, after), back, 1)
    for dest, old in zip(outs, earlier):
        dest[:before] = old[...]

    def filt(half, low, high_frame, band, part):
        size = high_frame - low
        values = []
        for u in range(size + TAPS - 1):
            at = (half * HALF + low + u + frames - TAPS) * ROWS + band * 16
            values.append(raw[part, at : at + 16, :].astype(jnp.float32))
        sums = [None] * size
        for tap in range(TAPS):
            weight = weights[tap, band * 16 : band * 16 + 16, :]
            for u in range(size):
                term = weight * values[u + TAPS - 1 - tap]
                sums[u] = term if sums[u] is None else sums[u] + term
        for u in range(size):
            at = (low + u) * ROWS + band * 16
            filtered[half][part, at : at + 16, :] = sums[u]

    twice = lax.rem(across + RADIX, LANES)

    def place(half, u):
        for band in range(ROWS // 16):
            at = (u + 1) * ROWS + band * 16 - down
            moved, turned = [], []
            for part in range(2):
                here = filtered[half][part, pl.ds(at, 16), :]
                above = filtered[half][part, pl.ds(at - 1, 16), :]
                value = jnp.where(inside, here, above)
                moved.append(pltpu.roll(value, across, 1))
                turned.append(pltpu.roll(value, twice, 1))
            parts = (
                jnp.where(high, moved[0], turned[1]),
                jnp.where(high, turned[0], moved[1]),
                jnp.where(high, moved[1], -turned[0]),
                jnp.where(high, turned[1], -moved[0]),
            )
            for which, value in enumerate(parts):
                low = which * ROWS + band * 16
                grouped[half * HALF + u, low : low + 16, :] = value.astype(jnp.bfloat16)

    def turn(base):
        wide = jnp.concatenate([grouped[base + u] for u in range(SOME)], axis=1)
        inner = jnp.dot(first[...], wide, preferred_element_type=jnp.float32)
        rows = []
        for u in range(SOME):
            cut = slice(u * LANES, (u + 1) * LANES)
            value = inner[:RADIX, cut] * tw_cos[...] + inner[RADIX:, cut] * tw_sin[...]
            rows.append(value.astype(jnp.bfloat16))
        inner = jnp.concatenate(rows, axis=0)
        result = lax.dot_general(
            rows_out, inner, (((1,), (1,)), ((), ())), preferred_element_type=jnp.float32
        ).astype(jnp.bfloat16)
        size = result.shape[0] // (2 * dests)
        for dest in range(dests):
            for part in range(2):
                low = (dest * 2 + part) * size
                for u in range(SOME // 2):
                    outs[dest][before, base // 2 + u, part] = result[
                        low : low + size, u * LANES : (u + 1) * LANES
                    ]

    rows_out = jnp.concatenate(
        [last[me ^ dg, ct + dc] for dg in range(PAIR) for dc in range(per_ct)], axis=0
    )
    pieces = [
        (low, high_frame, band, part)
        for low, high_frame in ((0, 9), (9, HALF + 1))
        for band in range(ROWS // 16)
        for part in range(2)
    ]
    each = len(pieces) // (HALF // SOME)
    halves = total // HALF
    for half in range(halves + 1):
        for n in range(HALF // SOME):
            if half < halves:
                for piece in pieces[n * each : (n + 1) * each]:
                    filt(half, *piece)
            if half:
                for u in range(SOME):
                    place(half - 1, n * SOME + u)
                turn((half - 1) * HALF + n * SOME)


def filterbank(index, half, meta, keep, halo_own, recv, halo_far, tables, earlier, dests):
    frames = keep.shape[2] // ROWS
    size = tables[-1].shape[2] // 2
    per_ct = tables[-1].shape[1] // 2
    before = earlier[0].shape[0] if earlier else 0
    all_rows = (PAIR + 1) * frames * ROWS
    shape = (before + 1, PAIR * frames // 2, 2, size, LANES)
    return pl.pallas_call(
        functools.partial(
            filterbank_kernel, index, before, frames, dests, per_ct, half
        ),
        out_shape=[jax.ShapeDtypeStruct(shape, jnp.bfloat16)] * dests,
        in_specs=[SMEM] + [VMEM] * (9 + len(earlier)),
        out_specs=[VMEM] * dests,
        scratch_shapes=[
            pltpu.VMEM((2, all_rows, LANES), jnp.bfloat16),
            pltpu.VMEM((TAPS, ROWS, LANES), jnp.float32),
            pltpu.VMEM((PAIR * frames, LANES, LANES), jnp.bfloat16),
        ]
        + [pltpu.VMEM((2, (HALF + 1) * ROWS, LANES), jnp.float32)] * (PAIR * frames // HALF),
        compiler_params=params(12),
        cost_estimate=cost(10**6, 2**18),
        name="filterbank",
    )(meta, keep, halo_own, recv, halo_far, *tables, *earlier)


SQUARE = [(p, q) for p in range(TILE) for q in range(TILE)]
CORNER = [(p, q) for p in range(TILE) for q in range(p, TILE)]


def pair_sets(own, parts):
    tiles = own // TILE
    per = tiles // parts
    whole = [(True, i, j, SQUARE) for i in range(tiles) for j in range(i + 1, tiles)]
    corner = [(True, i, i, CORNER) for i in range(tiles)]
    across = [(False, i, j, SQUARE) for i in range(0, tiles, 2) for j in range(tiles)]

    def early(block):
        return block[1] < per and block[2] < per

    def late(blocks):
        return [block for block in blocks if not early(block)]

    first = [block for block in whole + across + corner if early(block)]
    return [first, late(whole + corner), late(across)]


def pairs_in(blocks):
    return sum(len(block[3]) for block in blocks)


def chosen(t, values):
    result = jnp.int32(values[0])
    for n, value in enumerate(values[1:], 1):
        result = jnp.where(t == n, jnp.int32(value), result)
    return result


def correlate_kernel(layout, *refs):
    sources_at, blocks, own, terms, outer, span, per_ct = layout
    meta, sources = refs[0], refs[1 : 1 + len(sources_at)]
    rest = refs[1 + len(sources_at) :]
    earlier, outs, (spectra, sums, held) = rest[:terms], rest[terms:-3], rest[-3:]
    steps = spectra.shape[1]
    some = 8
    core, g, ct = meta[CORE_AT], meta[G_AT], meta[CT_AT]
    within = any(block[0] for block in blocks)
    across = any(not block[0] for block in blocks)

    for source, (far, dg, dc, part) in zip(sources, sources_at):
        device = lax.rem(ct - dc + per_ct, per_ct) * PAIR + (g ^ dg)
        base = (part * per_ct * PAIR + device) * JOIN
        wanted = None
        if across:
            side = 1 - core if far else core
            wanted = (side == 1) | (lax.rem(base // TILE, 2) == core)
            if within and not far:
                wanted = None
            base = base + side * own

        def bring(source=source, base=base):
            for item in range(source.shape[0]):

                def spread(n, carry, item=item):
                    for u in range(some):
                        real = source[item, n * some + u, 0].astype(jnp.float32)
                        imag = source[item, n * some + u, 1].astype(jnp.float32)
                        for which, value in enumerate((real, imag, real + imag, imag - real)):
                            spectra[base + item, n * some + u, which] = value
                    return carry

                lax.fori_loop(0, steps // some, spread, 0)

        if wanted is None:
            bring()
        else:
            pl.when(wanted)(bring)

    high = lax.broadcasted_iota(jnp.int32, (1, LANES), 1) < RADIX
    rows_outer = pairs_in(blocks) * span
    size = outer * span
    unroll = 4

    def block(left, right, pairs, first_row):
        def over(one, two, acc, sign):
            def frame(n, acc):
                acc = list(acc)
                for u in range(unroll):
                    a = [spectra[left + p, n * unroll + u, one] for p in range(TILE)]
                    b = [spectra[right + q, n * unroll + u, two] for q in range(TILE)]
                    for at, (p, q) in enumerate(pairs):
                        term = a[p] * b[q]
                        acc[at] = acc[at] + term if sign > 0 else acc[at] - term
                return tuple(acc)

            return lax.fori_loop(0, steps // unroll, frame, tuple(acc))

        count = len(pairs)
        first = over(2, 0, [jnp.zeros((size, LANES), jnp.float32)] * count, 1)
        for at in range(count):
            held[0, at] = first[at]
        real = over(1, 3, first, 1)
        for at in range(count):
            held[1, at] = real[at] + pltpu.roll(real[at], RADIX, 1)
        imag = over(0, 2, [held[0, at] for at in range(count)], -1)
        for at in range(count):
            folded = imag[at] + pltpu.roll(imag[at], RADIX, 1)
            both = jnp.where(high, held[1, at], folded)
            for o in range(outer):
                row = o * rows_outer + first_row + at * span
                sums[pl.ds(pl.multiple_of(row, span), span), :] = both[o * span : (o + 1) * span]

    done = 0
    while done < len(blocks):
        kind = (blocks[done][0], blocks[done][3])
        end = done
        while end < len(blocks) and (blocks[end][0], blocks[end][3]) == kind:
            end += 1
        run, row = blocks[done:end], pairs_in(blocks[:done]) * span

        def step(t, carry, run=run, row=row, kind=kind):
            left, right = chosen(t, [b[1] for b in run]), chosen(t, [b[2] for b in run])
            if not kind[0]:
                left, right = TILE * (left + core), own + TILE * right
            elif across:
                left, right = core * own + TILE * left, core * own + TILE * right
            else:
                left, right = TILE * left, TILE * right
            block(left, right, kind[1], row + t * len(kind[1]) * span)
            return carry

        lax.fori_loop(0, len(run), step, 0)
        done = end

    for r in range(outer):
        base = pl.multiple_of(lax.rem(meta[O_AT] + r, outer) * rows_outer, 16)
        outs[r][...] = sums[pl.ds(base, rows_outer), :].astype(outs[r].dtype)
    if terms:
        total = earlier[0][...].astype(jnp.float32)
        for term in earlier[1:]:
            total = total + term[...].astype(jnp.float32)
        outs[outer][...] = total


def correlate(meta, arrays, sources_at, blocks, own, sizes, name, earlier=()):
    outer, span, _ = sizes
    _, steps, _, size, _ = arrays[0].shape
    inputs = own if all(block[0] for block in blocks) else 2 * own
    rows = pairs_in(blocks) * span
    shapes = []
    for r in range(outer):
        dtype = jnp.float32 if r == 0 else jnp.bfloat16
        shapes.append(jax.ShapeDtypeStruct((rows, LANES), dtype))
    shapes += [jax.ShapeDtypeStruct(x.shape, jnp.float32) for x in earlier[:1]]
    layout = (sources_at, blocks, own, len(earlier)) + sizes
    return pl.pallas_call(
        functools.partial(correlate_kernel, layout),
        out_shape=shapes,
        in_specs=[SMEM] + [VMEM] * (len(arrays) + len(earlier)),
        out_specs=[VMEM] * len(shapes),
        scratch_shapes=[
            pltpu.VMEM((inputs, steps, 4, size, LANES), jnp.float32),
            pltpu.VMEM((outer * rows, LANES), jnp.float32),
            pltpu.VMEM((2, TILE * TILE, outer * span, LANES), jnp.float32),
        ],
        compiler_params=params(8 + inputs * steps * 4 * size * LANES * 4 // 2**20),
        cost_estimate=cost(10**6, 2**18),
        name=name,
    )(meta, *arrays, *earlier)


def assemble_kernel(own, outer, span, scale, sets, order, counts, *refs):
    meta = refs[0]
    out, joined = refs[-2:]
    sources, at = [], 1
    for count in counts:
        sources.append(refs[at : at + count])
        at += count
    near, far = sources[: len(sets)], sources[len(sets) :]
    lane = lax.broadcasted_iota(jnp.int32, (1, LANES), 1)
    high = lane < RADIX
    mirror = jnp.where(high, 1.0, -1.0).astype(jnp.float32)
    me = meta[CORE_AT]

    def added(parts, low, rows):
        total = parts[0][low : low + rows, :].astype(jnp.float32)
        for part in parts[1:]:
            total = total + part[low : low + rows, :].astype(jnp.float32)
        return total * scale

    def put(value, row, col):
        at = pl.multiple_of((row * 2 * own + col) * span, span)
        joined[pl.ds(at, span), :] = value

    sign = jnp.where(me == 0, jnp.ones_like(mirror), mirror)
    for blocks, mine, others in zip(sets, near, far):
        low = 0
        for within, i, j, pairs in blocks:
            rows = len(pairs) * span
            if within:
                total = added(mine, low, rows)
                turned = total * mirror
                for n, (p, q) in enumerate(pairs):
                    cut = slice(n * span, (n + 1) * span)
                    a, b = order[i * TILE + p], order[j * TILE + q]
                    put(total[cut], a, me * own + b)
                    if a != b:
                        put(turned[cut], b, me * own + a)
            else:
                for parts, side in ((mine, me), (others, 1 - me)):
                    total = added(parts, low, rows) * sign
                    for n, (p, q) in enumerate(pairs):
                        a = jnp.where(side == 0, order[i * TILE + p], order[(i + 1) * TILE + p])
                        b = order[j * TILE + q]
                        row = jnp.where(me == 0, a, b)
                        col = jnp.where(me == 0, own + b, a)
                        put(total[n * span : (n + 1) * span], row, col)
            low += rows

    def emit(a, carry):
        for tile in range(2 * own // 8):
            for pair in range(span // 2):
                loads = []
                for u in range(2):
                    at = (a * 2 * own + tile * 8) * span + pair * 2 + u
                    loads.append(joined[pl.ds(at, 8, stride=span), :])
                turned = [pltpu.roll(x, RADIX, 1) for x in loads]
                cut = slice(pair * LANES, (pair + 1) * LANES)
                out[0, a, tile * 8 : tile * 8 + 8, cut] = jnp.where(high, loads[0], turned[1])
                out[1, a, tile * 8 : tile * 8 + 8, cut] = jnp.where(high, turned[0], loads[1])
        return carry

    lax.fori_loop(0, own, emit, 0)


def assemble(meta, near, far, sets, order, own, span, scale):
    outer = len(near[1])
    counts = [len(arrays) for arrays in near + far]
    sources = [x for arrays in near + far for x in arrays]
    return pl.pallas_call(
        functools.partial(assemble_kernel, own, outer, span, scale, sets, order, counts),
        out_shape=jax.ShapeDtypeStruct((2, own, 2 * own, span * RADIX), jnp.float32),
        in_specs=[SMEM] + [VMEM] * len(sources),
        out_specs=VMEM,
        scratch_shapes=[pltpu.VMEM((own * 2 * own * span, LANES), jnp.float32)],
        compiler_params=params(10),
        cost_estimate=cost(10**6, 2**18),
        name="assemble",
    )(meta, *sources)


def fast_fits(in_count, frame_count):
    stn, tm, per_ct = (lax.axis_size(a) for a in ("stn", "tm", "ct"))
    groups = tm * per_ct
    if stn != 2 or tm % PAIR or in_count % (PAIR * JOIN) or RADIX % groups:
        return False
    outer, span = tm // PAIR, RADIX // groups
    own = in_count * per_ct
    return (
        frame_count >= TAPS
        and frame_count % HALF == 0
        and span in (2, 4, 8)
        and outer * span % 16 == 0
        and own % (PAIR * JOIN * 2 * TILE // 4) == 0
        and in_count == PAIR * JOIN * 2
        and per_ct * PAIR * JOIN % (2 * TILE) == 0
        and all(pairs_in(s) * span % 16 == 0 for s in pair_sets(own, 2))
    )


def fast(voltages, delays):
    tm, per_ct = lax.axis_size("tm"), lax.axis_size("ct")
    in_count = voltages.shape[1]
    frame_count = voltages.shape[2] // CHANNELS
    outer = tm // PAIR
    span = RADIX // (tm * per_ct)
    own = in_count * per_ct
    half = in_count // PAIR
    place_tm, place_ct = lax.axis_index("tm"), lax.axis_index("ct")
    core = lax.axis_index("stn")
    g, o = place_tm % PAIR, place_tm // PAIR

    swap = [(i, i ^ 1) for i in range(tm)]
    onward = [(i, i + PAIR) for i in range(tm - PAIR)]
    cores = [(0, 1), (1, 0)]

    scalars = [None] * DELAY_AT
    scalars[G_AT], scalars[O_AT], scalars[CORE_AT], scalars[CT_AT] = g, o, core, place_ct
    meta = jnp.concatenate([jnp.stack(scalars).astype(jnp.int32), delays])

    dests = [(dg, dc) for dg in range(PAIR) for dc in range(per_ct)]
    base = last_table(outer, per_ct, span)
    tables = [np.concatenate([filter_table()] * 2, axis=1), first_table(), *twiddle_tables()]
    tables = [jnp.asarray(t) for t in tables + [np.concatenate([base, base], axis=1)]]

    picked = pick(meta, voltages)
    sends, keeps = picked[:half], picked[half:]
    forward = [p for p in onward if p[0] % PAIR == 0]
    recvs = []
    for c in range(half):
        block = follow(sends[c], recvs[c - 2]) if c >= 2 else sends[c]
        recvs.append(lax.ppermute(block, "tm", swap))
    ahead = [p for p in onward if p[0] % PAIR == 1]
    halos = []
    for block in keeps:
        halos.append(lax.ppermute(follow(block, halos[-1]) if halos else block, "tm", ahead))

    parts = half // JOIN
    sets = pair_sets(own, parts)
    sizes = (outer, span, per_ct)
    arrays, places = [], []
    spectra, done = [], []
    for c in range(half):
        block = follow(recvs[c], done[c - 2]) if c >= 2 else recvs[c]
        far = lax.ppermute(block, "tm", forward)
        far = follow(far, done[c - 1]) if c else far
        spectra = filterbank(
            c, half, meta, keeps[c // JOIN], halos[c // JOIN], recvs[c], far, tables, spectra,
            len(dests),
        )
        done.append(spectra[0])
        if c % JOIN < JOIN - 1:
            continue
        for (dg, dc), block in zip(dests, spectra):
            route = []
            for i in range(tm):
                for j in range(per_ct):
                    target = (i ^ dg) * per_ct + (j + dc) % per_ct
                    route.append((i * per_ct + j, target))
            if dg or dc:
                if len(arrays) >= len(dests):
                    block = follow(block, arrays[-len(dests)])
                block = lax.ppermute(block, ("tm", "ct"), route)
            arrays.append(block)
            places.append((dg, dc, c // JOIN))
        spectra = []
    near = [(False,) + place for place in places]
    far = [(True,) + place for place in places]
    count = len(dests)
    others = [lax.ppermute(follow(block, done[-1]), "stn", cores) for block in arrays[:count]]
    early = correlate(
        meta, arrays[:count] + others, near[:count] + far[:count], sets[0], own // parts, sizes,
        "correlate_early",
    )
    others += [lax.ppermute(follow(block, early[0]), "stn", cores) for block in arrays[count:]]
    own_late = correlate(meta, arrays, near, sets[1], own, sizes, "correlate_own")

    def along(parts, after):
        moved = [parts[0]]
        for r in range(1, outer):
            route = [(i, (i + r * PAIR) % tm) for i in range(tm)]
            moved.append(lax.ppermute(follow(parts[r], after(r)), "tm", route))
        return moved

    early = along(early, lambda r: others)
    own_late = along(own_late, lambda r: early[r])
    *cross_late, early = correlate(
        meta, arrays + others, near + far, sets[2], own, sizes, "correlate_cross", early
    )
    cross_late = along(cross_late, lambda r: own_late[r])
    mine = [[early], own_late, cross_late]
    theirs = [[lax.ppermute(block, "stn", cores) for block in part] for part in (mine[0], mine[2])]
    theirs.insert(1, [])
    order = []
    for part in range(parts):
        for device in range(per_ct * PAIR):
            start = device // PAIR * in_count + device % PAIR * half + part * JOIN
            order += range(start, start + JOIN)
    scale = 1.0 / (tm * frame_count)
    result = assemble(meta, mine, theirs, sets, order, own, span, scale)
    return result.transpose(0, 3, 1, 2)


def general(voltages, delays):
    in_count = voltages.shape[1]
    frame_count = voltages.shape[2] // CHANNELS
    route = [(i, i + 1) for i in range(lax.axis_size("tm") - 1)]
    extended = jnp.concatenate([lax.ppermute(voltages, "tm", route), voltages], axis=2)
    span = (frame_count + TAPS - 1) * CHANNELS
    shifted = jax.vmap(
        lambda row, offset: lax.dynamic_slice_in_dim(row, CHANNELS - offset, span, 1),
        in_axes=(1, 0),
        out_axes=1,
    )(extended, delays)
    framed = shifted.reshape(2, in_count, frame_count + TAPS - 1, CHANNELS)
    table = jnp.asarray(filter_table()).reshape(TAPS, CHANNELS)
    total = jnp.zeros((2, in_count, frame_count, CHANNELS), jnp.float32)
    for tap in range(TAPS):
        low = TAPS - 1 - tap
        total = total + table[tap] * framed[:, :, low : low + frame_count].astype(jnp.float32)
    branches = jnp.moveaxis(total.astype(jnp.bfloat16), 0, 2)

    number = in_count * frame_count
    cosine, sine = dft_parts(RADIX)
    block = np.concatenate(
        [np.concatenate([cosine, sine], axis=1), np.concatenate([-sine, cosine], axis=1)], axis=0
    )
    block = jnp.asarray(block)
    stacked = branches.reshape(number, 2 * RADIX, RADIX)
    inner = jnp.einsum("kj,nja->nka", block, stacked, preferred_element_type=jnp.float32)
    inner = inner.reshape(number, 2, RADIX, RADIX)
    tw_cos, tw_sin = (jnp.asarray(t[:, :RADIX]) for t in twiddle_tables())
    real = inner[:, 0] * tw_cos + inner[:, 1] * tw_sin
    imag = inner[:, 1] * tw_cos - inner[:, 0] * tw_sin
    turned = jnp.stack([real, imag], axis=2).reshape(number, RADIX, 2 * RADIX)
    turned = turned.astype(jnp.bfloat16)
    result = jnp.einsum("lj,nkj->nlk", block, turned, preferred_element_type=jnp.float32)
    spectra = result.reshape(in_count, frame_count, 2, CHANNELS).astype(jnp.bfloat16)
    moved = lax.all_to_all(spectra, "tm", split_axis=3, concat_axis=1, tiled=True)
    moved = lax.all_to_all(moved, "ct", split_axis=3, concat_axis=0, tiled=True)
    local = moved.transpose(3, 2, 0, 1)
    swapped = jnp.stack([local[:, 1], -local[:, 0]], axis=1)
    summed = jnp.einsum(
        "ocjaf,cjbf->ocab",
        jnp.stack([local, swapped], axis=0),
        lax.all_gather(local, "stn", axis=2, tiled=True),
        preferred_element_type=jnp.float32,
    )
    return summed * (1.0 / local.shape[3])


def on_device(voltages, delays):
    if fast_fits(voltages.shape[1], voltages.shape[2] // CHANNELS):
        return fast(voltages, delays)
    return general(voltages, delays)


def solution(mesh):
    return jax.shard_map(
        on_device,
        mesh=mesh,
        in_specs=(P(None, ("stn", "ct"), "tm"), P(("stn", "ct"))),
        out_specs=P(None, ("tm", "ct"), "stn", None),
        check_vma=False,
    )
```

```python
import functools
import math

import jax
import jax.numpy as jnp
import numpy as np
from jax import lax
from jax.experimental import pallas as pl
from jax.experimental.pallas import tpu as pltpu
from jax.sharding import PartitionSpec as P

CHANNELS = 4096
RADIX = 64
TAPS = 16
LANES = 128
ROWS = CHANNELS // LANES
PAIR = 2
TILE = 4
JOIN = 2

G_AT, O_AT, CORE_AT, CT_AT, DELAY_AT = range(5)

VMEM = pl.BlockSpec(memory_space=pltpu.VMEM)
SMEM = pl.BlockSpec(memory_space=pltpu.SMEM)


def params(mib):
    return pltpu.CompilerParams(vmem_limit_bytes=mib * 2**20)


def cost(flops, size):
    return pl.CostEstimate(flops=flops, bytes_accessed=size, transcendentals=0)


def filter_table():
    length = TAPS * CHANNELS
    index = np.arange(length, dtype=np.float64)
    centred = (index - length / 2) / CHANNELS
    window = 0.5 - 0.5 * np.cos(2.0 * math.pi * index / length)
    factor = 1.0 / (48.0 * math.sqrt(CHANNELS))
    table = np.sinc(centred) * window * factor
    return table.reshape(TAPS, ROWS, LANES).astype(np.float32)


def dft_parts(radix):
    steps = np.arange(radix)
    angle = 2.0 * math.pi * (steps[:, None] * steps[None, :] % radix) / radix
    return np.cos(angle).astype(jnp.bfloat16), np.sin(angle).astype(jnp.bfloat16)


def first_table():
    cosine, sine = dft_parts(CHANNELS // RADIX)
    order = [2 * row + half for half in range(2) for row in range(ROWS)]
    cosine, sine = cosine[:, order], sine[:, order]
    upper = np.concatenate([cosine, sine], axis=1)
    lower = np.concatenate([-sine, cosine], axis=1)
    return np.concatenate([upper, lower], axis=0)


def last_table(outer, per_ct, span):
    cosine, sine = dft_parts(RADIX)
    blocks = []
    for g in range(PAIR):
        for ct in range(per_ct):
            steps = [
                ((o * PAIR + g) * per_ct + ct) * span + j for o in range(outer) for j in range(span)
            ]
            real = np.concatenate([cosine[steps], sine[steps]], axis=1)
            imag = np.concatenate([-sine[steps], cosine[steps]], axis=1)
            blocks.append(np.concatenate([real, imag], axis=0))
    return np.stack(blocks).reshape(PAIR, per_ct, -1, 2 * RADIX)


def twiddle_tables():
    rows = np.arange(CHANNELS // RADIX)
    cols = np.arange(RADIX)
    angle = 2.0 * math.pi * (rows[:, None] * cols[None, :] % CHANNELS) / CHANNELS
    cosine = np.cos(angle).astype(np.float32)
    sine = np.sin(angle).astype(np.float32)
    return np.concatenate([cosine, cosine], axis=1), np.concatenate([sine, sine], axis=1)


def pick_kernel(half, meta, block, *refs):
    outs, rows = refs[:-1], refs[-1]
    inputs, samples = block.shape[1], block.shape[2]
    step = 16
    for part in range(2):

        def spread(n, carry, part=part):
            low = pl.multiple_of(n * step * LANES, step * LANES)
            wide = block[part, :, pl.ds(low, step * LANES)].astype(jnp.float32)
            for u in range(step):
                at = pl.multiple_of((n * step + u) * inputs, inputs)
                rows[part, pl.ds(at, inputs), :] = wide[:, u * LANES : (u + 1) * LANES]
            return carry

        lax.fori_loop(0, samples // LANES // step, spread, 0)
    g = meta[G_AT]
    tall = 128
    for item in range(inputs):
        first = (1 - g) * half + item if item < half else g * half + item - half
        out = outs[item // JOIN].at[item % JOIN]

        def gather(n, carry, first=first, out=out):
            low = pl.multiple_of(n * tall, tall)
            for part in range(2):
                value = rows[part, pl.ds(low * inputs + first, tall, stride=inputs), :]
                out[part, pl.ds(low, tall), :] = value.astype(jnp.bfloat16)
            return carry

        lax.fori_loop(0, samples // LANES // tall, gather, 0)


def pick(meta, block):
    _, inputs, samples = block.shape
    half = inputs // PAIR
    one = (2, samples // LANES, LANES)
    shapes = [(JOIN,) + one] * (inputs // JOIN)
    return pl.pallas_call(
        functools.partial(pick_kernel, half),
        out_shape=[jax.ShapeDtypeStruct(s, jnp.bfloat16) for s in shapes],
        in_specs=[SMEM, VMEM],
        out_specs=[VMEM] * len(shapes),
        scratch_shapes=[pltpu.VMEM((2, samples // LANES * inputs, LANES), jnp.float32)],
        compiler_params=params(16),
        cost_estimate=cost(10**6, 2**18),
        name="pick",
    )(meta, block)


def follow(block, after):
    return lax.optimization_barrier((block, after))[0]


SOME = 4


def filterbank_kernel(late, part, frames, dests, per_ct, half_count, *refs):
    meta, refs = refs[0], refs[1:]
    me, ct = meta[G_AT], meta[CT_AT]
    if late:
        keep, recv = refs[:2]
        refs = refs[2:]
    else:
        halo, keep, recv = refs[:3]
        refs = refs[3:]
    coef, first, tw_cos, tw_sin, last = refs[:5]
    beside = () if late else refs[5 : 5 + dests]
    outs = refs[5 + len(beside) :][:dests]
    raw, weights, grouped = refs[5 + len(beside) + dests :][:3]
    filtered = refs[5 + len(beside) + dests + 3 :]
    block_rows = frames * ROWS
    lane = lax.broadcasted_iota(jnp.int32, (1, LANES), 1)
    high = lane < RADIX

    def bring(source, place):
        tall = 128

        def step(n, carry):
            low = pl.multiple_of(n * tall, tall)
            at = pl.multiple_of(place * block_rows + n * tall, tall)
            for item in range(JOIN):
                for c in range(2):
                    raw[item, c, pl.ds(at, tall), :] = source[item, c, pl.ds(low, tall), :]
            return carry

        lax.fori_loop(0, block_rows // tall, step, 0)

    if late:
        bring(keep, me)
        bring(recv, 1 - me)
    else:
        bring(halo, 0)
        pl.when(me == 0)(lambda: bring(keep, 1))
        pl.when(me != 0)(lambda: bring(recv, 1))
        for dest, block in zip(outs, beside):
            dest[:, frames // 2 :] = block[...]

    downs, acrosses = [], []
    for item in range(JOIN):
        delay = meta[DELAY_AT + me * half_count + part * JOIN + item]
        down, across = delay // LANES, delay % LANES
        downs.append(down)
        acrosses.append(across)
        back = lax.rem(LANES - across, LANES)
        for tap in range(TAPS):
            here = coef[tap, pl.ds(down, ROWS), :]
            after = coef[tap, pl.ds(down + 1, ROWS), :]
            turned = pltpu.roll(jnp.where(lane >= across, here, after), back, 1)
            weights[item, tap] = turned

    def filt(item, low, end, band, c):
        size = end - low
        values = []
        for u in range(size + TAPS - 1):
            at = (low + u + frames - TAPS) * ROWS + band * 16
            values.append(raw[item, c, at : at + 16, :].astype(jnp.float32))
        sums = [None] * size
        for tap in range(TAPS):
            weight = weights[item, tap, band * 16 : band * 16 + 16, :]
            for u in range(size):
                term = weight * values[u + TAPS - 1 - tap]
                sums[u] = term if sums[u] is None else sums[u] + term
        for u in range(size):
            at = (low + u) * ROWS + band * 16
            filtered[item][c, at : at + 16, :] = sums[u]

    def place(item, u):
        down, across = downs[item], acrosses[item]
        twice = lax.rem(across + RADIX, LANES)
        inside = lane < LANES - across
        for band in range(ROWS // 16):
            at = (u + 1) * ROWS + band * 16 - down
            moved, turned = [], []
            for c in range(2):
                here = filtered[item][c, pl.ds(at, 16), :]
                above = filtered[item][c, pl.ds(at - 1, 16), :]
                value = jnp.where(inside, here, above)
                moved.append(pltpu.roll(value, across, 1))
                turned.append(pltpu.roll(value, twice, 1))
            parts = (
                jnp.where(high, moved[0], turned[1]),
                jnp.where(high, turned[0], moved[1]),
                jnp.where(high, moved[1], -turned[0]),
                jnp.where(high, turned[1], -moved[0]),
            )
            for which, value in enumerate(parts):
                low = which * ROWS + band * 16
                grouped[item, u, low : low + 16, :] = value.astype(jnp.bfloat16)

    rows_out = jnp.concatenate(
        [last[me ^ dg, ct + dc] for dg in range(PAIR) for dc in range(per_ct)], axis=0
    )

    def turn(item, base):
        wide = jnp.concatenate([grouped[item, base + u] for u in range(SOME)], axis=1)
        inner = jnp.dot(first[...], wide, preferred_element_type=jnp.float32)
        rows = []
        for u in range(SOME):
            cut = slice(u * LANES, (u + 1) * LANES)
            value = inner[:RADIX, cut] * tw_cos[...] + inner[RADIX:, cut] * tw_sin[...]
            rows.append(value.astype(jnp.bfloat16))
        inner = jnp.concatenate(rows, axis=0)
        result = lax.dot_general(
            rows_out, inner, (((1,), (1,)), ((), ())), preferred_element_type=jnp.float32
        ).astype(jnp.bfloat16)
        size = result.shape[0] // (2 * dests)
        for dest in range(dests):
            for c in range(2):
                low = (dest * 2 + c) * size
                for u in range(SOME // 2):
                    outs[dest][item, base // 2 + u, c] = result[
                        low : low + size, u * LANES : (u + 1) * LANES
                    ]

    pieces = [
        (low, end, band, c)
        for low, end in ((0, frames // 2 + 1), (frames // 2 + 1, frames + 1))
        for band in range(ROWS // 16)
        for c in range(2)
    ]
    groups = frames // SOME
    each = len(pieces) // groups
    for item in range(JOIN + 1):
        for n in range(groups):
            if item < JOIN:
                for piece in pieces[n * each : (n + 1) * each]:
                    filt(item, *piece)
            if item:
                for u in range(SOME):
                    place(item - 1, n * SOME + u)
                turn(item - 1, n * SOME)


def filterbank(part, half, meta, sources, tables, beside, dests):
    late = not beside
    frames = sources[0].shape[2] // ROWS
    size = tables[-1].shape[2] // 2
    per_ct = tables[-1].shape[1] // 2
    pairs = frames // 2 if late else frames
    shape = (JOIN, pairs, 2, size, LANES)
    kernel = functools.partial(filterbank_kernel, late, part, frames, dests, per_ct, half)
    return pl.pallas_call(
        kernel,
        out_shape=[jax.ShapeDtypeStruct(shape, jnp.bfloat16)] * dests,
        in_specs=[SMEM] + [VMEM] * (len(sources) + 5 + len(beside)),
        out_specs=[VMEM] * dests,
        scratch_shapes=[
            pltpu.VMEM((JOIN, 2, 2 * frames * ROWS, LANES), jnp.bfloat16),
            pltpu.VMEM((JOIN, TAPS, ROWS, LANES), jnp.float32),
            pltpu.VMEM((JOIN, frames, LANES, LANES), jnp.bfloat16),
        ]
        + [pltpu.VMEM((2, (frames + 1) * ROWS, LANES), jnp.float32)] * JOIN,
        compiler_params=params(14),
        cost_estimate=cost(10**6, 2**18),
        name="filterbank_late" if late else "filterbank_early",
    )(meta, *sources, *tables, *beside)


SQUARE = [(p, q) for p in range(TILE) for q in range(TILE)]
CORNER = [(p, q) for p in range(TILE) for q in range(p, TILE)]


def pair_sets(own, parts):
    tiles = own // TILE
    per = tiles // parts
    whole = [(True, i, j, SQUARE) for i in range(tiles) for j in range(i + 1, tiles)]
    corner = [(True, i, i, CORNER) for i in range(tiles)]
    across = [(False, i, j, SQUARE) for i in range(0, tiles, 2) for j in range(tiles)]

    def early(block):
        return block[1] < per and block[2] < per

    def late(blocks):
        return [block for block in blocks if not early(block)]

    first = [block for block in whole + across + corner if early(block)]
    return [first, late(whole + corner), late(across)]


def pairs_in(blocks):
    return sum(len(block[3]) for block in blocks)


def chosen(t, values):
    result = jnp.int32(values[0])
    for n, value in enumerate(values[1:], 1):
        result = jnp.where(t == n, jnp.int32(value), result)
    return result


def correlate_kernel(layout, *refs):
    sources_at, blocks, own, terms, outer, span, per_ct = layout
    meta, sources = refs[0], refs[1 : 1 + len(sources_at)]
    rest = refs[1 + len(sources_at) :]
    earlier, outs, (spectra, sums, held) = rest[:terms], rest[terms:-3], rest[-3:]
    steps = spectra.shape[1]
    some = 8
    core, g, ct = meta[CORE_AT], meta[G_AT], meta[CT_AT]
    within = any(block[0] for block in blocks)
    across = any(not block[0] for block in blocks)

    for source, (far, dg, dc, part) in zip(sources, sources_at):
        device = lax.rem(ct - dc + per_ct, per_ct) * PAIR + (g ^ dg)
        base = (part * per_ct * PAIR + device) * JOIN
        wanted = None
        if across:
            side = 1 - core if far else core
            wanted = (side == 1) | (lax.rem(base // TILE, 2) == core)
            if within and not far:
                wanted = None
            base = base + side * own

        def bring(source=source, base=base):
            for item in range(source.shape[0]):

                def spread(n, carry, item=item):
                    for u in range(some):
                        real = source[item, n * some + u, 0].astype(jnp.float32)
                        imag = source[item, n * some + u, 1].astype(jnp.float32)
                        for which, value in enumerate((real, imag, real + imag, imag - real)):
                            spectra[base + item, n * some + u, which] = value
                    return carry

                lax.fori_loop(0, steps // some, spread, 0)

        if wanted is None:
            bring()
        else:
            pl.when(wanted)(bring)

    high = lax.broadcasted_iota(jnp.int32, (1, LANES), 1) < RADIX
    rows_outer = pairs_in(blocks) * span
    size = outer * span
    unroll = 4

    def block(left, right, pairs, first_row):
        def over(one, two, acc, sign):
            def frame(n, acc):
                acc = list(acc)
                for u in range(unroll):
                    a = [spectra[left + p, n * unroll + u, one] for p in range(TILE)]
                    b = [spectra[right + q, n * unroll + u, two] for q in range(TILE)]
                    for at, (p, q) in enumerate(pairs):
                        term = a[p] * b[q]
                        acc[at] = acc[at] + term if sign > 0 else acc[at] - term
                return tuple(acc)

            return lax.fori_loop(0, steps // unroll, frame, tuple(acc))

        count = len(pairs)
        first = over(2, 0, [jnp.zeros((size, LANES), jnp.float32)] * count, 1)
        for at in range(count):
            held[0, at] = first[at]
        real = over(1, 3, first, 1)
        for at in range(count):
            held[1, at] = real[at] + pltpu.roll(real[at], RADIX, 1)
        imag = over(0, 2, [held[0, at] for at in range(count)], -1)
        for at in range(count):
            folded = imag[at] + pltpu.roll(imag[at], RADIX, 1)
            both = jnp.where(high, held[1, at], folded)
            for o in range(outer):
                row = o * rows_outer + first_row + at * span
                sums[pl.ds(pl.multiple_of(row, span), span), :] = both[o * span : (o + 1) * span]

    done = 0
    while done < len(blocks):
        kind = (blocks[done][0], blocks[done][3])
        end = done
        while end < len(blocks) and (blocks[end][0], blocks[end][3]) == kind:
            end += 1
        run, row = blocks[done:end], pairs_in(blocks[:done]) * span

        def step(t, carry, run=run, row=row, kind=kind):
            left, right = chosen(t, [b[1] for b in run]), chosen(t, [b[2] for b in run])
            if not kind[0]:
                left, right = TILE * (left + core), own + TILE * right
            elif across:
                left, right = core * own + TILE * left, core * own + TILE * right
            else:
                left, right = TILE * left, TILE * right
            block(left, right, kind[1], row + t * len(kind[1]) * span)
            return carry

        lax.fori_loop(0, len(run), step, 0)
        done = end

    for r in range(outer):
        base = pl.multiple_of(lax.rem(meta[O_AT] + r, outer) * rows_outer, 16)
        outs[r][...] = sums[pl.ds(base, rows_outer), :].astype(outs[r].dtype)
    if terms:
        total = earlier[0][...].astype(jnp.float32)
        for term in earlier[1:]:
            total = total + term[...].astype(jnp.float32)
        outs[outer][...] = total


def correlate(meta, arrays, sources_at, blocks, own, sizes, name, earlier=()):
    outer, span, _ = sizes
    _, steps, _, size, _ = arrays[0].shape
    inputs = own if all(block[0] for block in blocks) else 2 * own
    rows = pairs_in(blocks) * span
    shapes = []
    for r in range(outer):
        dtype = jnp.float32 if r == 0 else jnp.bfloat16
        shapes.append(jax.ShapeDtypeStruct((rows, LANES), dtype))
    shapes += [jax.ShapeDtypeStruct(x.shape, jnp.float32) for x in earlier[:1]]
    layout = (sources_at, blocks, own, len(earlier)) + sizes
    return pl.pallas_call(
        functools.partial(correlate_kernel, layout),
        out_shape=shapes,
        in_specs=[SMEM] + [VMEM] * (len(arrays) + len(earlier)),
        out_specs=[VMEM] * len(shapes),
        scratch_shapes=[
            pltpu.VMEM((inputs, steps, 4, size, LANES), jnp.float32),
            pltpu.VMEM((outer * rows, LANES), jnp.float32),
            pltpu.VMEM((2, TILE * TILE, outer * span, LANES), jnp.float32),
        ],
        compiler_params=params(8 + inputs * steps * 4 * size * LANES * 4 // 2**20),
        cost_estimate=cost(10**6, 2**18),
        name=name,
    )(meta, *arrays, *earlier)


def assemble_kernel(own, outer, span, scale, sets, order, counts, *refs):
    meta = refs[0]
    out, joined = refs[-2:]
    sources, at = [], 1
    for count in counts:
        sources.append(refs[at : at + count])
        at += count
    near, far = sources[: len(sets)], sources[len(sets) :]
    lane = lax.broadcasted_iota(jnp.int32, (1, LANES), 1)
    high = lane < RADIX
    mirror = jnp.where(high, 1.0, -1.0).astype(jnp.float32)
    me = meta[CORE_AT]

    def added(parts, low, rows):
        total = parts[0][low : low + rows, :].astype(jnp.float32)
        for part in parts[1:]:
            total = total + part[low : low + rows, :].astype(jnp.float32)
        return total * scale

    def put(value, row, col):
        at = pl.multiple_of((row * 2 * own + col) * span, span)
        joined[pl.ds(at, span), :] = value

    sign = jnp.where(me == 0, jnp.ones_like(mirror), mirror)
    for blocks, mine, others in zip(sets, near, far):
        low = 0
        for within, i, j, pairs in blocks:
            rows = len(pairs) * span
            if within:
                total = added(mine, low, rows)
                turned = total * mirror
                for n, (p, q) in enumerate(pairs):
                    cut = slice(n * span, (n + 1) * span)
                    a, b = order[i * TILE + p], order[j * TILE + q]
                    put(total[cut], a, me * own + b)
                    if a != b:
                        put(turned[cut], b, me * own + a)
            else:
                for parts, side in ((mine, me), (others, 1 - me)):
                    total = added(parts, low, rows) * sign
                    for n, (p, q) in enumerate(pairs):
                        a = jnp.where(side == 0, order[i * TILE + p], order[(i + 1) * TILE + p])
                        b = order[j * TILE + q]
                        row = jnp.where(me == 0, a, b)
                        col = jnp.where(me == 0, own + b, a)
                        put(total[n * span : (n + 1) * span], row, col)
            low += rows

    def emit(a, carry):
        for tile in range(2 * own // 8):
            for pair in range(span // 2):
                loads = []
                for u in range(2):
                    at = (a * 2 * own + tile * 8) * span + pair * 2 + u
                    loads.append(joined[pl.ds(at, 8, stride=span), :])
                turned = [pltpu.roll(x, RADIX, 1) for x in loads]
                cut = slice(pair * LANES, (pair + 1) * LANES)
                out[0, a, tile * 8 : tile * 8 + 8, cut] = jnp.where(high, loads[0], turned[1])
                out[1, a, tile * 8 : tile * 8 + 8, cut] = jnp.where(high, turned[0], loads[1])
        return carry

    lax.fori_loop(0, own, emit, 0)


def assemble(meta, near, far, sets, order, own, span, scale):
    outer = len(near[1])
    counts = [len(arrays) for arrays in near + far]
    sources = [x for arrays in near + far for x in arrays]
    return pl.pallas_call(
        functools.partial(assemble_kernel, own, outer, span, scale, sets, order, counts),
        out_shape=jax.ShapeDtypeStruct((2, own, 2 * own, span * RADIX), jnp.float32),
        in_specs=[SMEM] + [VMEM] * len(sources),
        out_specs=VMEM,
        scratch_shapes=[pltpu.VMEM((own * 2 * own * span, LANES), jnp.float32)],
        compiler_params=params(10),
        cost_estimate=cost(10**6, 2**18),
        name="assemble",
    )(meta, *sources)


def fast_fits(in_count, frame_count):
    stn, tm, per_ct = (lax.axis_size(a) for a in ("stn", "tm", "ct"))
    groups = tm * per_ct
    if stn != 2 or tm % PAIR or in_count % (PAIR * JOIN) or RADIX % groups:
        return False
    outer, span = tm // PAIR, RADIX // groups
    own = in_count * per_ct
    return (
        frame_count >= TAPS
        and frame_count % (2 * SOME) == 0
        and span in (2, 4, 8)
        and outer * span % 16 == 0
        and own % (PAIR * JOIN * 2 * TILE // 4) == 0
        and in_count == PAIR * JOIN * 2
        and per_ct * PAIR * JOIN % (2 * TILE) == 0
        and all(pairs_in(s) * span % 16 == 0 for s in pair_sets(own, 2))
    )


def fast(voltages, delays):
    tm, per_ct = lax.axis_size("tm"), lax.axis_size("ct")
    in_count = voltages.shape[1]
    frame_count = voltages.shape[2] // CHANNELS
    outer = tm // PAIR
    span = RADIX // (tm * per_ct)
    own = in_count * per_ct
    half = in_count // PAIR
    place_tm, place_ct = lax.axis_index("tm"), lax.axis_index("ct")
    core = lax.axis_index("stn")
    g, o = place_tm % PAIR, place_tm // PAIR

    swap = [(i, i ^ 1) for i in range(tm)]
    onward = [(i, i + PAIR) for i in range(tm - PAIR)]
    cores = [(0, 1), (1, 0)]

    scalars = [None] * DELAY_AT
    scalars[G_AT], scalars[O_AT], scalars[CORE_AT], scalars[CT_AT] = g, o, core, place_ct
    meta = jnp.concatenate([jnp.stack(scalars).astype(jnp.int32), delays])

    dests = [(dg, dc) for dg in range(PAIR) for dc in range(per_ct)]
    base = last_table(outer, per_ct, span)
    tables = [np.concatenate([filter_table()] * 2, axis=1), first_table(), *twiddle_tables()]
    tables = [jnp.asarray(t) for t in tables + [np.concatenate([base, base], axis=1)]]

    parts = half // JOIN
    picked = pick(meta, voltages)
    sends, keeps = picked[:parts], picked[parts:]
    recvs = [lax.ppermute(block, "tm", swap) for block in sends]
    halos, lates = [], []
    for c in range(parts):
        recv = follow(recvs[c], lates[-1]) if lates else recvs[c]
        halos.append(lax.ppermute(jnp.where(g == 1, keeps[c], recv), "tm", onward))
        sources = [keeps[c], follow(recvs[c], halos[c - 1]) if c else recvs[c]]
        lates.append(filterbank(c, half, meta, sources, tables, [], len(dests)))

    sets = pair_sets(own, parts)
    sizes = (outer, span, per_ct)
    arrays, places = [], []
    done = []
    for c in range(parts):
        halo = follow(halos[c], recvs[c + 1]) if c + 1 < parts else halos[c]
        sources = [halo, keeps[c], recvs[c]]
        spectra = filterbank(c, half, meta, sources, tables, lates[c], len(dests))
        done.append(spectra[0])
        for (dg, dc), block in zip(dests, spectra):
            route = []
            for i in range(tm):
                for j in range(per_ct):
                    target = (i ^ dg) * per_ct + (j + dc) % per_ct
                    route.append((i * per_ct + j, target))
            if dg or dc:
                if len(arrays) >= len(dests):
                    block = follow(block, arrays[-len(dests)])
                block = lax.ppermute(block, ("tm", "ct"), route)
            arrays.append(block)
            places.append((dg, dc, c))

    near = [(False,) + place for place in places]
    far = [(True,) + place for place in places]
    count = len(dests)
    others = [lax.ppermute(follow(block, done[-1]), "stn", cores) for block in arrays[:count]]
    early = correlate(
        meta, arrays[:count] + others, near[:count] + far[:count], sets[0], own // parts, sizes,
        "correlate_early",
    )
    own_late = correlate(meta, arrays, near, sets[1], own, sizes, "correlate_own")

    def along(parts, after):
        moved = [parts[0]]
        for r in range(1, outer):
            route = [(i, (i + r * PAIR) % tm) for i in range(tm)]
            moved.append(lax.ppermute(follow(parts[r], after(r)), "tm", route))
        return moved

    early = along(early, lambda r: others)
    others += [lax.ppermute(follow(block, early), "stn", cores) for block in arrays[count:]]
    own_late = along(own_late, lambda r: others)
    *cross_late, early = correlate(
        meta, arrays + others, near + far, sets[2], own, sizes, "correlate_cross", early
    )
    cross_late = along(cross_late, lambda r: own_late[r])
    mine = [[early], own_late, cross_late]
    theirs = [[lax.ppermute(block, "stn", cores) for block in part] for part in (mine[0], mine[2])]
    theirs.insert(1, [])
    order = []
    for part in range(parts):
        for device in range(per_ct * PAIR):
            start = device // PAIR * in_count + device % PAIR * half + part * JOIN
            order += range(start, start + JOIN)
    scale = 1.0 / (tm * frame_count)
    result = assemble(meta, mine, theirs, sets, order, own, span, scale)
    return result.transpose(0, 3, 1, 2)


def general(voltages, delays):
    in_count = voltages.shape[1]
    frame_count = voltages.shape[2] // CHANNELS
    route = [(i, i + 1) for i in range(lax.axis_size("tm") - 1)]
    extended = jnp.concatenate([lax.ppermute(voltages, "tm", route), voltages], axis=2)
    span = (frame_count + TAPS - 1) * CHANNELS
    shifted = jax.vmap(
        lambda row, offset: lax.dynamic_slice_in_dim(row, CHANNELS - offset, span, 1),
        in_axes=(1, 0),
        out_axes=1,
    )(extended, delays)
    framed = shifted.reshape(2, in_count, frame_count + TAPS - 1, CHANNELS)
    table = jnp.asarray(filter_table()).reshape(TAPS, CHANNELS)
    total = jnp.zeros((2, in_count, frame_count, CHANNELS), jnp.float32)
    for tap in range(TAPS):
        low = TAPS - 1 - tap
        total = total + table[tap] * framed[:, :, low : low + frame_count].astype(jnp.float32)
    branches = jnp.moveaxis(total.astype(jnp.bfloat16), 0, 2)

    number = in_count * frame_count
    cosine, sine = dft_parts(RADIX)
    block = np.concatenate(
        [np.concatenate([cosine, sine], axis=1), np.concatenate([-sine, cosine], axis=1)], axis=0
    )
    block = jnp.asarray(block)
    stacked = branches.reshape(number, 2 * RADIX, RADIX)
    inner = jnp.einsum("kj,nja->nka", block, stacked, preferred_element_type=jnp.float32)
    inner = inner.reshape(number, 2, RADIX, RADIX)
    tw_cos, tw_sin = (jnp.asarray(t[:, :RADIX]) for t in twiddle_tables())
    real = inner[:, 0] * tw_cos + inner[:, 1] * tw_sin
    imag = inner[:, 1] * tw_cos - inner[:, 0] * tw_sin
    turned = jnp.stack([real, imag], axis=2).reshape(number, RADIX, 2 * RADIX)
    turned = turned.astype(jnp.bfloat16)
    result = jnp.einsum("lj,nkj->nlk", block, turned, preferred_element_type=jnp.float32)
    spectra = result.reshape(in_count, frame_count, 2, CHANNELS).astype(jnp.bfloat16)
    moved = lax.all_to_all(spectra, "tm", split_axis=3, concat_axis=1, tiled=True)
    moved = lax.all_to_all(moved, "ct", split_axis=3, concat_axis=0, tiled=True)
    local = moved.transpose(3, 2, 0, 1)
    swapped = jnp.stack([local[:, 1], -local[:, 0]], axis=1)
    summed = jnp.einsum(
        "ocjaf,cjbf->ocab",
        jnp.stack([local, swapped], axis=0),
        lax.all_gather(local, "stn", axis=2, tiled=True),
        preferred_element_type=jnp.float32,
    )
    return summed * (1.0 / local.shape[3])


def on_device(voltages, delays):
    if fast_fits(voltages.shape[1], voltages.shape[2] // CHANNELS):
        return fast(voltages, delays)
    return general(voltages, delays)


def solution(mesh):
    return jax.shard_map(
        on_device,
        mesh=mesh,
        in_specs=(P(None, ("stn", "ct"), "tm"), P(("stn", "ct"))),
        out_specs=P(None, ("tm", "ct"), "stn", None),
        check_vma=False,
    )
```

```python
import functools
import math

import jax
import jax.numpy as jnp
import numpy as np
from jax import lax
from jax.experimental import pallas as pl
from jax.experimental.pallas import tpu as pltpu
from jax.sharding import PartitionSpec as P

CHANNELS = 4096
RADIX = 64
TAPS = 16
LANES = 128
ROWS = CHANNELS // LANES
PAIR = 2
TILE = 4
JOIN = 2

VMEM = pl.BlockSpec(memory_space=pltpu.VMEM)
SMEM = pl.BlockSpec(memory_space=pltpu.SMEM)


def params(mib):
    return pltpu.CompilerParams(vmem_limit_bytes=mib * 2**20)


def position():
    place = lax.axis_index("tm")
    return lax.axis_index("stn"), place // PAIR, place % PAIR, lax.axis_index("ct")


def cost(flops, size):
    return pl.CostEstimate(flops=flops, bytes_accessed=size, transcendentals=0)


def filter_table():
    length = TAPS * CHANNELS
    index = np.arange(length, dtype=np.float64)
    centred = (index - length / 2) / CHANNELS
    window = 0.5 - 0.5 * np.cos(2.0 * math.pi * index / length)
    factor = 1.0 / (48.0 * math.sqrt(CHANNELS))
    table = np.sinc(centred) * window * factor
    return table.reshape(TAPS, ROWS, LANES).astype(np.float32)


def dft_parts(radix):
    steps = np.arange(radix)
    angle = 2.0 * math.pi * (steps[:, None] * steps[None, :] % radix) / radix
    return np.cos(angle).astype(jnp.bfloat16), np.sin(angle).astype(jnp.bfloat16)


def first_table():
    cosine, sine = dft_parts(CHANNELS // RADIX)
    order = [2 * row + half for half in range(2) for row in range(ROWS)]
    cosine, sine = cosine[:, order], sine[:, order]
    upper = np.concatenate([cosine, sine], axis=1)
    lower = np.concatenate([-sine, cosine], axis=1)
    return np.concatenate([upper, lower], axis=0)


def last_table(outer, per_ct, span):
    cosine, sine = dft_parts(RADIX)
    blocks = []
    for g in range(PAIR):
        for ct in range(per_ct):
            steps = [
                ((o * PAIR + g) * per_ct + ct) * span + j for o in range(outer) for j in range(span)
            ]
            real = np.concatenate([cosine[steps], sine[steps]], axis=1)
            imag = np.concatenate([-sine[steps], cosine[steps]], axis=1)
            blocks.append(np.concatenate([real, imag], axis=0))
    return np.stack(blocks).reshape(PAIR, per_ct, -1, 2 * RADIX)


def twiddle_tables():
    rows = np.arange(CHANNELS // RADIX)
    cols = np.arange(RADIX)
    angle = 2.0 * math.pi * (rows[:, None] * cols[None, :] % CHANNELS) / CHANNELS
    cosine = np.cos(angle).astype(np.float32)
    sine = np.sin(angle).astype(np.float32)
    return np.concatenate([cosine, cosine], axis=1), np.concatenate([sine, sine], axis=1)


def pick_kernel(half, block, *refs):
    outs, rows = refs[:-1], refs[-1]
    inputs, samples = block.shape[1], block.shape[2]
    tall = samples // LANES
    step = 16
    for part in range(2):
        for n in range(tall // step):
            cut = slice(n * step * LANES, (n + 1) * step * LANES)
            wide = block[part, :, cut].astype(jnp.float32)
            for u in range(step):
                at = (n * step + u) * inputs
                rows[part, at : at + inputs, :] = wide[:, u * LANES : (u + 1) * LANES]
    g = position()[2]
    for item in range(inputs):
        first = (1 - g) * half + item if item < half else g * half + item - half
        for part in range(2):
            value = rows[part, pl.ds(first, tall, stride=inputs), :]
            outs[item // JOIN][item % JOIN, part] = value.astype(jnp.bfloat16)


def pick(block):
    _, inputs, samples = block.shape
    half = inputs // PAIR
    steps = 8
    tall = samples // LANES // steps
    shape = jax.ShapeDtypeStruct((JOIN, 2, samples // LANES, LANES), jnp.bfloat16)
    return pl.pallas_call(
        functools.partial(pick_kernel, half),
        grid=(steps,),
        out_shape=[shape] * (inputs // JOIN),
        in_specs=[pl.BlockSpec((2, inputs, samples // steps), lambda t: (0, 0, t))],
        out_specs=[pl.BlockSpec((JOIN, 2, tall, LANES), lambda t: (0, 0, t, 0))] * (inputs // JOIN),
        scratch_shapes=[pltpu.VMEM((2, tall * inputs, LANES), jnp.float32)],
        compiler_params=params(56),
        cost_estimate=cost(10**6, 2**18),
        name="pick",
    )(block)


def follow(block, after):
    return lax.optimization_barrier((block, after))[0]


def joined(blocks):
    def kernel(*refs):
        sources, out = refs[:-1], refs[-1]
        for n, source in enumerate(sources):
            size = source.shape[0]
            for item in range(size):

                def step(m, carry, n=n, source=source, size=size, item=item):
                    cut = pl.ds(m * 4, 4)
                    out[n * size + item, cut] = source[item, cut]
                    return carry

                lax.fori_loop(0, source.shape[1] // 4, step, 0)

    shape = (sum(block.shape[0] for block in blocks),) + blocks[0].shape[1:]
    return pl.pallas_call(
        kernel,
        out_shape=jax.ShapeDtypeStruct(shape, blocks[0].dtype),
        in_specs=[VMEM] * len(blocks),
        out_specs=VMEM,
        compiler_params=params(8),
        cost_estimate=cost(10**6, 2**18),
        name="join",
    )(*blocks)


SOME = 4


def filterbank_kernel(late, part, frames, dests, per_ct, half_count, *refs):
    delays, refs = refs[0], refs[1:]
    _, _, me, ct = position()
    if late:
        keep, recv = refs[:2]
        refs = refs[2:]
    else:
        halo, keep, recv = refs[:3]
        refs = refs[3:]
    coef, first, tw_cos, tw_sin, last = refs[:5]
    beside = () if late else refs[5 : 5 + dests]
    outs = refs[5 + len(beside) :][:dests]
    raw, weights, grouped = refs[5 + len(beside) + dests :][:3]
    filtered = refs[5 + len(beside) + dests + 3 :]
    block_rows = frames * ROWS
    lane = lax.broadcasted_iota(jnp.int32, (1, LANES), 1)
    high = lane < RADIX

    def bring(source, place):
        tall = 128

        def step(n, carry):
            low = pl.multiple_of(n * tall, tall)
            at = pl.multiple_of(place * block_rows + n * tall, tall)
            for item in range(JOIN):
                for c in range(2):
                    raw[item, c, pl.ds(at, tall), :] = source[item, c, pl.ds(low, tall), :]
            return carry

        lax.fori_loop(0, block_rows // tall, step, 0)

    if late:
        bring(keep, me)
        bring(recv, 1 - me)
    else:
        bring(halo, 0)
        pl.when(me == 0)(lambda: bring(keep, 1))
        pl.when(me != 0)(lambda: bring(recv, 1))
        for dest, block in zip(outs, beside):
            dest[:, frames // 2 :] = block[...]

    downs, acrosses = [], []
    for item in range(JOIN):
        delay = delays[me * half_count + part * JOIN + item]
        down, across = delay // LANES, delay % LANES
        downs.append(down)
        acrosses.append(across)
        back = lax.rem(LANES - across, LANES)
        for tap in range(TAPS):
            here = coef[tap, pl.ds(down, ROWS), :]
            after = coef[tap, pl.ds(down + 1, ROWS), :]
            turned = pltpu.roll(jnp.where(lane >= across, here, after), back, 1)
            weights[item, tap] = turned

    def filt(item, low, end, band, c):
        size = end - low
        values = []
        for u in range(size + TAPS - 1):
            at = (low + u + frames - TAPS) * ROWS + band * 16
            values.append(raw[item, c, at : at + 16, :].astype(jnp.float32))
        sums = [None] * size
        for tap in range(TAPS):
            weight = weights[item, tap, band * 16 : band * 16 + 16, :]
            for u in range(size):
                term = weight * values[u + TAPS - 1 - tap]
                sums[u] = term if sums[u] is None else sums[u] + term
        for u in range(size):
            at = (low + u) * ROWS + band * 16
            filtered[item][c, at : at + 16, :] = sums[u]

    def place(item, u):
        down, across = downs[item], acrosses[item]
        twice = lax.rem(across + RADIX, LANES)
        inside = lane < LANES - across
        for band in range(ROWS // 16):
            at = (u + 1) * ROWS + band * 16 - down
            moved, turned = [], []
            for c in range(2):
                here = filtered[item][c, pl.ds(at, 16), :]
                above = filtered[item][c, pl.ds(at - 1, 16), :]
                value = jnp.where(inside, here, above)
                moved.append(pltpu.roll(value, across, 1))
                turned.append(pltpu.roll(value, twice, 1))
            parts = (
                jnp.where(high, moved[0], turned[1]),
                jnp.where(high, turned[0], moved[1]),
                jnp.where(high, moved[1], -turned[0]),
                jnp.where(high, turned[1], -moved[0]),
            )
            for which, value in enumerate(parts):
                low = which * ROWS + band * 16
                grouped[item, u, low : low + 16, :] = value.astype(jnp.bfloat16)

    rows_out = jnp.concatenate(
        [last[me ^ dg, ct + dc] for dg in range(PAIR) for dc in range(per_ct)], axis=0
    )

    def turn(item, base):
        wide = jnp.concatenate([grouped[item, base + u] for u in range(SOME)], axis=1)
        inner = jnp.dot(first[...], wide, preferred_element_type=jnp.float32)
        rows = []
        for u in range(SOME):
            cut = slice(u * LANES, (u + 1) * LANES)
            value = inner[:RADIX, cut] * tw_cos[...] + inner[RADIX:, cut] * tw_sin[...]
            rows.append(value.astype(jnp.bfloat16))
        inner = jnp.concatenate(rows, axis=0)
        result = lax.dot_general(
            rows_out, inner, (((1,), (1,)), ((), ())), preferred_element_type=jnp.float32
        ).astype(jnp.bfloat16)
        size = result.shape[0] // (2 * dests)
        for dest in range(dests):
            for c in range(2):
                low = (dest * 2 + c) * size
                for u in range(SOME // 2):
                    outs[dest][item, base // 2 + u, c] = result[
                        low : low + size, u * LANES : (u + 1) * LANES
                    ]

    pieces = [
        (low, end, band, c)
        for low, end in ((0, frames // 2 + 1), (frames // 2 + 1, frames + 1))
        for band in range(ROWS // 16)
        for c in range(2)
    ]
    groups = frames // SOME
    each = len(pieces) // groups
    for item in range(JOIN + 1):
        for n in range(groups):
            if item < JOIN:
                for piece in pieces[n * each : (n + 1) * each]:
                    filt(item, *piece)
            if item:
                for u in range(SOME):
                    place(item - 1, n * SOME + u)
                turn(item - 1, n * SOME)


def filterbank(part, half, delays, sources, tables, beside, dests):
    late = not beside
    frames = sources[0].shape[2] // ROWS
    size = tables[-1].shape[2] // 2
    per_ct = tables[-1].shape[1] // 2
    pairs = frames // 2 if late else frames
    shape = (JOIN, pairs, 2, size, LANES)
    kernel = functools.partial(filterbank_kernel, late, part, frames, dests, per_ct, half)
    return pl.pallas_call(
        kernel,
        out_shape=[jax.ShapeDtypeStruct(shape, jnp.bfloat16)] * dests,
        in_specs=[SMEM] + [VMEM] * (len(sources) + 5 + len(beside)),
        out_specs=[VMEM] * dests,
        scratch_shapes=[
            pltpu.VMEM((JOIN, 2, 2 * frames * ROWS, LANES), jnp.bfloat16),
            pltpu.VMEM((JOIN, TAPS, ROWS, LANES), jnp.float32),
            pltpu.VMEM((JOIN, frames, LANES, LANES), jnp.bfloat16),
        ]
        + [pltpu.VMEM((2, (frames + 1) * ROWS, LANES), jnp.float32)] * JOIN,
        compiler_params=params(14),
        cost_estimate=cost(10**6, 2**18),
        name="filterbank_late" if late else "filterbank_early",
    )(delays, *sources, *tables, *beside)


SQUARE = [(p, q) for p in range(TILE) for q in range(TILE)]
CORNER = [(p, q) for p in range(TILE) for q in range(p, TILE)]


def pair_sets(own, parts):
    tiles = own // TILE
    per = tiles // parts
    whole = [(True, i, j, SQUARE) for i in range(tiles) for j in range(i + 1, tiles)]
    corner = [(True, i, i, CORNER) for i in range(tiles)]
    across = [(False, i, j, SQUARE) for i in range(0, tiles, 2) for j in range(tiles)]

    def early(block):
        return block[1] < per and block[2] < per

    def late(blocks):
        return [block for block in blocks if not early(block)]

    first = [block for block in whole + across + corner if early(block)]
    return [first, late(whole + corner), late(across)]


def pairs_in(blocks):
    return sum(len(block[3]) for block in blocks)


def chosen(t, values):
    result = jnp.int32(values[0])
    for n, value in enumerate(values[1:], 1):
        result = jnp.where(t == n, jnp.int32(value), result)
    return result


def correlate_kernel(layout, *refs):
    sources_at, blocks, own, terms, outer, span, per_ct = layout
    sources, rest = refs[: len(sources_at)], refs[len(sources_at) :]
    earlier, outs, (spectra, sums, held) = rest[:terms], rest[terms:-3], rest[-3:]
    steps = spectra.shape[1]
    some = 8
    core, o, g, ct = position()
    within = any(block[0] for block in blocks)
    across = any(not block[0] for block in blocks)

    for source, (far, part) in zip(sources, sources_at):
        for n in range(PAIR * per_ct):
            dg, dc = n // per_ct, n % per_ct
            device = lax.rem(ct - dc + per_ct, per_ct) * PAIR + (g ^ dg)
            base = (part * per_ct * PAIR + device) * JOIN
            wanted = None
            if across:
                side = 1 - core if far else core
                wanted = (side == 1) | (lax.rem(base // TILE, 2) == core)
                if within and not far:
                    wanted = None
                base = base + side * own

            def bring(source=source, base=base, n=n):
                for item in range(JOIN):

                    def spread(m, carry, item=item):
                        for u in range(some):
                            real = source[n * JOIN + item, m * some + u, 0].astype(jnp.float32)
                            imag = source[n * JOIN + item, m * some + u, 1].astype(jnp.float32)
                            for which, value in enumerate((real, imag, real + imag, imag - real)):
                                spectra[base + item, m * some + u, which] = value
                        return carry

                    lax.fori_loop(0, steps // some, spread, 0)

            if wanted is None:
                bring()
            else:
                pl.when(wanted)(bring)

    high = lax.broadcasted_iota(jnp.int32, (1, LANES), 1) < RADIX
    rows_outer = pairs_in(blocks) * span
    size = outer * span
    unroll = 4

    def block(left, right, pairs, first_row):
        def over(one, two, acc, sign):
            def frame(n, acc):
                acc = list(acc)
                for u in range(unroll):
                    a = [spectra[left + p, n * unroll + u, one] for p in range(TILE)]
                    b = [spectra[right + q, n * unroll + u, two] for q in range(TILE)]
                    for at, (p, q) in enumerate(pairs):
                        term = a[p] * b[q]
                        acc[at] = acc[at] + term if sign > 0 else acc[at] - term
                return tuple(acc)

            return lax.fori_loop(0, steps // unroll, frame, tuple(acc))

        count = len(pairs)
        first = over(2, 0, [jnp.zeros((size, LANES), jnp.float32)] * count, 1)
        for at in range(count):
            held[0, at] = first[at]
        real = over(1, 3, first, 1)
        for at in range(count):
            held[1, at] = real[at] + pltpu.roll(real[at], RADIX, 1)
        imag = over(0, 2, [held[0, at] for at in range(count)], -1)
        for at in range(count):
            folded = imag[at] + pltpu.roll(imag[at], RADIX, 1)
            both = jnp.where(high, held[1, at], folded)
            for o in range(outer):
                row = o * rows_outer + first_row + at * span
                sums[pl.ds(pl.multiple_of(row, span), span), :] = both[o * span : (o + 1) * span]

    done = 0
    while done < len(blocks):
        kind = (blocks[done][0], blocks[done][3])
        end = done
        while end < len(blocks) and (blocks[end][0], blocks[end][3]) == kind:
            end += 1
        run, row = blocks[done:end], pairs_in(blocks[:done]) * span

        def step(t, carry, run=run, row=row, kind=kind):
            left, right = chosen(t, [b[1] for b in run]), chosen(t, [b[2] for b in run])
            if not kind[0]:
                left, right = TILE * (left + core), own + TILE * right
            elif across:
                left, right = core * own + TILE * left, core * own + TILE * right
            else:
                left, right = TILE * left, TILE * right
            block(left, right, kind[1], row + t * len(kind[1]) * span)
            return carry

        lax.fori_loop(0, len(run), step, 0)
        done = end

    for r in range(outer):
        base = pl.multiple_of(lax.rem(o + r, outer) * rows_outer, 16)
        outs[r][...] = sums[pl.ds(base, rows_outer), :].astype(outs[r].dtype)
    if terms:
        total = earlier[0][...].astype(jnp.float32)
        for term in earlier[1:]:
            total = total + term[...].astype(jnp.float32)
        outs[outer][...] = total


def correlate(arrays, sources_at, blocks, own, sizes, name, earlier=()):
    outer, span, _ = sizes
    _, steps, _, size, _ = arrays[0].shape
    inputs = own if all(block[0] for block in blocks) else 2 * own
    rows = pairs_in(blocks) * span
    shapes = []
    for r in range(outer):
        dtype = jnp.float32 if r == 0 else jnp.bfloat16
        shapes.append(jax.ShapeDtypeStruct((rows, LANES), dtype))
    shapes += [jax.ShapeDtypeStruct(x.shape, jnp.float32) for x in earlier[:1]]
    layout = (sources_at, blocks, own, len(earlier)) + sizes
    return pl.pallas_call(
        functools.partial(correlate_kernel, layout),
        out_shape=shapes,
        in_specs=[VMEM] * (len(arrays) + len(earlier)),
        out_specs=[VMEM] * len(shapes),
        scratch_shapes=[
            pltpu.VMEM((inputs, steps, 4, size, LANES), jnp.float32),
            pltpu.VMEM((outer * rows, LANES), jnp.float32),
            pltpu.VMEM((2, TILE * TILE, outer * span, LANES), jnp.float32),
        ],
        compiler_params=params(8 + inputs * steps * 4 * size * LANES * 4 // 2**20),
        cost_estimate=cost(10**6, 2**18),
        name=name,
    )(*arrays, *earlier)


def assemble_kernel(own, outer, span, scale, sets, order, counts, *refs):
    out, joined = refs[-2:]
    sources, at = [], 0
    for count in counts:
        sources.append(refs[at : at + count])
        at += count
    near, far = sources[: len(sets)], sources[len(sets) :]
    lane = lax.broadcasted_iota(jnp.int32, (1, LANES), 1)
    high = lane < RADIX
    mirror = jnp.where(high, 1.0, -1.0).astype(jnp.float32)
    me = position()[0]
    across = 2 * own * span
    mine_at = pl.multiple_of(me * own * span, 8)

    def added(parts, low, rows):
        total = parts[0][low : low + rows, :].astype(jnp.float32)
        for part in parts[1:]:
            total = total + part[low : low + rows, :].astype(jnp.float32)
        return total * scale

    def put(value, places, base=0):
        n = 0
        while n < len(places):
            wide = 1
            if places[n] % 8 == 0 and places[n + 1 : n + 2] == [places[n] + span] and span < 8:
                wide = 2
            rows = value[n * span : (n + wide) * span]
            joined[pl.ds(base + places[n], wide * span), :] = rows
            n += wide

    def inner(total, i, j, pairs):
        direct = [order[i * TILE + p] * across + order[j * TILE + q] * span for p, q in pairs]
        turned = [order[j * TILE + q] * across + order[i * TILE + p] * span for p, q in pairs]
        put(total, direct, mine_at)
        for n, (p, q) in enumerate(pairs):
            if (i, p) != (j, q):
                value = total[n * span : (n + 1) * span] * mirror
                put(value, [turned[n]], mine_at)

    def outer_pairs(core):
        for blocks, mine, others in zip(sets, near, far):
            low = 0
            for within, i, j, pairs in blocks:
                rows = len(pairs) * span
                if not within:
                    for parts, side in ((mine, core), (others, 1 - core)):
                        total = added(parts, low, rows)
                        a = [order[(i + side) * TILE + p] for p, _ in pairs]
                        b = [order[j * TILE + q] for _, q in pairs]
                        if core == 0:
                            put(total, [x * across + (own + y) * span for x, y in zip(a, b)])
                        else:
                            total = total * mirror
                            put(total, [y * across + x * span for x, y in zip(a, b)])
                low += rows

    for blocks, mine in zip(sets, near):
        low = 0
        for within, i, j, pairs in blocks:
            rows = len(pairs) * span
            if within:
                inner(added(mine, low, rows), i, j, pairs)
            low += rows
    pl.when(me == 0)(lambda: outer_pairs(0))
    pl.when(me != 0)(lambda: outer_pairs(1))

    def emit(a, carry):
        for tile in range(2 * own // 8):
            for pair in range(span // 2):
                loads = []
                for u in range(2):
                    at = (a * 2 * own + tile * 8) * span + pair * 2 + u
                    loads.append(joined[pl.ds(at, 8, stride=span), :])
                turned = [pltpu.roll(x, RADIX, 1) for x in loads]
                cut = slice(pair * LANES, (pair + 1) * LANES)
                out[0, a, tile * 8 : tile * 8 + 8, cut] = jnp.where(high, loads[0], turned[1])
                out[1, a, tile * 8 : tile * 8 + 8, cut] = jnp.where(high, turned[0], loads[1])
        return carry

    def emit_some(n, carry):
        for u in range(4):
            emit(n * 4 + u, carry)
        return carry

    lax.fori_loop(0, own // 4, emit_some, 0)


def assemble(near, far, sets, order, own, span, scale):
    outer = len(near[1])
    counts = [len(arrays) for arrays in near + far]
    sources = [x for arrays in near + far for x in arrays]
    return pl.pallas_call(
        functools.partial(assemble_kernel, own, outer, span, scale, sets, order, counts),
        out_shape=jax.ShapeDtypeStruct((2, own, 2 * own, span * RADIX), jnp.float32),
        in_specs=[VMEM] * len(sources),
        out_specs=VMEM,
        scratch_shapes=[pltpu.VMEM((own * 2 * own * span, LANES), jnp.float32)],
        compiler_params=params(10),
        cost_estimate=cost(10**6, 2**18),
        name="assemble",
    )(*sources)


def fast_fits(in_count, frame_count):
    stn, tm, per_ct = (lax.axis_size(a) for a in ("stn", "tm", "ct"))
    groups = tm * per_ct
    if stn != 2 or tm % PAIR or in_count % (PAIR * JOIN) or RADIX % groups:
        return False
    outer, span = tm // PAIR, RADIX // groups
    own = in_count * per_ct
    return (
        frame_count >= TAPS
        and frame_count % (2 * SOME) == 0
        and span in (2, 4, 8)
        and outer * span % 16 == 0
        and own % (PAIR * JOIN * 2 * TILE // 4) == 0
        and in_count == PAIR * JOIN * 2
        and per_ct * PAIR * JOIN % (2 * TILE) == 0
        and all(pairs_in(s) * span % 16 == 0 for s in pair_sets(own, 2))
    )


def fast(voltages, delays):
    tm, per_ct = lax.axis_size("tm"), lax.axis_size("ct")
    in_count = voltages.shape[1]
    frame_count = voltages.shape[2] // CHANNELS
    outer = tm // PAIR
    span = RADIX // (tm * per_ct)
    own = in_count * per_ct
    half = in_count // PAIR
    place_tm, place_ct = lax.axis_index("tm"), lax.axis_index("ct")
    g = place_tm % PAIR

    swap = [(i, i ^ 1) for i in range(tm)]
    onward = [(i, i + PAIR) for i in range(tm - PAIR)]
    cores = [(0, 1), (1, 0)]

    dests = [(dg, dc) for dg in range(PAIR) for dc in range(per_ct)]
    base = last_table(outer, per_ct, span)
    tables = [np.concatenate([filter_table()] * 2, axis=1), first_table(), *twiddle_tables()]
    tables = [jnp.asarray(t) for t in tables + [np.concatenate([base, base], axis=1)]]

    parts = half // JOIN
    picked = pick(voltages)
    sends, keeps = picked[:parts], picked[parts:]
    recvs = [lax.ppermute(block, "tm", swap) for block in sends]
    halos, lates = [], []
    for c in range(parts):
        recv = follow(recvs[c], lates[-1]) if lates else recvs[c]
        halos.append(lax.ppermute(jnp.where(g == 1, keeps[c], recv), "tm", onward))
        sources = [keeps[c], follow(recvs[c], halos[c - 1]) if c else recvs[c]]
        lates.append(filterbank(c, half, delays, sources, tables, [], len(dests)))

    sets = pair_sets(own, parts)
    sizes = (outer, span, per_ct)
    received = []
    for c in range(parts):
        halo = follow(halos[c], recvs[c + 1]) if c + 1 < parts else halos[c]
        sources = [halo, keeps[c], recvs[c]]
        spectra = filterbank(c, half, delays, sources, tables, lates[c], len(dests))
        arrays = []
        for n, ((dg, dc), block) in enumerate(zip(dests, spectra)):
            route = []
            for i in range(tm):
                for j in range(per_ct):
                    target = (i ^ dg) * per_ct + (j + dc) % per_ct
                    route.append((i * per_ct + j, target))
            if dg or dc:
                block = follow(block, received[-1][n]) if received else block
                block = lax.ppermute(block, ("tm", "ct"), route)
            arrays.append(block)
        received.append(arrays)

    def along(parts, after):
        moved = [parts[0]]
        for r in range(1, outer):
            route = [(i, (i + r * PAIR) % tm) for i in range(tm)]
            moved.append(lax.ppermute(follow(parts[r], after(r)), "tm", route))
        return moved

    near = [joined([follow(block, spectra[0]) for block in received[0]])]
    far = [lax.ppermute(near[0], "stn", cores)]
    early = correlate(
        near + far, [(False, 0), (True, 0)], sets[0], own // parts, sizes, "correlate_early"
    )
    early = along(early, lambda r: [])
    near.append(joined([follow(block, early[1:3]) for block in received[1]]))
    far.append(lax.ppermute(near[1], "stn", cores))
    sources_at = [(False, c) for c in range(parts)] + [(True, c) for c in range(parts)]
    own_late = correlate(near, sources_at[:parts], sets[1], own, sizes, "correlate_own")
    own_late = along(own_late, lambda r: [far[1], early[r]])
    *cross_late, early = correlate(
        near + far, sources_at, sets[2], own, sizes, "correlate_cross", early
    )
    cross_late = along(cross_late, lambda r: own_late[r])
    mine = [[early], own_late, cross_late]
    theirs = [[lax.ppermute(block, "stn", cores) for block in part] for part in (mine[0], mine[2])]
    theirs.insert(1, [])
    order = []
    for part in range(parts):
        for device in range(per_ct * PAIR):
            start = device // PAIR * in_count + device % PAIR * half + part * JOIN
            order += range(start, start + JOIN)
    scale = 1.0 / (tm * frame_count)
    result = assemble(mine, theirs, sets, order, own, span, scale)
    return result.transpose(0, 3, 1, 2)


def general(voltages, delays):
    in_count = voltages.shape[1]
    frame_count = voltages.shape[2] // CHANNELS
    route = [(i, i + 1) for i in range(lax.axis_size("tm") - 1)]
    extended = jnp.concatenate([lax.ppermute(voltages, "tm", route), voltages], axis=2)
    span = (frame_count + TAPS - 1) * CHANNELS
    shifted = jax.vmap(
        lambda row, offset: lax.dynamic_slice_in_dim(row, CHANNELS - offset, span, 1),
        in_axes=(1, 0),
        out_axes=1,
    )(extended, delays)
    framed = shifted.reshape(2, in_count, frame_count + TAPS - 1, CHANNELS)
    table = jnp.asarray(filter_table()).reshape(TAPS, CHANNELS)
    total = jnp.zeros((2, in_count, frame_count, CHANNELS), jnp.float32)
    for tap in range(TAPS):
        low = TAPS - 1 - tap
        total = total + table[tap] * framed[:, :, low : low + frame_count].astype(jnp.float32)
    branches = jnp.moveaxis(total.astype(jnp.bfloat16), 0, 2)

    number = in_count * frame_count
    cosine, sine = dft_parts(RADIX)
    block = np.concatenate(
        [np.concatenate([cosine, sine], axis=1), np.concatenate([-sine, cosine], axis=1)], axis=0
    )
    block = jnp.asarray(block)
    stacked = branches.reshape(number, 2 * RADIX, RADIX)
    inner = jnp.einsum("kj,nja->nka", block, stacked, preferred_element_type=jnp.float32)
    inner = inner.reshape(number, 2, RADIX, RADIX)
    tw_cos, tw_sin = (jnp.asarray(t[:, :RADIX]) for t in twiddle_tables())
    real = inner[:, 0] * tw_cos + inner[:, 1] * tw_sin
    imag = inner[:, 1] * tw_cos - inner[:, 0] * tw_sin
    turned = jnp.stack([real, imag], axis=2).reshape(number, RADIX, 2 * RADIX)
    turned = turned.astype(jnp.bfloat16)
    result = jnp.einsum("lj,nkj->nlk", block, turned, preferred_element_type=jnp.float32)
    spectra = result.reshape(in_count, frame_count, 2, CHANNELS).astype(jnp.bfloat16)
    moved = lax.all_to_all(spectra, "tm", split_axis=3, concat_axis=1, tiled=True)
    moved = lax.all_to_all(moved, "ct", split_axis=3, concat_axis=0, tiled=True)
    local = moved.transpose(3, 2, 0, 1)
    swapped = jnp.stack([local[:, 1], -local[:, 0]], axis=1)
    summed = jnp.einsum(
        "ocjaf,cjbf->ocab",
        jnp.stack([local, swapped], axis=0),
        lax.all_gather(local, "stn", axis=2, tiled=True),
        preferred_element_type=jnp.float32,
    )
    return summed * (1.0 / local.shape[3])


def on_device(voltages, delays):
    if fast_fits(voltages.shape[1], voltages.shape[2] // CHANNELS):
        return fast(voltages, delays)
    return general(voltages, delays)


def solution(mesh):
    return jax.shard_map(
        on_device,
        mesh=mesh,
        in_specs=(P(None, ("stn", "ct"), "tm"), P(("stn", "ct"))),
        out_specs=P(None, ("tm", "ct"), "stn", None),
        check_vma=False,
    )
```

```python
import functools
import math

import jax
import jax.numpy as jnp
import numpy as np
from jax import lax
from jax.experimental import pallas as pl
from jax.experimental.pallas import tpu as pltpu
from jax.sharding import PartitionSpec as P

CHANNELS = 4096
RADIX = 64
TAPS = 16
LANES = 128
ROWS = CHANNELS // LANES
PAIR = 2
TILE = 4
JOIN = 2

VMEM = pl.BlockSpec(memory_space=pltpu.VMEM)
SMEM = pl.BlockSpec(memory_space=pltpu.SMEM)


def params(mib):
    return pltpu.CompilerParams(vmem_limit_bytes=mib * 2**20)


def position():
    place = lax.axis_index("tm")
    return lax.axis_index("stn"), place // PAIR, place % PAIR, lax.axis_index("ct")


def cost(flops, size):
    return pl.CostEstimate(flops=flops, bytes_accessed=size, transcendentals=0)


def filter_table():
    length = TAPS * CHANNELS
    index = np.arange(length, dtype=np.float64)
    centred = (index - length / 2) / CHANNELS
    window = 0.5 - 0.5 * np.cos(2.0 * math.pi * index / length)
    factor = 1.0 / (48.0 * math.sqrt(CHANNELS))
    table = np.sinc(centred) * window * factor
    return table.reshape(TAPS, ROWS, LANES).astype(np.float32)


def dft_parts(radix):
    steps = np.arange(radix)
    angle = 2.0 * math.pi * (steps[:, None] * steps[None, :] % radix) / radix
    return np.cos(angle).astype(jnp.bfloat16), np.sin(angle).astype(jnp.bfloat16)


def first_table():
    cosine, sine = dft_parts(CHANNELS // RADIX)
    order = [2 * row + half for half in range(2) for row in range(ROWS)]
    cosine, sine = cosine[:, order], sine[:, order]
    upper = np.concatenate([cosine, sine], axis=1)
    lower = np.concatenate([-sine, cosine], axis=1)
    return np.concatenate([upper, lower], axis=0)


def last_table(outer, per_ct, span):
    cosine, sine = dft_parts(RADIX)
    blocks = []
    for g in range(PAIR):
        for ct in range(per_ct):
            steps = [
                ((o * PAIR + g) * per_ct + ct) * span + j for o in range(outer) for j in range(span)
            ]
            real = np.concatenate([cosine[steps], sine[steps]], axis=1)
            imag = np.concatenate([-sine[steps], cosine[steps]], axis=1)
            blocks.append(np.concatenate([real, imag], axis=0))
    return np.stack(blocks).reshape(PAIR, per_ct, -1, 2 * RADIX)


def twiddle_tables():
    rows = np.arange(CHANNELS // RADIX)
    cols = np.arange(RADIX)
    angle = 2.0 * math.pi * (rows[:, None] * cols[None, :] % CHANNELS) / CHANNELS
    cosine = np.cos(angle).astype(np.float32)
    sine = np.sin(angle).astype(np.float32)
    return np.concatenate([cosine, cosine], axis=1), np.concatenate([sine, sine], axis=1)


def pick_kernel(half, own, block, *refs):
    outs, rows = refs[:-1], refs[-1]
    inputs, samples = block.shape[1], block.shape[2]
    step = 32
    for part in range(2):

        def spread(n, carry, part=part):
            low = pl.multiple_of(n * step * LANES, step * LANES)
            wide = block[part, :, pl.ds(low, step * LANES)].astype(jnp.float32)
            for u in range(step):
                at = pl.multiple_of((n * step + u) * inputs, inputs)
                rows[part, pl.ds(at, inputs), :] = wide[:, u * LANES : (u + 1) * LANES]
            return carry

        lax.fori_loop(0, samples // LANES // step, spread, 0)
    g = position()[2]
    first = (g if own else 1 - g) * half
    tall = 64

    def gather(n, carry):
        low = pl.multiple_of(n * tall, tall)
        for item in range(half):
            for part in range(2):
                at = low * inputs + first + item
                value = rows[part, pl.ds(at, tall, stride=inputs), :].astype(jnp.bfloat16)
                outs[item // JOIN][item % JOIN, part, pl.ds(low, tall), :] = value
        return carry

    lax.fori_loop(0, samples // LANES // tall, gather, 0)


def pick(block, own):
    _, inputs, samples = block.shape
    half = inputs // PAIR
    shape = jax.ShapeDtypeStruct((JOIN, 2, samples // LANES, LANES), jnp.bfloat16)
    return pl.pallas_call(
        functools.partial(pick_kernel, half, own),
        out_shape=[shape] * (half // JOIN),
        in_specs=[VMEM],
        out_specs=[VMEM] * (half // JOIN),
        scratch_shapes=[pltpu.VMEM((2, samples // LANES * inputs, LANES), jnp.float32)],
        compiler_params=params(12),
        cost_estimate=cost(10**6, 2**18),
        name="pick",
    )(block)


def follow(block, after):
    return lax.optimization_barrier((block, after))[0]


def joined(blocks):
    def kernel(*refs):
        sources, out = refs[:-1], refs[-1]
        for n, source in enumerate(sources):
            size = source.shape[0]
            for item in range(size):

                def step(m, carry, n=n, source=source, size=size, item=item):
                    cut = pl.ds(m * 4, 4)
                    out[n * size + item, cut] = source[item, cut]
                    return carry

                lax.fori_loop(0, source.shape[1] // 4, step, 0)

    shape = (sum(block.shape[0] for block in blocks),) + blocks[0].shape[1:]
    return pl.pallas_call(
        kernel,
        out_shape=jax.ShapeDtypeStruct(shape, blocks[0].dtype),
        in_specs=[VMEM] * len(blocks),
        out_specs=VMEM,
        compiler_params=params(8),
        cost_estimate=cost(10**6, 2**18),
        name="join",
    )(*blocks)


SOME = 4


def filterbank_kernel(late, before, part, frames, dests, per_ct, half_count, *refs):
    delays, refs = refs[0], refs[1:]
    _, _, me, ct = position()
    if late:
        keep, recv = refs[:2]
        refs = refs[2:]
    else:
        halo, keep, recv = refs[:3]
        refs = refs[3:]
    coef, first, tw_cos, tw_sin, last = refs[:5]
    beside = refs[5 : 5 + dests] if before else ()
    outs = refs[5 + len(beside) :][:dests]
    raw, weights, grouped = refs[5 + len(beside) + dests :][:3]
    filtered = refs[5 + len(beside) + dests + 3 :]
    block_rows = frames * ROWS
    lane = lax.broadcasted_iota(jnp.int32, (1, LANES), 1)
    high = lane < RADIX

    def bring(source, place):
        tall = 128

        def step(n, carry):
            low = pl.multiple_of(n * tall, tall)
            at = pl.multiple_of(place * block_rows + n * tall, tall)
            for item in range(JOIN):
                for c in range(2):
                    raw[item, c, pl.ds(at, tall), :] = source[item, c, pl.ds(low, tall), :]
            return carry

        lax.fori_loop(0, block_rows // tall, step, 0)

    if late:
        bring(keep, me)
        bring(recv, 1 - me)
    else:
        bring(halo, 0)
        pl.when(me == 0)(lambda: bring(keep, 1))
        pl.when(me != 0)(lambda: bring(recv, 1))
    for dest, block in zip(outs, beside):
        dest[:before] = block[...]

    downs, acrosses = [], []
    for item in range(JOIN):
        delay = delays[me * half_count + part * JOIN + item]
        down, across = delay // LANES, delay % LANES
        downs.append(down)
        acrosses.append(across)
        back = lax.rem(LANES - across, LANES)
        for tap in range(TAPS):
            here = coef[tap, pl.ds(down, ROWS), :]
            after = coef[tap, pl.ds(down + 1, ROWS), :]
            turned = pltpu.roll(jnp.where(lane >= across, here, after), back, 1)
            weights[item, tap] = turned

    def filt(item, low, end, band, c):
        size = end - low
        values = []
        for u in range(size + TAPS - 1):
            at = (low + u + frames - TAPS) * ROWS + band * 16
            values.append(raw[item, c, at : at + 16, :].astype(jnp.float32))
        sums = [None] * size
        for tap in range(TAPS):
            weight = weights[item, tap, band * 16 : band * 16 + 16, :]
            for u in range(size):
                term = weight * values[u + TAPS - 1 - tap]
                sums[u] = term if sums[u] is None else sums[u] + term
        for u in range(size):
            at = (low + u) * ROWS + band * 16
            filtered[item][c, at : at + 16, :] = sums[u]

    def place(item, u):
        down, across = downs[item], acrosses[item]
        twice = lax.rem(across + RADIX, LANES)
        inside = lane < LANES - across
        for band in range(ROWS // 16):
            at = (u + 1) * ROWS + band * 16 - down
            moved, turned = [], []
            for c in range(2):
                here = filtered[item][c, pl.ds(at, 16), :]
                above = filtered[item][c, pl.ds(at - 1, 16), :]
                value = jnp.where(inside, here, above)
                moved.append(pltpu.roll(value, across, 1))
                turned.append(pltpu.roll(value, twice, 1))
            parts = (
                jnp.where(high, moved[0], turned[1]),
                jnp.where(high, turned[0], moved[1]),
                jnp.where(high, moved[1], -turned[0]),
                jnp.where(high, turned[1], -moved[0]),
            )
            for which, value in enumerate(parts):
                low = which * ROWS + band * 16
                grouped[item, u, low : low + 16, :] = value.astype(jnp.bfloat16)

    rows_out = jnp.concatenate(
        [last[me ^ dg, ct + dc] for dg in range(PAIR) for dc in range(per_ct)], axis=0
    )

    def turn(item, base):
        wide = jnp.concatenate([grouped[item, base + u] for u in range(SOME)], axis=1)
        inner = jnp.dot(first[...], wide, preferred_element_type=jnp.float32)
        rows = []
        for u in range(SOME):
            cut = slice(u * LANES, (u + 1) * LANES)
            value = inner[:RADIX, cut] * tw_cos[...] + inner[RADIX:, cut] * tw_sin[...]
            rows.append(value.astype(jnp.bfloat16))
        inner = jnp.concatenate(rows, axis=0)
        result = lax.dot_general(
            rows_out, inner, (((1,), (1,)), ((), ())), preferred_element_type=jnp.float32
        ).astype(jnp.bfloat16)
        size = result.shape[0] // (2 * dests)
        for dest in range(dests):
            for c in range(2):
                low = (dest * 2 + c) * size
                for u in range(SOME // 2):
                    outs[dest][before + item, base // 2 + u, c] = result[
                        low : low + size, u * LANES : (u + 1) * LANES
                    ]

    pieces = [
        (low, end, band, c)
        for low, end in ((0, frames // 2 + 1), (frames // 2 + 1, frames + 1))
        for band in range(ROWS // 16)
        for c in range(2)
    ]
    groups = frames // SOME
    each = len(pieces) // groups
    for item in range(JOIN + 1):
        for n in range(groups):
            if item < JOIN:
                for piece in pieces[n * each : (n + 1) * each]:
                    filt(item, *piece)
            if item:
                for u in range(SOME):
                    place(item - 1, n * SOME + u)
                turn(item - 1, n * SOME)


def filterbank(part, half, delays, sources, tables, beside, dests):
    late = len(sources) == 2
    frames = sources[0].shape[2] // ROWS
    size = tables[-1].shape[2] // 2
    per_ct = tables[-1].shape[1] // 2
    before = beside[0].shape[0] if beside else 0
    shape = (before + JOIN, frames // 2, 2, size, LANES)
    kernel = functools.partial(
        filterbank_kernel, late, before, part, frames, dests, per_ct, half
    )
    return pl.pallas_call(
        kernel,
        out_shape=[jax.ShapeDtypeStruct(shape, jnp.bfloat16)] * dests,
        in_specs=[SMEM] + [VMEM] * (len(sources) + 5 + len(beside)),
        out_specs=[VMEM] * dests,
        scratch_shapes=[
            pltpu.VMEM((JOIN, 2, 2 * frames * ROWS, LANES), jnp.bfloat16),
            pltpu.VMEM((JOIN, TAPS, ROWS, LANES), jnp.float32),
            pltpu.VMEM((JOIN, frames, LANES, LANES), jnp.bfloat16),
        ]
        + [pltpu.VMEM((2, (frames + 1) * ROWS, LANES), jnp.float32)] * JOIN,
        compiler_params=params(14),
        cost_estimate=cost(10**6, 2**18),
        name="filterbank_late" if late else "filterbank_early",
    )(delays, *sources, *tables, *beside)


SQUARE = [(p, q) for p in range(TILE) for q in range(TILE)]
CORNER = [(p, q) for p in range(TILE) for q in range(p, TILE)]


def pair_sets(own):
    tiles = own // TILE
    whole = [(True, i, j, SQUARE) for i in range(tiles) for j in range(i + 1, tiles)]
    corner = [(True, i, i, CORNER) for i in range(tiles)]
    across = [(False, i, j, SQUARE) for i in range(0, tiles, 2) for j in range(tiles)]
    return [whole + corner, across]


def pairs_in(blocks):
    return sum(len(block[3]) for block in blocks)


def chosen(t, values):
    result = jnp.int32(values[0])
    for n, value in enumerate(values[1:], 1):
        result = jnp.where(t == n, jnp.int32(value), result)
    return result


def correlate_kernel(layout, *refs):
    sources_at, blocks, own, added, outer, span, per_ct = layout
    sources, rest = refs[: len(sources_at)], refs[len(sources_at) :]
    if added is None:
        outs, (spectra, held), sums = (), rest[-2:], rest[0]
    else:
        first_sums, outs, (spectra, held, sums) = rest[0], rest[1:-3], rest[-3:]
    steps = spectra.shape[1]
    core, o, g, ct = position()
    within = any(block[0] for block in blocks)
    across = any(not block[0] for block in blocks)

    for source, (far, groups) in zip(sources, sources_at):
        for n in range(PAIR * per_ct):
            dg, dc = n // per_ct, n % per_ct
            device = lax.rem(ct - dc + per_ct, per_ct) * PAIR + (g ^ dg)
            for at, part in enumerate(groups):
                base = (part * per_ct * PAIR + device) * JOIN
                wanted = None
                if across:
                    side = 1 - core if far else core
                    wanted = (side == 1) | (lax.rem(base // TILE, 2) == core)
                    if within and not far:
                        wanted = None
                    base = base + side * own

                def bring(source=source, base=base, first=(n * len(groups) + at) * JOIN):
                    for item in range(JOIN):
                        for m in range(steps):
                            real = source[first + item, m, 0].astype(jnp.float32)
                            imag = source[first + item, m, 1].astype(jnp.float32)
                            for which, value in enumerate((real, imag, real + imag, imag - real)):
                                spectra[base + item, m, which] = value

                if wanted is None:
                    bring()
                else:
                    pl.when(wanted)(bring)

    high = lax.broadcasted_iota(jnp.int32, (1, LANES), 1) < RADIX
    rows_outer = pairs_in(blocks) * span
    size = outer * span
    unroll = 4

    def block(left, right, pairs, first_row):
        def over(one, two, acc, sign):
            def frame(n, acc):
                acc = list(acc)
                for u in range(unroll):
                    a = [spectra[left + p, n * unroll + u, one] for p in range(TILE)]
                    b = [spectra[right + q, n * unroll + u, two] for q in range(TILE)]
                    for at, (p, q) in enumerate(pairs):
                        term = a[p] * b[q]
                        acc[at] = acc[at] + term if sign > 0 else acc[at] - term
                return tuple(acc)

            return lax.fori_loop(0, steps // unroll, frame, tuple(acc))

        count = len(pairs)
        first = over(2, 0, [jnp.zeros((size, LANES), jnp.float32)] * count, 1)
        for at in range(count):
            held[0, at] = first[at]
        real = over(1, 3, first, 1)
        for at in range(count):
            held[1, at] = real[at] + pltpu.roll(real[at], RADIX, 1)
        imag = over(0, 2, [held[0, at] for at in range(count)], -1)
        for at in range(count):
            folded = imag[at] + pltpu.roll(imag[at], RADIX, 1)
            both = jnp.where(high, held[1, at], folded)
            for o in range(outer):
                row = o * rows_outer + first_row + at * span
                sums[pl.ds(pl.multiple_of(row, span), span), :] = both[o * span : (o + 1) * span]

    done = 0
    while done < len(blocks):
        kind = (blocks[done][0], blocks[done][3])
        end = done
        while end < len(blocks) and (blocks[end][0], blocks[end][3]) == kind:
            end += 1
        run, row = blocks[done:end], pairs_in(blocks[:done]) * span

        def step(t, carry, run=run, row=row, kind=kind):
            left, right = chosen(t, [b[1] for b in run]), chosen(t, [b[2] for b in run])
            if not kind[0]:
                left, right = TILE * (left + core), own + TILE * right
            elif across:
                left, right = core * own + TILE * left, core * own + TILE * right
            else:
                left, right = TILE * left, TILE * right
            block(left, right, kind[1], row + t * len(kind[1]) * span)
            return carry

        lax.fori_loop(0, len(run), step, 0)
        done = end

    for r in range(len(outs)):
        owner = lax.rem(o + r, outer)
        value = sums[pl.ds(pl.multiple_of(owner * rows_outer, 16), rows_outer), :]
        stride = first_sums.shape[0] // outer
        at = pl.multiple_of(owner * stride + added, 16)
        value = value + first_sums[pl.ds(at, rows_outer), :]
        outs[r][...] = value.astype(outs[r].dtype)


def correlate(arrays, sources_at, blocks, own, sizes, name, first_sums=None, added=None):
    outer, span, _ = sizes
    _, steps, _, size, _ = arrays[0].shape
    inputs = own if all(block[0] for block in blocks) else 2 * own
    rows = pairs_in(blocks) * span
    total = (outer * rows, LANES)
    scratch = [
        pltpu.VMEM((inputs, steps, 4, size, LANES), jnp.float32),
        pltpu.VMEM((2, TILE * TILE, outer * span, LANES), jnp.float32),
    ]
    if first_sums is None:
        shapes = [jax.ShapeDtypeStruct(total, jnp.float32)]
    else:
        types = [jnp.float32] + [jnp.bfloat16] * (outer - 1)
        shapes = [jax.ShapeDtypeStruct((rows, LANES), dtype) for dtype in types]
        arrays = [*arrays, first_sums]
        scratch.append(pltpu.VMEM(total, jnp.float32))
    layout = (sources_at, blocks, own, added) + sizes
    return pl.pallas_call(
        functools.partial(correlate_kernel, layout),
        out_shape=shapes,
        in_specs=[VMEM] * len(arrays),
        out_specs=[VMEM] * len(shapes),
        scratch_shapes=scratch,
        compiler_params=params(12 + inputs * steps * 4 * size * LANES * 4 // 2**20),
        cost_estimate=cost(10**6, 2**18),
        name=name,
    )(*arrays)


def assemble_kernel(own, outer, span, scale, sets, order, counts, *refs):
    out, joined = refs[-2:]
    sources, at = [], 0
    for count in counts:
        sources.append(refs[at : at + count])
        at += count
    near, far = sources[: len(sets)], sources[len(sets) :]
    lane = lax.broadcasted_iota(jnp.int32, (1, LANES), 1)
    high = lane < RADIX
    mirror = jnp.where(high, 1.0, -1.0).astype(jnp.float32)
    me = position()[0]
    across = 2 * own * span
    mine_at = pl.multiple_of(me * own * span, 8)

    def added(parts, low, rows):
        total = parts[0][low : low + rows, :].astype(jnp.float32)
        for part in parts[1:]:
            total = total + part[low : low + rows, :].astype(jnp.float32)
        return total * scale

    def put(value, places, base=0):
        n = 0
        while n < len(places):
            wide = 1
            if places[n] % 8 == 0 and places[n + 1 : n + 2] == [places[n] + span] and span < 8:
                wide = 2
            rows = value[n * span : (n + wide) * span]
            joined[pl.ds(base + places[n], wide * span), :] = rows
            n += wide

    def inner(total, i, j, pairs):
        direct = [order[i * TILE + p] * across + order[j * TILE + q] * span for p, q in pairs]
        turned = [order[j * TILE + q] * across + order[i * TILE + p] * span for p, q in pairs]
        put(total, direct, mine_at)
        for n, (p, q) in enumerate(pairs):
            if (i, p) != (j, q):
                value = total[n * span : (n + 1) * span] * mirror
                put(value, [turned[n]], mine_at)

    def outer_pairs(core):
        for blocks, mine, others in zip(sets, near, far):
            low = 0
            for within, i, j, pairs in blocks:
                rows = len(pairs) * span
                if not within:
                    for parts, side in ((mine, core), (others, 1 - core)):
                        total = added(parts, low, rows)
                        a = [order[(i + side) * TILE + p] for p, _ in pairs]
                        b = [order[j * TILE + q] for _, q in pairs]
                        if core == 0:
                            put(total, [x * across + (own + y) * span for x, y in zip(a, b)])
                        else:
                            total = total * mirror
                            put(total, [y * across + x * span for x, y in zip(a, b)])
                low += rows

    for blocks, mine in zip(sets, near):
        low = 0
        for within, i, j, pairs in blocks:
            rows = len(pairs) * span
            if within:
                inner(added(mine, low, rows), i, j, pairs)
            low += rows
    pl.when(me == 0)(lambda: outer_pairs(0))
    pl.when(me != 0)(lambda: outer_pairs(1))

    def emit(a, carry):
        for tile in range(2 * own // 8):
            for pair in range(span // 2):
                loads = []
                for u in range(2):
                    at = (a * 2 * own + tile * 8) * span + pair * 2 + u
                    loads.append(joined[pl.ds(at, 8, stride=span), :])
                turned = [pltpu.roll(x, RADIX, 1) for x in loads]
                cut = slice(pair * LANES, (pair + 1) * LANES)
                out[0, a, tile * 8 : tile * 8 + 8, cut] = jnp.where(high, loads[0], turned[1])
                out[1, a, tile * 8 : tile * 8 + 8, cut] = jnp.where(high, turned[0], loads[1])
        return carry

    def emit_some(n, carry):
        for u in range(4):
            emit(n * 4 + u, carry)
        return carry

    lax.fori_loop(0, own // 4, emit_some, 0)


def assemble(near, far, sets, order, own, span, scale):
    outer = len(near[0])
    counts = [len(arrays) for arrays in near + far]
    sources = [x for arrays in near + far for x in arrays]
    return pl.pallas_call(
        functools.partial(assemble_kernel, own, outer, span, scale, sets, order, counts),
        out_shape=jax.ShapeDtypeStruct((2, own, 2 * own, span * RADIX), jnp.float32),
        in_specs=[VMEM] * len(sources),
        out_specs=VMEM,
        scratch_shapes=[pltpu.VMEM((own * 2 * own * span, LANES), jnp.float32)],
        compiler_params=params(10),
        cost_estimate=cost(10**6, 2**18),
        name="assemble",
    )(*sources)


def fast_fits(in_count, frame_count):
    stn, tm, per_ct = (lax.axis_size(a) for a in ("stn", "tm", "ct"))
    groups = tm * per_ct
    if stn != 2 or tm % PAIR or in_count % (PAIR * JOIN) or RADIX % groups:
        return False
    outer, span = tm // PAIR, RADIX // groups
    own = in_count * per_ct
    return (
        frame_count >= TAPS
        and frame_count % (2 * SOME) == 0
        and span in (2, 4, 8)
        and outer * span % 16 == 0
        and own % (PAIR * JOIN * 2 * TILE // 4) == 0
        and in_count == PAIR * JOIN * 2
        and per_ct * PAIR * JOIN % (2 * TILE) == 0
        and all(pairs_in(s) * span % 16 == 0 for s in pair_sets(own))
    )


def fast(voltages, delays):
    tm, per_ct = lax.axis_size("tm"), lax.axis_size("ct")
    in_count = voltages.shape[1]
    frame_count = voltages.shape[2] // CHANNELS
    outer = tm // PAIR
    span = RADIX // (tm * per_ct)
    own = in_count * per_ct
    half = in_count // PAIR
    place_tm, place_ct = lax.axis_index("tm"), lax.axis_index("ct")
    g = place_tm % PAIR

    swap = [(i, i ^ 1) for i in range(tm)]
    onward = [(i, i + PAIR) for i in range(tm - PAIR)]
    cores = [(0, 1), (1, 0)]

    dests = [(dg, dc) for dg in range(PAIR) for dc in range(per_ct)]
    base = last_table(outer, per_ct, span)
    tables = [np.concatenate([filter_table()] * 2, axis=1), first_table(), *twiddle_tables()]
    tables = [jnp.asarray(t) for t in tables + [np.concatenate([base, base], axis=1)]]

    parts = half // JOIN
    sends = pick(voltages, False)
    keeps = pick(follow(voltages, sends[0]), True)
    recvs = [lax.ppermute(block, "tm", swap) for block in sends]
    count = len(dests)
    late, halos = [], []
    for c in range(parts):
        late = filterbank(c, half, delays, [keeps[c], recvs[c]], tables, late, count)
        recv = follow(recvs[c], [late[0], halos[-1]]) if c else recvs[c]
        halos.append(lax.ppermute(jnp.where(g == 1, keeps[c], recv), "tm", onward))

    def sent(spectra, after):
        arrays = []
        for n, ((dg, dc), block) in enumerate(zip(dests, spectra)):
            route = []
            for i in range(tm):
                for j in range(per_ct):
                    target = (i ^ dg) * per_ct + (j + dc) % per_ct
                    route.append((i * per_ct + j, target))
            if dg or dc:
                block = lax.ppermute(follow(block, after[n]) if after else block, ("tm", "ct"), route)
            arrays.append(block)
        return arrays

    received = [sent(late, [])]
    spectra = []
    for c in range(parts):
        halo = follow(halos[c], late[0]) if c == 0 else halos[c]
        sources = [halo, keeps[c], recvs[c]]
        spectra = filterbank(c, half, delays, sources, tables, spectra, count)
    received.append(sent(spectra, received[0]))

    def along(parts, after):
        moved = [parts[0]]
        for r in range(1, outer):
            route = [(i, (i + r * PAIR) % tm) for i in range(tm)]
            moved.append(lax.ppermute(follow(parts[r], after(r)), "tm", route))
        return moved

    sets = pair_sets(own)
    sizes = (outer, span, per_ct)
    both = [(False, range(parts)), (True, range(parts))]
    near = joined([follow(block, spectra[0]) for block in received[0]])
    far = lax.ppermute(near, "stn", cores)
    (first_sums,) = correlate([near, far], both, sets[0] + sets[1], own, sizes, "correlate_late")
    near = joined([follow(block, first_sums) for block in received[1]])
    far = lax.ppermute(near, "stn", cores)
    inner = correlate([near], both[:1], sets[0], own, sizes, "correlate_own", first_sums, 0)
    inner = along(inner, lambda r: far)
    cross = correlate(
        [near, far], both, sets[1], own, sizes, "correlate_cross", first_sums,
        pairs_in(sets[0]) * span,
    )
    cross = along(cross, lambda r: inner[r])
    mine = [inner, cross]
    theirs = [[], [lax.ppermute(block, "stn", cores) for block in cross]]
    order = []
    for part in range(parts):
        for device in range(per_ct * PAIR):
            start = device // PAIR * in_count + device % PAIR * half + part * JOIN
            order += range(start, start + JOIN)
    scale = 1.0 / (tm * frame_count)
    result = assemble(mine, theirs, sets, order, own, span, scale)
    return result.transpose(0, 3, 1, 2)


def general(voltages, delays):
    in_count = voltages.shape[1]
    frame_count = voltages.shape[2] // CHANNELS
    route = [(i, i + 1) for i in range(lax.axis_size("tm") - 1)]
    extended = jnp.concatenate([lax.ppermute(voltages, "tm", route), voltages], axis=2)
    span = (frame_count + TAPS - 1) * CHANNELS
    shifted = jax.vmap(
        lambda row, offset: lax.dynamic_slice_in_dim(row, CHANNELS - offset, span, 1),
        in_axes=(1, 0),
        out_axes=1,
    )(extended, delays)
    framed = shifted.reshape(2, in_count, frame_count + TAPS - 1, CHANNELS)
    table = jnp.asarray(filter_table()).reshape(TAPS, CHANNELS)
    total = jnp.zeros((2, in_count, frame_count, CHANNELS), jnp.float32)
    for tap in range(TAPS):
        low = TAPS - 1 - tap
        total = total + table[tap] * framed[:, :, low : low + frame_count].astype(jnp.float32)
    branches = jnp.moveaxis(total.astype(jnp.bfloat16), 0, 2)

    number = in_count * frame_count
    cosine, sine = dft_parts(RADIX)
    block = np.concatenate(
        [np.concatenate([cosine, sine], axis=1), np.concatenate([-sine, cosine], axis=1)], axis=0
    )
    block = jnp.asarray(block)
    stacked = branches.reshape(number, 2 * RADIX, RADIX)
    inner = jnp.einsum("kj,nja->nka", block, stacked, preferred_element_type=jnp.float32)
    inner = inner.reshape(number, 2, RADIX, RADIX)
    tw_cos, tw_sin = (jnp.asarray(t[:, :RADIX]) for t in twiddle_tables())
    real = inner[:, 0] * tw_cos + inner[:, 1] * tw_sin
    imag = inner[:, 1] * tw_cos - inner[:, 0] * tw_sin
    turned = jnp.stack([real, imag], axis=2).reshape(number, RADIX, 2 * RADIX)
    turned = turned.astype(jnp.bfloat16)
    result = jnp.einsum("lj,nkj->nlk", block, turned, preferred_element_type=jnp.float32)
    spectra = result.reshape(in_count, frame_count, 2, CHANNELS).astype(jnp.bfloat16)
    moved = lax.all_to_all(spectra, "tm", split_axis=3, concat_axis=1, tiled=True)
    moved = lax.all_to_all(moved, "ct", split_axis=3, concat_axis=0, tiled=True)
    local = moved.transpose(3, 2, 0, 1)
    swapped = jnp.stack([local[:, 1], -local[:, 0]], axis=1)
    summed = jnp.einsum(
        "ocjaf,cjbf->ocab",
        jnp.stack([local, swapped], axis=0),
        lax.all_gather(local, "stn", axis=2, tiled=True),
        preferred_element_type=jnp.float32,
    )
    return summed * (1.0 / local.shape[3])


def on_device(voltages, delays):
    if fast_fits(voltages.shape[1], voltages.shape[2] // CHANNELS):
        return fast(voltages, delays)
    return general(voltages, delays)


def solution(mesh):
    return jax.shard_map(
        on_device,
        mesh=mesh,
        in_specs=(P(None, ("stn", "ct"), "tm"), P(("stn", "ct"))),
        out_specs=P(None, ("tm", "ct"), "stn", None),
        check_vma=False,
    )
```

```python
import functools
import math

import jax
import jax.numpy as jnp
import numpy as np
from jax import lax
from jax.experimental import pallas as pl
from jax.experimental.pallas import tpu as pltpu
from jax.sharding import PartitionSpec as P

CHANNELS = 4096
RADIX = 64
TAPS = 16
LANES = 128
ROWS = CHANNELS // LANES
PAIR = 2
TILE = 4
JOIN = 2

VMEM = pl.BlockSpec(memory_space=pltpu.VMEM)
SMEM = pl.BlockSpec(memory_space=pltpu.SMEM)


def params(mib):
    return pltpu.CompilerParams(vmem_limit_bytes=mib * 2**20)


def position():
    place = lax.axis_index("tm")
    return lax.axis_index("stn"), place // PAIR, place % PAIR, lax.axis_index("ct")


def cost(flops, size):
    return pl.CostEstimate(flops=flops, bytes_accessed=size, transcendentals=0)


def filter_table():
    length = TAPS * CHANNELS
    index = np.arange(length, dtype=np.float64)
    centred = (index - length / 2) / CHANNELS
    window = 0.5 - 0.5 * np.cos(2.0 * math.pi * index / length)
    factor = 1.0 / (48.0 * math.sqrt(CHANNELS))
    table = np.sinc(centred) * window * factor
    return table.reshape(TAPS, ROWS, LANES).astype(np.float32)


def dft_parts(radix):
    steps = np.arange(radix)
    angle = 2.0 * math.pi * (steps[:, None] * steps[None, :] % radix) / radix
    return np.cos(angle).astype(jnp.bfloat16), np.sin(angle).astype(jnp.bfloat16)


def first_table():
    cosine, sine = dft_parts(CHANNELS // RADIX)
    order = [2 * row + half for half in range(2) for row in range(ROWS)]
    cosine, sine = cosine[:, order], sine[:, order]
    upper = np.concatenate([cosine, sine], axis=1)
    lower = np.concatenate([-sine, cosine], axis=1)
    return np.concatenate([upper, lower], axis=0)


def last_table(outer, per_ct, span):
    cosine, sine = dft_parts(RADIX)
    blocks = []
    for g in range(PAIR):
        for ct in range(per_ct):
            steps = [
                ((o * PAIR + g) * per_ct + ct) * span + j for o in range(outer) for j in range(span)
            ]
            real = np.concatenate([cosine[steps], sine[steps]], axis=1)
            imag = np.concatenate([-sine[steps], cosine[steps]], axis=1)
            blocks.append(np.concatenate([real, imag], axis=0))
    return np.stack(blocks).reshape(PAIR, per_ct, -1, 2 * RADIX)


def twiddle_tables():
    rows = np.arange(CHANNELS // RADIX)
    cols = np.arange(RADIX)
    angle = 2.0 * math.pi * (rows[:, None] * cols[None, :] % CHANNELS) / CHANNELS
    cosine = np.cos(angle).astype(np.float32)
    sine = np.sin(angle).astype(np.float32)
    return np.concatenate([cosine, cosine], axis=1), np.concatenate([sine, sine], axis=1)


def pick_kernel(half, own, block, *refs):
    outs, rows = refs[:-1], refs[-1]
    inputs, samples = block.shape[1], block.shape[2]
    step = 32
    for part in range(2):

        def spread(n, carry, part=part):
            low = pl.multiple_of(n * step * LANES, step * LANES)
            wide = block[part, :, pl.ds(low, step * LANES)].astype(jnp.float32)
            for u in range(step):
                at = pl.multiple_of((n * step + u) * inputs, inputs)
                rows[part, pl.ds(at, inputs), :] = wide[:, u * LANES : (u + 1) * LANES]
            return carry

        lax.fori_loop(0, samples // LANES // step, spread, 0)
    g = position()[2]
    first = (g if own else 1 - g) * half
    tall = 64

    def gather(n, carry):
        low = pl.multiple_of(n * tall, tall)
        for item in range(half):
            for part in range(2):
                at = low * inputs + first + item
                value = rows[part, pl.ds(at, tall, stride=inputs), :].astype(jnp.bfloat16)
                outs[item // JOIN][item % JOIN, part, pl.ds(low, tall), :] = value
        return carry

    lax.fori_loop(0, samples // LANES // tall, gather, 0)


def pick(block, own):
    _, inputs, samples = block.shape
    half = inputs // PAIR
    shape = jax.ShapeDtypeStruct((JOIN, 2, samples // LANES, LANES), jnp.bfloat16)
    return pl.pallas_call(
        functools.partial(pick_kernel, half, own),
        out_shape=[shape] * (half // JOIN),
        in_specs=[VMEM],
        out_specs=[VMEM] * (half // JOIN),
        scratch_shapes=[pltpu.VMEM((2, samples // LANES * inputs, LANES), jnp.float32)],
        compiler_params=params(12),
        cost_estimate=cost(10**6, 2**18),
        name="pick",
    )(block)


def follow(block, after):
    return lax.optimization_barrier((block, after))[0]


def joined(blocks):
    def kernel(*refs):
        sources, out = refs[:-1], refs[-1]
        for n, source in enumerate(sources):
            size = source.shape[0]
            for item in range(size):

                def step(m, carry, n=n, source=source, size=size, item=item):
                    cut = pl.ds(m * 4, 4)
                    out[n * size + item, cut] = source[item, cut]
                    return carry

                lax.fori_loop(0, source.shape[1] // 4, step, 0)

    shape = (sum(block.shape[0] for block in blocks),) + blocks[0].shape[1:]
    return pl.pallas_call(
        kernel,
        out_shape=jax.ShapeDtypeStruct(shape, blocks[0].dtype),
        in_specs=[VMEM] * len(blocks),
        out_specs=VMEM,
        compiler_params=params(8),
        cost_estimate=cost(10**6, 2**18),
        name="join",
    )(*blocks)


SOME = 4


def filterbank_kernel(late, part, frames, dests, per_ct, half_count, *refs):
    delays, refs = refs[0], refs[1:]
    _, _, me, ct = position()
    if late:
        keep, recv = refs[:2]
        refs = refs[2:]
    else:
        halo, keep, recv = refs[:3]
        refs = refs[3:]
    coef, first, tw_cos, tw_sin, last = refs[:5]
    beside = () if late else refs[5 : 5 + dests]
    outs = refs[5 + len(beside) :][:dests]
    raw, weights, grouped = refs[5 + len(beside) + dests :][:3]
    filtered = refs[5 + len(beside) + dests + 3 :]
    block_rows = frames * ROWS
    lane = lax.broadcasted_iota(jnp.int32, (1, LANES), 1)
    high = lane < RADIX

    def bring(source, place):
        tall = 128

        def step(n, carry):
            low = pl.multiple_of(n * tall, tall)
            at = pl.multiple_of(place * block_rows + n * tall, tall)
            for item in range(JOIN):
                for c in range(2):
                    raw[item, c, pl.ds(at, tall), :] = source[item, c, pl.ds(low, tall), :]
            return carry

        lax.fori_loop(0, block_rows // tall, step, 0)

    if late:
        bring(keep, me)
        bring(recv, 1 - me)
    else:
        bring(halo, 0)
        pl.when(me == 0)(lambda: bring(keep, 1))
        pl.when(me != 0)(lambda: bring(recv, 1))
        for dest, block in zip(outs, beside):
            dest[:, frames // 2 :] = block[...]

    downs, acrosses = [], []
    for item in range(JOIN):
        delay = delays[me * half_count + part * JOIN + item]
        down, across = delay // LANES, delay % LANES
        downs.append(down)
        acrosses.append(across)
        back = lax.rem(LANES - across, LANES)
        for tap in range(TAPS):
            here = coef[tap, pl.ds(down, ROWS), :]
            after = coef[tap, pl.ds(down + 1, ROWS), :]
            turned = pltpu.roll(jnp.where(lane >= across, here, after), back, 1)
            weights[item, tap] = turned

    def filt(item, low, end, band, c):
        size = end - low
        values = []
        for u in range(size + TAPS - 1):
            at = (low + u + frames - TAPS) * ROWS + band * 16
            values.append(raw[item, c, at : at + 16, :].astype(jnp.float32))
        sums = [None] * size
        for tap in range(TAPS):
            weight = weights[item, tap, band * 16 : band * 16 + 16, :]
            for u in range(size):
                term = weight * values[u + TAPS - 1 - tap]
                sums[u] = term if sums[u] is None else sums[u] + term
        for u in range(size):
            at = (low + u) * ROWS + band * 16
            filtered[item][c, at : at + 16, :] = sums[u]

    def place(item, u):
        down, across = downs[item], acrosses[item]
        twice = lax.rem(across + RADIX, LANES)
        inside = lane < LANES - across
        for band in range(ROWS // 16):
            at = (u + 1) * ROWS + band * 16 - down
            moved, turned = [], []
            for c in range(2):
                here = filtered[item][c, pl.ds(at, 16), :]
                above = filtered[item][c, pl.ds(at - 1, 16), :]
                value = jnp.where(inside, here, above)
                moved.append(pltpu.roll(value, across, 1))
                turned.append(pltpu.roll(value, twice, 1))
            parts = (
                jnp.where(high, moved[0], turned[1]),
                jnp.where(high, turned[0], moved[1]),
                jnp.where(high, moved[1], -turned[0]),
                jnp.where(high, turned[1], -moved[0]),
            )
            for which, value in enumerate(parts):
                low = which * ROWS + band * 16
                grouped[item, u, low : low + 16, :] = value.astype(jnp.bfloat16)

    rows_out = jnp.concatenate(
        [last[me ^ dg, ct + dc] for dg in range(PAIR) for dc in range(per_ct)], axis=0
    )

    def turn(item, base):
        wide = jnp.concatenate([grouped[item, base + u] for u in range(SOME)], axis=1)
        inner = jnp.dot(first[...], wide, preferred_element_type=jnp.float32)
        rows = []
        for u in range(SOME):
            cut = slice(u * LANES, (u + 1) * LANES)
            value = inner[:RADIX, cut] * tw_cos[...] + inner[RADIX:, cut] * tw_sin[...]
            rows.append(value.astype(jnp.bfloat16))
        inner = jnp.concatenate(rows, axis=0)
        result = lax.dot_general(
            rows_out, inner, (((1,), (1,)), ((), ())), preferred_element_type=jnp.float32
        ).astype(jnp.bfloat16)
        size = result.shape[0] // (2 * dests)
        for dest in range(dests):
            for c in range(2):
                low = (dest * 2 + c) * size
                for u in range(SOME // 2):
                    outs[dest][item, base // 2 + u, c] = result[
                        low : low + size, u * LANES : (u + 1) * LANES
                    ]

    pieces = [
        (low, end, band, c)
        for low, end in ((0, frames // 2 + 1), (frames // 2 + 1, frames + 1))
        for band in range(ROWS // 16)
        for c in range(2)
    ]
    groups = frames // SOME
    each = len(pieces) // groups
    for item in range(JOIN + 1):
        for n in range(groups):
            if item < JOIN:
                for piece in pieces[n * each : (n + 1) * each]:
                    filt(item, *piece)
            if item:
                for u in range(SOME):
                    place(item - 1, n * SOME + u)
                turn(item - 1, n * SOME)


def filterbank(part, half, delays, sources, tables, beside, dests):
    late = not beside
    frames = sources[0].shape[2] // ROWS
    size = tables[-1].shape[2] // 2
    per_ct = tables[-1].shape[1] // 2
    pairs = frames // 2 if late else frames
    shape = (JOIN, pairs, 2, size, LANES)
    kernel = functools.partial(filterbank_kernel, late, part, frames, dests, per_ct, half)
    return pl.pallas_call(
        kernel,
        out_shape=[jax.ShapeDtypeStruct(shape, jnp.bfloat16)] * dests,
        in_specs=[SMEM] + [VMEM] * (len(sources) + 5 + len(beside)),
        out_specs=[VMEM] * dests,
        scratch_shapes=[
            pltpu.VMEM((JOIN, 2, 2 * frames * ROWS, LANES), jnp.bfloat16),
            pltpu.VMEM((JOIN, TAPS, ROWS, LANES), jnp.float32),
            pltpu.VMEM((JOIN, frames, LANES, LANES), jnp.bfloat16),
        ]
        + [pltpu.VMEM((2, (frames + 1) * ROWS, LANES), jnp.float32)] * JOIN,
        compiler_params=params(14),
        cost_estimate=cost(10**6, 2**18),
        name="filterbank_late" if late else "filterbank_early",
    )(delays, *sources, *tables, *beside)


SQUARE = [(p, q) for p in range(TILE) for q in range(TILE)]
CORNER = [(p, q) for p in range(TILE) for q in range(p, TILE)]


def pair_sets(own, parts):
    tiles = own // TILE
    per = tiles // parts
    whole = [(True, i, j, SQUARE) for i in range(tiles) for j in range(i + 1, tiles)]
    corner = [(True, i, i, CORNER) for i in range(tiles)]
    across = [(False, i, j, SQUARE) for i in range(0, tiles, 2) for j in range(tiles)]

    def early(block):
        return block[1] < per and block[2] < per

    def late(blocks):
        return [block for block in blocks if not early(block)]

    first = [block for block in whole + across + corner if early(block)]
    return [first, late(whole + corner + across)]


def pairs_in(blocks):
    return sum(len(block[3]) for block in blocks)


def chosen(t, values):
    result = jnp.int32(values[0])
    for n, value in enumerate(values[1:], 1):
        result = jnp.where(t == n, jnp.int32(value), result)
    return result


def correlate_kernel(layout, *refs):
    sources_at, blocks, own, owners, outer, span, per_ct = layout
    sources, rest = refs[: len(sources_at)], refs[len(sources_at) :]
    outs, (spectra, sums, held) = rest[-3 - len(owners) : -3], rest[-3:]
    earlier = rest[: -3 - len(owners)]
    steps, size = spectra.shape[1], spectra.shape[3]
    core, o, g, ct = position()
    whole = size == outer * span
    base_owner = 0 if whole else (o // 2 if 0 in owners else 1 - o // 2) * 2
    within = any(block[0] for block in blocks)
    across = any(not block[0] for block in blocks)

    for source, (far, part) in zip(sources, sources_at):
        for n in range(PAIR * per_ct):
            dg, dc = n // per_ct, n % per_ct
            device = lax.rem(ct - dc + per_ct, per_ct) * PAIR + (g ^ dg)
            base = (part * per_ct * PAIR + device) * JOIN
            wanted = None
            side = 1 - core if far else core
            if far:
                wanted = (side == 1) | (lax.rem(base // TILE, 2) == core)
            base = base + side * own

            def bring(source=source, base=base, n=n):
                for item in range(JOIN):

                    def spread(m, carry, item=item):
                        for u in range(8):
                            parts = []
                            for c in range(2):
                                value = source[n * JOIN + item, m * 8 + u, c].astype(jnp.float32)
                                if not whole:
                                    value = jnp.where(base_owner == 0, value[:size], value[size:])
                                parts.append(value)
                            real, imag = parts
                            for which, value in enumerate((real, imag, real + imag, imag - real)):
                                spectra[base + item, m * 8 + u, which] = value
                        return carry

                    lax.fori_loop(0, steps // 8, spread, 0)

            if wanted is None:
                bring()
            else:
                pl.when(wanted)(bring)

    high = lax.broadcasted_iota(jnp.int32, (1, LANES), 1) < RADIX
    rows_outer = pairs_in(blocks) * span
    unroll = 4 if whole else 8

    def block(left, right, pairs, first_row):
        def over(one, two, acc, sign):
            def frame(n, acc):
                acc = list(acc)
                for u in range(unroll):
                    a = [spectra[left + p, n * unroll + u, one] for p in range(TILE)]
                    b = [spectra[right + q, n * unroll + u, two] for q in range(TILE)]
                    for at, (p, q) in enumerate(pairs):
                        term = a[p] * b[q]
                        acc[at] = acc[at] + term if sign > 0 else acc[at] - term
                return tuple(acc)

            return lax.fori_loop(0, steps // unroll, frame, tuple(acc))

        count = len(pairs)
        first = over(2, 0, [jnp.zeros((size, LANES), jnp.float32)] * count, 1)
        for at in range(count):
            held[0, at] = first[at]
        real = over(1, 3, first, 1)
        for at in range(count):
            held[1, at] = real[at] + pltpu.roll(real[at], RADIX, 1)
        imag = over(0, 2, [held[0, at] for at in range(count)], -1)
        for at in range(count):
            folded = imag[at] + pltpu.roll(imag[at], RADIX, 1)
            both = jnp.where(high, held[1, at], folded)
            for u in range(size // span):
                row = u * rows_outer + first_row + at * span
                sums[pl.ds(pl.multiple_of(row, span), span), :] = both[u * span : (u + 1) * span]

    done = 0
    while done < len(blocks):
        kind = (blocks[done][0], blocks[done][3])
        end = done
        while end < len(blocks) and (blocks[end][0], blocks[end][3]) == kind:
            end += 1
        run, row = blocks[done:end], pairs_in(blocks[:done]) * span

        def step(t, carry, run=run, row=row, kind=kind):
            left, right = chosen(t, [b[1] for b in run]), chosen(t, [b[2] for b in run])
            if not kind[0]:
                left, right = TILE * (left + core), own + TILE * right
            else:
                left, right = core * own + TILE * left, core * own + TILE * right
            block(left, right, kind[1], row + t * len(kind[1]) * span)
            return carry

        lax.fori_loop(0, len(run), step, 0)
        done = end

    before = earlier[0].shape[0] if earlier else 0
    for n, x in enumerate(owners):
        at = pl.multiple_of(((o ^ x) - base_owner) * rows_outer, 16)
        outs[n][before:, :] = sums[pl.ds(at, rows_outer), :].astype(outs[n].dtype)
        if earlier:
            outs[n][:before, :] = earlier[n][...]


def correlate(arrays, sources_at, blocks, own, owners, sizes, name, earlier=()):
    outer, span, _ = sizes
    _, steps, _, size, _ = arrays[0].shape
    if len(owners) < outer:
        size = 2 * span
    rows = pairs_in(blocks) * span
    before = earlier[0].shape[0] if earlier else 0
    types = [jnp.bfloat16 if x else jnp.float32 for x in owners]
    scratch = pltpu.VMEM((2 * own, steps, 4, size, LANES), jnp.float32)
    layout = (sources_at, blocks, own, owners) + sizes
    return pl.pallas_call(
        functools.partial(correlate_kernel, layout),
        out_shape=[jax.ShapeDtypeStruct((before + rows, LANES), dtype) for dtype in types],
        in_specs=[VMEM] * (len(arrays) + len(earlier)),
        out_specs=[VMEM] * len(owners),
        scratch_shapes=[
            scratch,
            pltpu.VMEM((size // span * rows, LANES), jnp.float32),
            pltpu.VMEM((2, TILE * TILE, size, LANES), jnp.float32),
        ],
        compiler_params=params(12 + 2 * own * steps * 4 * size * LANES * 4 // 2**20),
        cost_estimate=cost(10**6, 2**18),
        name=name,
    )(*arrays, *earlier)


def summed(early, late):
    def kernel(*refs):
        out = refs[-1]
        split = refs[0].shape[0]
        out[:split, :] = refs[0][...].astype(jnp.float32) + refs[1][...].astype(jnp.float32)
        out[split:, :] = refs[2][...].astype(jnp.float32) + refs[3][...].astype(jnp.float32)

    rows = early[0].shape[0] + late[0].shape[0]
    return pl.pallas_call(
        kernel,
        out_shape=jax.ShapeDtypeStruct((rows, LANES), jnp.float32),
        in_specs=[VMEM] * 4,
        out_specs=VMEM,
        compiler_params=params(8),
        cost_estimate=cost(10**6, 36 * 2**20),
        name="sum_far",
    )(*early, *late)


def assemble_kernel(own, span, scale, sets, order, terms, *refs):
    out, joined = refs[-2:]
    count = len(refs) // 2 - 1
    near = [[(refs[n], low) for n, low in term] for term in terms]
    far = [[(refs[count + n], low) for n, low in term] for term in terms]
    lane = lax.broadcasted_iota(jnp.int32, (1, LANES), 1)
    high = lane < RADIX
    mirror = jnp.where(high, 1.0, -1.0).astype(jnp.float32)
    me = position()[0]
    across = 2 * own * span
    mine_at = pl.multiple_of(me * own * span, 8)

    def added(parts, low, rows):
        total = None
        for ref, first in parts:
            term = ref[first + low : first + low + rows, :].astype(jnp.float32)
            total = term if total is None else total + term
        return total * scale

    def put(value, places, base=0):
        n = 0
        while n < len(places):
            wide = 1
            if places[n] % 8 == 0 and places[n + 1 : n + 2] == [places[n] + span] and span < 8:
                wide = 2
            rows = value[n * span : (n + wide) * span]
            joined[pl.ds(base + places[n], wide * span), :] = rows
            n += wide

    def inner(total, i, j, pairs):
        direct = [order[i * TILE + p] * across + order[j * TILE + q] * span for p, q in pairs]
        turned = [order[j * TILE + q] * across + order[i * TILE + p] * span for p, q in pairs]
        put(total, direct, mine_at)
        for n, (p, q) in enumerate(pairs):
            if (i, p) != (j, q):
                value = total[n * span : (n + 1) * span] * mirror
                put(value, [turned[n]], mine_at)

    def outer_pairs(core):
        for blocks, mine, others in zip(sets, near, far):
            low = 0
            for within, i, j, pairs in blocks:
                rows = len(pairs) * span
                if not within:
                    for parts, side in ((mine, core), (others, 1 - core)):
                        total = added(parts, low, rows)
                        a = [order[(i + side) * TILE + p] for p, _ in pairs]
                        b = [order[j * TILE + q] for _, q in pairs]
                        if core == 0:
                            put(total, [x * across + (own + y) * span for x, y in zip(a, b)])
                        else:
                            total = total * mirror
                            put(total, [y * across + x * span for x, y in zip(a, b)])
                low += rows

    for blocks, mine in zip(sets, near):
        low = 0
        for within, i, j, pairs in blocks:
            rows = len(pairs) * span
            if within:
                inner(added(mine, low, rows), i, j, pairs)
            low += rows
    pl.when(me == 0)(lambda: outer_pairs(0))
    pl.when(me != 0)(lambda: outer_pairs(1))

    def emit(a, carry):
        for tile in range(2 * own // 8):
            for pair in range(span // 2):
                loads = []
                for u in range(2):
                    at = (a * 2 * own + tile * 8) * span + pair * 2 + u
                    loads.append(joined[pl.ds(at, 8, stride=span), :])
                turned = [pltpu.roll(x, RADIX, 1) for x in loads]
                cut = slice(pair * LANES, (pair + 1) * LANES)
                out[0, a, tile * 8 : tile * 8 + 8, cut] = jnp.where(high, loads[0], turned[1])
                out[1, a, tile * 8 : tile * 8 + 8, cut] = jnp.where(high, turned[0], loads[1])
        return carry

    def emit_some(n, carry):
        for u in range(4):
            emit(n * 4 + u, carry)
        return carry

    lax.fori_loop(0, own // 4, emit_some, 0)


def assemble(near, far, terms, sets, order, own, span, scale):
    return pl.pallas_call(
        functools.partial(assemble_kernel, own, span, scale, sets, order, terms),
        out_shape=jax.ShapeDtypeStruct((2, own, 2 * own, span * RADIX), jnp.float32),
        in_specs=[VMEM] * (len(near) + len(far)),
        out_specs=VMEM,
        scratch_shapes=[pltpu.VMEM((own * 2 * own * span, LANES), jnp.float32)],
        compiler_params=params(12),
        cost_estimate=cost(10**6, 2**18),
        name="assemble",
    )(*near, *far)


def fast_fits(in_count, frame_count):
    stn, tm, per_ct = (lax.axis_size(a) for a in ("stn", "tm", "ct"))
    groups = tm * per_ct
    if stn != 2 or tm % PAIR or in_count % (PAIR * JOIN) or RADIX % groups:
        return False
    outer, span = tm // PAIR, RADIX // groups
    own = in_count * per_ct
    return (
        frame_count >= TAPS
        and frame_count % (2 * SOME) == 0
        and outer == 4
        and span == 4
        and outer * span % 16 == 0
        and own % (PAIR * JOIN * 2 * TILE // 4) == 0
        and in_count == PAIR * JOIN * 2
        and per_ct * PAIR * JOIN % (2 * TILE) == 0
        and all(pairs_in(s) * span % 16 == 0 for s in pair_sets(own, 2))
    )


def fast(voltages, delays):
    tm, per_ct = lax.axis_size("tm"), lax.axis_size("ct")
    in_count = voltages.shape[1]
    frame_count = voltages.shape[2] // CHANNELS
    outer = tm // PAIR
    span = RADIX // (tm * per_ct)
    own = in_count * per_ct
    half = in_count // PAIR
    place_tm, place_ct = lax.axis_index("tm"), lax.axis_index("ct")
    g = place_tm % PAIR

    swap = [(i, i ^ 1) for i in range(tm)]
    onward = [(i, i + PAIR) for i in range(tm - PAIR)]
    cores = [(0, 1), (1, 0)]

    dests = [(dg, dc) for dg in range(PAIR) for dc in range(per_ct)]
    base = last_table(outer, per_ct, span)
    tables = [np.concatenate([filter_table()] * 2, axis=1), first_table(), *twiddle_tables()]
    tables = [jnp.asarray(t) for t in tables + [np.concatenate([base, base], axis=1)]]

    parts = half // JOIN
    sends = pick(voltages, False)
    keeps = pick(follow(voltages, sends[0]), True)
    recvs = [lax.ppermute(block, "tm", swap) for block in sends]
    halos, lates = [], []
    for c in range(parts):
        recv = follow(recvs[c], lates[-1]) if lates else recvs[c]
        halos.append(lax.ppermute(jnp.where(g == 1, keeps[c], recv), "tm", onward))
        sources = [keeps[c], follow(recvs[c], halos[c - 1]) if c else recvs[c]]
        lates.append(filterbank(c, half, delays, sources, tables, [], len(dests)))

    sets = pair_sets(own, parts)
    sizes = (outer, span, per_ct)
    received = []
    for c in range(parts):
        halo = follow(halos[c], recvs[c + 1]) if c + 1 < parts else halos[c]
        sources = [halo, keeps[c], recvs[c]]
        spectra = filterbank(c, half, delays, sources, tables, lates[c], len(dests))
        arrays = []
        for n, ((dg, dc), block) in enumerate(zip(dests, spectra)):
            route = []
            for i in range(tm):
                for j in range(per_ct):
                    target = (i ^ dg) * per_ct + (j + dc) % per_ct
                    route.append((i * per_ct + j, target))
            if dg or dc:
                block = follow(block, received[-1][n]) if received else block
                block = lax.ppermute(block, ("tm", "ct"), route)
            arrays.append(block)
        received.append(arrays)

    def along(block, x):
        route = [(i, ((i // PAIR) ^ x) * PAIR + i % PAIR) for i in range(tm)]
        return lax.ppermute(block, "tm", route)

    near = [joined([follow(block, spectra[0]) for block in received[0]])]
    far = [lax.ppermute(near[0], "stn", cores)]
    early = correlate(
        near + far, [(False, 0), (True, 0)], sets[0], own // parts, (0, 1, 2, 3), sizes,
        "correlate_early",
    )
    early = [*early[:2], *[along(early[x], x) for x in (2, 3)]]
    near.append(joined([follow(block, early[2:]) for block in received[1]]))
    far.append(lax.ppermute(near[1], "stn", cores))
    sources_at = [(False, c) for c in range(parts)] + [(True, c) for c in range(parts)]
    beyond = correlate(near + far, sources_at, sets[1], own, (2, 3), sizes, "correlate_far")
    near[0] = follow(near[0], beyond[0])
    kept, beside = correlate(
        near + far, sources_at, sets[1], own, (0, 1), sizes, "correlate_near", early[:2]
    )
    beyond = [along(block, x) for block, x in zip(beyond, (2, 3))]
    beside = along(beside, 1)
    beyond = summed(early[2:], beyond)
    mine = [kept, beside, beyond]
    after = [kept, follow(beside, beyond), beyond]
    theirs = [lax.ppermute(block, "stn", cores) for block in after]
    first = pairs_in(sets[0]) * span
    terms = [[(n, low) for n in range(3)] for low in (0, first)]
    order = []
    for part in range(parts):
        for device in range(per_ct * PAIR):
            start = device // PAIR * in_count + device % PAIR * half + part * JOIN
            order += range(start, start + JOIN)
    scale = 1.0 / (tm * frame_count)
    result = assemble(mine, theirs, terms, sets, order, own, span, scale)
    return result.transpose(0, 3, 1, 2)


def general(voltages, delays):
    in_count = voltages.shape[1]
    frame_count = voltages.shape[2] // CHANNELS
    route = [(i, i + 1) for i in range(lax.axis_size("tm") - 1)]
    extended = jnp.concatenate([lax.ppermute(voltages, "tm", route), voltages], axis=2)
    span = (frame_count + TAPS - 1) * CHANNELS
    shifted = jax.vmap(
        lambda row, offset: lax.dynamic_slice_in_dim(row, CHANNELS - offset, span, 1),
        in_axes=(1, 0),
        out_axes=1,
    )(extended, delays)
    framed = shifted.reshape(2, in_count, frame_count + TAPS - 1, CHANNELS)
    table = jnp.asarray(filter_table()).reshape(TAPS, CHANNELS)
    total = jnp.zeros((2, in_count, frame_count, CHANNELS), jnp.float32)
    for tap in range(TAPS):
        low = TAPS - 1 - tap
        total = total + table[tap] * framed[:, :, low : low + frame_count].astype(jnp.float32)
    branches = jnp.moveaxis(total.astype(jnp.bfloat16), 0, 2)

    number = in_count * frame_count
    cosine, sine = dft_parts(RADIX)
    block = np.concatenate(
        [np.concatenate([cosine, sine], axis=1), np.concatenate([-sine, cosine], axis=1)], axis=0
    )
    block = jnp.asarray(block)
    stacked = branches.reshape(number, 2 * RADIX, RADIX)
    inner = jnp.einsum("kj,nja->nka", block, stacked, preferred_element_type=jnp.float32)
    inner = inner.reshape(number, 2, RADIX, RADIX)
    tw_cos, tw_sin = (jnp.asarray(t[:, :RADIX]) for t in twiddle_tables())
    real = inner[:, 0] * tw_cos + inner[:, 1] * tw_sin
    imag = inner[:, 1] * tw_cos - inner[:, 0] * tw_sin
    turned = jnp.stack([real, imag], axis=2).reshape(number, RADIX, 2 * RADIX)
    turned = turned.astype(jnp.bfloat16)
    result = jnp.einsum("lj,nkj->nlk", block, turned, preferred_element_type=jnp.float32)
    spectra = result.reshape(in_count, frame_count, 2, CHANNELS).astype(jnp.bfloat16)
    moved = lax.all_to_all(spectra, "tm", split_axis=3, concat_axis=1, tiled=True)
    moved = lax.all_to_all(moved, "ct", split_axis=3, concat_axis=0, tiled=True)
    local = moved.transpose(3, 2, 0, 1)
    swapped = jnp.stack([local[:, 1], -local[:, 0]], axis=1)
    summed = jnp.einsum(
        "ocjaf,cjbf->ocab",
        jnp.stack([local, swapped], axis=0),
        lax.all_gather(local, "stn", axis=2, tiled=True),
        preferred_element_type=jnp.float32,
    )
    return summed * (1.0 / local.shape[3])


def on_device(voltages, delays):
    if fast_fits(voltages.shape[1], voltages.shape[2] // CHANNELS):
        return fast(voltages, delays)
    return general(voltages, delays)


def solution(mesh):
    return jax.shard_map(
        on_device,
        mesh=mesh,
        in_specs=(P(None, ("stn", "ct"), "tm"), P(("stn", "ct"))),
        out_specs=P(None, ("tm", "ct"), "stn", None),
        check_vma=False,
    )
```

```python
import functools
import math

import jax
import jax.numpy as jnp
import numpy as np
from jax import lax
from jax.experimental import pallas as pl
from jax.experimental.pallas import tpu as pltpu
from jax.sharding import PartitionSpec as P

CHANNELS = 4096
RADIX = 64
TAPS = 16
LANES = 128
ROWS = CHANNELS // LANES
PAIR = 2
TILE = 4
JOIN = 2

VMEM = pl.BlockSpec(memory_space=pltpu.VMEM)
SMEM = pl.BlockSpec(memory_space=pltpu.SMEM)


def params(mib):
    return pltpu.CompilerParams(vmem_limit_bytes=mib * 2**20)


def position():
    place = lax.axis_index("tm")
    return lax.axis_index("stn"), place // PAIR, place % PAIR, lax.axis_index("ct")


def cost(flops, size):
    return pl.CostEstimate(flops=flops, bytes_accessed=size, transcendentals=0)


def filter_table():
    length = TAPS * CHANNELS
    index = np.arange(length, dtype=np.float64)
    centred = (index - length / 2) / CHANNELS
    window = 0.5 - 0.5 * np.cos(2.0 * math.pi * index / length)
    factor = 1.0 / (48.0 * math.sqrt(CHANNELS))
    table = np.sinc(centred) * window * factor
    return table.reshape(TAPS, ROWS, LANES).astype(np.float32)


def dft_parts(radix):
    steps = np.arange(radix)
    angle = 2.0 * math.pi * (steps[:, None] * steps[None, :] % radix) / radix
    return np.cos(angle).astype(jnp.bfloat16), np.sin(angle).astype(jnp.bfloat16)


def first_table():
    cosine, sine = dft_parts(CHANNELS // RADIX)
    order = [2 * row + half for half in range(2) for row in range(ROWS)]
    cosine, sine = cosine[:, order], sine[:, order]
    upper = np.concatenate([cosine, sine], axis=1)
    lower = np.concatenate([-sine, cosine], axis=1)
    return np.concatenate([upper, lower], axis=0)


def last_table(outer, per_ct, span):
    cosine, sine = dft_parts(RADIX)
    blocks = []
    for g in range(PAIR):
        for ct in range(per_ct):
            steps = [
                ((o * PAIR + g) * per_ct + ct) * span + j for o in range(outer) for j in range(span)
            ]
            real = np.concatenate([cosine[steps], sine[steps]], axis=1)
            imag = np.concatenate([-sine[steps], cosine[steps]], axis=1)
            blocks.append(np.concatenate([real, imag], axis=0))
    return np.stack(blocks).reshape(PAIR, per_ct, -1, 2 * RADIX)


def twiddle_tables():
    rows = np.arange(CHANNELS // RADIX)
    cols = np.arange(RADIX)
    angle = 2.0 * math.pi * (rows[:, None] * cols[None, :] % CHANNELS) / CHANNELS
    cosine = np.cos(angle).astype(np.float32)
    sine = np.sin(angle).astype(np.float32)
    return np.concatenate([cosine, cosine], axis=1), np.concatenate([sine, sine], axis=1)


def pick_kernel(half, own, block, *refs):
    outs, rows = refs[:-1], refs[-1]
    inputs, samples = block.shape[1], block.shape[2]
    step = 32
    for part in range(2):

        def spread(n, carry, part=part):
            low = pl.multiple_of(n * step * LANES, step * LANES)
            wide = block[part, :, pl.ds(low, step * LANES)].astype(jnp.float32)
            for u in range(step):
                at = pl.multiple_of((n * step + u) * inputs, inputs)
                rows[part, pl.ds(at, inputs), :] = wide[:, u * LANES : (u + 1) * LANES]
            return carry

        lax.fori_loop(0, samples // LANES // step, spread, 0)
    g = position()[2]
    first = (g if own else 1 - g) * half
    tall = 64

    def gather(n, carry):
        low = pl.multiple_of(n * tall, tall)
        for item in range(half):
            for part in range(2):
                at = low * inputs + first + item
                value = rows[part, pl.ds(at, tall, stride=inputs), :].astype(jnp.bfloat16)
                outs[item // JOIN][item % JOIN, part, pl.ds(low, tall), :] = value
        return carry

    lax.fori_loop(0, samples // LANES // tall, gather, 0)


def pick(block, own):
    _, inputs, samples = block.shape
    half = inputs // PAIR
    shape = jax.ShapeDtypeStruct((JOIN, 2, samples // LANES, LANES), jnp.bfloat16)
    return pl.pallas_call(
        functools.partial(pick_kernel, half, own),
        out_shape=[shape] * (half // JOIN),
        in_specs=[VMEM],
        out_specs=[VMEM] * (half // JOIN),
        scratch_shapes=[pltpu.VMEM((2, samples // LANES * inputs, LANES), jnp.float32)],
        compiler_params=params(12),
        cost_estimate=cost(10**6, 2**18),
        name="pick",
    )(block)


def follow(block, after):
    return lax.optimization_barrier((block, after))[0]


def joined(blocks):
    def kernel(*refs):
        sources, out = refs[:-1], refs[-1]
        for n, source in enumerate(sources):
            size = source.shape[0]
            for item in range(size):

                def step(m, carry, n=n, source=source, size=size, item=item):
                    cut = pl.ds(m * 4, 4)
                    out[n * size + item, cut] = source[item, cut]
                    return carry

                lax.fori_loop(0, source.shape[1] // 4, step, 0)

    shape = (sum(block.shape[0] for block in blocks),) + blocks[0].shape[1:]
    return pl.pallas_call(
        kernel,
        out_shape=jax.ShapeDtypeStruct(shape, blocks[0].dtype),
        in_specs=[VMEM] * len(blocks),
        out_specs=VMEM,
        compiler_params=params(8),
        cost_estimate=cost(10**6, 2**18),
        name="join",
    )(*blocks)


SOME = 4


def filterbank_kernel(late, part, frames, dests, per_ct, half_count, *refs):
    delays, refs = refs[0], refs[1:]
    _, _, me, ct = position()
    if late:
        keep, recv = refs[:2]
        refs = refs[2:]
    else:
        halo, keep, recv = refs[:3]
        refs = refs[3:]
    coef, first, tw_cos, tw_sin, last = refs[:5]
    beside = () if late else refs[5 : 5 + dests]
    outs = refs[5 + len(beside) :][:dests]
    raw, weights, grouped = refs[5 + len(beside) + dests :][:3]
    filtered = refs[5 + len(beside) + dests + 3 :]
    block_rows = frames * ROWS
    lane = lax.broadcasted_iota(jnp.int32, (1, LANES), 1)
    high = lane < RADIX

    def bring(source, place):
        tall = 128

        def step(n, carry):
            low = pl.multiple_of(n * tall, tall)
            at = pl.multiple_of(place * block_rows + n * tall, tall)
            for item in range(JOIN):
                for c in range(2):
                    raw[item, c, pl.ds(at, tall), :] = source[item, c, pl.ds(low, tall), :]
            return carry

        lax.fori_loop(0, block_rows // tall, step, 0)

    if late:
        bring(keep, me)
        bring(recv, 1 - me)
    else:
        bring(halo, 0)
        pl.when(me == 0)(lambda: bring(keep, 1))
        pl.when(me != 0)(lambda: bring(recv, 1))
        for dest, block in zip(outs, beside):
            dest[:, frames // 2 :] = block[...]

    downs, acrosses = [], []
    for item in range(JOIN):
        delay = delays[me * half_count + part * JOIN + item]
        down, across = delay // LANES, delay % LANES
        downs.append(down)
        acrosses.append(across)
        back = lax.rem(LANES - across, LANES)
        for tap in range(TAPS):
            here = coef[tap, pl.ds(down, ROWS), :]
            after = coef[tap, pl.ds(down + 1, ROWS), :]
            turned = pltpu.roll(jnp.where(lane >= across, here, after), back, 1)
            weights[item, tap] = turned

    def filt(item, low, end, band, c):
        size = end - low
        values = []
        for u in range(size + TAPS - 1):
            at = (low + u + frames - TAPS) * ROWS + band * 16
            values.append(raw[item, c, at : at + 16, :].astype(jnp.float32))
        sums = [None] * size
        for tap in range(TAPS):
            weight = weights[item, tap, band * 16 : band * 16 + 16, :]
            for u in range(size):
                term = weight * values[u + TAPS - 1 - tap]
                sums[u] = term if sums[u] is None else sums[u] + term
        for u in range(size):
            at = (low + u) * ROWS + band * 16
            filtered[item][c, at : at + 16, :] = sums[u]

    def place(item, u):
        down, across = downs[item], acrosses[item]
        twice = lax.rem(across + RADIX, LANES)
        inside = lane < LANES - across
        for band in range(ROWS // 16):
            at = (u + 1) * ROWS + band * 16 - down
            moved, turned = [], []
            for c in range(2):
                here = filtered[item][c, pl.ds(at, 16), :]
                above = filtered[item][c, pl.ds(at - 1, 16), :]
                value = jnp.where(inside, here, above)
                moved.append(pltpu.roll(value, across, 1))
                turned.append(pltpu.roll(value, twice, 1))
            parts = (
                jnp.where(high, moved[0], turned[1]),
                jnp.where(high, turned[0], moved[1]),
                jnp.where(high, moved[1], -turned[0]),
                jnp.where(high, turned[1], -moved[0]),
            )
            for which, value in enumerate(parts):
                low = which * ROWS + band * 16
                grouped[item, u, low : low + 16, :] = value.astype(jnp.bfloat16)

    rows_out = jnp.concatenate(
        [last[me ^ dg, ct + dc] for dg in range(PAIR) for dc in range(per_ct)], axis=0
    )

    def turn(item, base):
        wide = jnp.concatenate([grouped[item, base + u] for u in range(SOME)], axis=1)
        inner = jnp.dot(first[...], wide, preferred_element_type=jnp.float32)
        rows = []
        for u in range(SOME):
            cut = slice(u * LANES, (u + 1) * LANES)
            value = inner[:RADIX, cut] * tw_cos[...] + inner[RADIX:, cut] * tw_sin[...]
            rows.append(value.astype(jnp.bfloat16))
        inner = jnp.concatenate(rows, axis=0)
        result = lax.dot_general(
            rows_out, inner, (((1,), (1,)), ((), ())), preferred_element_type=jnp.float32
        ).astype(jnp.bfloat16)
        size = result.shape[0] // (2 * dests)
        for dest in range(dests):
            for c in range(2):
                low = (dest * 2 + c) * size
                for u in range(SOME // 2):
                    outs[dest][item, base // 2 + u, c] = result[
                        low : low + size, u * LANES : (u + 1) * LANES
                    ]

    pieces = [
        (low, end, band, c)
        for low, end in ((0, frames // 2 + 1), (frames // 2 + 1, frames + 1))
        for band in range(ROWS // 16)
        for c in range(2)
    ]
    groups = frames // SOME
    each = len(pieces) // groups
    for item in range(JOIN + 1):
        for n in range(groups):
            if item < JOIN:
                for piece in pieces[n * each : (n + 1) * each]:
                    filt(item, *piece)
            if item:
                for u in range(SOME):
                    place(item - 1, n * SOME + u)
                turn(item - 1, n * SOME)


def filterbank(part, half, delays, sources, tables, beside, dests):
    late = not beside
    frames = sources[0].shape[2] // ROWS
    size = tables[-1].shape[2] // 2
    per_ct = tables[-1].shape[1] // 2
    pairs = frames // 2 if late else frames
    shape = (JOIN, pairs, 2, size, LANES)
    kernel = functools.partial(filterbank_kernel, late, part, frames, dests, per_ct, half)
    return pl.pallas_call(
        kernel,
        out_shape=[jax.ShapeDtypeStruct(shape, jnp.bfloat16)] * dests,
        in_specs=[SMEM] + [VMEM] * (len(sources) + 5 + len(beside)),
        out_specs=[VMEM] * dests,
        scratch_shapes=[
            pltpu.VMEM((JOIN, 2, 2 * frames * ROWS, LANES), jnp.bfloat16),
            pltpu.VMEM((JOIN, TAPS, ROWS, LANES), jnp.float32),
            pltpu.VMEM((JOIN, frames, LANES, LANES), jnp.bfloat16),
        ]
        + [pltpu.VMEM((2, (frames + 1) * ROWS, LANES), jnp.float32)] * JOIN,
        compiler_params=params(14),
        cost_estimate=cost(10**6, 2**18),
        name="filterbank_late" if late else "filterbank_early",
    )(delays, *sources, *tables, *beside)


SQUARE = [(p, q) for p in range(TILE) for q in range(TILE)]
CORNER = [(p, q) for p in range(TILE) for q in range(p, TILE)]


def pair_sets(own, parts):
    tiles = own // TILE
    per = tiles // parts
    whole = [(True, i, j, SQUARE) for i in range(tiles) for j in range(i + 1, tiles)]
    corner = [(True, i, i, CORNER) for i in range(tiles)]
    across = [(False, i, j, SQUARE) for i in range(0, tiles, 2) for j in range(tiles)]

    def early(block):
        return block[1] < per and block[2] < per

    def late(blocks):
        return [block for block in blocks if not early(block)]

    first = [block for block in whole + across + corner if early(block)]
    return [first, late(whole + corner + across)]


def pairs_in(blocks):
    return sum(len(block[3]) for block in blocks)


def chosen(t, values):
    result = jnp.int32(values[0])
    for n, value in enumerate(values[1:], 1):
        result = jnp.where(t == n, jnp.int32(value), result)
    return result


def correlate_kernel(layout, *refs):
    sources_at, blocks, own, owners, outer, span, per_ct = layout
    sources, rest = refs[: len(sources_at)], refs[len(sources_at) :]
    outs, (spectra, sums, held) = rest[-3 - len(owners) : -3], rest[-3:]
    earlier = rest[: -3 - len(owners)]
    steps, size = spectra.shape[1], spectra.shape[3]
    core, o, g, ct = position()
    whole = size == outer * span
    base_owner = 0 if whole else (o // 2 if 0 in owners else 1 - o // 2) * 2
    within = any(block[0] for block in blocks)
    across = any(not block[0] for block in blocks)

    for source, (far, part) in zip(sources, sources_at):
        for n in range(PAIR * per_ct):
            dg, dc = n // per_ct, n % per_ct
            device = lax.rem(ct - dc + per_ct, per_ct) * PAIR + (g ^ dg)
            base = (part * per_ct * PAIR + device) * JOIN
            wanted = None
            side = 1 - core if far else core
            if far:
                wanted = (side == 1) | (lax.rem(base // TILE, 2) == core)
            base = base + side * own

            def bring(source=source, base=base, n=n):
                for item in range(JOIN):

                    def spread(m, carry, item=item):
                        for u in range(8):
                            parts = []
                            for c in range(2):
                                value = source[n * JOIN + item, m * 8 + u, c].astype(jnp.float32)
                                if not whole:
                                    value = jnp.where(base_owner == 0, value[:size], value[size:])
                                parts.append(value)
                            real, imag = parts
                            for which, value in enumerate((real, imag, real + imag, imag - real)):
                                spectra[base + item, m * 8 + u, which] = value
                        return carry

                    lax.fori_loop(0, steps // 8, spread, 0)

            if wanted is None:
                bring()
            else:
                pl.when(wanted)(bring)

    high = lax.broadcasted_iota(jnp.int32, (1, LANES), 1) < RADIX
    rows_outer = pairs_in(blocks) * span
    unroll = 4 if whole else 8

    def block(left, right, pairs, first_row):
        def over(one, two, acc, sign):
            def frame(n, acc):
                acc = list(acc)
                for u in range(unroll):
                    a = [spectra[left + p, n * unroll + u, one] for p in range(TILE)]
                    b = [spectra[right + q, n * unroll + u, two] for q in range(TILE)]
                    for at, (p, q) in enumerate(pairs):
                        term = a[p] * b[q]
                        acc[at] = acc[at] + term if sign > 0 else acc[at] - term
                return tuple(acc)

            return lax.fori_loop(0, steps // unroll, frame, tuple(acc))

        count = len(pairs)
        first = over(2, 0, [jnp.zeros((size, LANES), jnp.float32)] * count, 1)
        for at in range(count):
            held[0, at] = first[at]
        real = over(1, 3, first, 1)
        for at in range(count):
            held[1, at] = real[at] + pltpu.roll(real[at], RADIX, 1)
        imag = over(0, 2, [held[0, at] for at in range(count)], -1)
        for at in range(count):
            folded = imag[at] + pltpu.roll(imag[at], RADIX, 1)
            both = jnp.where(high, held[1, at], folded)
            for u in range(size // span):
                row = u * rows_outer + first_row + at * span
                sums[pl.ds(pl.multiple_of(row, span), span), :] = both[u * span : (u + 1) * span]

    done = 0
    while done < len(blocks):
        kind = (blocks[done][0], blocks[done][3])
        end = done
        while end < len(blocks) and (blocks[end][0], blocks[end][3]) == kind:
            end += 1
        run, row = blocks[done:end], pairs_in(blocks[:done]) * span

        def step(t, carry, run=run, row=row, kind=kind):
            left, right = chosen(t, [b[1] for b in run]), chosen(t, [b[2] for b in run])
            if not kind[0]:
                left, right = TILE * (left + core), own + TILE * right
            else:
                left, right = core * own + TILE * left, core * own + TILE * right
            block(left, right, kind[1], row + t * len(kind[1]) * span)
            return carry

        lax.fori_loop(0, len(run), step, 0)
        done = end

    before = earlier[0].shape[0] if earlier else 0
    for n, x in enumerate(owners):
        at = pl.multiple_of(((o ^ x) - base_owner) * rows_outer, 16)
        outs[n][before:, :] = sums[pl.ds(at, rows_outer), :].astype(outs[n].dtype)
        if earlier:
            outs[n][:before, :] = earlier[n][...]


def correlate(arrays, sources_at, blocks, own, owners, sizes, name, earlier=()):
    outer, span, _ = sizes
    _, steps, _, size, _ = arrays[0].shape
    if len(owners) < outer:
        size = 2 * span
    rows = pairs_in(blocks) * span
    before = earlier[0].shape[0] if earlier else 0
    types = [jnp.bfloat16 if x else jnp.float32 for x in owners]
    scratch = pltpu.VMEM((2 * own, steps, 4, size, LANES), jnp.float32)
    layout = (sources_at, blocks, own, owners) + sizes
    return pl.pallas_call(
        functools.partial(correlate_kernel, layout),
        out_shape=[jax.ShapeDtypeStruct((before + rows, LANES), dtype) for dtype in types],
        in_specs=[VMEM] * (len(arrays) + len(earlier)),
        out_specs=[VMEM] * len(owners),
        scratch_shapes=[
            scratch,
            pltpu.VMEM((size // span * rows, LANES), jnp.float32),
            pltpu.VMEM((2, TILE * TILE, size, LANES), jnp.float32),
        ],
        compiler_params=params(12 + 2 * own * steps * 4 * size * LANES * 4 // 2**20),
        cost_estimate=cost(10**6, 2**18),
        name=name,
    )(*arrays, *earlier)


def summed(early, late):
    def kernel(*refs):
        out = refs[-1]
        split = refs[0].shape[0]
        out[:split, :] = refs[0][...].astype(jnp.float32) + refs[1][...].astype(jnp.float32)
        out[split:, :] = refs[2][...].astype(jnp.float32) + refs[3][...].astype(jnp.float32)

    rows = early[0].shape[0] + late[0].shape[0]
    return pl.pallas_call(
        kernel,
        out_shape=jax.ShapeDtypeStruct((rows, LANES), jnp.float32),
        in_specs=[VMEM] * 4,
        out_specs=VMEM,
        compiler_params=params(8),
        cost_estimate=cost(10**6, 36 * 2**20),
        name="sum_far",
    )(*early, *late)


def assemble_kernel(own, span, scale, sets, order, terms, *refs):
    out, joined = refs[-2:]
    count = len(refs) // 2 - 1
    near = [[(refs[n], low) for n, low in term] for term in terms]
    far = [[(refs[count + n], low) for n, low in term] for term in terms]
    lane = lax.broadcasted_iota(jnp.int32, (1, LANES), 1)
    high = lane < RADIX
    mirror = jnp.where(high, 1.0, -1.0).astype(jnp.float32)
    me = position()[0]
    across = 2 * own * span
    mine_at = pl.multiple_of(me * own * span, 8)

    def added(parts, low, rows):
        total = None
        for ref, first in parts:
            term = ref[first + low : first + low + rows, :].astype(jnp.float32)
            total = term if total is None else total + term
        return total * scale

    def put(value, places, base=0):
        n = 0
        while n < len(places):
            wide = 1
            if places[n] % 8 == 0 and places[n + 1 : n + 2] == [places[n] + span] and span < 8:
                wide = 2
            rows = value[n * span : (n + wide) * span]
            joined[pl.ds(base + places[n], wide * span), :] = rows
            n += wide

    def inner(total, i, j, pairs):
        direct = [order[i * TILE + p] * across + order[j * TILE + q] * span for p, q in pairs]
        turned = [order[j * TILE + q] * across + order[i * TILE + p] * span for p, q in pairs]
        put(total, direct, mine_at)
        for n, (p, q) in enumerate(pairs):
            if (i, p) != (j, q):
                value = total[n * span : (n + 1) * span] * mirror
                put(value, [turned[n]], mine_at)

    def outer_pairs(core):
        for blocks, mine, others in zip(sets, near, far):
            low = 0
            for within, i, j, pairs in blocks:
                rows = len(pairs) * span
                if not within:
                    for parts, side in ((mine, core), (others, 1 - core)):
                        total = added(parts, low, rows)
                        a = [order[(i + side) * TILE + p] for p, _ in pairs]
                        b = [order[j * TILE + q] for _, q in pairs]
                        if core == 0:
                            put(total, [x * across + (own + y) * span for x, y in zip(a, b)])
                        else:
                            total = total * mirror
                            put(total, [y * across + x * span for x, y in zip(a, b)])
                low += rows

    for blocks, mine in zip(sets, near):
        low = 0
        for within, i, j, pairs in blocks:
            rows = len(pairs) * span
            if within:
                inner(added(mine, low, rows), i, j, pairs)
            low += rows
    pl.when(me == 0)(lambda: outer_pairs(0))
    pl.when(me != 0)(lambda: outer_pairs(1))

    def emit(a, carry):
        for tile in range(2 * own // 8):
            for pair in range(span // 2):
                loads = []
                for u in range(2):
                    at = (a * 2 * own + tile * 8) * span + pair * 2 + u
                    loads.append(joined[pl.ds(at, 8, stride=span), :])
                turned = [pltpu.roll(x, RADIX, 1) for x in loads]
                cut = slice(pair * LANES, (pair + 1) * LANES)
                out[0, a, tile * 8 : tile * 8 + 8, cut] = jnp.where(high, loads[0], turned[1])
                out[1, a, tile * 8 : tile * 8 + 8, cut] = jnp.where(high, turned[0], loads[1])
        return carry

    def emit_some(n, carry):
        for u in range(4):
            emit(n * 4 + u, carry)
        return carry

    lax.fori_loop(0, own // 4, emit_some, 0)


def assemble(near, far, terms, sets, order, own, span, scale):
    return pl.pallas_call(
        functools.partial(assemble_kernel, own, span, scale, sets, order, terms),
        out_shape=jax.ShapeDtypeStruct((2, own, 2 * own, span * RADIX), jnp.float32),
        in_specs=[VMEM] * (len(near) + len(far)),
        out_specs=VMEM,
        scratch_shapes=[pltpu.VMEM((own * 2 * own * span, LANES), jnp.float32)],
        compiler_params=params(12),
        cost_estimate=cost(10**6, 2**18),
        name="assemble",
    )(*near, *far)


def fast_fits(in_count, frame_count):
    stn, tm, per_ct = (lax.axis_size(a) for a in ("stn", "tm", "ct"))
    groups = tm * per_ct
    if stn != 2 or tm % PAIR or in_count % (PAIR * JOIN) or RADIX % groups:
        return False
    outer, span = tm // PAIR, RADIX // groups
    own = in_count * per_ct
    return (
        frame_count >= TAPS
        and frame_count % (2 * SOME) == 0
        and outer == 4
        and span == 4
        and outer * span % 16 == 0
        and own % (PAIR * JOIN * 2 * TILE // 4) == 0
        and in_count == PAIR * JOIN * 2
        and per_ct * PAIR * JOIN % (2 * TILE) == 0
        and all(pairs_in(s) * span % 16 == 0 for s in pair_sets(own, 2))
    )


def fast(voltages, delays):
    tm, per_ct = lax.axis_size("tm"), lax.axis_size("ct")
    in_count = voltages.shape[1]
    frame_count = voltages.shape[2] // CHANNELS
    outer = tm // PAIR
    span = RADIX // (tm * per_ct)
    own = in_count * per_ct
    half = in_count // PAIR
    place_tm, place_ct = lax.axis_index("tm"), lax.axis_index("ct")
    g = place_tm % PAIR

    swap = [(i, i ^ 1) for i in range(tm)]
    onward = [(i, i + PAIR) for i in range(tm - PAIR)]
    cores = [(0, 1), (1, 0)]

    dests = [(dg, dc) for dg in range(PAIR) for dc in range(per_ct)]
    base = last_table(outer, per_ct, span)
    tables = [np.concatenate([filter_table()] * 2, axis=1), first_table(), *twiddle_tables()]
    tables = [jnp.asarray(t) for t in tables + [np.concatenate([base, base], axis=1)]]

    parts = half // JOIN
    sends = pick(voltages, False)
    keeps = pick(follow(voltages, sends[0]), True)
    recvs = [lax.ppermute(block, "tm", swap) for block in sends]
    halos, lates = [], []
    for c in range(parts):
        recv = follow(recvs[c], [lates[-1][0], halos[-1]]) if lates else recvs[c]
        halos.append(lax.ppermute(jnp.where(g == 1, keeps[c], recv), "tm", onward))
        sources = [keeps[c], follow(recvs[c], halos[c - 1]) if c else recvs[c]]
        lates.append(filterbank(c, half, delays, sources, tables, [], len(dests)))

    sets = pair_sets(own, parts)
    sizes = (outer, span, per_ct)
    received = []
    for c in range(parts):
        halo = follow(halos[c], recvs[c + 1]) if c + 1 < parts else halos[c]
        sources = [halo, keeps[c], recvs[c]]
        spectra = filterbank(c, half, delays, sources, tables, lates[c], len(dests))
        arrays = []
        for n, ((dg, dc), block) in enumerate(zip(dests, spectra)):
            route = []
            for i in range(tm):
                for j in range(per_ct):
                    target = (i ^ dg) * per_ct + (j + dc) % per_ct
                    route.append((i * per_ct + j, target))
            if dg or dc:
                block = follow(block, received[-1][n]) if received else block
                block = lax.ppermute(block, ("tm", "ct"), route)
            arrays.append(block)
        received.append(arrays)

    def along(block, x):
        route = [(i, ((i // PAIR) ^ x) * PAIR + i % PAIR) for i in range(tm)]
        return lax.ppermute(block, "tm", route)

    near = [joined([follow(block, spectra[0]) for block in received[0]])]
    far = [lax.ppermute(near[0], "stn", cores)]
    early = correlate(
        near + far, [(False, 0), (True, 0)], sets[0], own // parts, (0, 1, 2, 3), sizes,
        "correlate_early",
    )
    early = [*early[:2], *[along(early[x], x) for x in (2, 3)]]
    near.append(joined([follow(block, early[2:]) for block in received[1]]))
    far.append(lax.ppermute(near[1], "stn", cores))
    sources_at = [(False, c) for c in range(parts)] + [(True, c) for c in range(parts)]
    beyond = correlate(near + far, sources_at, sets[1], own, (2, 3), sizes, "correlate_far")
    near[0] = follow(near[0], beyond[0])
    kept, beside = correlate(
        near + far, sources_at, sets[1], own, (0, 1), sizes, "correlate_near", early[:2]
    )
    beyond = [along(block, x) for block, x in zip(beyond, (2, 3))]
    beside = along(beside, 1)
    beyond = summed(early[2:], beyond)
    mine = [kept, beside, beyond]
    after = [kept, follow(beside, beyond), beyond]
    theirs = [lax.ppermute(block, "stn", cores) for block in after]
    first = pairs_in(sets[0]) * span
    terms = [[(n, low) for n in range(3)] for low in (0, first)]
    order = []
    for part in range(parts):
        for device in range(per_ct * PAIR):
            start = device // PAIR * in_count + device % PAIR * half + part * JOIN
            order += range(start, start + JOIN)
    scale = 1.0 / (tm * frame_count)
    result = assemble(mine, theirs, terms, sets, order, own, span, scale)
    return result.transpose(0, 3, 1, 2)


def general(voltages, delays):
    in_count = voltages.shape[1]
    frame_count = voltages.shape[2] // CHANNELS
    route = [(i, i + 1) for i in range(lax.axis_size("tm") - 1)]
    extended = jnp.concatenate([lax.ppermute(voltages, "tm", route), voltages], axis=2)
    span = (frame_count + TAPS - 1) * CHANNELS
    shifted = jax.vmap(
        lambda row, offset: lax.dynamic_slice_in_dim(row, CHANNELS - offset, span, 1),
        in_axes=(1, 0),
        out_axes=1,
    )(extended, delays)
    framed = shifted.reshape(2, in_count, frame_count + TAPS - 1, CHANNELS)
    table = jnp.asarray(filter_table()).reshape(TAPS, CHANNELS)
    total = jnp.zeros((2, in_count, frame_count, CHANNELS), jnp.float32)
    for tap in range(TAPS):
        low = TAPS - 1 - tap
        total = total + table[tap] * framed[:, :, low : low + frame_count].astype(jnp.float32)
    branches = jnp.moveaxis(total.astype(jnp.bfloat16), 0, 2)

    number = in_count * frame_count
    cosine, sine = dft_parts(RADIX)
    block = np.concatenate(
        [np.concatenate([cosine, sine], axis=1), np.concatenate([-sine, cosine], axis=1)], axis=0
    )
    block = jnp.asarray(block)
    stacked = branches.reshape(number, 2 * RADIX, RADIX)
    inner = jnp.einsum("kj,nja->nka", block, stacked, preferred_element_type=jnp.float32)
    inner = inner.reshape(number, 2, RADIX, RADIX)
    tw_cos, tw_sin = (jnp.asarray(t[:, :RADIX]) for t in twiddle_tables())
    real = inner[:, 0] * tw_cos + inner[:, 1] * tw_sin
    imag = inner[:, 1] * tw_cos - inner[:, 0] * tw_sin
    turned = jnp.stack([real, imag], axis=2).reshape(number, RADIX, 2 * RADIX)
    turned = turned.astype(jnp.bfloat16)
    result = jnp.einsum("lj,nkj->nlk", block, turned, preferred_element_type=jnp.float32)
    spectra = result.reshape(in_count, frame_count, 2, CHANNELS).astype(jnp.bfloat16)
    moved = lax.all_to_all(spectra, "tm", split_axis=3, concat_axis=1, tiled=True)
    moved = lax.all_to_all(moved, "ct", split_axis=3, concat_axis=0, tiled=True)
    local = moved.transpose(3, 2, 0, 1)
    swapped = jnp.stack([local[:, 1], -local[:, 0]], axis=1)
    summed = jnp.einsum(
        "ocjaf,cjbf->ocab",
        jnp.stack([local, swapped], axis=0),
        lax.all_gather(local, "stn", axis=2, tiled=True),
        preferred_element_type=jnp.float32,
    )
    return summed * (1.0 / local.shape[3])


def on_device(voltages, delays):
    if fast_fits(voltages.shape[1], voltages.shape[2] // CHANNELS):
        return fast(voltages, delays)
    return general(voltages, delays)


def solution(mesh):
    return jax.shard_map(
        on_device,
        mesh=mesh,
        in_specs=(P(None, ("stn", "ct"), "tm"), P(("stn", "ct"))),
        out_specs=P(None, ("tm", "ct"), "stn", None),
        check_vma=False,
    )
```

```python
import functools
import math

import jax
import jax.numpy as jnp
import numpy as np
from jax import lax
from jax.experimental import pallas as pl
from jax.experimental.pallas import tpu as pltpu
from jax.sharding import PartitionSpec as P

CHANNELS = 4096
RADIX = 64
TAPS = 16
LANES = 128
ROWS = CHANNELS // LANES
PAIR = 2
TILE = 4
JOIN = 2

VMEM = pl.BlockSpec(memory_space=pltpu.VMEM)
SMEM = pl.BlockSpec(memory_space=pltpu.SMEM)


def params(mib):
    return pltpu.CompilerParams(vmem_limit_bytes=mib * 2**20)


def position():
    place = lax.axis_index("tm")
    return lax.axis_index("stn"), place // PAIR, place % PAIR, lax.axis_index("ct")


def cost(flops, size):
    return pl.CostEstimate(flops=flops, bytes_accessed=size, transcendentals=0)


def filter_table():
    length = TAPS * CHANNELS
    index = np.arange(length, dtype=np.float64)
    centred = (index - length / 2) / CHANNELS
    window = 0.5 - 0.5 * np.cos(2.0 * math.pi * index / length)
    factor = 1.0 / (48.0 * math.sqrt(CHANNELS))
    table = np.sinc(centred) * window * factor
    return table.reshape(TAPS, ROWS, LANES).astype(np.float32)


def dft_parts(radix):
    steps = np.arange(radix)
    angle = 2.0 * math.pi * (steps[:, None] * steps[None, :] % radix) / radix
    return np.cos(angle).astype(jnp.bfloat16), np.sin(angle).astype(jnp.bfloat16)


def first_table():
    cosine, sine = dft_parts(CHANNELS // RADIX)
    order = [2 * row + half for half in range(2) for row in range(ROWS)]
    cosine, sine = cosine[:, order], sine[:, order]
    upper = np.concatenate([cosine, sine], axis=1)
    lower = np.concatenate([-sine, cosine], axis=1)
    return np.concatenate([upper, lower], axis=0)


def last_table(outer, per_ct, span):
    cosine, sine = dft_parts(RADIX)
    blocks = []
    for g in range(PAIR):
        for ct in range(per_ct):
            steps = [
                ((o * PAIR + g) * per_ct + ct) * span + j for o in range(outer) for j in range(span)
            ]
            real = np.concatenate([cosine[steps], sine[steps]], axis=1)
            imag = np.concatenate([-sine[steps], cosine[steps]], axis=1)
            blocks.append(np.concatenate([real, imag], axis=0))
    return np.stack(blocks).reshape(PAIR, per_ct, -1, 2 * RADIX)


def twiddle_tables():
    rows = np.arange(CHANNELS // RADIX)
    cols = np.arange(RADIX)
    angle = 2.0 * math.pi * (rows[:, None] * cols[None, :] % CHANNELS) / CHANNELS
    cosine = np.cos(angle).astype(np.float32)
    sine = np.sin(angle).astype(np.float32)
    return np.concatenate([cosine, cosine], axis=1), np.concatenate([sine, sine], axis=1)


def pick_kernel(half, block, *refs):
    outs, rows = refs[:-1], refs[-1]
    inputs, samples = block.shape[1], block.shape[2]
    step = 32
    for part in range(2):

        def spread(n, carry, part=part):
            low = pl.multiple_of(n * step * LANES, step * LANES)
            wide = block[part, :, pl.ds(low, step * LANES)].astype(jnp.float32)
            for u in range(step):
                at = pl.multiple_of((n * step + u) * inputs, inputs)
                rows[part, pl.ds(at, inputs), :] = wide[:, u * LANES : (u + 1) * LANES]
            return carry

        lax.fori_loop(0, samples // LANES // step, spread, 0)
    g = position()[2]
    tall = 64

    def gather(n, carry):
        low = pl.multiple_of(n * tall, tall)
        for item in range(inputs):
            first = (1 - g) * half + item if item < half else g * half + item - half
            for part in range(2):
                at = low * inputs + first
                value = rows[part, pl.ds(at, tall, stride=inputs), :].astype(jnp.bfloat16)
                outs[item // JOIN][item % JOIN, part, pl.ds(low, tall), :] = value
        return carry

    lax.fori_loop(0, samples // LANES // tall, gather, 0)


def pick(block):
    _, inputs, samples = block.shape
    shape = jax.ShapeDtypeStruct((JOIN, 2, samples // LANES, LANES), jnp.bfloat16)
    return pl.pallas_call(
        functools.partial(pick_kernel, inputs // PAIR),
        out_shape=[shape] * (inputs // JOIN),
        in_specs=[VMEM],
        out_specs=[VMEM] * (inputs // JOIN),
        scratch_shapes=[pltpu.VMEM((2, samples // LANES * inputs, LANES), jnp.float32)],
        compiler_params=params(16),
        cost_estimate=cost(10**6, 2**18),
        name="pick",
    )(block)


def follow(block, after):
    return lax.optimization_barrier((block, after))[0]


def joined(blocks):
    def kernel(*refs):
        sources, out = refs[:-1], refs[-1]
        for n, source in enumerate(sources):
            size = source.shape[0]
            for item in range(size):

                def step(m, carry, n=n, source=source, size=size, item=item):
                    cut = pl.ds(m * 4, 4)
                    out[n * size + item, cut] = source[item, cut]
                    return carry

                lax.fori_loop(0, source.shape[1] // 4, step, 0)

    shape = (sum(block.shape[0] for block in blocks),) + blocks[0].shape[1:]
    return pl.pallas_call(
        kernel,
        out_shape=jax.ShapeDtypeStruct(shape, blocks[0].dtype),
        in_specs=[VMEM] * len(blocks),
        out_specs=VMEM,
        compiler_params=params(8),
        cost_estimate=cost(10**6, 2**18),
        name="join",
    )(*blocks)


SOME = 4


def filterbank_kernel(late, part, frames, dests, per_ct, half_count, *refs):
    delays, refs = refs[0], refs[1:]
    _, _, me, ct = position()
    if late:
        keep, recv = refs[:2]
        refs = refs[2:]
    else:
        halo, keep, recv = refs[:3]
        refs = refs[3:]
    coef, first, tw_cos, tw_sin, last = refs[:5]
    beside = () if late else refs[5 : 5 + dests]
    outs = refs[5 + len(beside) :][:dests]
    raw, weights, grouped = refs[5 + len(beside) + dests :][:3]
    filtered = refs[5 + len(beside) + dests + 3 :]
    block_rows = frames * ROWS
    lane = lax.broadcasted_iota(jnp.int32, (1, LANES), 1)
    high = lane < RADIX

    def bring(source, place):
        tall = 128

        def step(n, carry):
            low = pl.multiple_of(n * tall, tall)
            at = pl.multiple_of(place * block_rows + n * tall, tall)
            for item in range(JOIN):
                for c in range(2):
                    raw[item, c, pl.ds(at, tall), :] = source[item, c, pl.ds(low, tall), :]
            return carry

        lax.fori_loop(0, block_rows // tall, step, 0)

    if late:
        bring(keep, me)
        bring(recv, 1 - me)
    else:
        bring(halo, 0)
        pl.when(me == 0)(lambda: bring(keep, 1))
        pl.when(me != 0)(lambda: bring(recv, 1))
        for dest, block in zip(outs, beside):
            dest[:, frames // 2 :] = block[...]

    downs, acrosses = [], []
    for item in range(JOIN):
        delay = delays[me * half_count + part * JOIN + item]
        down, across = delay // LANES, delay % LANES
        downs.append(down)
        acrosses.append(across)
        back = lax.rem(LANES - across, LANES)
        for tap in range(TAPS):
            here = coef[tap, pl.ds(down, ROWS), :]
            after = coef[tap, pl.ds(down + 1, ROWS), :]
            turned = pltpu.roll(jnp.where(lane >= across, here, after), back, 1)
            weights[item, tap] = turned

    def filt(item, low, end, band, c):
        size = end - low
        values = []
        for u in range(size + TAPS - 1):
            at = (low + u + frames - TAPS) * ROWS + band * 16
            values.append(raw[item, c, at : at + 16, :].astype(jnp.float32))
        sums = [None] * size
        for tap in range(TAPS):
            weight = weights[item, tap, band * 16 : band * 16 + 16, :]
            for u in range(size):
                term = weight * values[u + TAPS - 1 - tap]
                sums[u] = term if sums[u] is None else sums[u] + term
        for u in range(size):
            at = (low + u) * ROWS + band * 16
            filtered[item][c, at : at + 16, :] = sums[u]

    def place(item, u):
        down, across = downs[item], acrosses[item]
        twice = lax.rem(across + RADIX, LANES)
        inside = lane < LANES - across
        for band in range(ROWS // 16):
            at = (u + 1) * ROWS + band * 16 - down
            moved, turned = [], []
            for c in range(2):
                here = filtered[item][c, pl.ds(at, 16), :]
                above = filtered[item][c, pl.ds(at - 1, 16), :]
                value = jnp.where(inside, here, above)
                moved.append(pltpu.roll(value, across, 1))
                turned.append(pltpu.roll(value, twice, 1))
            parts = (
                jnp.where(high, moved[0], turned[1]),
                jnp.where(high, turned[0], moved[1]),
                jnp.where(high, moved[1], -turned[0]),
                jnp.where(high, turned[1], -moved[0]),
            )
            for which, value in enumerate(parts):
                low = which * ROWS + band * 16
                grouped[item, u, low : low + 16, :] = value.astype(jnp.bfloat16)

    rows_out = jnp.concatenate(
        [last[me ^ dg, ct + dc] for dg in range(PAIR) for dc in range(per_ct)], axis=0
    )

    def turn(item, base):
        wide = jnp.concatenate([grouped[item, base + u] for u in range(SOME)], axis=1)
        inner = jnp.dot(first[...], wide, preferred_element_type=jnp.float32)
        rows = []
        for u in range(SOME):
            cut = slice(u * LANES, (u + 1) * LANES)
            value = inner[:RADIX, cut] * tw_cos[...] + inner[RADIX:, cut] * tw_sin[...]
            rows.append(value.astype(jnp.bfloat16))
        inner = jnp.concatenate(rows, axis=0)
        result = lax.dot_general(
            rows_out, inner, (((1,), (1,)), ((), ())), preferred_element_type=jnp.float32
        ).astype(jnp.bfloat16)
        size = result.shape[0] // (2 * dests)
        for dest in range(dests):
            for c in range(2):
                low = (dest * 2 + c) * size
                for u in range(SOME // 2):
                    outs[dest][item, base // 2 + u, c] = result[
                        low : low + size, u * LANES : (u + 1) * LANES
                    ]

    pieces = [
        (low, end, band, c)
        for low, end in ((0, frames // 2 + 1), (frames // 2 + 1, frames + 1))
        for band in range(ROWS // 16)
        for c in range(2)
    ]
    groups = frames // SOME
    each = len(pieces) // groups
    for item in range(JOIN + 1):
        for n in range(groups):
            if item < JOIN:
                for piece in pieces[n * each : (n + 1) * each]:
                    filt(item, *piece)
            if item:
                for u in range(SOME):
                    place(item - 1, n * SOME + u)
                turn(item - 1, n * SOME)


def filterbank(part, half, delays, sources, tables, beside, dests):
    late = not beside
    frames = sources[0].shape[2] // ROWS
    size = tables[-1].shape[2] // 2
    per_ct = tables[-1].shape[1] // 2
    pairs = frames // 2 if late else frames
    shape = (JOIN, pairs, 2, size, LANES)
    kernel = functools.partial(filterbank_kernel, late, part, frames, dests, per_ct, half)
    return pl.pallas_call(
        kernel,
        out_shape=[jax.ShapeDtypeStruct(shape, jnp.bfloat16)] * dests,
        in_specs=[SMEM] + [VMEM] * (len(sources) + 5 + len(beside)),
        out_specs=[VMEM] * dests,
        scratch_shapes=[
            pltpu.VMEM((JOIN, 2, 2 * frames * ROWS, LANES), jnp.bfloat16),
            pltpu.VMEM((JOIN, TAPS, ROWS, LANES), jnp.float32),
            pltpu.VMEM((JOIN, frames, LANES, LANES), jnp.bfloat16),
        ]
        + [pltpu.VMEM((2, (frames + 1) * ROWS, LANES), jnp.float32)] * JOIN,
        compiler_params=params(14),
        cost_estimate=cost(10**6, 2**18),
        name="filterbank_late" if late else "filterbank_early",
    )(delays, *sources, *tables, *beside)


SQUARE = [(p, q) for p in range(TILE) for q in range(TILE)]
CORNER = [(p, q) for p in range(TILE) for q in range(p, TILE)]


def pair_sets(own, parts):
    tiles = own // TILE
    per = tiles // parts
    whole = [(True, i, j, SQUARE) for i in range(tiles) for j in range(i + 1, tiles)]
    corner = [(True, i, i, CORNER) for i in range(tiles)]
    across = [(False, i, j, SQUARE) for i in range(0, tiles, 2) for j in range(tiles)]

    def early(block):
        return block[1] < per and block[2] < per

    def late(blocks):
        return [block for block in blocks if not early(block)]

    first = [block for block in whole + across + corner if early(block)]
    return [first, late(whole + corner + across)]


def pairs_in(blocks):
    return sum(len(block[3]) for block in blocks)


def chosen(t, values):
    result = jnp.int32(values[0])
    for n, value in enumerate(values[1:], 1):
        result = jnp.where(t == n, jnp.int32(value), result)
    return result


def correlate_kernel(layout, *refs):
    sources_at, blocks, own, owners, outer, span, per_ct = layout
    sources, rest = refs[: len(sources_at)], refs[len(sources_at) :]
    outs, (spectra, sums, held) = rest[-3 - len(owners) : -3], rest[-3:]
    earlier = rest[: -3 - len(owners)]
    steps, size = spectra.shape[1], spectra.shape[3]
    core, o, g, ct = position()
    whole = size == outer * span
    base_owner = 0 if whole else (o // 2 if 0 in owners else 1 - o // 2) * 2
    within = any(block[0] for block in blocks)
    across = any(not block[0] for block in blocks)

    for source, (far, part) in zip(sources, sources_at):
        for n in range(PAIR * per_ct):
            dg, dc = n // per_ct, n % per_ct
            device = lax.rem(ct - dc + per_ct, per_ct) * PAIR + (g ^ dg)
            base = (part * per_ct * PAIR + device) * JOIN
            wanted = None
            side = 1 - core if far else core
            if far:
                wanted = (side == 1) | (lax.rem(base // TILE, 2) == core)
            base = base + side * own

            def bring(source=source, base=base, n=n):
                for item in range(JOIN):

                    def spread(m, carry, item=item):
                        for u in range(8):
                            parts = []
                            for c in range(2):
                                value = source[n * JOIN + item, m * 8 + u, c].astype(jnp.float32)
                                if not whole:
                                    value = jnp.where(base_owner == 0, value[:size], value[size:])
                                parts.append(value)
                            real, imag = parts
                            for which, value in enumerate((real, imag, real + imag, imag - real)):
                                spectra[base + item, m * 8 + u, which] = value
                        return carry

                    lax.fori_loop(0, steps // 8, spread, 0)

            if wanted is None:
                bring()
            else:
                pl.when(wanted)(bring)

    high = lax.broadcasted_iota(jnp.int32, (1, LANES), 1) < RADIX
    rows_outer = pairs_in(blocks) * span
    unroll = 4 if whole else 8

    def block(left, right, pairs, first_row):
        def over(one, two, acc, sign):
            def frame(n, acc):
                acc = list(acc)
                for u in range(unroll):
                    a = [spectra[left + p, n * unroll + u, one] for p in range(TILE)]
                    b = [spectra[right + q, n * unroll + u, two] for q in range(TILE)]
                    for at, (p, q) in enumerate(pairs):
                        term = a[p] * b[q]
                        acc[at] = acc[at] + term if sign > 0 else acc[at] - term
                return tuple(acc)

            return lax.fori_loop(0, steps // unroll, frame, tuple(acc))

        count = len(pairs)
        first = over(2, 0, [jnp.zeros((size, LANES), jnp.float32)] * count, 1)
        for at in range(count):
            held[0, at] = first[at]
        real = over(1, 3, first, 1)
        for at in range(count):
            held[1, at] = real[at] + pltpu.roll(real[at], RADIX, 1)
        imag = over(0, 2, [held[0, at] for at in range(count)], -1)
        for at in range(count):
            folded = imag[at] + pltpu.roll(imag[at], RADIX, 1)
            both = jnp.where(high, held[1, at], folded)
            for u in range(size // span):
                row = u * rows_outer + first_row + at * span
                sums[pl.ds(pl.multiple_of(row, span), span), :] = both[u * span : (u + 1) * span]

    done = 0
    while done < len(blocks):
        kind = (blocks[done][0], blocks[done][3])
        end = done
        while end < len(blocks) and (blocks[end][0], blocks[end][3]) == kind:
            end += 1
        run, row = blocks[done:end], pairs_in(blocks[:done]) * span

        def step(t, carry, run=run, row=row, kind=kind):
            left, right = chosen(t, [b[1] for b in run]), chosen(t, [b[2] for b in run])
            if not kind[0]:
                left, right = TILE * (left + core), own + TILE * right
            else:
                left, right = core * own + TILE * left, core * own + TILE * right
            block(left, right, kind[1], row + t * len(kind[1]) * span)
            return carry

        lax.fori_loop(0, len(run), step, 0)
        done = end

    before = earlier[0].shape[0] if earlier else 0
    for n, x in enumerate(owners):
        at = pl.multiple_of(((o ^ x) - base_owner) * rows_outer, 16)
        outs[n][before:, :] = sums[pl.ds(at, rows_outer), :].astype(outs[n].dtype)
        if earlier:
            outs[n][:before, :] = earlier[n][...]


def correlate(arrays, sources_at, blocks, own, owners, sizes, name, earlier=()):
    outer, span, _ = sizes
    _, steps, _, size, _ = arrays[0].shape
    if len(owners) < outer:
        size = 2 * span
    rows = pairs_in(blocks) * span
    before = earlier[0].shape[0] if earlier else 0
    types = [jnp.bfloat16 if x else jnp.float32 for x in owners]
    scratch = pltpu.VMEM((2 * own, steps, 4, size, LANES), jnp.float32)
    layout = (sources_at, blocks, own, owners) + sizes
    return pl.pallas_call(
        functools.partial(correlate_kernel, layout),
        out_shape=[jax.ShapeDtypeStruct((before + rows, LANES), dtype) for dtype in types],
        in_specs=[VMEM] * (len(arrays) + len(earlier)),
        out_specs=[VMEM] * len(owners),
        scratch_shapes=[
            scratch,
            pltpu.VMEM((size // span * rows, LANES), jnp.float32),
            pltpu.VMEM((2, TILE * TILE, size, LANES), jnp.float32),
        ],
        compiler_params=params(12 + 2 * own * steps * 4 * size * LANES * 4 // 2**20),
        cost_estimate=cost(10**6, 2**18),
        name=name,
    )(*arrays, *earlier)


def summed(early, late):
    def kernel(*refs):
        out = refs[-1]
        split = refs[0].shape[0]
        out[:split, :] = refs[0][...].astype(jnp.float32) + refs[1][...].astype(jnp.float32)
        out[split:, :] = refs[2][...].astype(jnp.float32) + refs[3][...].astype(jnp.float32)

    rows = early[0].shape[0] + late[0].shape[0]
    return pl.pallas_call(
        kernel,
        out_shape=jax.ShapeDtypeStruct((rows, LANES), jnp.float32),
        in_specs=[VMEM] * 4,
        out_specs=VMEM,
        compiler_params=params(8),
        cost_estimate=cost(10**6, 36 * 2**20),
        name="sum_far",
    )(*early, *late)


def assemble_kernel(own, span, scale, sets, order, terms, *refs):
    out, joined = refs[-2:]
    count = len(refs) // 2 - 1
    near = [[(refs[n], low) for n, low in term] for term in terms]
    far = [[(refs[count + n], low) for n, low in term] for term in terms]
    lane = lax.broadcasted_iota(jnp.int32, (1, LANES), 1)
    high = lane < RADIX
    mirror = jnp.where(high, 1.0, -1.0).astype(jnp.float32)
    me = position()[0]
    across = 2 * own * span
    mine_at = pl.multiple_of(me * own * span, 8)

    def added(parts, low, rows):
        total = None
        for ref, first in parts:
            term = ref[first + low : first + low + rows, :].astype(jnp.float32)
            total = term if total is None else total + term
        return total * scale

    def put(value, places, base=0):
        n = 0
        while n < len(places):
            wide = 1
            if places[n] % 8 == 0 and places[n + 1 : n + 2] == [places[n] + span] and span < 8:
                wide = 2
            rows = value[n * span : (n + wide) * span]
            joined[pl.ds(base + places[n], wide * span), :] = rows
            n += wide

    def inner(total, i, j, pairs):
        direct = [order[i * TILE + p] * across + order[j * TILE + q] * span for p, q in pairs]
        turned = [order[j * TILE + q] * across + order[i * TILE + p] * span for p, q in pairs]
        put(total, direct, mine_at)
        for n, (p, q) in enumerate(pairs):
            if (i, p) != (j, q):
                value = total[n * span : (n + 1) * span] * mirror
                put(value, [turned[n]], mine_at)

    def outer_pairs(core):
        for blocks, mine, others in zip(sets, near, far):
            low = 0
            for within, i, j, pairs in blocks:
                rows = len(pairs) * span
                if not within:
                    for parts, side in ((mine, core), (others, 1 - core)):
                        total = added(parts, low, rows)
                        a = [order[(i + side) * TILE + p] for p, _ in pairs]
                        b = [order[j * TILE + q] for _, q in pairs]
                        if core == 0:
                            put(total, [x * across + (own + y) * span for x, y in zip(a, b)])
                        else:
                            total = total * mirror
                            put(total, [y * across + x * span for x, y in zip(a, b)])
                low += rows

    for blocks, mine in zip(sets, near):
        low = 0
        for within, i, j, pairs in blocks:
            rows = len(pairs) * span
            if within:
                inner(added(mine, low, rows), i, j, pairs)
            low += rows
    pl.when(me == 0)(lambda: outer_pairs(0))
    pl.when(me != 0)(lambda: outer_pairs(1))

    def emit(a, carry):
        for tile in range(2 * own // 8):
            for pair in range(span // 2):
                loads = []
                for u in range(2):
                    at = (a * 2 * own + tile * 8) * span + pair * 2 + u
                    loads.append(joined[pl.ds(at, 8, stride=span), :])
                turned = [pltpu.roll(x, RADIX, 1) for x in loads]
                cut = slice(pair * LANES, (pair + 1) * LANES)
                out[0, a, tile * 8 : tile * 8 + 8, cut] = jnp.where(high, loads[0], turned[1])
                out[1, a, tile * 8 : tile * 8 + 8, cut] = jnp.where(high, turned[0], loads[1])
        return carry

    def emit_some(n, carry):
        for u in range(4):
            emit(n * 4 + u, carry)
        return carry

    lax.fori_loop(0, own // 4, emit_some, 0)


def assemble(near, far, terms, sets, order, own, span, scale):
    return pl.pallas_call(
        functools.partial(assemble_kernel, own, span, scale, sets, order, terms),
        out_shape=jax.ShapeDtypeStruct((2, own, 2 * own, span * RADIX), jnp.float32),
        in_specs=[VMEM] * (len(near) + len(far)),
        out_specs=VMEM,
        scratch_shapes=[pltpu.VMEM((own * 2 * own * span, LANES), jnp.float32)],
        compiler_params=params(12),
        cost_estimate=cost(10**6, 2**18),
        name="assemble",
    )(*near, *far)


def fast_fits(in_count, frame_count):
    stn, tm, per_ct = (lax.axis_size(a) for a in ("stn", "tm", "ct"))
    groups = tm * per_ct
    if stn != 2 or tm % PAIR or in_count % (PAIR * JOIN) or RADIX % groups:
        return False
    outer, span = tm // PAIR, RADIX // groups
    own = in_count * per_ct
    return (
        frame_count >= TAPS
        and frame_count % (2 * SOME) == 0
        and outer == 4
        and span == 4
        and outer * span % 16 == 0
        and own % (PAIR * JOIN * 2 * TILE // 4) == 0
        and in_count == PAIR * JOIN * 2
        and per_ct * PAIR * JOIN % (2 * TILE) == 0
        and all(pairs_in(s) * span % 16 == 0 for s in pair_sets(own, 2))
    )


def fast(voltages, delays):
    tm, per_ct = lax.axis_size("tm"), lax.axis_size("ct")
    in_count = voltages.shape[1]
    frame_count = voltages.shape[2] // CHANNELS
    outer = tm // PAIR
    span = RADIX // (tm * per_ct)
    own = in_count * per_ct
    half = in_count // PAIR
    place_tm, place_ct = lax.axis_index("tm"), lax.axis_index("ct")
    g = place_tm % PAIR

    swap = [(i, i ^ 1) for i in range(tm)]
    onward = [(i, i + PAIR) for i in range(tm - PAIR)]
    cores = [(0, 1), (1, 0)]

    dests = [(dg, dc) for dg in range(PAIR) for dc in range(per_ct)]
    base = last_table(outer, per_ct, span)
    tables = [np.concatenate([filter_table()] * 2, axis=1), first_table(), *twiddle_tables()]
    tables = [jnp.asarray(t) for t in tables + [np.concatenate([base, base], axis=1)]]

    parts = half // JOIN
    picked = pick(voltages)
    sends, keeps = picked[:parts], picked[parts:]
    recvs = [lax.ppermute(block, "tm", swap) for block in sends]
    halos, lates = [], []
    for c in range(parts):
        recv = follow(recvs[c], lates[-1]) if lates else recvs[c]
        halos.append(lax.ppermute(jnp.where(g == 1, keeps[c], recv), "tm", onward))
        sources = [keeps[c], follow(recvs[c], halos[c - 1]) if c else recvs[c]]
        lates.append(filterbank(c, half, delays, sources, tables, [], len(dests)))

    sets = pair_sets(own, parts)
    sizes = (outer, span, per_ct)
    received = []
    for c in range(parts):
        halo = follow(halos[c], recvs[c + 1]) if c + 1 < parts else halos[c]
        sources = [halo, keeps[c], recvs[c]]
        spectra = filterbank(c, half, delays, sources, tables, lates[c], len(dests))
        arrays = []
        for n, ((dg, dc), block) in enumerate(zip(dests, spectra)):
            route = []
            for i in range(tm):
                for j in range(per_ct):
                    target = (i ^ dg) * per_ct + (j + dc) % per_ct
                    route.append((i * per_ct + j, target))
            if dg or dc:
                block = follow(block, received[-1][n]) if received else block
                block = lax.ppermute(block, ("tm", "ct"), route)
            arrays.append(block)
        received.append(arrays)

    def along(block, x):
        route = [(i, ((i // PAIR) ^ x) * PAIR + i % PAIR) for i in range(tm)]
        return lax.ppermute(block, "tm", route)

    near = [joined([follow(block, spectra[0]) for block in received[0]])]
    far = [lax.ppermute(near[0], "stn", cores)]
    early = correlate(
        near + far, [(False, 0), (True, 0)], sets[0], own // parts, (0, 1, 2, 3), sizes,
        "correlate_early",
    )
    early = [*early[:2], *[along(early[x], x) for x in (2, 3)]]
    near.append(joined([follow(block, early[2:]) for block in received[1]]))
    far.append(lax.ppermute(near[1], "stn", cores))
    sources_at = [(False, c) for c in range(parts)] + [(True, c) for c in range(parts)]
    beyond = correlate(near + far, sources_at, sets[1], own, (2, 3), sizes, "correlate_far")
    near[0] = follow(near[0], beyond[0])
    kept, beside = correlate(
        near + far, sources_at, sets[1], own, (0, 1), sizes, "correlate_near", early[:2]
    )
    beyond = [along(block, x) for block, x in zip(beyond, (2, 3))]
    beside = along(beside, 1)
    beyond = summed(early[2:], beyond)
    mine = [kept, beside, beyond]
    after = [kept, follow(beside, beyond), beyond]
    theirs = [lax.ppermute(block, "stn", cores) for block in after]
    first = pairs_in(sets[0]) * span
    terms = [[(n, low) for n in range(3)] for low in (0, first)]
    order = []
    for part in range(parts):
        for device in range(per_ct * PAIR):
            start = device // PAIR * in_count + device % PAIR * half + part * JOIN
            order += range(start, start + JOIN)
    scale = 1.0 / (tm * frame_count)
    result = assemble(mine, theirs, terms, sets, order, own, span, scale)
    return result.transpose(0, 3, 1, 2)


def general(voltages, delays):
    in_count = voltages.shape[1]
    frame_count = voltages.shape[2] // CHANNELS
    route = [(i, i + 1) for i in range(lax.axis_size("tm") - 1)]
    extended = jnp.concatenate([lax.ppermute(voltages, "tm", route), voltages], axis=2)
    span = (frame_count + TAPS - 1) * CHANNELS
    shifted = jax.vmap(
        lambda row, offset: lax.dynamic_slice_in_dim(row, CHANNELS - offset, span, 1),
        in_axes=(1, 0),
        out_axes=1,
    )(extended, delays)
    framed = shifted.reshape(2, in_count, frame_count + TAPS - 1, CHANNELS)
    table = jnp.asarray(filter_table()).reshape(TAPS, CHANNELS)
    total = jnp.zeros((2, in_count, frame_count, CHANNELS), jnp.float32)
    for tap in range(TAPS):
        low = TAPS - 1 - tap
        total = total + table[tap] * framed[:, :, low : low + frame_count].astype(jnp.float32)
    branches = jnp.moveaxis(total.astype(jnp.bfloat16), 0, 2)

    number = in_count * frame_count
    cosine, sine = dft_parts(RADIX)
    block = np.concatenate(
        [np.concatenate([cosine, sine], axis=1), np.concatenate([-sine, cosine], axis=1)], axis=0
    )
    block = jnp.asarray(block)
    stacked = branches.reshape(number, 2 * RADIX, RADIX)
    inner = jnp.einsum("kj,nja->nka", block, stacked, preferred_element_type=jnp.float32)
    inner = inner.reshape(number, 2, RADIX, RADIX)
    tw_cos, tw_sin = (jnp.asarray(t[:, :RADIX]) for t in twiddle_tables())
    real = inner[:, 0] * tw_cos + inner[:, 1] * tw_sin
    imag = inner[:, 1] * tw_cos - inner[:, 0] * tw_sin
    turned = jnp.stack([real, imag], axis=2).reshape(number, RADIX, 2 * RADIX)
    turned = turned.astype(jnp.bfloat16)
    result = jnp.einsum("lj,nkj->nlk", block, turned, preferred_element_type=jnp.float32)
    spectra = result.reshape(in_count, frame_count, 2, CHANNELS).astype(jnp.bfloat16)
    moved = lax.all_to_all(spectra, "tm", split_axis=3, concat_axis=1, tiled=True)
    moved = lax.all_to_all(moved, "ct", split_axis=3, concat_axis=0, tiled=True)
    local = moved.transpose(3, 2, 0, 1)
    swapped = jnp.stack([local[:, 1], -local[:, 0]], axis=1)
    summed = jnp.einsum(
        "ocjaf,cjbf->ocab",
        jnp.stack([local, swapped], axis=0),
        lax.all_gather(local, "stn", axis=2, tiled=True),
        preferred_element_type=jnp.float32,
    )
    return summed * (1.0 / local.shape[3])


def on_device(voltages, delays):
    if fast_fits(voltages.shape[1], voltages.shape[2] // CHANNELS):
        return fast(voltages, delays)
    return general(voltages, delays)


def solution(mesh):
    return jax.shard_map(
        on_device,
        mesh=mesh,
        in_specs=(P(None, ("stn", "ct"), "tm"), P(("stn", "ct"))),
        out_specs=P(None, ("tm", "ct"), "stn", None),
        check_vma=False,
    )
```

```python
import functools
import math

import jax
import jax.numpy as jnp
import numpy as np
from jax import lax
from jax.experimental import pallas as pl
from jax.experimental.pallas import tpu as pltpu
from jax.sharding import PartitionSpec as P

CHANNELS = 4096
RADIX = 64
TAPS = 16
LANES = 128
ROWS = CHANNELS // LANES
PAIR = 2
TILE = 4
JOIN = 2

VMEM = pl.BlockSpec(memory_space=pltpu.VMEM)
SMEM = pl.BlockSpec(memory_space=pltpu.SMEM)


def params(mib):
    return pltpu.CompilerParams(vmem_limit_bytes=mib * 2**20)


def position():
    place = lax.axis_index("tm")
    return lax.axis_index("stn"), place // PAIR, place % PAIR, lax.axis_index("ct")


def cost(flops, size):
    return pl.CostEstimate(flops=flops, bytes_accessed=size, transcendentals=0)


def filter_table():
    length = TAPS * CHANNELS
    index = np.arange(length, dtype=np.float64)
    centred = (index - length / 2) / CHANNELS
    window = 0.5 - 0.5 * np.cos(2.0 * math.pi * index / length)
    factor = 1.0 / (48.0 * math.sqrt(CHANNELS))
    table = np.sinc(centred) * window * factor
    return table.reshape(TAPS, ROWS, LANES).astype(np.float32)


def dft_parts(radix):
    steps = np.arange(radix)
    angle = 2.0 * math.pi * (steps[:, None] * steps[None, :] % radix) / radix
    return np.cos(angle).astype(jnp.bfloat16), np.sin(angle).astype(jnp.bfloat16)


def first_table():
    cosine, sine = dft_parts(CHANNELS // RADIX)
    order = [2 * row + half for half in range(2) for row in range(ROWS)]
    cosine, sine = cosine[:, order], sine[:, order]
    upper = np.concatenate([cosine, sine], axis=1)
    lower = np.concatenate([-sine, cosine], axis=1)
    return np.concatenate([upper, lower], axis=0)


def last_table(outer, per_ct, span):
    cosine, sine = dft_parts(RADIX)
    blocks = []
    for g in range(PAIR):
        for ct in range(per_ct):
            steps = [
                ((o * PAIR + g) * per_ct + ct) * span + j for o in range(outer) for j in range(span)
            ]
            real = np.concatenate([cosine[steps], sine[steps]], axis=1)
            imag = np.concatenate([-sine[steps], cosine[steps]], axis=1)
            blocks.append(np.concatenate([real, imag], axis=0))
    return np.stack(blocks).reshape(PAIR, per_ct, -1, 2 * RADIX)


def twiddle_tables():
    rows = np.arange(CHANNELS // RADIX)
    cols = np.arange(RADIX)
    angle = 2.0 * math.pi * (rows[:, None] * cols[None, :] % CHANNELS) / CHANNELS
    cosine = np.cos(angle).astype(np.float32)
    sine = np.sin(angle).astype(np.float32)
    return np.concatenate([cosine, cosine], axis=1), np.concatenate([sine, sine], axis=1)


def pick_kernel(half, block, *refs):
    outs, rows = refs[:-1], refs[-1]
    inputs, samples = block.shape[1], block.shape[2]
    step = 32
    for part in range(2):

        def spread(n, carry, part=part):
            low = pl.multiple_of(n * step * LANES, step * LANES)
            wide = block[part, :, pl.ds(low, step * LANES)].astype(jnp.float32)
            for u in range(step):
                at = pl.multiple_of((n * step + u) * inputs, inputs)
                rows[part, pl.ds(at, inputs), :] = wide[:, u * LANES : (u + 1) * LANES]
            return carry

        lax.fori_loop(0, samples // LANES // step, spread, 0)
    g = position()[2]
    tall = 64

    def gather(n, carry):
        low = pl.multiple_of(n * tall, tall)
        for item in range(inputs):
            first = (1 - g) * half + item if item < half else g * half + item - half
            for part in range(2):
                at = low * inputs + first
                value = rows[part, pl.ds(at, tall, stride=inputs), :].astype(jnp.bfloat16)
                outs[item // JOIN][item % JOIN, part, pl.ds(low, tall), :] = value
        return carry

    lax.fori_loop(0, samples // LANES // tall, gather, 0)


def pick(block):
    _, inputs, samples = block.shape
    shape = jax.ShapeDtypeStruct((JOIN, 2, samples // LANES, LANES), jnp.bfloat16)
    return pl.pallas_call(
        functools.partial(pick_kernel, inputs // PAIR),
        out_shape=[shape] * (inputs // JOIN),
        in_specs=[VMEM],
        out_specs=[VMEM] * (inputs // JOIN),
        scratch_shapes=[pltpu.VMEM((2, samples // LANES * inputs, LANES), jnp.float32)],
        compiler_params=params(16),
        cost_estimate=cost(10**6, 2**18),
        name="pick",
    )(block)


def follow(block, after):
    return lax.optimization_barrier((block, after))[0]


def joined(blocks):
    def kernel(*refs):
        sources, out = refs[:-1], refs[-1]
        for n, source in enumerate(sources):
            size = source.shape[0]
            for item in range(size):

                def step(m, carry, n=n, source=source, size=size, item=item):
                    cut = pl.ds(m * 4, 4)
                    out[n * size + item, cut] = source[item, cut]
                    return carry

                lax.fori_loop(0, source.shape[1] // 4, step, 0)

    shape = (sum(block.shape[0] for block in blocks),) + blocks[0].shape[1:]
    return pl.pallas_call(
        kernel,
        out_shape=jax.ShapeDtypeStruct(shape, blocks[0].dtype),
        in_specs=[VMEM] * len(blocks),
        out_specs=VMEM,
        compiler_params=params(8),
        cost_estimate=cost(10**6, 2**18),
        name="join",
    )(*blocks)


SOME = 4


def filterbank_kernel(late, part, frames, dests, per_ct, half_count, *refs):
    delays, refs = refs[0], refs[1:]
    _, _, me, ct = position()
    if late:
        keep, recv = refs[:2]
        refs = refs[2:]
    else:
        halo, keep, recv = refs[:3]
        refs = refs[3:]
    coef, first, tw_cos, tw_sin, last = refs[:5]
    beside = () if late else refs[5 : 5 + dests]
    outs = refs[5 + len(beside) :][:dests]
    raw, weights, grouped = refs[5 + len(beside) + dests :][:3]
    filtered = refs[5 + len(beside) + dests + 3 :]
    block_rows = frames * ROWS
    lane = lax.broadcasted_iota(jnp.int32, (1, LANES), 1)
    high = lane < RADIX

    def bring(source, place):
        tall = 128

        def step(n, carry):
            low = pl.multiple_of(n * tall, tall)
            at = pl.multiple_of(place * block_rows + n * tall, tall)
            for item in range(JOIN):
                for c in range(2):
                    raw[item, c, pl.ds(at, tall), :] = source[item, c, pl.ds(low, tall), :]
            return carry

        lax.fori_loop(0, block_rows // tall, step, 0)

    if late:
        bring(keep, me)
        bring(recv, 1 - me)
    else:
        bring(halo, 0)
        pl.when(me == 0)(lambda: bring(keep, 1))
        pl.when(me != 0)(lambda: bring(recv, 1))
        for dest, block in zip(outs, beside):
            dest[:, frames // 2 :] = block[...]

    downs, acrosses = [], []
    for item in range(JOIN):
        delay = delays[me * half_count + part * JOIN + item]
        down, across = delay // LANES, delay % LANES
        downs.append(down)
        acrosses.append(across)
        back = lax.rem(LANES - across, LANES)
        for tap in range(TAPS):
            here = coef[tap, pl.ds(down, ROWS), :]
            after = coef[tap, pl.ds(down + 1, ROWS), :]
            turned = pltpu.roll(jnp.where(lane >= across, here, after), back, 1)
            weights[item, tap] = turned

    def filt(item, low, end, band, c):
        size = end - low
        values = []
        for u in range(size + TAPS - 1):
            at = (low + u + frames - TAPS) * ROWS + band * 16
            values.append(raw[item, c, at : at + 16, :].astype(jnp.float32))
        sums = [None] * size
        for tap in range(TAPS):
            weight = weights[item, tap, band * 16 : band * 16 + 16, :]
            for u in range(size):
                term = weight * values[u + TAPS - 1 - tap]
                sums[u] = term if sums[u] is None else sums[u] + term
        for u in range(size):
            at = (low + u) * ROWS + band * 16
            filtered[item][c, at : at + 16, :] = sums[u]

    def place(item, u):
        down, across = downs[item], acrosses[item]
        twice = lax.rem(across + RADIX, LANES)
        inside = lane < LANES - across
        for band in range(ROWS // 16):
            at = (u + 1) * ROWS + band * 16 - down
            moved, turned = [], []
            for c in range(2):
                here = filtered[item][c, pl.ds(at, 16), :]
                above = filtered[item][c, pl.ds(at - 1, 16), :]
                value = jnp.where(inside, here, above)
                moved.append(pltpu.roll(value, across, 1))
                turned.append(pltpu.roll(value, twice, 1))
            parts = (
                jnp.where(high, moved[0], turned[1]),
                jnp.where(high, turned[0], moved[1]),
                jnp.where(high, moved[1], -turned[0]),
                jnp.where(high, turned[1], -moved[0]),
            )
            for which, value in enumerate(parts):
                low = which * ROWS + band * 16
                grouped[item, u, low : low + 16, :] = value.astype(jnp.bfloat16)

    rows_out = jnp.concatenate(
        [last[me ^ dg, ct + dc] for dg in range(PAIR) for dc in range(per_ct)], axis=0
    )

    def turn(item, base):
        wide = jnp.concatenate([grouped[item, base + u] for u in range(SOME)], axis=1)
        inner = jnp.dot(first[...], wide, preferred_element_type=jnp.float32)
        rows = []
        for u in range(SOME):
            cut = slice(u * LANES, (u + 1) * LANES)
            value = inner[:RADIX, cut] * tw_cos[...] + inner[RADIX:, cut] * tw_sin[...]
            rows.append(value.astype(jnp.bfloat16))
        inner = jnp.concatenate(rows, axis=0)
        result = lax.dot_general(
            rows_out, inner, (((1,), (1,)), ((), ())), preferred_element_type=jnp.float32
        ).astype(jnp.bfloat16)
        size = result.shape[0] // (2 * dests)
        for dest in range(dests):
            for c in range(2):
                low = (dest * 2 + c) * size
                for u in range(SOME // 2):
                    outs[dest][item, base // 2 + u, c] = result[
                        low : low + size, u * LANES : (u + 1) * LANES
                    ]

    pieces = [
        (low, end, band, c)
        for low, end in ((0, frames // 2 + 1), (frames // 2 + 1, frames + 1))
        for band in range(ROWS // 16)
        for c in range(2)
    ]
    groups = frames // SOME
    each = len(pieces) // groups
    for item in range(JOIN + 1):
        for n in range(groups):
            if item < JOIN:
                for piece in pieces[n * each : (n + 1) * each]:
                    filt(item, *piece)
            if item:
                for u in range(SOME):
                    place(item - 1, n * SOME + u)
                turn(item - 1, n * SOME)


def filterbank(part, half, delays, sources, tables, beside, dests):
    late = not beside
    frames = sources[0].shape[2] // ROWS
    size = tables[-1].shape[2] // 2
    per_ct = tables[-1].shape[1] // 2
    pairs = frames // 2 if late else frames
    shape = (JOIN, pairs, 2, size, LANES)
    kernel = functools.partial(filterbank_kernel, late, part, frames, dests, per_ct, half)
    return pl.pallas_call(
        kernel,
        out_shape=[jax.ShapeDtypeStruct(shape, jnp.bfloat16)] * dests,
        in_specs=[SMEM] + [VMEM] * (len(sources) + 5 + len(beside)),
        out_specs=[VMEM] * dests,
        scratch_shapes=[
            pltpu.VMEM((JOIN, 2, 2 * frames * ROWS, LANES), jnp.bfloat16),
            pltpu.VMEM((JOIN, TAPS, ROWS, LANES), jnp.float32),
            pltpu.VMEM((JOIN, frames, LANES, LANES), jnp.bfloat16),
        ]
        + [pltpu.VMEM((2, (frames + 1) * ROWS, LANES), jnp.float32)] * JOIN,
        compiler_params=params(14),
        cost_estimate=cost(10**6, 2**18),
        name="filterbank_late" if late else "filterbank_early",
    )(delays, *sources, *tables, *beside)


SQUARE = [(p, q) for p in range(TILE) for q in range(TILE)]
CORNER = [(p, q) for p in range(TILE) for q in range(p, TILE)]


def pair_sets(own, parts):
    tiles = own // TILE
    per = tiles // parts
    whole = [(True, i, j, SQUARE) for i in range(tiles) for j in range(i + 1, tiles)]
    corner = [(True, i, i, CORNER) for i in range(tiles)]
    across = [(False, i, j, SQUARE) for i in range(0, tiles, 2) for j in range(tiles)]

    def early(block):
        return block[1] < per and block[2] < per

    def late(blocks):
        return [block for block in blocks if not early(block)]

    first = [block for block in whole + across + corner if early(block)]
    return [first, late(whole + corner), late(across)]


def pairs_in(blocks):
    return sum(len(block[3]) for block in blocks)


def chosen(t, values):
    result = jnp.int32(values[0])
    for n, value in enumerate(values[1:], 1):
        result = jnp.where(t == n, jnp.int32(value), result)
    return result


def correlate_kernel(layout, *refs):
    sources_at, blocks, own, owners, outer, span, per_ct = layout
    sources, rest = refs[: len(sources_at)], refs[len(sources_at) :]
    outs, (spectra, sums, held) = rest[-3 - len(owners) : -3], rest[-3:]
    earlier = rest[: -3 - len(owners)]
    steps, size = spectra.shape[1], spectra.shape[3]
    core, o, g, ct = position()
    whole = size == outer * span
    base_owner = 0 if whole else (o // 2 if 0 in owners else 1 - o // 2) * 2
    within = any(block[0] for block in blocks)
    across = any(not block[0] for block in blocks)

    for source, (far, part) in zip(sources, sources_at):
        for n in range(PAIR * per_ct):
            dg, dc = n // per_ct, n % per_ct
            device = lax.rem(ct - dc + per_ct, per_ct) * PAIR + (g ^ dg)
            base = (part * per_ct * PAIR + device) * JOIN
            wanted = None
            side = 1 - core if far else core
            if far or not within:
                wanted = (side == 1) | (lax.rem(base // TILE, 2) == core)
            base = base + side * own

            def bring(source=source, base=base, n=n):
                for item in range(JOIN):

                    def spread(m, carry, item=item):
                        for u in range(8):
                            parts = []
                            for c in range(2):
                                value = source[n * JOIN + item, m * 8 + u, c].astype(jnp.float32)
                                if not whole:
                                    value = jnp.where(base_owner == 0, value[:size], value[size:])
                                parts.append(value)
                            real, imag = parts
                            for which, value in enumerate((real, imag, real + imag, imag - real)):
                                spectra[base + item, m * 8 + u, which] = value
                        return carry

                    lax.fori_loop(0, steps // 8, spread, 0)

            if wanted is None:
                bring()
            else:
                pl.when(wanted)(bring)

    high = lax.broadcasted_iota(jnp.int32, (1, LANES), 1) < RADIX
    rows_outer = pairs_in(blocks) * span
    unroll = 4 if whole else 8

    def block(left, right, pairs, first_row):
        def over(one, two, acc, sign):
            def frame(n, acc):
                acc = list(acc)
                for u in range(unroll):
                    a = [spectra[left + p, n * unroll + u, one] for p in range(TILE)]
                    b = [spectra[right + q, n * unroll + u, two] for q in range(TILE)]
                    for at, (p, q) in enumerate(pairs):
                        term = a[p] * b[q]
                        acc[at] = acc[at] + term if sign > 0 else acc[at] - term
                return tuple(acc)

            return lax.fori_loop(0, steps // unroll, frame, tuple(acc))

        count = len(pairs)
        first = over(2, 0, [jnp.zeros((size, LANES), jnp.float32)] * count, 1)
        for at in range(count):
            held[0, at] = first[at]
        real = over(1, 3, first, 1)
        for at in range(count):
            held[1, at] = real[at] + pltpu.roll(real[at], RADIX, 1)
        imag = over(0, 2, [held[0, at] for at in range(count)], -1)
        for at in range(count):
            folded = imag[at] + pltpu.roll(imag[at], RADIX, 1)
            both = jnp.where(high, held[1, at], folded)
            for u in range(size // span):
                row = u * rows_outer + first_row + at * span
                sums[pl.ds(pl.multiple_of(row, span), span), :] = both[u * span : (u + 1) * span]

    done = 0
    while done < len(blocks):
        kind = (blocks[done][0], blocks[done][3])
        end = done
        while end < len(blocks) and (blocks[end][0], blocks[end][3]) == kind:
            end += 1
        run, row = blocks[done:end], pairs_in(blocks[:done]) * span

        def step(t, carry, run=run, row=row, kind=kind):
            left, right = chosen(t, [b[1] for b in run]), chosen(t, [b[2] for b in run])
            if not kind[0]:
                left, right = TILE * (left + core), own + TILE * right
            else:
                left, right = core * own + TILE * left, core * own + TILE * right
            block(left, right, kind[1], row + t * len(kind[1]) * span)
            return carry

        lax.fori_loop(0, len(run), step, 0)
        done = end

    before = earlier[0].shape[0] if earlier else 0
    for n, x in enumerate(owners):
        at = pl.multiple_of(((o ^ x) - base_owner) * rows_outer, 16)
        outs[n][before:, :] = sums[pl.ds(at, rows_outer), :].astype(outs[n].dtype)
        if earlier:
            outs[n][:before, :] = earlier[n][...]


def correlate(arrays, sources_at, blocks, own, owners, sizes, name, earlier=()):
    outer, span, _ = sizes
    _, steps, _, size, _ = arrays[0].shape
    if len(owners) < outer:
        size = 2 * span
    rows = pairs_in(blocks) * span
    before = earlier[0].shape[0] if earlier else 0
    types = [jnp.bfloat16 if x else jnp.float32 for x in owners]
    scratch = pltpu.VMEM((2 * own, steps, 4, size, LANES), jnp.float32)
    layout = (sources_at, blocks, own, owners) + sizes
    return pl.pallas_call(
        functools.partial(correlate_kernel, layout),
        out_shape=[jax.ShapeDtypeStruct((before + rows, LANES), dtype) for dtype in types],
        in_specs=[VMEM] * (len(arrays) + len(earlier)),
        out_specs=[VMEM] * len(owners),
        scratch_shapes=[
            scratch,
            pltpu.VMEM((size // span * rows, LANES), jnp.float32),
            pltpu.VMEM((2, TILE * TILE, size, LANES), jnp.float32),
        ],
        compiler_params=params(12 + 2 * own * steps * 4 * size * LANES * 4 // 2**20),
        cost_estimate=cost(10**6, 2**18),
        name=name,
    )(*arrays, *earlier)


def summed(early, late):
    def kernel(*refs):
        out = refs[-1]
        split = refs[0].shape[0]
        out[:split, :] = refs[0][...].astype(jnp.float32) + refs[1][...].astype(jnp.float32)
        out[split:, :] = refs[2][...].astype(jnp.float32) + refs[3][...].astype(jnp.float32)

    rows = early[0].shape[0] + late[0].shape[0]
    return pl.pallas_call(
        kernel,
        out_shape=jax.ShapeDtypeStruct((rows, LANES), jnp.float32),
        in_specs=[VMEM] * 4,
        out_specs=VMEM,
        compiler_params=params(8),
        cost_estimate=cost(10**6, 36 * 2**20),
        name="sum_far",
    )(*early, *late)


def assemble_kernel(own, span, scale, sets, order, terms, *refs):
    out, joined = refs[-2:]
    count = len(refs) // 2 - 1
    near = [[(refs[n], low) for n, low in term] for term in terms]
    far = [[(refs[count + n], low) for n, low in term] for term in terms]
    lane = lax.broadcasted_iota(jnp.int32, (1, LANES), 1)
    high = lane < RADIX
    mirror = jnp.where(high, 1.0, -1.0).astype(jnp.float32)
    me = position()[0]
    across = 2 * own * span
    mine_at = pl.multiple_of(me * own * span, 8)

    def added(parts, low, rows):
        total = None
        for ref, first in parts:
            term = ref[first + low : first + low + rows, :].astype(jnp.float32)
            total = term if total is None else total + term
        return total * scale

    def put(value, places, base=0):
        n = 0
        while n < len(places):
            wide = 1
            if places[n] % 8 == 0 and places[n + 1 : n + 2] == [places[n] + span] and span < 8:
                wide = 2
            rows = value[n * span : (n + wide) * span]
            joined[pl.ds(base + places[n], wide * span), :] = rows
            n += wide

    def inner(total, i, j, pairs):
        direct = [order[i * TILE + p] * across + order[j * TILE + q] * span for p, q in pairs]
        turned = [order[j * TILE + q] * across + order[i * TILE + p] * span for p, q in pairs]
        put(total, direct, mine_at)
        for n, (p, q) in enumerate(pairs):
            if (i, p) != (j, q):
                value = total[n * span : (n + 1) * span] * mirror
                put(value, [turned[n]], mine_at)

    def outer_pairs(core):
        for blocks, mine, others in zip(sets, near, far):
            low = 0
            for within, i, j, pairs in blocks:
                rows = len(pairs) * span
                if not within:
                    for parts, side in ((mine, core), (others, 1 - core)):
                        total = added(parts, low, rows)
                        a = [order[(i + side) * TILE + p] for p, _ in pairs]
                        b = [order[j * TILE + q] for _, q in pairs]
                        if core == 0:
                            put(total, [x * across + (own + y) * span for x, y in zip(a, b)])
                        else:
                            total = total * mirror
                            put(total, [y * across + x * span for x, y in zip(a, b)])
                low += rows

    for blocks, mine in zip(sets, near):
        low = 0
        for within, i, j, pairs in blocks:
            rows = len(pairs) * span
            if within:
                inner(added(mine, low, rows), i, j, pairs)
            low += rows
    pl.when(me == 0)(lambda: outer_pairs(0))
    pl.when(me != 0)(lambda: outer_pairs(1))

    def emit(a, carry):
        for tile in range(2 * own // 8):
            for pair in range(span // 2):
                loads = []
                for u in range(2):
                    at = (a * 2 * own + tile * 8) * span + pair * 2 + u
                    loads.append(joined[pl.ds(at, 8, stride=span), :])
                turned = [pltpu.roll(x, RADIX, 1) for x in loads]
                cut = slice(pair * LANES, (pair + 1) * LANES)
                out[0, a, tile * 8 : tile * 8 + 8, cut] = jnp.where(high, loads[0], turned[1])
                out[1, a, tile * 8 : tile * 8 + 8, cut] = jnp.where(high, turned[0], loads[1])
        return carry

    def emit_some(n, carry):
        for u in range(4):
            emit(n * 4 + u, carry)
        return carry

    lax.fori_loop(0, own // 4, emit_some, 0)


def assemble(near, far, terms, sets, order, own, span, scale):
    return pl.pallas_call(
        functools.partial(assemble_kernel, own, span, scale, sets, order, terms),
        out_shape=jax.ShapeDtypeStruct((2, own, 2 * own, span * RADIX), jnp.float32),
        in_specs=[VMEM] * (len(near) + len(far)),
        out_specs=VMEM,
        scratch_shapes=[pltpu.VMEM((own * 2 * own * span, LANES), jnp.float32)],
        compiler_params=params(12),
        cost_estimate=cost(10**6, 2**18),
        name="assemble",
    )(*near, *far)


def fast_fits(in_count, frame_count):
    stn, tm, per_ct = (lax.axis_size(a) for a in ("stn", "tm", "ct"))
    groups = tm * per_ct
    if stn != 2 or tm % PAIR or in_count % (PAIR * JOIN) or RADIX % groups:
        return False
    outer, span = tm // PAIR, RADIX // groups
    own = in_count * per_ct
    return (
        frame_count >= TAPS
        and frame_count % (2 * SOME) == 0
        and outer == 4
        and span == 4
        and outer * span % 16 == 0
        and own % (PAIR * JOIN * 2 * TILE // 4) == 0
        and in_count == PAIR * JOIN * 2
        and per_ct * PAIR * JOIN % (2 * TILE) == 0
        and all(pairs_in(s) * span % 16 == 0 for s in pair_sets(own, 2))
    )


def fast(voltages, delays):
    tm, per_ct = lax.axis_size("tm"), lax.axis_size("ct")
    in_count = voltages.shape[1]
    frame_count = voltages.shape[2] // CHANNELS
    outer = tm // PAIR
    span = RADIX // (tm * per_ct)
    own = in_count * per_ct
    half = in_count // PAIR
    place_tm, place_ct = lax.axis_index("tm"), lax.axis_index("ct")
    g = place_tm % PAIR

    swap = [(i, i ^ 1) for i in range(tm)]
    onward = [(i, i + PAIR) for i in range(tm - PAIR)]
    cores = [(0, 1), (1, 0)]

    dests = [(dg, dc) for dg in range(PAIR) for dc in range(per_ct)]
    base = last_table(outer, per_ct, span)
    tables = [np.concatenate([filter_table()] * 2, axis=1), first_table(), *twiddle_tables()]
    tables = [jnp.asarray(t) for t in tables + [np.concatenate([base, base], axis=1)]]

    parts = half // JOIN
    picked = pick(voltages)
    sends, keeps = picked[:parts], picked[parts:]
    recvs = [lax.ppermute(block, "tm", swap) for block in sends]
    halos, lates = [], []
    for c in range(parts):
        recv = follow(recvs[c], lates[-1]) if lates else recvs[c]
        halos.append(lax.ppermute(jnp.where(g == 1, keeps[c], recv), "tm", onward))
        sources = [keeps[c], follow(recvs[c], halos[c - 1]) if c else recvs[c]]
        lates.append(filterbank(c, half, delays, sources, tables, [], len(dests)))

    sets = pair_sets(own, parts)
    sizes = (outer, span, per_ct)
    received = []
    for c in range(parts):
        halo = follow(halos[c], recvs[c + 1]) if c + 1 < parts else halos[c]
        sources = [halo, keeps[c], recvs[c]]
        spectra = filterbank(c, half, delays, sources, tables, lates[c], len(dests))
        arrays = []
        for n, ((dg, dc), block) in enumerate(zip(dests, spectra)):
            route = []
            for i in range(tm):
                for j in range(per_ct):
                    target = (i ^ dg) * per_ct + (j + dc) % per_ct
                    route.append((i * per_ct + j, target))
            if dg or dc:
                block = follow(block, received[-1][n]) if received else block
                block = lax.ppermute(block, ("tm", "ct"), route)
            arrays.append(block)
        received.append(arrays)

    def along(block, x):
        route = [(i, ((i // PAIR) ^ x) * PAIR + i % PAIR) for i in range(tm)]
        return lax.ppermute(block, "tm", route)

    near = [joined([follow(block, spectra[0]) for block in received[0]])]
    far = [lax.ppermute(near[0], "stn", cores)]
    early = correlate(
        near + far, [(False, 0), (True, 0)], sets[0], own // parts, (0, 1, 2, 3), sizes,
        "correlate_early",
    )
    early = [*early[:2], *[along(early[x], x) for x in (2, 3)]]
    near.append(joined([follow(block, early[2:]) for block in received[1]]))
    far.append(lax.ppermute(near[1], "stn", cores))
    sources_at = [(False, c) for c in range(parts)] + [(True, c) for c in range(parts)]
    beyond = correlate(near, sources_at[:parts], sets[1], own, (2, 3), sizes, "far_own")
    beyond = correlate(
        near + far, sources_at, sets[2], own, (2, 3), sizes, "far_cross", beyond
    )
    sets = [sets[0], sets[1] + sets[2]]
    near[0] = follow(near[0], beyond[0])
    kept, beside = correlate(
        near + far, sources_at, sets[1], own, (0, 1), sizes, "correlate_near", early[:2]
    )
    beyond = [along(block, x) for block, x in zip(beyond, (2, 3))]
    beside = along(beside, 1)
    beyond = summed(early[2:], beyond)
    mine = [kept, beside, beyond]
    after = [kept, follow(beside, beyond), beyond]
    theirs = [lax.ppermute(block, "stn", cores) for block in after]
    first = pairs_in(sets[0]) * span
    terms = [[(n, low) for n in range(3)] for low in (0, first)]
    order = []
    for part in range(parts):
        for device in range(per_ct * PAIR):
            start = device // PAIR * in_count + device % PAIR * half + part * JOIN
            order += range(start, start + JOIN)
    scale = 1.0 / (tm * frame_count)
    result = assemble(mine, theirs, terms, sets, order, own, span, scale)
    return result.transpose(0, 3, 1, 2)


def general(voltages, delays):
    in_count = voltages.shape[1]
    frame_count = voltages.shape[2] // CHANNELS
    route = [(i, i + 1) for i in range(lax.axis_size("tm") - 1)]
    extended = jnp.concatenate([lax.ppermute(voltages, "tm", route), voltages], axis=2)
    span = (frame_count + TAPS - 1) * CHANNELS
    shifted = jax.vmap(
        lambda row, offset: lax.dynamic_slice_in_dim(row, CHANNELS - offset, span, 1),
        in_axes=(1, 0),
        out_axes=1,
    )(extended, delays)
    framed = shifted.reshape(2, in_count, frame_count + TAPS - 1, CHANNELS)
    table = jnp.asarray(filter_table()).reshape(TAPS, CHANNELS)
    total = jnp.zeros((2, in_count, frame_count, CHANNELS), jnp.float32)
    for tap in range(TAPS):
        low = TAPS - 1 - tap
        total = total + table[tap] * framed[:, :, low : low + frame_count].astype(jnp.float32)
    branches = jnp.moveaxis(total.astype(jnp.bfloat16), 0, 2)

    number = in_count * frame_count
    cosine, sine = dft_parts(RADIX)
    block = np.concatenate(
        [np.concatenate([cosine, sine], axis=1), np.concatenate([-sine, cosine], axis=1)], axis=0
    )
    block = jnp.asarray(block)
    stacked = branches.reshape(number, 2 * RADIX, RADIX)
    inner = jnp.einsum("kj,nja->nka", block, stacked, preferred_element_type=jnp.float32)
    inner = inner.reshape(number, 2, RADIX, RADIX)
    tw_cos, tw_sin = (jnp.asarray(t[:, :RADIX]) for t in twiddle_tables())
    real = inner[:, 0] * tw_cos + inner[:, 1] * tw_sin
    imag = inner[:, 1] * tw_cos - inner[:, 0] * tw_sin
    turned = jnp.stack([real, imag], axis=2).reshape(number, RADIX, 2 * RADIX)
    turned = turned.astype(jnp.bfloat16)
    result = jnp.einsum("lj,nkj->nlk", block, turned, preferred_element_type=jnp.float32)
    spectra = result.reshape(in_count, frame_count, 2, CHANNELS).astype(jnp.bfloat16)
    moved = lax.all_to_all(spectra, "tm", split_axis=3, concat_axis=1, tiled=True)
    moved = lax.all_to_all(moved, "ct", split_axis=3, concat_axis=0, tiled=True)
    local = moved.transpose(3, 2, 0, 1)
    swapped = jnp.stack([local[:, 1], -local[:, 0]], axis=1)
    summed = jnp.einsum(
        "ocjaf,cjbf->ocab",
        jnp.stack([local, swapped], axis=0),
        lax.all_gather(local, "stn", axis=2, tiled=True),
        preferred_element_type=jnp.float32,
    )
    return summed * (1.0 / local.shape[3])


def on_device(voltages, delays):
    if fast_fits(voltages.shape[1], voltages.shape[2] // CHANNELS):
        return fast(voltages, delays)
    return general(voltages, delays)


def solution(mesh):
    return jax.shard_map(
        on_device,
        mesh=mesh,
        in_specs=(P(None, ("stn", "ct"), "tm"), P(("stn", "ct"))),
        out_specs=P(None, ("tm", "ct"), "stn", None),
        check_vma=False,
    )
```

```python
import functools
import math

import jax
import jax.numpy as jnp
import numpy as np
from jax import lax
from jax.experimental import pallas as pl
from jax.experimental.pallas import tpu as pltpu
from jax.sharding import PartitionSpec as P

CHANNELS = 4096
RADIX = 64
TAPS = 16
LANES = 128
ROWS = CHANNELS // LANES
PAIR = 2
TILE = 4
JOIN = 2

VMEM = pl.BlockSpec(memory_space=pltpu.VMEM)
SMEM = pl.BlockSpec(memory_space=pltpu.SMEM)


def params(mib):
    return pltpu.CompilerParams(vmem_limit_bytes=mib * 2**20)


def position():
    place = lax.axis_index("tm")
    return lax.axis_index("stn"), place // PAIR, place % PAIR, lax.axis_index("ct")


def cost(flops, size):
    return pl.CostEstimate(flops=flops, bytes_accessed=size, transcendentals=0)


def filter_table():
    length = TAPS * CHANNELS
    index = np.arange(length, dtype=np.float64)
    centred = (index - length / 2) / CHANNELS
    window = 0.5 - 0.5 * np.cos(2.0 * math.pi * index / length)
    factor = 1.0 / (48.0 * math.sqrt(CHANNELS))
    table = np.sinc(centred) * window * factor
    return table.reshape(TAPS, ROWS, LANES).astype(np.float32)


def dft_parts(radix):
    steps = np.arange(radix)
    angle = 2.0 * math.pi * (steps[:, None] * steps[None, :] % radix) / radix
    return np.cos(angle).astype(jnp.bfloat16), np.sin(angle).astype(jnp.bfloat16)


def first_table():
    cosine, sine = dft_parts(CHANNELS // RADIX)
    order = [2 * row + half for half in range(2) for row in range(ROWS)]
    cosine, sine = cosine[:, order], sine[:, order]
    upper = np.concatenate([cosine, sine], axis=1)
    lower = np.concatenate([-sine, cosine], axis=1)
    return np.concatenate([upper, lower], axis=0)


def last_table(outer, per_ct, span):
    cosine, sine = dft_parts(RADIX)
    blocks = []
    for g in range(PAIR):
        for ct in range(per_ct):
            steps = [
                ((o * PAIR + g) * per_ct + ct) * span + j for o in range(outer) for j in range(span)
            ]
            real = np.concatenate([cosine[steps], sine[steps]], axis=1)
            imag = np.concatenate([-sine[steps], cosine[steps]], axis=1)
            blocks.append(np.concatenate([real, imag], axis=0))
    return np.stack(blocks).reshape(PAIR, per_ct, -1, 2 * RADIX)


def twiddle_tables():
    rows = np.arange(CHANNELS // RADIX)
    cols = np.arange(RADIX)
    angle = 2.0 * math.pi * (rows[:, None] * cols[None, :] % CHANNELS) / CHANNELS
    cosine = np.cos(angle).astype(np.float32)
    sine = np.sin(angle).astype(np.float32)
    return np.concatenate([cosine, cosine], axis=1), np.concatenate([sine, sine], axis=1)


def pick_kernel(half, block, *refs):
    outs, rows = refs[:-1], refs[-1]
    inputs, samples = block.shape[1], block.shape[2]
    step = 32
    for part in range(2):

        def spread(n, carry, part=part):
            low = pl.multiple_of(n * step * LANES, step * LANES)
            wide = block[part, :, pl.ds(low, step * LANES)].astype(jnp.float32)
            for u in range(step):
                at = pl.multiple_of((n * step + u) * inputs, inputs)
                rows[part, pl.ds(at, inputs), :] = wide[:, u * LANES : (u + 1) * LANES]
            return carry

        lax.fori_loop(0, samples // LANES // step, spread, 0)
    g = position()[2]
    tall = 64

    def gather(n, carry):
        low = pl.multiple_of(n * tall, tall)
        for item in range(inputs):
            first = (1 - g) * half + item if item < half else g * half + item - half
            for part in range(2):
                at = low * inputs + first
                value = rows[part, pl.ds(at, tall, stride=inputs), :].astype(jnp.bfloat16)
                outs[item // JOIN][item % JOIN, part, pl.ds(low, tall), :] = value
        return carry

    lax.fori_loop(0, samples // LANES // tall, gather, 0)


def pick(block):
    _, inputs, samples = block.shape
    shape = jax.ShapeDtypeStruct((JOIN, 2, samples // LANES, LANES), jnp.bfloat16)
    return pl.pallas_call(
        functools.partial(pick_kernel, inputs // PAIR),
        out_shape=[shape] * (inputs // JOIN),
        in_specs=[VMEM],
        out_specs=[VMEM] * (inputs // JOIN),
        scratch_shapes=[pltpu.VMEM((2, samples // LANES * inputs, LANES), jnp.float32)],
        compiler_params=params(16),
        cost_estimate=cost(10**6, 2**18),
        name="pick",
    )(block)


def follow(block, after):
    return lax.optimization_barrier((block, after))[0]


def joined(blocks):
    def kernel(*refs):
        sources, out = refs[:-1], refs[-1]
        for n, source in enumerate(sources):
            size = source.shape[0]
            for item in range(size):

                def step(m, carry, n=n, source=source, size=size, item=item):
                    cut = pl.ds(m * 4, 4)
                    out[n * size + item, cut] = source[item, cut]
                    return carry

                lax.fori_loop(0, source.shape[1] // 4, step, 0)

    shape = (sum(block.shape[0] for block in blocks),) + blocks[0].shape[1:]
    return pl.pallas_call(
        kernel,
        out_shape=jax.ShapeDtypeStruct(shape, blocks[0].dtype),
        in_specs=[VMEM] * len(blocks),
        out_specs=VMEM,
        compiler_params=params(8),
        cost_estimate=cost(10**6, 2**18),
        name="join",
    )(*blocks)


SOME = 4


def filterbank_kernel(late, part, frames, dests, per_ct, half_count, *refs):
    delays, refs = refs[0], refs[1:]
    _, _, me, ct = position()
    if late:
        keep, recv = refs[:2]
        refs = refs[2:]
    else:
        halo, keep, recv = refs[:3]
        refs = refs[3:]
    coef, first, tw_cos, tw_sin, last = refs[:5]
    beside = () if late else refs[5 : 5 + dests]
    outs = refs[5 + len(beside) :][:dests]
    raw, weights, grouped = refs[5 + len(beside) + dests :][:3]
    filtered = refs[5 + len(beside) + dests + 3 :]
    block_rows = frames * ROWS
    lane = lax.broadcasted_iota(jnp.int32, (1, LANES), 1)
    high = lane < RADIX

    def bring(source, place):
        tall = 128

        def step(n, carry):
            low = pl.multiple_of(n * tall, tall)
            at = pl.multiple_of(place * block_rows + n * tall, tall)
            for item in range(JOIN):
                for c in range(2):
                    raw[item, c, pl.ds(at, tall), :] = source[item, c, pl.ds(low, tall), :]
            return carry

        lax.fori_loop(0, block_rows // tall, step, 0)

    if late:
        bring(keep, me)
        bring(recv, 1 - me)
    else:
        bring(halo, 0)
        pl.when(me == 0)(lambda: bring(keep, 1))
        pl.when(me != 0)(lambda: bring(recv, 1))
        for dest, block in zip(outs, beside):
            dest[:, frames // 2 :] = block[...]

    downs, acrosses = [], []
    for item in range(JOIN):
        delay = delays[me * half_count + part * JOIN + item]
        down, across = delay // LANES, delay % LANES
        downs.append(down)
        acrosses.append(across)
        back = lax.rem(LANES - across, LANES)
        for tap in range(TAPS):
            here = coef[tap, pl.ds(down, ROWS), :]
            after = coef[tap, pl.ds(down + 1, ROWS), :]
            turned = pltpu.roll(jnp.where(lane >= across, here, after), back, 1)
            weights[item, tap] = turned

    def filt(item, low, end, band, c):
        size = end - low
        values = []
        for u in range(size + TAPS - 1):
            at = (low + u + frames - TAPS) * ROWS + band * 16
            values.append(raw[item, c, at : at + 16, :].astype(jnp.float32))
        sums = [None] * size
        for tap in range(TAPS):
            weight = weights[item, tap, band * 16 : band * 16 + 16, :]
            for u in range(size):
                term = weight * values[u + TAPS - 1 - tap]
                sums[u] = term if sums[u] is None else sums[u] + term
        for u in range(size):
            at = (low + u) * ROWS + band * 16
            filtered[item][c, at : at + 16, :] = sums[u]

    def place(item, u):
        down, across = downs[item], acrosses[item]
        twice = lax.rem(across + RADIX, LANES)
        inside = lane < LANES - across
        for band in range(ROWS // 16):
            at = (u + 1) * ROWS + band * 16 - down
            moved, turned = [], []
            for c in range(2):
                here = filtered[item][c, pl.ds(at, 16), :]
                above = filtered[item][c, pl.ds(at - 1, 16), :]
                value = jnp.where(inside, here, above)
                moved.append(pltpu.roll(value, across, 1))
                turned.append(pltpu.roll(value, twice, 1))
            parts = (
                jnp.where(high, moved[0], turned[1]),
                jnp.where(high, turned[0], moved[1]),
                jnp.where(high, moved[1], -turned[0]),
                jnp.where(high, turned[1], -moved[0]),
            )
            for which, value in enumerate(parts):
                low = which * ROWS + band * 16
                grouped[item, u, low : low + 16, :] = value.astype(jnp.bfloat16)

    rows_out = jnp.concatenate(
        [last[me ^ dg, ct + dc] for dg in range(PAIR) for dc in range(per_ct)], axis=0
    )

    def turn(item, base):
        wide = jnp.concatenate([grouped[item, base + u] for u in range(SOME)], axis=1)
        inner = jnp.dot(first[...], wide, preferred_element_type=jnp.float32)
        rows = []
        for u in range(SOME):
            cut = slice(u * LANES, (u + 1) * LANES)
            value = inner[:RADIX, cut] * tw_cos[...] + inner[RADIX:, cut] * tw_sin[...]
            rows.append(value.astype(jnp.bfloat16))
        inner = jnp.concatenate(rows, axis=0)
        result = lax.dot_general(
            rows_out, inner, (((1,), (1,)), ((), ())), preferred_element_type=jnp.float32
        ).astype(jnp.bfloat16)
        size = result.shape[0] // (2 * dests)
        for dest in range(dests):
            for c in range(2):
                low = (dest * 2 + c) * size
                for u in range(SOME // 2):
                    outs[dest][item, base // 2 + u, c] = result[
                        low : low + size, u * LANES : (u + 1) * LANES
                    ]

    pieces = [
        (low, end, band, c)
        for low, end in ((0, frames // 2 + 1), (frames // 2 + 1, frames + 1))
        for band in range(ROWS // 16)
        for c in range(2)
    ]
    groups = frames // SOME
    each = len(pieces) // groups
    for item in range(JOIN + 1):
        for n in range(groups):
            if item < JOIN:
                for piece in pieces[n * each : (n + 1) * each]:
                    filt(item, *piece)
            if item:
                for u in range(SOME):
                    place(item - 1, n * SOME + u)
                turn(item - 1, n * SOME)


def filterbank(part, half, delays, sources, tables, beside, dests):
    late = not beside
    frames = sources[0].shape[2] // ROWS
    size = tables[-1].shape[2] // 2
    per_ct = tables[-1].shape[1] // 2
    pairs = frames // 2 if late else frames
    shape = (JOIN, pairs, 2, size, LANES)
    kernel = functools.partial(filterbank_kernel, late, part, frames, dests, per_ct, half)
    return pl.pallas_call(
        kernel,
        out_shape=[jax.ShapeDtypeStruct(shape, jnp.bfloat16)] * dests,
        in_specs=[SMEM] + [VMEM] * (len(sources) + 5 + len(beside)),
        out_specs=[VMEM] * dests,
        scratch_shapes=[
            pltpu.VMEM((JOIN, 2, 2 * frames * ROWS, LANES), jnp.bfloat16),
            pltpu.VMEM((JOIN, TAPS, ROWS, LANES), jnp.float32),
            pltpu.VMEM((JOIN, frames, LANES, LANES), jnp.bfloat16),
        ]
        + [pltpu.VMEM((2, (frames + 1) * ROWS, LANES), jnp.float32)] * JOIN,
        compiler_params=params(14),
        cost_estimate=cost(10**6, 2**18),
        name="filterbank_late" if late else "filterbank_early",
    )(delays, *sources, *tables, *beside)


SQUARE = [(p, q) for p in range(TILE) for q in range(TILE)]
CORNER = [(p, q) for p in range(TILE) for q in range(p, TILE)]


def pair_sets(own, parts):
    tiles = own // TILE
    per = tiles // parts
    whole = [(True, i, j, SQUARE) for i in range(tiles) for j in range(i + 1, tiles)]
    corner = [(True, i, i, CORNER) for i in range(tiles)]
    across = [(False, i, j, SQUARE) for i in range(0, tiles, 2) for j in range(tiles)]

    def early(block):
        return block[1] < per and block[2] < per

    def late(blocks):
        return [block for block in blocks if not early(block)]

    first = [block for block in whole + across + corner if early(block)]
    return [first, late(whole + corner), late(across)]


def pairs_in(blocks):
    return sum(len(block[3]) for block in blocks)


def chosen(t, values):
    result = jnp.int32(values[0])
    for n, value in enumerate(values[1:], 1):
        result = jnp.where(t == n, jnp.int32(value), result)
    return result


def correlate_kernel(layout, *refs):
    sources_at, blocks, own, owners, outer, span, per_ct = layout
    sources, rest = refs[: len(sources_at)], refs[len(sources_at) :]
    outs, (spectra, sums, held) = rest[-3 - len(owners) : -3], rest[-3:]
    earlier = rest[: -3 - len(owners)]
    steps, size = spectra.shape[1], spectra.shape[3]
    core, o, g, ct = position()
    whole = size == outer * span
    base_owner = 0 if whole else (o // 2 if 0 in owners else 1 - o // 2) * 2
    within = any(block[0] for block in blocks)
    across = any(not block[0] for block in blocks)

    for source, (far, part) in zip(sources, sources_at):
        for n in range(PAIR * per_ct):
            dg, dc = n // per_ct, n % per_ct
            device = lax.rem(ct - dc + per_ct, per_ct) * PAIR + (g ^ dg)
            base = (part * per_ct * PAIR + device) * JOIN
            wanted = None
            side = 1 - core if far else core
            if far or not within:
                wanted = (side == 1) | (lax.rem(base // TILE, 2) == core)
            base = base + side * own

            def bring(source=source, base=base, n=n):
                for item in range(JOIN):

                    def spread(m, carry, item=item):
                        for u in range(8):
                            parts = []
                            for c in range(2):
                                value = source[n * JOIN + item, m * 8 + u, c].astype(jnp.float32)
                                if not whole:
                                    value = jnp.where(base_owner == 0, value[:size], value[size:])
                                parts.append(value)
                            real, imag = parts
                            for which, value in enumerate((real, imag, real + imag, imag - real)):
                                spectra[base + item, m * 8 + u, which] = value
                        return carry

                    lax.fori_loop(0, steps // 8, spread, 0)

            if wanted is None:
                bring()
            else:
                pl.when(wanted)(bring)

    high = lax.broadcasted_iota(jnp.int32, (1, LANES), 1) < RADIX
    rows_outer = pairs_in(blocks) * span
    unroll = 4 if whole else 8

    def block(left, right, pairs, first_row):
        def over(one, two, acc, sign):
            def frame(n, acc):
                acc = list(acc)
                for u in range(unroll):
                    a = [spectra[left + p, n * unroll + u, one] for p in range(TILE)]
                    b = [spectra[right + q, n * unroll + u, two] for q in range(TILE)]
                    for at, (p, q) in enumerate(pairs):
                        term = a[p] * b[q]
                        acc[at] = acc[at] + term if sign > 0 else acc[at] - term
                return tuple(acc)

            return lax.fori_loop(0, steps // unroll, frame, tuple(acc))

        count = len(pairs)
        first = over(2, 0, [jnp.zeros((size, LANES), jnp.float32)] * count, 1)
        for at in range(count):
            held[0, at] = first[at]
        real = over(1, 3, first, 1)
        for at in range(count):
            held[1, at] = real[at] + pltpu.roll(real[at], RADIX, 1)
        imag = over(0, 2, [held[0, at] for at in range(count)], -1)
        for at in range(count):
            folded = imag[at] + pltpu.roll(imag[at], RADIX, 1)
            both = jnp.where(high, held[1, at], folded)
            for u in range(size // span):
                row = u * rows_outer + first_row + at * span
                sums[pl.ds(pl.multiple_of(row, span), span), :] = both[u * span : (u + 1) * span]

    done = 0
    while done < len(blocks):
        kind = (blocks[done][0], blocks[done][3])
        end = done
        while end < len(blocks) and (blocks[end][0], blocks[end][3]) == kind:
            end += 1
        run, row = blocks[done:end], pairs_in(blocks[:done]) * span

        def step(t, carry, run=run, row=row, kind=kind):
            left, right = chosen(t, [b[1] for b in run]), chosen(t, [b[2] for b in run])
            if not kind[0]:
                left, right = TILE * (left + core), own + TILE * right
            else:
                left, right = core * own + TILE * left, core * own + TILE * right
            block(left, right, kind[1], row + t * len(kind[1]) * span)
            return carry

        lax.fori_loop(0, len(run), step, 0)
        done = end

    before = earlier[0].shape[0] if earlier else 0
    for n, x in enumerate(owners):
        at = pl.multiple_of(((o ^ x) - base_owner) * rows_outer, 16)
        outs[n][before:, :] = sums[pl.ds(at, rows_outer), :].astype(outs[n].dtype)
        if earlier:
            outs[n][:before, :] = earlier[n][...]


def correlate(arrays, sources_at, blocks, own, owners, sizes, name, earlier=()):
    outer, span, _ = sizes
    _, steps, _, size, _ = arrays[0].shape
    if len(owners) < outer:
        size = 2 * span
    rows = pairs_in(blocks) * span
    before = earlier[0].shape[0] if earlier else 0
    types = [jnp.bfloat16 if x else jnp.float32 for x in owners]
    scratch = pltpu.VMEM((2 * own, steps, 4, size, LANES), jnp.float32)
    layout = (sources_at, blocks, own, owners) + sizes
    return pl.pallas_call(
        functools.partial(correlate_kernel, layout),
        out_shape=[jax.ShapeDtypeStruct((before + rows, LANES), dtype) for dtype in types],
        in_specs=[VMEM] * (len(arrays) + len(earlier)),
        out_specs=[VMEM] * len(owners),
        scratch_shapes=[
            scratch,
            pltpu.VMEM((size // span * rows, LANES), jnp.float32),
            pltpu.VMEM((2, TILE * TILE, size, LANES), jnp.float32),
        ],
        compiler_params=params(12 + 2 * own * steps * 4 * size * LANES * 4 // 2**20),
        cost_estimate=cost(10**6, 2**18),
        name=name,
    )(*arrays, *earlier)


def summed(early, late):
    def kernel(*refs):
        out = refs[-1]
        split = refs[0].shape[0]
        out[:split, :] = refs[0][...].astype(jnp.float32) + refs[1][...].astype(jnp.float32)
        out[split:, :] = refs[2][...].astype(jnp.float32) + refs[3][...].astype(jnp.float32)

    rows = early[0].shape[0] + late[0].shape[0]
    return pl.pallas_call(
        kernel,
        out_shape=jax.ShapeDtypeStruct((rows, LANES), jnp.float32),
        in_specs=[VMEM] * 4,
        out_specs=VMEM,
        compiler_params=params(8),
        cost_estimate=cost(10**6, 36 * 2**20),
        name="sum_far",
    )(*early, *late)


def assemble_kernel(own, span, scale, sets, order, terms, *refs):
    out, joined = refs[-2:]
    count = len(refs) // 2 - 1
    near = [[(refs[n], low) for n, low in term] for term in terms]
    far = [[(refs[count + n], low) for n, low in term] for term in terms]
    lane = lax.broadcasted_iota(jnp.int32, (1, LANES), 1)
    high = lane < RADIX
    mirror = jnp.where(high, 1.0, -1.0).astype(jnp.float32)
    me = position()[0]
    across = 2 * own * span
    mine_at = pl.multiple_of(me * own * span, 8)

    def added(parts, low, rows):
        total = None
        for ref, first in parts:
            term = ref[first + low : first + low + rows, :].astype(jnp.float32)
            total = term if total is None else total + term
        return total * scale

    def put(value, places, base=0):
        n = 0
        while n < len(places):
            wide = 1
            if places[n] % 8 == 0 and places[n + 1 : n + 2] == [places[n] + span] and span < 8:
                wide = 2
            rows = value[n * span : (n + wide) * span]
            joined[pl.ds(base + places[n], wide * span), :] = rows
            n += wide

    def inner(total, i, j, pairs):
        direct = [order[i * TILE + p] * across + order[j * TILE + q] * span for p, q in pairs]
        turned = [order[j * TILE + q] * across + order[i * TILE + p] * span for p, q in pairs]
        put(total, direct, mine_at)
        for n, (p, q) in enumerate(pairs):
            if (i, p) != (j, q):
                value = total[n * span : (n + 1) * span] * mirror
                put(value, [turned[n]], mine_at)

    def outer_pairs(core):
        for blocks, mine, others in zip(sets, near, far):
            low = 0
            for within, i, j, pairs in blocks:
                rows = len(pairs) * span
                if not within:
                    for parts, side in ((mine, core), (others, 1 - core)):
                        total = added(parts, low, rows)
                        a = [order[(i + side) * TILE + p] for p, _ in pairs]
                        b = [order[j * TILE + q] for _, q in pairs]
                        if core == 0:
                            put(total, [x * across + (own + y) * span for x, y in zip(a, b)])
                        else:
                            total = total * mirror
                            put(total, [y * across + x * span for x, y in zip(a, b)])
                low += rows

    for blocks, mine in zip(sets, near):
        low = 0
        for within, i, j, pairs in blocks:
            rows = len(pairs) * span
            if within:
                inner(added(mine, low, rows), i, j, pairs)
            low += rows
    pl.when(me == 0)(lambda: outer_pairs(0))
    pl.when(me != 0)(lambda: outer_pairs(1))

    def emit(a, carry):
        for tile in range(2 * own // 8):
            for pair in range(span // 2):
                loads = []
                for u in range(2):
                    at = (a * 2 * own + tile * 8) * span + pair * 2 + u
                    loads.append(joined[pl.ds(at, 8, stride=span), :])
                turned = [pltpu.roll(x, RADIX, 1) for x in loads]
                cut = slice(pair * LANES, (pair + 1) * LANES)
                out[0, a, tile * 8 : tile * 8 + 8, cut] = jnp.where(high, loads[0], turned[1])
                out[1, a, tile * 8 : tile * 8 + 8, cut] = jnp.where(high, turned[0], loads[1])
        return carry

    def emit_some(n, carry):
        for u in range(4):
            emit(n * 4 + u, carry)
        return carry

    lax.fori_loop(0, own // 4, emit_some, 0)


def assemble(near, far, terms, sets, order, own, span, scale):
    return pl.pallas_call(
        functools.partial(assemble_kernel, own, span, scale, sets, order, terms),
        out_shape=jax.ShapeDtypeStruct((2, own, 2 * own, span * RADIX), jnp.float32),
        in_specs=[VMEM] * (len(near) + len(far)),
        out_specs=VMEM,
        scratch_shapes=[pltpu.VMEM((own * 2 * own * span, LANES), jnp.float32)],
        compiler_params=params(12),
        cost_estimate=cost(10**6, 2**18),
        name="assemble",
    )(*near, *far)


def fast_fits(in_count, frame_count):
    stn, tm, per_ct = (lax.axis_size(a) for a in ("stn", "tm", "ct"))
    groups = tm * per_ct
    if stn != 2 or tm % PAIR or in_count % (PAIR * JOIN) or RADIX % groups:
        return False
    outer, span = tm // PAIR, RADIX // groups
    own = in_count * per_ct
    return (
        frame_count >= TAPS
        and frame_count % (2 * SOME) == 0
        and outer == 4
        and span == 4
        and outer * span % 16 == 0
        and own % (PAIR * JOIN * 2 * TILE // 4) == 0
        and in_count == PAIR * JOIN * 2
        and per_ct * PAIR * JOIN % (2 * TILE) == 0
        and all(pairs_in(s) * span % 16 == 0 for s in pair_sets(own, 2))
    )


def fast(voltages, delays):
    tm, per_ct = lax.axis_size("tm"), lax.axis_size("ct")
    in_count = voltages.shape[1]
    frame_count = voltages.shape[2] // CHANNELS
    outer = tm // PAIR
    span = RADIX // (tm * per_ct)
    own = in_count * per_ct
    half = in_count // PAIR
    place_tm, place_ct = lax.axis_index("tm"), lax.axis_index("ct")
    g = place_tm % PAIR

    swap = [(i, i ^ 1) for i in range(tm)]
    onward = [(i, i + PAIR) for i in range(tm - PAIR)]
    cores = [(0, 1), (1, 0)]

    dests = [(dg, dc) for dg in range(PAIR) for dc in range(per_ct)]
    base = last_table(outer, per_ct, span)
    tables = [np.concatenate([filter_table()] * 2, axis=1), first_table(), *twiddle_tables()]
    tables = [jnp.asarray(t) for t in tables + [np.concatenate([base, base], axis=1)]]

    parts = half // JOIN
    picked = pick(voltages)
    sends, keeps = picked[:parts], picked[parts:]
    recvs = [lax.ppermute(block, "tm", swap) for block in sends]
    halos, lates = [], []
    for c in range(parts):
        recv = follow(recvs[c], lates[-1]) if lates else recvs[c]
        halos.append(lax.ppermute(jnp.where(g == 1, keeps[c], recv), "tm", onward))
        sources = [keeps[c], follow(recvs[c], halos[c - 1]) if c else recvs[c]]
        lates.append(filterbank(c, half, delays, sources, tables, [], len(dests)))

    sets = pair_sets(own, parts)
    sizes = (outer, span, per_ct)
    received = []
    for c in range(parts):
        halo = follow(halos[c], recvs[c + 1]) if c + 1 < parts else halos[c]
        sources = [halo, keeps[c], recvs[c]]
        spectra = filterbank(c, half, delays, sources, tables, lates[c], len(dests))
        arrays = []
        for n, ((dg, dc), block) in enumerate(zip(dests, spectra)):
            route = []
            for i in range(tm):
                for j in range(per_ct):
                    target = (i ^ dg) * per_ct + (j + dc) % per_ct
                    route.append((i * per_ct + j, target))
            if dg or dc:
                block = follow(block, received[-1][n]) if received else block
                block = lax.ppermute(block, ("tm", "ct"), route)
            arrays.append(block)
        received.append(arrays)

    def along(block, x):
        route = [(i, ((i // PAIR) ^ x) * PAIR + i % PAIR) for i in range(tm)]
        return lax.ppermute(block, "tm", route)

    near = [joined([follow(block, spectra[0]) for block in received[0]])]
    far = [lax.ppermute(near[0], "stn", cores)]
    early = correlate(
        near + far, [(False, 0), (True, 0)], sets[0], own // parts, (0, 1, 2, 3), sizes,
        "correlate_early",
    )
    early = [*early[:2], *[along(early[x], x) for x in (2, 3)]]
    near.append(joined([follow(block, early[3]) for block in received[1]]))
    far.append(lax.ppermute(near[1], "stn", cores))
    sources_at = [(False, c) for c in range(parts)] + [(True, c) for c in range(parts)]
    beyond = correlate(near, sources_at[:parts], sets[1], own, (2, 3), sizes, "far_own")
    far[1] = follow(far[1], early[2])
    beyond = correlate(
        near + far, sources_at, sets[2], own, (2, 3), sizes, "far_cross", beyond
    )
    sets = [sets[0], sets[1] + sets[2]]
    near[0] = follow(near[0], beyond[0])
    kept, beside = correlate(
        near + far, sources_at, sets[1], own, (0, 1), sizes, "correlate_near", early[:2]
    )
    beyond = [along(block, x) for block, x in zip(beyond, (2, 3))]
    beside = along(beside, 1)
    beyond = summed(early[2:], beyond)
    mine = [kept, beside, beyond]
    after = [kept, follow(beside, beyond), beyond]
    theirs = [lax.ppermute(block, "stn", cores) for block in after]
    first = pairs_in(sets[0]) * span
    terms = [[(n, low) for n in range(3)] for low in (0, first)]
    order = []
    for part in range(parts):
        for device in range(per_ct * PAIR):
            start = device // PAIR * in_count + device % PAIR * half + part * JOIN
            order += range(start, start + JOIN)
    scale = 1.0 / (tm * frame_count)
    result = assemble(mine, theirs, terms, sets, order, own, span, scale)
    return result.transpose(0, 3, 1, 2)


def general(voltages, delays):
    in_count = voltages.shape[1]
    frame_count = voltages.shape[2] // CHANNELS
    route = [(i, i + 1) for i in range(lax.axis_size("tm") - 1)]
    extended = jnp.concatenate([lax.ppermute(voltages, "tm", route), voltages], axis=2)
    span = (frame_count + TAPS - 1) * CHANNELS
    shifted = jax.vmap(
        lambda row, offset: lax.dynamic_slice_in_dim(row, CHANNELS - offset, span, 1),
        in_axes=(1, 0),
        out_axes=1,
    )(extended, delays)
    framed = shifted.reshape(2, in_count, frame_count + TAPS - 1, CHANNELS)
    table = jnp.asarray(filter_table()).reshape(TAPS, CHANNELS)
    total = jnp.zeros((2, in_count, frame_count, CHANNELS), jnp.float32)
    for tap in range(TAPS):
        low = TAPS - 1 - tap
        total = total + table[tap] * framed[:, :, low : low + frame_count].astype(jnp.float32)
    branches = jnp.moveaxis(total.astype(jnp.bfloat16), 0, 2)

    number = in_count * frame_count
    cosine, sine = dft_parts(RADIX)
    block = np.concatenate(
        [np.concatenate([cosine, sine], axis=1), np.concatenate([-sine, cosine], axis=1)], axis=0
    )
    block = jnp.asarray(block)
    stacked = branches.reshape(number, 2 * RADIX, RADIX)
    inner = jnp.einsum("kj,nja->nka", block, stacked, preferred_element_type=jnp.float32)
    inner = inner.reshape(number, 2, RADIX, RADIX)
    tw_cos, tw_sin = (jnp.asarray(t[:, :RADIX]) for t in twiddle_tables())
    real = inner[:, 0] * tw_cos + inner[:, 1] * tw_sin
    imag = inner[:, 1] * tw_cos - inner[:, 0] * tw_sin
    turned = jnp.stack([real, imag], axis=2).reshape(number, RADIX, 2 * RADIX)
    turned = turned.astype(jnp.bfloat16)
    result = jnp.einsum("lj,nkj->nlk", block, turned, preferred_element_type=jnp.float32)
    spectra = result.reshape(in_count, frame_count, 2, CHANNELS).astype(jnp.bfloat16)
    moved = lax.all_to_all(spectra, "tm", split_axis=3, concat_axis=1, tiled=True)
    moved = lax.all_to_all(moved, "ct", split_axis=3, concat_axis=0, tiled=True)
    local = moved.transpose(3, 2, 0, 1)
    swapped = jnp.stack([local[:, 1], -local[:, 0]], axis=1)
    summed = jnp.einsum(
        "ocjaf,cjbf->ocab",
        jnp.stack([local, swapped], axis=0),
        lax.all_gather(local, "stn", axis=2, tiled=True),
        preferred_element_type=jnp.float32,
    )
    return summed * (1.0 / local.shape[3])


def on_device(voltages, delays):
    if fast_fits(voltages.shape[1], voltages.shape[2] // CHANNELS):
        return fast(voltages, delays)
    return general(voltages, delays)


def solution(mesh):
    return jax.shard_map(
        on_device,
        mesh=mesh,
        in_specs=(P(None, ("stn", "ct"), "tm"), P(("stn", "ct"))),
        out_specs=P(None, ("tm", "ct"), "stn", None),
        check_vma=False,
    )
```
